32 devices in a mesh: parts: 2 (over y), seq: 4 (over z), mp: 2 (over x), rep: 2 (over core).
Axes of the slice: x: 2, y: 2, z: 4, core: 2. Of those that a mesh axis runs over, the one named last changes fastest.
Arguments:
- queries: bfloat16 [6144, 4096], P(('parts', 'seq'), ('mp', 'rep')), parts along dimension 0, may hold values from -110 to 110
- key_weight: bfloat16 [1024, 4096], P(None, ('mp', 'rep')), may hold values from -0.1875 to 0.1875
- value_weight: bfloat16 [1024, 4096], P(None, ('mp', 'rep')), may hold values from -0.1875 to 0.1875
- enc_gain: float32 [1024], P(('mp', 'rep')), may hold values from 0.25 to 1.75
- store: bfloat16 [128, 128, 1024], P(('parts', 'seq'), None, ('mp', 'rep')), parts along dimension 0, may hold values from -330 to 330
- nbr_owner: int32 [96, 2], P(('parts', 'seq')), parts along dimension 0, may hold values from 0 to 3, all different within a row; in each aligned block of 12 rows (0 to 11, 12 to 23, ...) at most 12 rows name the same one
- nbr_slot: int32 [96, 2], P(('parts', 'seq')), parts along dimension 0, may hold values from 0 to 15
- nbr_count: int32 [96], P(('parts', 'seq')), parts along dimension 0, may hold values from 1 to 2
Outputs:
- attended: bfloat16 [6144, 4096], P(('parts', 'seq'), ('mp', 'rep')), parts along dimension 0
The draws below stay inside these ranges and needn't reach their ends.
There are 2 independent parts, one for each index of `parts`. The reference program is written for one: setup_inputs(seed, part) draws one part's arguments, and reference() takes and returns one part's arrays. A program takes and returns all parts, laid end to end along the dimension named above; an argument that names none is the same for every part. Nothing has to cross between parts.
Inputs may be any that keep to these rules, and one draw needn't show every extreme that they name: `nbr_owner`: in each aligned block of 12 stretches no owner is named more than 12 times, and the 2 owners of one stretch differ.
All inputs are finite; a program needn't handle non-finite values.
Results may differ from the reference program's by a relative error of at most 0.0089.
Values may be sent and summed in bfloat16 or wider, within the bound.
No kernel may reach another device: no remote copies, remote signals or barrier semaphores. Data moves between devices by JAX's collectives and lax.ppermute only.
A program may use at most 128 MiB of HBM per device.

```python
import math
import jax
import jax.numpy as jnp
import numpy as np
from jax import lax

HEADS = 32
HEAD_DIM = 128
DE = 1024
NLEN = 128
STRETCH = 64
KMAX = 2
CH_DEV = 12
NB_DEV = 16
CAP = 12
STRETCHES = 48
TOKENS = 3072
ENTRIES = 64
N_SEQ = 4


def draw_queries(key, part):
    key = jax.random.fold_in(key, 11)
    shape = (TOKENS, HEADS * HEAD_DIM)
    return jnp.clip(jax.random.normal(key, shape, jnp.float32), -6.0, 6.0).astype(jnp.bfloat16)


def draw_store(key, part):
    key = jax.random.fold_in(key, 23)
    first, second, third = jax.random.split(key, 3)
    shape = (ENTRIES, NLEN, DE)
    rows = jnp.exp(jax.random.uniform(second, (ENTRIES, NLEN, 1), jnp.float32, 0.0, 2.3))
    ramp = jnp.log(3.0) * jnp.arange(DE, dtype=jnp.float32) / DE
    columns = jnp.exp(ramp + jax.random.uniform(third, (DE,), jnp.float32, -0.35, 0.35))
    noise = jnp.clip(jax.random.normal(first, shape, jnp.float32), -6.0, 6.0)
    return (noise * rows * columns).astype(jnp.bfloat16)


def set_ends(drawn, key, low, high):
    place = [jax.random.randint(jax.random.fold_in(key, axis), (), 0, length) for axis, length in enumerate(drawn.shape)]
    longest = drawn.shape.index(max(drawn.shape))
    beside = place[:longest] + [(place[longest] + 1) % drawn.shape[longest]] + place[longest + 1:]
    return drawn.at[tuple(place)].set(low).at[tuple(beside)].set(high)


def levels(own_key, dims, pieces, smallest, top_value):
    gain = 1.0
    for dim, shards_of in pieces:
        steps = jax.random.uniform(jax.random.fold_in(jax.random.fold_in(own_key, 6), dim), (shards_of,), jnp.float32, smallest / len(pieces), top_value / len(pieces))
        gain = gain * jnp.repeat(jnp.exp(steps), dims[dim] // shards_of).reshape((-1,) + (1,) * (len(dims) - 1 - dim))
    return gain


def assign_block(rng, own, number, rows, number_of, top, bound, slope):
    order = jax.random.permutation(rng, number_of)
    heavy_load, ordinary = load_shares(number_of, rows * top, bound, slope, True), load_shares(number_of, rows * top, bound, slope, False)
    places = jnp.arange(number_of)

    def named(lengths, rotation):
        used = int((lengths > 0).sum())
        fixed = max(1, used // 4)
        shifted = fixed + (places - fixed + rotation * (used - fixed)) % max(1, number_of - fixed)
        return jnp.zeros((number_of,), jnp.int32).at[order[jnp.where(places < fixed, places, shifted)]].set(jnp.asarray(lengths, jnp.int32))

    lengths = jnp.where(number % 4 == 0, named(heavy_load, number // 4), named(ordinary, number - number // 4 - 1))
    mixed = jax.random.permutation(jax.random.fold_in(own, 3), number_of)
    source_of, sink = mixed[0:number_of // 2 * 2:2], mixed[1:number_of // 2 * 2:2]
    slack = jnp.minimum(lengths[source_of] - 1, bound - lengths[sink]) // 2
    slack = jnp.where((source_of == order[0]) | (sink == order[0]) | (lengths[sink] == 0), 0, jnp.maximum(slack, 0))
    shifted = jax.random.randint(jax.random.fold_in(own, 4), (number_of // 2,), 0, 1 << 20) % (slack + 1)
    lengths = lengths.at[source_of].add(-shifted).at[sink].add(shifted)
    labels = jnp.searchsorted(jnp.cumsum(lengths), jnp.arange(rows * top), side="right").astype(jnp.int32)
    listing = labels.reshape(top, rows).T
    listing = listing[jax.random.permutation(jax.random.fold_in(own, 1), rows)]
    rotation = jax.random.randint(jax.random.fold_in(own, 2), (rows, 1), 0, top)
    return jnp.take_along_axis(listing, (jnp.arange(top)[None, :] + rotation) % top, axis=1)


def load_shares(number_of, total, limit, lean, full):
    weights = [(1 << 20) // math.isqrt(grade ** lean) + 1 for grade in range(1, number_of + 1)]
    largest = limit if full else min(limit, max(-(-total // number_of), total * weights[0] // sum(weights)))
    least = 1 if total - largest >= number_of - 1 else 0
    counts, surplus = [largest] + [least] * (number_of - 1), total - largest - least * (number_of - 1)
    while surplus > 0:
        free = [i for i in range(1, number_of) if counts[i] < largest] or [i for i in range(1, number_of) if counts[i] < limit]
        mass, budget = sum([weights[i] for i in free]), surplus
        for i in free:
            more = min(limit - counts[i], max(1, budget * weights[i] // mass), surplus)
            counts[i] = counts[i] + more
            surplus = surplus - more
    return np.array(counts)


def gaussian(own_key, dims, scale, limit, cuts=(), held_as=jnp.bfloat16):
    array = scale * jax.random.normal(own_key, dims, jnp.float32)
    if cuts:
        array = array * levels(own_key, dims, cuts, -0.22, 0.18)
    return jnp.clip(array, -limit, limit).astype(held_as)


def setup_inputs(seed: int = 0, part: int = 0) -> dict:
    seeds = jax.random.split(jax.random.key(seed), 9)
    own_keys = jax.random.split(jax.random.fold_in(seeds[8], part), 9)
    queries = draw_queries(jax.random.fold_in(jax.random.fold_in(seeds[8], part), 71), part)
    key_weight = gaussian(seeds[1], (DE, HEADS * HEAD_DIM), DE ** -0.5, 0.1875, ((1, 4),))
    value_weight = gaussian(seeds[2], (DE, HEADS * HEAD_DIM), DE ** -0.5, 0.1875, ((1, 4),))
    enc_gain = jnp.clip(1.0 + 0.15 * jax.random.normal(seeds[3], (DE,), jnp.float32), 0.25, 1.75)
    store = draw_store(jax.random.fold_in(jax.random.fold_in(seeds[8], part), 71), part)
    nbr_owner_keys = jax.random.split(jax.random.fold_in(own_keys[5], 1), STRETCHES // CH_DEV)
    nbr_owner_turns = jax.random.permutation(jax.random.fold_in(own_keys[5], 3), STRETCHES // CH_DEV)
    nbr_owner = jax.vmap(lambda own, number: assign_block(jax.random.fold_in(own_keys[5], 2), own, number, CH_DEV, N_SEQ, KMAX, CAP, 2))(nbr_owner_keys, nbr_owner_turns).reshape((STRETCHES, KMAX))
    nbr_slot = set_ends(jax.random.randint(own_keys[6], (STRETCHES, KMAX), 0, NB_DEV), jax.random.fold_in(own_keys[6], 1), 0, NB_DEV - 1).astype(jnp.int32)
    nbr_count = set_ends(jax.random.randint(own_keys[7], (STRETCHES,), 1, KMAX + 1), jax.random.fold_in(own_keys[7], 1), 1, KMAX).astype(jnp.int32)
    return {"queries": queries, "key_weight": key_weight, "value_weight": value_weight, "enc_gain": enc_gain, "store": store, "nbr_owner": nbr_owner, "nbr_slot": nbr_slot, "nbr_count": nbr_count}


EPS = 1e-06

def reference(queries, key_weight, value_weight, enc_gain, store, nbr_owner, nbr_slot, nbr_count):
    raw = store.astype(jnp.float32)
    mean_sq = lax.optimization_barrier(jnp.mean(raw * raw, axis=2, keepdims=True))
    normed = (raw * lax.rsqrt(mean_sq + EPS) * enc_gain.astype(jnp.float32)).astype(jnp.bfloat16)
    entry = (nbr_owner * NB_DEV + nbr_slot).astype(jnp.int32)
    kept = jnp.arange(KMAX, dtype=jnp.int32)[None, :] < nbr_count[:, None]
    query_blocks = queries.reshape(STRETCHES, STRETCH, HEADS, HEAD_DIM)
    factor = 1.0 / math.sqrt(HEAD_DIM)

    def one(index):
        states = normed[entry[index]].reshape(KMAX * NLEN, DE)
        keys = jnp.dot(states, key_weight, preferred_element_type=jnp.float32).astype(jnp.bfloat16)
        values = jnp.dot(states, value_weight, preferred_element_type=jnp.float32).astype(jnp.bfloat16)
        keys = keys.reshape(KMAX * NLEN, HEADS, HEAD_DIM).astype(jnp.float32)
        values = values.reshape(KMAX * NLEN, HEADS, HEAD_DIM).astype(jnp.float32)
        query = query_blocks[index + 1].astype(jnp.float32)
        scores = jnp.einsum('qhd,khd->hqk', query, keys) * factor
        allowed = jnp.repeat(kept[index], NLEN)
        scores = jnp.where(allowed[None, None, :], scores, -1e+30)
        top = lax.optimization_barrier(jnp.max(scores, axis=2, keepdims=True))
        expo = jnp.exp(scores - top)
        weights = (expo / lax.optimization_barrier(jnp.sum(expo, axis=2, keepdims=True))).astype(jnp.bfloat16)
        mixed = jnp.einsum('hqk,khd->qhd', weights.astype(jnp.float32), values)
        return mixed.astype(jnp.bfloat16).reshape(STRETCH, HEADS * HEAD_DIM)
    outputs = lax.map(one, jnp.arange(STRETCHES - 1, dtype=jnp.int32))
    first = jnp.zeros((1, STRETCH, HEADS * HEAD_DIM), jnp.bfloat16)
    return jnp.concatenate([first, outputs], axis=0).reshape(TOKENS, HEADS * HEAD_DIM)
```

```python
import math

import jax
import jax.numpy as jnp
from jax import lax
from jax.experimental import pallas as pl
from jax.experimental.pallas import tpu as pltpu
from jax.sharding import PartitionSpec as P

HEAD_DIM = 128
DE = 1024
NLEN = 128
STRETCH = 64
KMAX = 2
EPS = 1e-06

SEQ_SPEC = ("parts", "seq")
FEATURES = ("mp", "rep")
VMEM_LIMIT = 48 * 1024 * 1024


def shifted(value, axis, steps):
    count = lax.axis_size(axis)
    first, last = max(0, -steps), min(count, count - steps)
    return lax.ppermute(value, axis, [(source, source + steps) for source in range(first, last)])


def swapped(value, axis):
    return lax.ppermute(value, axis, [(0, 1), (1, 0)])


def project_kernel(places, gain_ref, *refs):
    *pieces, key_weight, value_weight, keys_out, values_out, normed = refs
    rows = normed.shape[0]
    width = pieces[0].shape[2]
    raw = [piece[...].reshape(rows, width).astype(jnp.float32) for piece in pieces]
    squares = sum(jnp.sum(part * part, axis=1, keepdims=True) for part in raw)
    scale = lax.rsqrt(squares / DE + EPS)
    for index, part in enumerate(raw):
        start = pl.multiple_of(places[index] * width, width)
        normed[:, pl.ds(start, width)] = (part * scale * gain_ref[:, pl.ds(start, width)]).astype(jnp.bfloat16)
    states = normed[...]
    for weight, out in ((key_weight, keys_out), (value_weight, values_out)):
        out[...] = jnp.dot(states, weight[...], preferred_element_type=jnp.float32).astype(jnp.bfloat16).reshape(out.shape)


def project(places, gain, pieces, key_weight, value_weight, group):
    count, tokens, width = pieces[0].shape
    columns = key_weight.shape[1]
    out = jax.ShapeDtypeStruct((count, tokens, columns), jnp.bfloat16)
    piece_spec = pl.BlockSpec((group, tokens, width), lambda i, _: (i, 0, 0))
    weight_spec = pl.BlockSpec((DE, columns), lambda i, _: (0, 0))
    out_spec = pl.BlockSpec((group, tokens, columns), lambda i, _: (i, 0, 0))
    return pl.pallas_call(
        project_kernel,
        out_shape=(out, out),
        grid_spec=pltpu.PrefetchScalarGridSpec(
            num_scalar_prefetch=1,
            grid=(count // group,),
            in_specs=[pl.BlockSpec((1, DE), lambda i, _: (0, 0))] + [piece_spec] * len(pieces) + [weight_spec] * 2,
            out_specs=(out_spec, out_spec),
            scratch_shapes=[pltpu.VMEM((group * tokens, DE), jnp.bfloat16)],
        ),
        compiler_params=pltpu.CompilerParams(vmem_limit_bytes=VMEM_LIMIT),
        cost_estimate=pl.CostEstimate(
            flops=4 * count * tokens * DE * columns,
            bytes_accessed=2 * (count * tokens * (DE + 2 * columns) + 2 * DE * columns),
            transcendentals=0,
        ),
        name="project",
    )(places, gain, *pieces, key_weight, value_weight)


def attend_kernel(slots, counts, query_ref, first_keys, second_keys, first_values, second_values, out_ref):
    stretch = pl.program_id(0)
    count = counts[stretch]

    @pl.when(count == 0)
    def _():
        out_ref[...] = jnp.zeros_like(out_ref)

    @pl.when(count > 0)
    def _():
        columns = query_ref.shape[1]
        span = lax.broadcasted_iota(jnp.int32, (1, KMAX * NLEN), 1)
        allowed = span < count * NLEN
        for head in range(columns // HEAD_DIM):
            part = slice(head * HEAD_DIM, (head + 1) * HEAD_DIM)
            keys = jnp.concatenate([first_keys[0, :, part], second_keys[0, :, part]], axis=0)
            values = jnp.concatenate([first_values[0, :, part], second_values[0, :, part]], axis=0)
            scores = lax.dot_general(
                query_ref[:, part], keys, (((1,), (1,)), ((), ())), preferred_element_type=jnp.float32
            ) * (1.0 / math.sqrt(HEAD_DIM))
            scores = jnp.where(allowed, scores, -1e30)
            expo = jnp.exp(scores - jnp.max(scores, axis=1, keepdims=True))
            weights = (expo / jnp.sum(expo, axis=1, keepdims=True)).astype(jnp.bfloat16)
            out_ref[:, part] = jnp.dot(weights, values, preferred_element_type=jnp.float32).astype(jnp.bfloat16)


def attend(slots, counts, queries, keys, values):
    stretches = counts.shape[0]
    columns = queries.shape[1]

    def entry(k):
        return pl.BlockSpec((1, NLEN, columns), lambda i, slots, _: (slots[i * KMAX + k], 0, 0))

    query_spec = pl.BlockSpec((STRETCH, columns), lambda i, *_: (i, 0))
    return pl.pallas_call(
        attend_kernel,
        out_shape=jax.ShapeDtypeStruct(queries.shape, jnp.bfloat16),
        grid_spec=pltpu.PrefetchScalarGridSpec(
            num_scalar_prefetch=2,
            grid=(stretches,),
            in_specs=[query_spec, entry(0), entry(1), entry(0), entry(1)],
            out_specs=query_spec,
        ),
        compiler_params=pltpu.CompilerParams(vmem_limit_bytes=VMEM_LIMIT),
        cost_estimate=pl.CostEstimate(
            flops=4 * stretches * STRETCH * KMAX * NLEN * columns,
            bytes_accessed=4 * stretches * columns * (STRETCH + KMAX * NLEN),
            transcendentals=stretches * STRETCH * KMAX * NLEN * columns // HEAD_DIM,
        ),
        name="attend",
    )(slots, counts, queries, keys, keys, values, values)


def previous_rows(nbr_owner, nbr_slot, nbr_count):
    rows = jnp.concatenate([nbr_owner, nbr_slot, nbr_count[:, None]], axis=1)
    rows = jnp.concatenate([shifted(rows[-1:], "seq", 1), rows[:-1]], axis=0)
    return rows[:, :KMAX], rows[:, KMAX : 2 * KMAX], rows[:, 2 * KMAX]


def fetch_by_request(store, owners, slots):
    owners_axis = lax.axis_size("seq")
    stretches = owners.shape[0]
    depth = min(stretches, max(2, 2 * stretches * KMAX // owners_axis) + 1)
    owners, slots = owners.reshape(-1), slots.reshape(-1)
    order = jnp.arange(owners.shape[0], dtype=jnp.int32)
    before = (owners[:, None] == owners[None, :]) & (order[None, :] < order[:, None])
    target = owners * depth + jnp.sum(before.astype(jnp.int32), axis=1)
    hits = target[:, None] == jnp.arange(owners_axis * depth, dtype=jnp.int32)[None, :]
    table = jnp.sum(jnp.where(hits, slots[:, None], 0), axis=0).reshape(owners_axis, depth)
    asked = lax.all_to_all(table, "seq", split_axis=0, concat_axis=0, tiled=True)
    arrived = lax.all_to_all(store[asked], "seq", split_axis=0, concat_axis=0, tiled=True)
    fetched = arrived.reshape(owners_axis * depth, NLEN, store.shape[2])[target]
    return [lax.all_gather(fetched, FEATURES, axis=2, tiled=True)], jnp.zeros((1,), jnp.int32)


def fetch_all(store, owners, slots):
    seq = lax.axis_index("seq")
    size = lax.axis_size("seq")
    everything = [store]
    for distance in range(1, size):
        for steps in (distance, -distance):
            everything.append(shifted(store, "seq", steps))
    ahead = owners - seq
    place = jnp.where(ahead == 0, 0, jnp.where(ahead < 0, -2 * ahead - 1, 2 * ahead))
    pool = jnp.concatenate(everything, axis=0)
    mine = pool[(place * store.shape[0] + slots).reshape(-1)]
    across = swapped(mine, "mp")
    pieces = [mine, swapped(mine, "rep"), across, swapped(across, "rep")]
    block = 2 * lax.axis_index("mp") + lax.axis_index("rep")
    return pieces, jnp.stack([block, block ^ 1, block ^ 2, block ^ 3]).astype(jnp.int32)


def body(queries, key_weight, value_weight, enc_gain, store, nbr_owner, nbr_slot, nbr_count):
    stretches = nbr_owner.shape[0]
    gain = lax.all_gather(enc_gain, FEATURES, axis=0, tiled=True)[None]
    owners, slots, counts = previous_rows(nbr_owner, nbr_slot, nbr_count)
    small = lax.axis_size("seq") <= 4 and lax.axis_size("mp") == 2 and lax.axis_size("rep") == 2
    pieces, places = (fetch_all if small else fetch_by_request)(store, owners, slots)
    keys, values = project(places, gain, pieces, key_weight, value_weight, 4)
    order = jnp.arange(stretches * KMAX, dtype=jnp.int32)
    return attend(order, counts, queries, keys, values)


def solution(mesh):
    in_specs = (
        P(SEQ_SPEC, FEATURES),
        P(None, FEATURES),
        P(None, FEATURES),
        P(FEATURES),
        P(SEQ_SPEC, None, FEATURES),
        P(SEQ_SPEC, None),
        P(SEQ_SPEC, None),
        P(SEQ_SPEC),
    )
    out_specs = P(SEQ_SPEC, FEATURES)
    return jax.shard_map(body, mesh=mesh, in_specs=in_specs, out_specs=out_specs, check_vma=False)
```

```python
import math

import jax
import jax.numpy as jnp
from jax import lax
from jax.experimental import pallas as pl
from jax.experimental.pallas import tpu as pltpu
from jax.sharding import PartitionSpec as P

HEAD_DIM = 128
DE = 1024
NLEN = 128
STRETCH = 64
KMAX = 2
EPS = 1e-06

SEQ_SPEC = ("parts", "seq")
FEATURES = ("mp", "rep")
VMEM_LIMIT = 48 * 1024 * 1024

CHIPS = 4
ENTRIES_EACH = 16
AHEAD = 8
ROUNDS = 3
CAP = 6
FIRST_ROUND = ENTRIES_EACH + 2 * AHEAD
LANES = 128


def shifted(value, axis, steps):
    count = lax.axis_size(axis)
    first, last = max(0, -steps), min(count, count - steps)
    return lax.ppermute(value, axis, [(source, source + steps) for source in range(first, last)])


def swapped(value, axis):
    return lax.ppermute(value, axis, [(0, 1), (1, 0)])


def project_kernel(gain_ref, *refs, held):
    *pieces, key_weight, value_weight = refs[: len(refs) - 3 - held]
    keys_out, values_out, normed = refs[-3:]
    rows = normed.shape[0]
    width = pieces[0].shape[2]
    raw = [piece[...].reshape(rows, width).astype(jnp.float32) for piece in pieces]
    squares = sum(jnp.sum(part * part, axis=1, keepdims=True) for part in raw)
    scale = lax.rsqrt(squares / DE + EPS)
    for index, part in enumerate(raw):
        place = slice(index * width, (index + 1) * width)
        normed[:, place] = (part * scale * gain_ref[:, place]).astype(jnp.bfloat16)
    states = normed[...]
    for weight, out in ((key_weight, keys_out), (value_weight, values_out)):
        out[...] = jnp.dot(states, weight[...], preferred_element_type=jnp.float32).astype(jnp.bfloat16).reshape(out.shape)


def project(gain, pieces, key_weight, value_weight, group, total, first=0, held=()):
    count, tokens, width = pieces[0].shape
    columns = key_weight.shape[1]
    out = jax.ShapeDtypeStruct((total, tokens, columns), jnp.bfloat16)
    piece_spec = pl.BlockSpec((group, tokens, width), lambda i: (i, 0, 0))
    weight_spec = pl.BlockSpec((DE, columns), lambda i: (0, 0))
    out_spec = pl.BlockSpec((group, tokens, columns), lambda i: (i + first // group, 0, 0))
    operands = (gain, *pieces, key_weight, value_weight, *held)

    def kernel(*refs):
        project_kernel(*refs, held=len(held))

    return pl.pallas_call(
        kernel,
        out_shape=(out, out),
        grid=(count // group,),
        in_specs=[pl.BlockSpec((1, DE), lambda i: (0, 0))]
        + [piece_spec] * len(pieces)
        + [weight_spec] * 2
        + [pl.BlockSpec(memory_space=pl.ANY)] * len(held),
        out_specs=(out_spec, out_spec),
        scratch_shapes=[pltpu.VMEM((group * tokens, DE), jnp.bfloat16)],
        input_output_aliases={len(operands) - len(held) + i: i for i in range(len(held))},
        compiler_params=pltpu.CompilerParams(vmem_limit_bytes=VMEM_LIMIT),
        cost_estimate=pl.CostEstimate(
            flops=4 * count * tokens * DE * columns,
            bytes_accessed=2 * (count * tokens * (DE + 2 * columns) + 2 * DE * columns),
            transcendentals=0,
        ),
        name="project",
    )(*operands)


SAME_COLUMNS = (((1,), (1,)), ((), ()))
SAME_ROWS = (((0,), (0,)), ((), ()))


def attend_stretch(query_ref, keys, values, out_ref):
    wide = 2 * HEAD_DIM
    factor = math.log2(math.e) / math.sqrt(HEAD_DIM)
    parts = [slice(start, start + wide) for start in range(0, query_ref.shape[1], wide)]
    scores = []
    for part in parts:
        query = query_ref[:, part]
        left, right = query[:, :HEAD_DIM], query[:, HEAD_DIM:]
        zero = jnp.zeros_like(left)
        both = jnp.concatenate([jnp.concatenate([left, zero], 1), jnp.concatenate([zero, right], 1)], 0)
        scores.append(
            [lax.dot_general(k[0, :, part], both, SAME_COLUMNS, preferred_element_type=jnp.float32) for k in keys]
        )
    weights = []
    for blocks in scores:
        top = blocks[0].max(0, keepdims=True)
        for block in blocks[1:]:
            top = jnp.maximum(top, block.max(0, keepdims=True))
        expo = [jnp.exp2((block - top) * factor) for block in blocks]
        share = 1.0 / sum(block.sum(0, keepdims=True) for block in expo)
        weights.append([(block * share).astype(jnp.bfloat16) for block in expo])
    for part, blocks in zip(parts, weights):
        mixed = sum(
            lax.dot_general(block, v[0, :, part], SAME_ROWS, preferred_element_type=jnp.float32)
            for block, v in zip(blocks, values)
        )
        middle = part.start + HEAD_DIM
        out_ref[:, part.start : middle] = mixed[:STRETCH, :HEAD_DIM].astype(jnp.bfloat16)
        out_ref[:, middle : part.stop] = mixed[STRETCH:, HEAD_DIM:].astype(jnp.bfloat16)


def attend_kernel(slots, counts, query_ref, first_keys, second_keys, first_values, second_values, out_ref):
    count = counts[pl.program_id(0)]

    @pl.when(count == 0)
    def _():
        out_ref[...] = jnp.zeros_like(out_ref)

    @pl.when(count == 1)
    def _():
        attend_stretch(query_ref, [first_keys], [first_values], out_ref)

    @pl.when(count == 2)
    def _():
        attend_stretch(query_ref, [first_keys, second_keys], [first_values, second_values], out_ref)


def attend(slots, counts, queries, keys, values):
    stretches = counts.shape[0]
    columns = queries.shape[1]

    def entry(k):
        return pl.BlockSpec((1, NLEN, columns), lambda i, slots, _: (slots[i * KMAX + k], 0, 0))

    query_spec = pl.BlockSpec((STRETCH, columns), lambda i, *_: (i, 0))
    return pl.pallas_call(
        attend_kernel,
        out_shape=jax.ShapeDtypeStruct(queries.shape, jnp.bfloat16),
        grid_spec=pltpu.PrefetchScalarGridSpec(
            num_scalar_prefetch=2,
            grid=(stretches,),
            in_specs=[query_spec, entry(0), entry(1), entry(0), entry(1)],
            out_specs=query_spec,
        ),
        compiler_params=pltpu.CompilerParams(vmem_limit_bytes=VMEM_LIMIT),
        cost_estimate=pl.CostEstimate(
            flops=8 * stretches * STRETCH * KMAX * NLEN * columns,
            bytes_accessed=4 * stretches * columns * (STRETCH + KMAX * NLEN),
            transcendentals=stretches * STRETCH * KMAX * NLEN * columns // HEAD_DIM,
        ),
        name="attend",
    )(slots, counts, queries, keys, keys, values, values)


def plan_kernel(place, table, plan_ref, far_ref, loc_ref, lists_ref, need_ref, where_ref, picks_ref, slots_ref):
    f32 = jnp.float32
    rows, groups = 4 * CHIPS, 2 * CHIPS
    me = place[0]
    each = table.shape[0] // groups
    lane = lax.broadcasted_iota(jnp.int32, (1, LANES), 1)

    bases = []
    for group in range(groups):
        offset = jnp.bitwise_xor(me, group)
        bases.append(((offset & 1) + ((offset >> 2) & 1) * 2 + ((offset >> 1) & 1) * 4) * each)
    need = []
    for group in range(groups):
        wanted = [bases[group] + j for j in range(each - KMAX)]
        if group % CHIPS > 0:
            wanted += [bases[group - 1] + each - KMAX + k for k in range(KMAX)]
        hit = jnp.zeros((1, LANES), f32)
        for index in wanted:
            hit = jnp.where(lane == table[index], 1.0, hit)
        need.append(hit)
        need_ref[group : group + 1, :] = hit
    for part in range(2):
        for down in range(2):
            for chip in range(CHIPS):
                reach = jnp.zeros((1, LANES), f32)
                for hops in range(1, CHIPS):
                    to = chip - hops if down else chip + hops
                    if 0 <= to < CHIPS:
                        reach = jnp.where(need[part * CHIPS + to] > 0, float(hops), reach)
                behind = lane >= chip * ENTRIES_EACH if down else lane < (chip + 1) * ENTRIES_EACH
                row = part * 2 * CHIPS + down * CHIPS + chip
                far_ref[row : row + 1, :] = jnp.where(behind, reach, 0.0)

    row = lax.broadcasted_iota(jnp.int32, (rows, LANES), 0)
    entry = lax.broadcasted_iota(jnp.int32, (rows, LANES), 1)
    chip, down = row & (CHIPS - 1), (row >> 2) & 1
    owner, slot = entry >> 4, entry & (ENTRIES_EACH - 1)
    source = jnp.where(down == 1, chip + 1, chip - 1)
    early = slot < AHEAD
    loc = jnp.where(
        owner == chip,
        slot,
        jnp.where((owner == source) & (owner < CHIPS) & early, ENTRIES_EACH + down * AHEAD + slot, -1),
    ).astype(f32)
    sent = jnp.where((owner == chip) & early, 1.0, 0.0)
    far = far_ref[...]
    needed = need_ref[...]
    swept = jnp.zeros((groups, LANES), f32)
    slot_of = jnp.zeros((groups, LANES), f32)
    lists = jnp.zeros((rows, LANES), f32)
    picks = jnp.zeros((groups, LANES), f32)
    one, two = lax.broadcasted_iota(jnp.int32, (LANES, LANES), 0), lax.broadcasted_iota(jnp.int32, (LANES, LANES), 1)
    earlier = jnp.where(one < two, 1.0, 0.0).astype(jnp.bfloat16)
    to, source = lax.broadcasted_iota(jnp.int32, (rows, rows), 0), lax.broadcasted_iota(jnp.int32, (rows, rows), 1)
    up_step = ((to >> 2) & 1 == 0) & (to & 3 > 0) & (source == to - 1)
    down_step = ((to >> 2) & 1 == 1) & (to & 3 < 3) & (source == to + 1)
    step = jnp.where(up_step | down_step, 1.0, 0.0).astype(jnp.bfloat16)
    entry_lane = entry[:groups]

    def ranked(mask):
        return jnp.dot(mask.astype(jnp.bfloat16), earlier, preferred_element_type=f32)

    for number in range(ROUNDS + 1):
        loc_ref[...] = loc
        for part in range(2):
            top = part * 2 * CHIPS
            where_ref[part * CHIPS : (part + 1) * CHIPS, :] = jnp.maximum(
                loc_ref[top : top + CHIPS, :], loc_ref[top + CHIPS : top + 2 * CHIPS, :]
            )
        held = where_ref[...]
        ready = jnp.where((needed > 0) & (held >= 0) & (swept == 0), 1.0, 0.0)
        rank = ranked(ready)
        taken = jnp.where((ready > 0) & (rank < CAP), 1.0, 0.0)
        swept = swept + taken
        slot_of = slot_of + taken * (rank + number * CAP)
        for b in range(CAP):
            pick = jnp.sum(jnp.where((taken > 0) & (rank == b), held, 0.0), axis=1, keepdims=True)
            picks = jnp.where(entry_lane == number * CAP + b, pick, picks)
        if number == ROUNDS:
            break
        ready = jnp.where((far > 0) & (loc >= 0) & (sent == 0), 1.0, 0.0)
        rank = jnp.zeros((rows, LANES), f32)
        above = jnp.zeros((rows, 1), f32)
        for hops in range(CHIPS - 1, 0, -1):
            level = jnp.where(far == hops, ready, 0.0)
            rank = jnp.where(far == hops, ranked(level) + above, rank)
            above = above + jnp.sum(level, axis=1, keepdims=True)
        taken = jnp.where((ready > 0) & (rank < CAP), 1.0, 0.0)
        sent = sent + taken
        for b in range(CAP):
            pick = jnp.sum(jnp.where((taken > 0) & (rank == b), loc, 0.0), axis=1, keepdims=True)
            lists = jnp.where(entry == number * CAP + b, pick, lists)
        came = jnp.dot(step, (taken * (rank + 1)).astype(jnp.bfloat16), preferred_element_type=f32)
        base = FIRST_ROUND + number * 2 * CAP + down * CAP - 1
        loc = jnp.where(came > 0, came + base.astype(f32), loc)
    lists_ref[...] = lists
    picks_ref[...] = picks
    slots_ref[...] = slot_of
    missing = jnp.sum(jnp.where((far > 0) & (sent == 0), 1.0, 0.0)) + jnp.sum(
        jnp.where((needed > 0) & (swept == 0), 1.0, 0.0)
    )
    mine = (me >> 2) * 2 * CHIPS + (me & 3)
    plan_ref[...] = jnp.zeros(plan_ref.shape, jnp.int32)
    plan_ref[0:1, :] = lists_ref[pl.ds(mine, 1), :].astype(jnp.int32)
    plan_ref[1:2, :] = lists_ref[pl.ds(mine + CHIPS, 1), :].astype(jnp.int32)
    plan_ref[2:3, :] = picks_ref[pl.ds(me, 1), :].astype(jnp.int32)
    plan_ref[3:4, :] = slots_ref[pl.ds(me, 1), :].astype(jnp.int32)
    plan_ref[4:5, :] = jnp.full((1, LANES), missing, f32).astype(jnp.int32)


def make_plan(place, table):
    rows, groups = 4 * CHIPS, 2 * CHIPS
    tall, short = pltpu.VMEM((rows, LANES), jnp.float32), pltpu.VMEM((groups, LANES), jnp.float32)
    return pl.pallas_call(
        plan_kernel,
        out_shape=jax.ShapeDtypeStruct((8, LANES), jnp.int32),
        in_specs=[pl.BlockSpec(memory_space=pltpu.SMEM)] * 2,
        out_specs=pl.BlockSpec(memory_space=pltpu.VMEM),
        scratch_shapes=[tall, tall, tall, short, short, short, short],
        name="plan",
    )(place, table)


def pack(plan, number, pool):
    kinds = 3 if number < ROUNDS else 1
    starts = [0]
    for array in pool:
        starts.append(starts[-1] + array.shape[0])

    def kernel(plan_ref, *refs):
        sources, outs, sems = refs[: len(pool)], refs[len(pool) : -1], refs[-1]
        for kind, out in enumerate(outs):
            line = kind + 3 - kinds
            for b in range(CAP):
                at = plan_ref[line * LANES + number * CAP + b]
                for source, low, high in zip(sources, starts, starts[1:]):

                    @pl.when((at >= low) & (at < high))
                    def _(source=source, low=low, out=out, b=b, at=at, sem=sems.at[kind * CAP + b]):
                        pltpu.make_async_copy(source.at[at - low], out.at[b], sem).start()

        for kind, out in enumerate(outs):
            for b in range(CAP):
                pltpu.make_async_copy(sources[0].at[0], out.at[b], sems.at[kind * CAP + b]).wait()

    shape = jax.ShapeDtypeStruct((CAP,) + pool[0].shape[1:], pool[0].dtype)
    return pl.pallas_call(
        kernel,
        out_shape=(shape,) * kinds,
        grid_spec=pltpu.PrefetchScalarGridSpec(
            num_scalar_prefetch=1,
            in_specs=[pl.BlockSpec(memory_space=pl.ANY)] * len(pool),
            out_specs=(pl.BlockSpec(memory_space=pl.ANY),) * kinds,
            scratch_shapes=[pltpu.SemaphoreType.DMA((kinds * CAP,))],
        ),
        cost_estimate=pl.CostEstimate(flops=0, bytes_accessed=kinds * CAP * 2 * 65536, transcendentals=0),
        name="pack",
    )(plan, *pool)


def previous_rows(nbr_owner, nbr_slot, nbr_count):
    rows = jnp.concatenate([nbr_owner, nbr_slot, nbr_count[:, None]], axis=1)
    rows = jnp.concatenate([shifted(rows[-1:], "seq", 1), rows[:-1]], axis=0)
    return rows[:, :KMAX], rows[:, KMAX : 2 * KMAX], rows[:, 2 * KMAX]


def fetch_by_request(store, owners, slots):
    owners_axis = lax.axis_size("seq")
    stretches = owners.shape[0]
    depth = min(stretches, max(2, 2 * stretches * KMAX // owners_axis) + 1)
    owners, slots = owners.reshape(-1), slots.reshape(-1)
    order = jnp.arange(owners.shape[0], dtype=jnp.int32)
    before = (owners[:, None] == owners[None, :]) & (order[None, :] < order[:, None])
    target = owners * depth + jnp.sum(before.astype(jnp.int32), axis=1)
    hits = target[:, None] == jnp.arange(owners_axis * depth, dtype=jnp.int32)[None, :]
    table = jnp.sum(jnp.where(hits, slots[:, None], 0), axis=0).reshape(owners_axis, depth)
    asked = lax.all_to_all(table, "seq", split_axis=0, concat_axis=0, tiled=True)
    arrived = lax.all_to_all(store[asked], "seq", split_axis=0, concat_axis=0, tiled=True)
    fetched = arrived.reshape(owners_axis * depth, NLEN, store.shape[2])[target]
    return lax.all_gather(fetched, FEATURES, axis=2, tiled=True)


def four_pieces(value):
    across = swapped(value, "mp")
    return [value, swapped(value, "rep"), across, swapped(across, "rep")]


def fetch_all(store, owners, slots):
    seq = lax.axis_index("seq")
    everything = [store]
    for distance in range(1, lax.axis_size("seq")):
        for steps in (distance, -distance):
            everything.append(shifted(store, "seq", steps))
    ahead = owners - seq
    place = jnp.where(ahead == 0, 0, jnp.where(ahead < 0, -2 * ahead - 1, 2 * ahead))
    pool = jnp.concatenate(everything, axis=0)
    return pool[(place * store.shape[0] + slots).reshape(-1)]


def in_order_of_pieces(weight):
    block = 2 * lax.axis_index("mp") + lax.axis_index("rep")
    width = DE // 4
    return jnp.concatenate([lax.dynamic_slice_in_dim(weight, (block ^ i) * width, width, 0) for i in range(4)], axis=0)


def exchanged_table(codes):
    groups = 2 * CHIPS

    def by_offset(value, offset):
        return lax.ppermute(value, SEQ_SPEC, [(group, group ^ offset) for group in range(groups)])

    near = jnp.stack([codes] + [by_offset(codes, offset) for offset in (1, 4, 5)])
    return jnp.concatenate([near, by_offset(near, 2)], axis=0)


def streamed(queries, key_weight, value_weight, enc_gain, store, nbr_owner, nbr_slot, nbr_count):
    stretches = nbr_owner.shape[0]
    total = stretches * KMAX
    seq = lax.axis_index("seq")
    me = lax.axis_index("parts") * CHIPS + seq
    kept = jnp.arange(KMAX, dtype=jnp.int32)[None, :] < nbr_count[:, None]
    codes = jnp.where(kept, nbr_owner * ENTRIES_EACH + nbr_slot, -1).reshape(-1)
    table = exchanged_table(codes)
    early_up, early_down = shifted(store[:AHEAD], "seq", 1), shifted(store[:AHEAD], "seq", -1)
    plan = make_plan(me.reshape(1).astype(jnp.int32), table.reshape(-1)).reshape(-1)
    missing = plan[4 * LANES]

    offset = jnp.where(seq > 0, (seq ^ (seq - 1)) & 3, 0)
    behind = table[(offset & 1) + ((offset >> 1) & 1) * 4]
    asked = jnp.concatenate([jnp.where(seq > 0, behind[total - KMAX :], -1), codes[: total - KMAX]])
    asked = asked.reshape(stretches, KMAX)
    counts = jnp.sum((asked >= 0).astype(jnp.int32), axis=1)
    first = jnp.maximum(asked[:, 0], 0)
    asked = jnp.stack([first, jnp.where(asked[:, 1] >= 0, asked[:, 1], first)], axis=1).reshape(-1)

    gain = jnp.concatenate(four_pieces(enc_gain[None]), axis=1)
    key_weight, value_weight = in_order_of_pieces(key_weight), in_order_of_pieces(value_weight)

    def planned():
        slots = plan[3 * LANES : 4 * LANES][asked]
        pool = [store, early_up, early_down]
        held = ()
        for number in range(ROUNDS + 1):
            *ways, mine = pack(plan, number, pool)
            if ways:
                pool += [shifted(ways[0], "seq", 1), shifted(ways[1], "seq", -1)]
            held = project(gain, four_pieces(mine), key_weight, value_weight, 3, total, number * CAP, held)
        return attend(slots, counts, queries, *held)

    def whole():
        mine = fetch_all(store, asked >> 4, asked & (ENTRIES_EACH - 1))
        keys, values = project(gain, four_pieces(mine), key_weight, value_weight, 4, total)
        return attend(jnp.arange(total, dtype=jnp.int32), counts, queries, keys, values)

    return lax.cond(missing == 0, planned, whole)


def requested(queries, key_weight, value_weight, enc_gain, store, nbr_owner, nbr_slot, nbr_count):
    gain = lax.all_gather(enc_gain, FEATURES, axis=0, tiled=True)[None]
    owners, slots, counts = previous_rows(nbr_owner, nbr_slot, nbr_count)
    total = owners.size
    pieces = [fetch_by_request(store, owners, slots)]
    keys, values = project(gain, pieces, key_weight, value_weight, 4, total)
    return attend(jnp.arange(total, dtype=jnp.int32), counts, queries, keys, values)


def solution(mesh):
    in_specs = (
        P(SEQ_SPEC, FEATURES),
        P(None, FEATURES),
        P(None, FEATURES),
        P(FEATURES),
        P(SEQ_SPEC, None, FEATURES),
        P(SEQ_SPEC, None),
        P(SEQ_SPEC, None),
        P(SEQ_SPEC),
    )
    out_specs = P(SEQ_SPEC, FEATURES)
    shape = dict(mesh.shape)
    small = shape == {"parts": 2, "seq": CHIPS, "mp": 2, "rep": 2}
    body = streamed if small else requested
    return jax.shard_map(body, mesh=mesh, in_specs=in_specs, out_specs=out_specs, check_vma=False)
```

```python
import math

import jax
import jax.numpy as jnp
from jax import lax
from jax.experimental import pallas as pl
from jax.experimental.pallas import tpu as pltpu
from jax.sharding import PartitionSpec as P

HEAD_DIM = 128
DE = 1024
NLEN = 128
STRETCH = 64
KMAX = 2
EPS = 1e-06

SEQ_SPEC = ("parts", "seq")
FEATURES = ("mp", "rep")
VMEM_LIMIT = 48 * 1024 * 1024

CHIPS = 4
ENTRIES_EACH = 16
AHEAD = 8
ROUNDS = 3
CAP = 6
FIRST_ROUND = ENTRIES_EACH + 2 * AHEAD
LANES = 128


def shifted(value, axis, steps):
    count = lax.axis_size(axis)
    first, last = max(0, -steps), min(count, count - steps)
    return lax.ppermute(value, axis, [(source, source + steps) for source in range(first, last)])


def swapped(value, axis):
    return lax.ppermute(value, axis, [(0, 1), (1, 0)])


def project_kernel(gain_ref, *refs, held):
    *pieces, key_weight, value_weight = refs[: len(refs) - 3 - held]
    keys_out, values_out, normed = refs[-3:]
    rows = normed.shape[0]
    width = pieces[0].shape[2]
    raw = [piece[...].reshape(rows, width).astype(jnp.float32) for piece in pieces]
    squares = sum(jnp.sum(part * part, axis=1, keepdims=True) for part in raw)
    scale = lax.rsqrt(squares / DE + EPS)
    for index, part in enumerate(raw):
        place = slice(index * width, (index + 1) * width)
        normed[:, place] = (part * scale * gain_ref[:, place]).astype(jnp.bfloat16)
    states = normed[...]
    for weight, out in ((key_weight, keys_out), (value_weight, values_out)):
        out[...] = jnp.dot(states, weight[...], preferred_element_type=jnp.float32).astype(jnp.bfloat16).reshape(out.shape)


def project(gain, pieces, key_weight, value_weight, group, total, first=0, held=()):
    count, tokens, width = pieces[0].shape
    columns = key_weight.shape[1]
    out = jax.ShapeDtypeStruct((total, tokens, columns), jnp.bfloat16)
    piece_spec = pl.BlockSpec((group, tokens, width), lambda i: (i, 0, 0))
    weight_spec = pl.BlockSpec((DE, columns), lambda i: (0, 0))
    out_spec = pl.BlockSpec((group, tokens, columns), lambda i: (i + first // group, 0, 0))
    operands = (gain, *pieces, key_weight, value_weight, *held)

    def kernel(*refs):
        project_kernel(*refs, held=len(held))

    return pl.pallas_call(
        kernel,
        out_shape=(out, out),
        grid=(count // group,),
        in_specs=[pl.BlockSpec((1, DE), lambda i: (0, 0))]
        + [piece_spec] * len(pieces)
        + [weight_spec] * 2
        + [pl.BlockSpec(memory_space=pl.ANY)] * len(held),
        out_specs=(out_spec, out_spec),
        scratch_shapes=[pltpu.VMEM((group * tokens, DE), jnp.bfloat16)],
        input_output_aliases={len(operands) - len(held) + i: i for i in range(len(held))},
        compiler_params=pltpu.CompilerParams(vmem_limit_bytes=VMEM_LIMIT),
        cost_estimate=pl.CostEstimate(
            flops=4 * count * tokens * DE * columns,
            bytes_accessed=2 * (count * tokens * (DE + 2 * columns) + 2 * DE * columns),
            transcendentals=0,
        ),
        name="project",
    )(*operands)


SAME_COLUMNS = (((1,), (1,)), ((), ()))
SAME_ROWS = (((0,), (0,)), ((), ()))


def attend_stretch(query_ref, keys, values, out_ref):
    wide = 2 * HEAD_DIM
    factor = math.log2(math.e) / math.sqrt(HEAD_DIM)
    parts = [slice(start, start + wide) for start in range(0, query_ref.shape[1], wide)]
    scores = []
    for part in parts:
        query = query_ref[:, part]
        left, right = query[:, :HEAD_DIM], query[:, HEAD_DIM:]
        zero = jnp.zeros_like(left)
        both = jnp.concatenate([jnp.concatenate([left, zero], 1), jnp.concatenate([zero, right], 1)], 0)
        scores.append(
            [lax.dot_general(k[0, :, part], both, SAME_COLUMNS, preferred_element_type=jnp.float32) for k in keys]
        )
    weights = []
    for blocks in scores:
        top = blocks[0].max(0, keepdims=True)
        for block in blocks[1:]:
            top = jnp.maximum(top, block.max(0, keepdims=True))
        expo = [jnp.exp2((block - top) * factor) for block in blocks]
        share = 1.0 / sum(block.sum(0, keepdims=True) for block in expo)
        weights.append([(block * share).astype(jnp.bfloat16) for block in expo])
    for part, blocks in zip(parts, weights):
        mixed = sum(
            lax.dot_general(block, v[0, :, part], SAME_ROWS, preferred_element_type=jnp.float32)
            for block, v in zip(blocks, values)
        )
        middle = part.start + HEAD_DIM
        out_ref[:, part.start : middle] = mixed[:STRETCH, :HEAD_DIM].astype(jnp.bfloat16)
        out_ref[:, middle : part.stop] = mixed[STRETCH:, HEAD_DIM:].astype(jnp.bfloat16)


def attend_kernel(slots, counts, query_ref, first_keys, second_keys, first_values, second_values, out_ref):
    count = counts[pl.program_id(0)]

    @pl.when(count == 0)
    def _():
        out_ref[...] = jnp.zeros_like(out_ref)

    @pl.when(count == 1)
    def _():
        attend_stretch(query_ref, [first_keys], [first_values], out_ref)

    @pl.when(count == 2)
    def _():
        attend_stretch(query_ref, [first_keys, second_keys], [first_values, second_values], out_ref)


def attend(slots, counts, queries, keys, values):
    stretches = counts.shape[0]
    columns = queries.shape[1]

    def entry(k):
        return pl.BlockSpec((1, NLEN, columns), lambda i, slots, _: (slots[i * KMAX + k], 0, 0))

    query_spec = pl.BlockSpec((STRETCH, columns), lambda i, *_: (i, 0))
    return pl.pallas_call(
        attend_kernel,
        out_shape=jax.ShapeDtypeStruct(queries.shape, jnp.bfloat16),
        grid_spec=pltpu.PrefetchScalarGridSpec(
            num_scalar_prefetch=2,
            grid=(stretches,),
            in_specs=[query_spec, entry(0), entry(1), entry(0), entry(1)],
            out_specs=query_spec,
        ),
        compiler_params=pltpu.CompilerParams(vmem_limit_bytes=VMEM_LIMIT),
        cost_estimate=pl.CostEstimate(
            flops=8 * stretches * STRETCH * KMAX * NLEN * columns,
            bytes_accessed=4 * stretches * columns * (STRETCH + KMAX * NLEN),
            transcendentals=stretches * STRETCH * KMAX * NLEN * columns // HEAD_DIM,
        ),
        name="attend",
    )(slots, counts, queries, keys, keys, values, values)


def plan_kernel(place, table, plan_ref, far_ref, loc_ref, lists_ref, need_ref, where_ref, picks_ref, slots_ref):
    f32 = jnp.float32
    rows, groups = 4 * CHIPS, 2 * CHIPS
    me = place[0]
    each = table.shape[0] // groups
    lane = lax.broadcasted_iota(jnp.int32, (1, LANES), 1)

    bases = []
    for group in range(groups):
        offset = jnp.bitwise_xor(me, group)
        bases.append(offset * each)
    need = []
    for group in range(groups):
        wanted = [bases[group] + j for j in range(each - KMAX)]
        if group % CHIPS > 0:
            wanted += [bases[group - 1] + each - KMAX + k for k in range(KMAX)]
        hit = jnp.zeros((1, LANES), f32)
        for index in wanted:
            hit = jnp.where(lane == table[index], 1.0, hit)
        need.append(hit)
        need_ref[group : group + 1, :] = hit
    for part in range(2):
        for down in range(2):
            for chip in range(CHIPS):
                reach = jnp.zeros((1, LANES), f32)
                for hops in range(1, CHIPS):
                    to = chip - hops if down else chip + hops
                    if 0 <= to < CHIPS:
                        reach = jnp.where(need[part * CHIPS + to] > 0, float(hops), reach)
                behind = lane >= chip * ENTRIES_EACH if down else lane < (chip + 1) * ENTRIES_EACH
                row = part * 2 * CHIPS + down * CHIPS + chip
                far_ref[row : row + 1, :] = jnp.where(behind, reach, 0.0)

    row = lax.broadcasted_iota(jnp.int32, (rows, LANES), 0)
    entry = lax.broadcasted_iota(jnp.int32, (rows, LANES), 1)
    chip, down = row & (CHIPS - 1), (row >> 2) & 1
    owner, slot = entry >> 4, entry & (ENTRIES_EACH - 1)
    source = jnp.where(down == 1, chip + 1, chip - 1)
    early = slot < AHEAD
    loc = jnp.where(
        owner == chip,
        slot,
        jnp.where((owner == source) & (owner < CHIPS) & early, ENTRIES_EACH + down * AHEAD + slot, -1),
    ).astype(f32)
    sent = jnp.where((owner == chip) & early, 1.0, 0.0)
    far = far_ref[...]
    needed = need_ref[...]
    swept = jnp.zeros((groups, LANES), f32)
    slot_of = jnp.zeros((groups, LANES), f32)
    lists = jnp.full((rows, LANES), -1.0, f32)
    picks = jnp.full((groups, LANES), -1.0, f32)
    one, two = lax.broadcasted_iota(jnp.int32, (LANES, LANES), 0), lax.broadcasted_iota(jnp.int32, (LANES, LANES), 1)
    earlier = jnp.where(one < two, 1.0, 0.0).astype(jnp.bfloat16)
    to, source = lax.broadcasted_iota(jnp.int32, (rows, rows), 0), lax.broadcasted_iota(jnp.int32, (rows, rows), 1)
    up_step = ((to >> 2) & 1 == 0) & (to & 3 > 0) & (source == to - 1)
    down_step = ((to >> 2) & 1 == 1) & (to & 3 < 3) & (source == to + 1)
    step = jnp.where(up_step | down_step, 1.0, 0.0).astype(jnp.bfloat16)
    entry_lane = entry[:groups]

    def ranked(mask):
        return jnp.dot(mask.astype(jnp.bfloat16), earlier, preferred_element_type=f32)

    for number in range(ROUNDS + 1):
        loc_ref[...] = loc
        for part in range(2):
            top = part * 2 * CHIPS
            where_ref[part * CHIPS : (part + 1) * CHIPS, :] = jnp.maximum(
                loc_ref[top : top + CHIPS, :], loc_ref[top + CHIPS : top + 2 * CHIPS, :]
            )
        held = where_ref[...]
        ready = jnp.where((needed > 0) & (held >= 0) & (swept == 0), 1.0, 0.0)
        rank = ranked(ready)
        taken = jnp.where((ready > 0) & (rank < CAP), 1.0, 0.0)
        swept = swept + taken
        slot_of = slot_of + taken * (rank + number * CAP)
        for b in range(CAP):
            pick = jnp.max(jnp.where((taken > 0) & (rank == b), held, -1.0), axis=1, keepdims=True)
            picks = jnp.where(entry_lane == number * CAP + b, pick, picks)
        if number == ROUNDS:
            break
        ready = jnp.where((far > 0) & (loc >= 0) & (sent == 0), 1.0, 0.0)
        rank = jnp.zeros((rows, LANES), f32)
        above = jnp.zeros((rows, 1), f32)
        for hops in range(CHIPS - 1, 0, -1):
            level = jnp.where(far == hops, ready, 0.0)
            rank = jnp.where(far == hops, ranked(level) + above, rank)
            above = above + jnp.sum(level, axis=1, keepdims=True)
        taken = jnp.where((ready > 0) & (rank < CAP), 1.0, 0.0)
        sent = sent + taken
        for b in range(CAP):
            pick = jnp.max(jnp.where((taken > 0) & (rank == b), loc, -1.0), axis=1, keepdims=True)
            lists = jnp.where(entry == number * CAP + b, pick, lists)
        came = jnp.dot(step, (taken * (rank + 1)).astype(jnp.bfloat16), preferred_element_type=f32)
        base = FIRST_ROUND + number * 2 * CAP + down * CAP - 1
        loc = jnp.where(came > 0, came + base.astype(f32), loc)
    lists_ref[...] = lists
    picks_ref[...] = picks
    slots_ref[...] = slot_of
    missing = jnp.sum(jnp.where((far > 0) & (sent == 0), 1.0, 0.0)) + jnp.sum(
        jnp.where((needed > 0) & (swept == 0), 1.0, 0.0)
    )
    mine = (me >> 2) * 2 * CHIPS + (me & 3)
    plan_ref[...] = jnp.zeros(plan_ref.shape, jnp.int32)
    plan_ref[0:1, :] = lists_ref[pl.ds(mine, 1), :].astype(jnp.int32)
    plan_ref[1:2, :] = lists_ref[pl.ds(mine + CHIPS, 1), :].astype(jnp.int32)
    plan_ref[2:3, :] = picks_ref[pl.ds(me, 1), :].astype(jnp.int32)
    plan_ref[3:4, :] = slots_ref[pl.ds(me, 1), :].astype(jnp.int32)
    plan_ref[4:5, :] = jnp.full((1, LANES), missing, f32).astype(jnp.int32)


def make_plan(place, table):
    rows, groups = 4 * CHIPS, 2 * CHIPS
    tall, short = pltpu.VMEM((rows, LANES), jnp.float32), pltpu.VMEM((groups, LANES), jnp.float32)
    return pl.pallas_call(
        plan_kernel,
        out_shape=jax.ShapeDtypeStruct((8, LANES), jnp.int32),
        in_specs=[pl.BlockSpec(memory_space=pltpu.SMEM)] * 2,
        out_specs=pl.BlockSpec(memory_space=pltpu.VMEM),
        scratch_shapes=[tall, tall, tall, short, short, short, short],
        name="plan",
    )(place, table)


def pack(plan, number, pool):
    kinds = 3 if number < ROUNDS else 1
    starts = [0]
    for array in pool:
        starts.append(starts[-1] + array.shape[0])

    def kernel(plan_ref, *refs):
        sources, outs, sems = refs[: len(pool)], refs[len(pool) : -1], refs[-1]
        for kind, out in enumerate(outs):
            line = kind + 3 - kinds
            for b in range(CAP):
                at = plan_ref[line * LANES + number * CAP + b]
                for source, low, high in zip(sources, starts, starts[1:]):

                    @pl.when((at >= low) & (at < high))
                    def _(source=source, low=low, out=out, b=b, at=at, sem=sems.at[kind * CAP + b]):
                        pltpu.make_async_copy(source.at[at - low], out.at[b], sem).start()

        for kind, out in enumerate(outs):
            line = kind + 3 - kinds
            for b in range(CAP):

                @pl.when(plan_ref[line * LANES + number * CAP + b] >= 0)
                def _(out=out, b=b, sem=sems.at[kind * CAP + b]):
                    pltpu.make_async_copy(sources[0].at[0], out.at[b], sem).wait()

    shape = jax.ShapeDtypeStruct((CAP,) + pool[0].shape[1:], pool[0].dtype)
    return pl.pallas_call(
        kernel,
        out_shape=(shape,) * kinds,
        grid_spec=pltpu.PrefetchScalarGridSpec(
            num_scalar_prefetch=1,
            in_specs=[pl.BlockSpec(memory_space=pl.ANY)] * len(pool),
            out_specs=(pl.BlockSpec(memory_space=pl.ANY),) * kinds,
            scratch_shapes=[pltpu.SemaphoreType.DMA((kinds * CAP,))],
        ),
        cost_estimate=pl.CostEstimate(flops=0, bytes_accessed=kinds * CAP * 2 * 65536, transcendentals=0),
        name="pack",
    )(plan, *pool)


def previous_rows(nbr_owner, nbr_slot, nbr_count):
    rows = jnp.concatenate([nbr_owner, nbr_slot, nbr_count[:, None]], axis=1)
    rows = jnp.concatenate([shifted(rows[-1:], "seq", 1), rows[:-1]], axis=0)
    return rows[:, :KMAX], rows[:, KMAX : 2 * KMAX], rows[:, 2 * KMAX]


def fetch_by_request(store, owners, slots):
    owners_axis = lax.axis_size("seq")
    stretches = owners.shape[0]
    depth = min(stretches, max(2, 2 * stretches * KMAX // owners_axis) + 1)
    owners, slots = owners.reshape(-1), slots.reshape(-1)
    order = jnp.arange(owners.shape[0], dtype=jnp.int32)
    before = (owners[:, None] == owners[None, :]) & (order[None, :] < order[:, None])
    target = owners * depth + jnp.sum(before.astype(jnp.int32), axis=1)
    hits = target[:, None] == jnp.arange(owners_axis * depth, dtype=jnp.int32)[None, :]
    table = jnp.sum(jnp.where(hits, slots[:, None], 0), axis=0).reshape(owners_axis, depth)
    asked = lax.all_to_all(table, "seq", split_axis=0, concat_axis=0, tiled=True)
    arrived = lax.all_to_all(store[asked], "seq", split_axis=0, concat_axis=0, tiled=True)
    fetched = arrived.reshape(owners_axis * depth, NLEN, store.shape[2])[target]
    return lax.all_gather(fetched, FEATURES, axis=2, tiled=True)


def four_pieces(value):
    across = swapped(value, "mp")
    return [value, swapped(value, "rep"), across, swapped(across, "rep")]


def fetch_all(store, owners, slots):
    seq = lax.axis_index("seq")
    everything = [store]
    for distance in range(1, lax.axis_size("seq")):
        for steps in (distance, -distance):
            everything.append(shifted(store, "seq", steps))
    ahead = owners - seq
    place = jnp.where(ahead == 0, 0, jnp.where(ahead < 0, -2 * ahead - 1, 2 * ahead))
    pool = jnp.concatenate(everything, axis=0)
    return pool[(place * store.shape[0] + slots).reshape(-1)]


def in_order_of_pieces(weight):
    block = 2 * lax.axis_index("mp") + lax.axis_index("rep")
    width = DE // 4
    return jnp.concatenate([lax.dynamic_slice_in_dim(weight, (block ^ i) * width, width, 0) for i in range(4)], axis=0)


def exchanged_table(codes):
    own_part = [codes]
    for offset in range(1, CHIPS):
        own_part.append(lax.ppermute(codes, "seq", [(chip, chip ^ offset) for chip in range(CHIPS)]))
    own_part = jnp.stack(own_part)
    return jnp.concatenate([own_part, swapped(own_part, "parts")], axis=0)


def streamed(queries, key_weight, value_weight, enc_gain, store, nbr_owner, nbr_slot, nbr_count):
    stretches = nbr_owner.shape[0]
    total = stretches * KMAX
    seq = lax.axis_index("seq")
    me = lax.axis_index("parts") * CHIPS + seq
    kept = jnp.arange(KMAX, dtype=jnp.int32)[None, :] < nbr_count[:, None]
    codes = jnp.where(kept, nbr_owner * ENTRIES_EACH + nbr_slot, -1).reshape(-1)
    table = exchanged_table(codes)
    early_up, early_down = shifted(store[:AHEAD], "seq", 1), shifted(store[:AHEAD], "seq", -1)
    plan = make_plan(me.reshape(1).astype(jnp.int32), table.reshape(-1)).reshape(-1)
    missing = plan[4 * LANES]

    offset = jnp.where(seq > 0, (seq ^ (seq - 1)) & 3, 0)
    behind = table[offset]
    asked = jnp.concatenate([jnp.where(seq > 0, behind[total - KMAX :], -1), codes[: total - KMAX]])
    asked = asked.reshape(stretches, KMAX)
    counts = jnp.sum((asked >= 0).astype(jnp.int32), axis=1)
    first = jnp.maximum(asked[:, 0], 0)
    asked = jnp.stack([first, jnp.where(asked[:, 1] >= 0, asked[:, 1], first)], axis=1).reshape(-1)

    plan, key_weight, value_weight, enc_gain = lax.optimization_barrier((plan, key_weight, value_weight, enc_gain))
    gain = jnp.concatenate(four_pieces(enc_gain[None]), axis=1)
    key_weight, value_weight = in_order_of_pieces(key_weight), in_order_of_pieces(value_weight)

    def planned():
        slots = plan[3 * LANES : 4 * LANES][asked]
        pool = [store, early_up, early_down]
        held = ()
        for number in range(ROUNDS + 1):
            *ways, mine = pack(plan, number, pool)
            pieces = [mine, swapped(mine, "rep"), swapped(mine, "mp")]
            if ways:
                arrived = [shifted(ways[0], "seq", 1), shifted(ways[1], "seq", -1)]
                *arrived, pieces[1], pieces[2] = lax.optimization_barrier((*arrived, pieces[1], pieces[2]))
                pool += arrived
            pieces.append(swapped(pieces[2], "rep"))
            held = project(gain, pieces, key_weight, value_weight, 3, total, number * CAP, held)
        return attend(slots, counts, queries, *held)

    def whole():
        mine = fetch_all(store, asked >> 4, asked & (ENTRIES_EACH - 1))
        keys, values = project(gain, four_pieces(mine), key_weight, value_weight, 4, total)
        return attend(jnp.arange(total, dtype=jnp.int32), counts, queries, keys, values)

    return lax.cond(missing == 0, planned, whole)


def requested(queries, key_weight, value_weight, enc_gain, store, nbr_owner, nbr_slot, nbr_count):
    gain = lax.all_gather(enc_gain, FEATURES, axis=0, tiled=True)[None]
    owners, slots, counts = previous_rows(nbr_owner, nbr_slot, nbr_count)
    total = owners.size
    pieces = [fetch_by_request(store, owners, slots)]
    keys, values = project(gain, pieces, key_weight, value_weight, 4, total)
    return attend(jnp.arange(total, dtype=jnp.int32), counts, queries, keys, values)


def solution(mesh):
    in_specs = (
        P(SEQ_SPEC, FEATURES),
        P(None, FEATURES),
        P(None, FEATURES),
        P(FEATURES),
        P(SEQ_SPEC, None, FEATURES),
        P(SEQ_SPEC, None),
        P(SEQ_SPEC, None),
        P(SEQ_SPEC),
    )
    out_specs = P(SEQ_SPEC, FEATURES)
    shape = dict(mesh.shape)
    small = shape == {"parts": 2, "seq": CHIPS, "mp": 2, "rep": 2}
    body = streamed if small else requested
    return jax.shard_map(body, mesh=mesh, in_specs=in_specs, out_specs=out_specs, check_vma=False)
```

```python
import math

import jax
import jax.numpy as jnp
from jax import lax
from jax.experimental import pallas as pl
from jax.experimental.pallas import tpu as pltpu
from jax.sharding import PartitionSpec as P

HEAD_DIM = 128
DE = 1024
NLEN = 128
STRETCH = 64
KMAX = 2
EPS = 1e-06

SEQ_SPEC = ("parts", "seq")
FEATURES = ("mp", "rep")
VMEM_LIMIT = 48 * 1024 * 1024

CHIPS = 4
ENTRIES_EACH = 16
AHEAD = 8
ROUNDS = 3
CAP = 6
FIRST_ROUND = ENTRIES_EACH + 2 * AHEAD
LANES = 128


def shifted(value, axis, steps):
    count = lax.axis_size(axis)
    first, last = max(0, -steps), min(count, count - steps)
    return lax.ppermute(value, axis, [(source, source + steps) for source in range(first, last)])


def swapped(value, axis):
    return lax.ppermute(value, axis, [(0, 1), (1, 0)])


def project_kernel(gain_ref, *refs, held):
    *pieces, key_weight, value_weight = refs[: len(refs) - 3 - held]
    keys_out, values_out, normed = refs[-3:]
    rows = normed.shape[0]
    width = pieces[0].shape[2]
    raw = [piece[...].reshape(rows, width).astype(jnp.float32) for piece in pieces]
    squares = sum(jnp.sum(part * part, axis=1, keepdims=True) for part in raw)
    scale = lax.rsqrt(squares / DE + EPS)
    for index, part in enumerate(raw):
        place = slice(index * width, (index + 1) * width)
        normed[:, place] = (part * scale * gain_ref[:, place]).astype(jnp.bfloat16)
    states = normed[...]
    for weight, out in ((key_weight, keys_out), (value_weight, values_out)):
        out[...] = jnp.dot(states, weight[...], preferred_element_type=jnp.float32).astype(jnp.bfloat16).reshape(out.shape)


def project(gain, pieces, key_weight, value_weight, group, total, first=0, held=()):
    count, tokens, width = pieces[0].shape
    columns = key_weight.shape[1]
    out = jax.ShapeDtypeStruct((total, tokens, columns), jnp.bfloat16)
    piece_spec = pl.BlockSpec((group, tokens, width), lambda i: (i, 0, 0))
    weight_spec = pl.BlockSpec((DE, columns), lambda i: (0, 0))
    out_spec = pl.BlockSpec((group, tokens, columns), lambda i: (i + first // group, 0, 0))
    operands = (gain, *pieces, key_weight, value_weight, *held)

    def kernel(*refs):
        project_kernel(*refs, held=len(held))

    return pl.pallas_call(
        kernel,
        out_shape=(out, out),
        grid=(count // group,),
        in_specs=[pl.BlockSpec((1, DE), lambda i: (0, 0))]
        + [piece_spec] * len(pieces)
        + [weight_spec] * 2
        + [pl.BlockSpec(memory_space=pl.ANY)] * len(held),
        out_specs=(out_spec, out_spec),
        scratch_shapes=[pltpu.VMEM((group * tokens, DE), jnp.bfloat16)],
        input_output_aliases={len(operands) - len(held) + i: i for i in range(len(held))},
        compiler_params=pltpu.CompilerParams(vmem_limit_bytes=VMEM_LIMIT),
        cost_estimate=pl.CostEstimate(
            flops=4 * count * tokens * DE * columns,
            bytes_accessed=2 * (count * tokens * (DE + 2 * columns) + 2 * DE * columns),
            transcendentals=0,
        ),
        name="project",
    )(*operands)


SAME_COLUMNS = (((1,), (1,)), ((), ()))
SAME_ROWS = (((0,), (0,)), ((), ()))


def attend_kernel(slots, counts, query_ref, *refs):
    *entries, out_ref = refs
    keys, values = entries[: len(entries) // 2], entries[len(entries) // 2 :]
    together = len(keys) // KMAX
    wide = 2 * HEAD_DIM
    factor = math.log2(math.e) / math.sqrt(HEAD_DIM)
    count = [counts[pl.program_id(0) * together + g] for g in range(together)]
    work = [(g, start) for g in range(together) for start in range(0, query_ref.shape[1], wide)]

    def scored(g, start):
        query = query_ref[g * STRETCH : (g + 1) * STRETCH, start : start + wide]
        left, right = query[:, :HEAD_DIM], query[:, HEAD_DIM:]
        zero = jnp.zeros_like(left)
        both = jnp.concatenate([jnp.concatenate([left, zero], 1), jnp.concatenate([zero, right], 1)], 0)
        one, two = [
            lax.dot_general(
                keys[g * KMAX + k][0, :, start : start + wide], both, SAME_COLUMNS, preferred_element_type=jnp.float32
            )
            for k in range(KMAX)
        ]
        return one, jnp.where(count[g] == 2, two, -1e30)

    def weighed(one, two):
        top = jnp.maximum(one, two).max(0, keepdims=True)
        one, two = jnp.exp2((one - top) * factor), jnp.exp2((two - top) * factor)
        share = 1.0 / (one + two).sum(0, keepdims=True)
        return (one * share).astype(jnp.bfloat16), (two * share).astype(jnp.bfloat16)

    def mix(g, start, weights):
        mixed = sum(
            lax.dot_general(
                weights[k], values[g * KMAX + k][0, :, start : start + wide], SAME_ROWS, preferred_element_type=jnp.float32
            )
            for k in range(KMAX)
        )
        mixed = jnp.where(count[g] > 0, mixed, 0.0).astype(jnp.bfloat16)
        rows = slice(g * STRETCH, (g + 1) * STRETCH)
        out_ref[rows, start : start + HEAD_DIM] = mixed[:STRETCH, :HEAD_DIM]
        out_ref[rows, start + HEAD_DIM : start + wide] = mixed[STRETCH:, HEAD_DIM:]

    scores = [scored(*piece) for piece in work]
    weights = [weighed(*pair) for pair in scores]
    for piece, pair in zip(work, weights):
        mix(*piece, pair)


def attend(slots, counts, queries, keys, values, together=3):
    stretches = counts.shape[0]
    columns = queries.shape[1]

    def entry(i):
        return pl.BlockSpec((1, NLEN, columns), lambda step, slots, _: (slots[step * together * KMAX + i], 0, 0))

    query_spec = pl.BlockSpec((together * STRETCH, columns), lambda i, *_: (i, 0))
    entries = [entry(i) for i in range(together * KMAX)]
    return pl.pallas_call(
        attend_kernel,
        out_shape=jax.ShapeDtypeStruct(queries.shape, jnp.bfloat16),
        grid_spec=pltpu.PrefetchScalarGridSpec(
            num_scalar_prefetch=2,
            grid=(stretches // together,),
            in_specs=[query_spec] + entries * 2,
            out_specs=query_spec,
        ),
        compiler_params=pltpu.CompilerParams(vmem_limit_bytes=VMEM_LIMIT),
        cost_estimate=pl.CostEstimate(
            flops=8 * stretches * STRETCH * KMAX * NLEN * columns,
            bytes_accessed=4 * stretches * columns * (STRETCH + KMAX * NLEN),
            transcendentals=stretches * STRETCH * KMAX * NLEN * columns // HEAD_DIM,
        ),
        name="attend",
    )(slots, counts, queries, *[keys] * len(entries), *[values] * len(entries))


def plan_kernel(place, table, plan_ref, far_ref, loc_ref, lists_ref, need_ref, where_ref, picks_ref, slots_ref):
    f32 = jnp.float32
    rows, groups = 4 * CHIPS, 2 * CHIPS
    me = place[0]
    each = table.shape[0] // groups
    lane = lax.broadcasted_iota(jnp.int32, (1, LANES), 1)

    bases = []
    for group in range(groups):
        offset = jnp.bitwise_xor(me, group)
        bases.append(offset * each)
    need = []
    for group in range(groups):
        wanted = [bases[group] + j for j in range(each - KMAX)]
        if group % CHIPS > 0:
            wanted += [bases[group - 1] + each - KMAX + k for k in range(KMAX)]
        hit = jnp.zeros((1, LANES), f32)
        for index in wanted:
            hit = jnp.where(lane == table[index], 1.0, hit)
        need.append(hit)
        need_ref[group : group + 1, :] = hit
    for part in range(2):
        for down in range(2):
            for chip in range(CHIPS):
                reach = jnp.zeros((1, LANES), f32)
                for hops in range(1, CHIPS):
                    to = chip - hops if down else chip + hops
                    if 0 <= to < CHIPS:
                        reach = jnp.where(need[part * CHIPS + to] > 0, float(hops), reach)
                behind = lane >= chip * ENTRIES_EACH if down else lane < (chip + 1) * ENTRIES_EACH
                row = part * 2 * CHIPS + down * CHIPS + chip
                far_ref[row : row + 1, :] = jnp.where(behind, reach, 0.0)

    row = lax.broadcasted_iota(jnp.int32, (rows, LANES), 0)
    entry = lax.broadcasted_iota(jnp.int32, (rows, LANES), 1)
    chip, down = row & (CHIPS - 1), (row >> 2) & 1
    owner, slot = entry >> 4, entry & (ENTRIES_EACH - 1)
    source = jnp.where(down == 1, chip + 1, chip - 1)
    early = slot < AHEAD
    loc = jnp.where(
        owner == chip,
        slot,
        jnp.where((owner == source) & (owner < CHIPS) & early, ENTRIES_EACH + down * AHEAD + slot, -1),
    ).astype(f32)
    sent = jnp.where((owner == chip) & early, 1.0, 0.0)
    far = far_ref[...]
    needed = need_ref[...]
    swept = jnp.zeros((groups, LANES), f32)
    slot_of = jnp.zeros((groups, LANES), f32)
    lists = jnp.full((rows, LANES), -1.0, f32)
    picks = jnp.full((groups, LANES), -1.0, f32)
    one, two = lax.broadcasted_iota(jnp.int32, (LANES, LANES), 0), lax.broadcasted_iota(jnp.int32, (LANES, LANES), 1)
    earlier = jnp.where(one < two, 1.0, 0.0).astype(jnp.bfloat16)
    to, source = lax.broadcasted_iota(jnp.int32, (rows, rows), 0), lax.broadcasted_iota(jnp.int32, (rows, rows), 1)
    up_step = ((to >> 2) & 1 == 0) & (to & 3 > 0) & (source == to - 1)
    down_step = ((to >> 2) & 1 == 1) & (to & 3 < 3) & (source == to + 1)
    step = jnp.where(up_step | down_step, 1.0, 0.0).astype(jnp.bfloat16)
    entry_lane = entry[:groups]

    def ranked(mask):
        return jnp.dot(mask.astype(jnp.bfloat16), earlier, preferred_element_type=f32)

    for number in range(ROUNDS + 1):
        loc_ref[...] = loc
        for part in range(2):
            top = part * 2 * CHIPS
            where_ref[part * CHIPS : (part + 1) * CHIPS, :] = jnp.maximum(
                loc_ref[top : top + CHIPS, :], loc_ref[top + CHIPS : top + 2 * CHIPS, :]
            )
        held = where_ref[...]
        ready = jnp.where((needed > 0) & (held >= 0) & (swept == 0), 1.0, 0.0)
        rank = ranked(ready)
        taken = jnp.where((ready > 0) & (rank < CAP), 1.0, 0.0)
        swept = swept + taken
        slot_of = slot_of + taken * (rank + number * CAP)
        for b in range(CAP):
            pick = jnp.max(jnp.where((taken > 0) & (rank == b), held, -1.0), axis=1, keepdims=True)
            picks = jnp.where(entry_lane == number * CAP + b, pick, picks)
        if number == ROUNDS:
            break
        ready = jnp.where((far > 0) & (loc >= 0) & (sent == 0), 1.0, 0.0)
        rank = jnp.zeros((rows, LANES), f32)
        above = jnp.zeros((rows, 1), f32)
        for hops in range(CHIPS - 1, 0, -1):
            level = jnp.where(far == hops, ready, 0.0)
            rank = jnp.where(far == hops, ranked(level) + above, rank)
            above = above + jnp.sum(level, axis=1, keepdims=True)
        taken = jnp.where((ready > 0) & (rank < CAP), 1.0, 0.0)
        sent = sent + taken
        for b in range(CAP):
            pick = jnp.max(jnp.where((taken > 0) & (rank == b), loc, -1.0), axis=1, keepdims=True)
            lists = jnp.where(entry == number * CAP + b, pick, lists)
        came = jnp.dot(step, (taken * (rank + 1)).astype(jnp.bfloat16), preferred_element_type=f32)
        base = FIRST_ROUND + number * 2 * CAP + down * CAP - 1
        loc = jnp.where(came > 0, came + base.astype(f32), loc)
    lists_ref[...] = lists
    picks_ref[...] = picks
    slots_ref[...] = slot_of
    missing = jnp.sum(jnp.where((far > 0) & (sent == 0), 1.0, 0.0)) + jnp.sum(
        jnp.where((needed > 0) & (swept == 0), 1.0, 0.0)
    )
    mine = (me >> 2) * 2 * CHIPS + (me & 3)
    plan_ref[...] = jnp.zeros(plan_ref.shape, jnp.int32)
    plan_ref[0:1, :] = lists_ref[pl.ds(mine, 1), :].astype(jnp.int32)
    plan_ref[1:2, :] = lists_ref[pl.ds(mine + CHIPS, 1), :].astype(jnp.int32)
    plan_ref[2:3, :] = picks_ref[pl.ds(me, 1), :].astype(jnp.int32)
    plan_ref[3:4, :] = slots_ref[pl.ds(me, 1), :].astype(jnp.int32)
    plan_ref[4:5, :] = jnp.full((1, LANES), missing, f32).astype(jnp.int32)


def make_plan(place, table):
    rows, groups = 4 * CHIPS, 2 * CHIPS
    tall, short = pltpu.VMEM((rows, LANES), jnp.float32), pltpu.VMEM((groups, LANES), jnp.float32)
    return pl.pallas_call(
        plan_kernel,
        out_shape=jax.ShapeDtypeStruct((8, LANES), jnp.int32),
        in_specs=[pl.BlockSpec(memory_space=pltpu.SMEM)] * 2,
        out_specs=pl.BlockSpec(memory_space=pltpu.VMEM),
        scratch_shapes=[tall, tall, tall, short, short, short, short],
        name="plan",
    )(place, table)


def pack(plan, number, pool):
    kinds = 3 if number < ROUNDS else 1
    starts = [0]
    for array in pool:
        starts.append(starts[-1] + array.shape[0])

    def kernel(plan_ref, *refs):
        sources, outs = refs[: len(pool)], refs[len(pool) :]
        for kind, out in enumerate(outs):
            line = kind + 3 - kinds
            for b in range(CAP):
                at = plan_ref[line * LANES + number * CAP + b]
                for source, low, high in zip(sources, starts, starts[1:]):

                    @pl.when((at >= low) & (at < high))
                    def _(source=source, low=low, out=out, b=b, at=at):
                        out[b] = source[at - low]

    shape = jax.ShapeDtypeStruct((CAP,) + pool[0].shape[1:], pool[0].dtype)
    in_vmem = pl.BlockSpec(memory_space=pltpu.VMEM)
    return pl.pallas_call(
        kernel,
        out_shape=(shape,) * kinds,
        grid_spec=pltpu.PrefetchScalarGridSpec(
            num_scalar_prefetch=1, in_specs=[in_vmem] * len(pool), out_specs=(in_vmem,) * kinds
        ),
        compiler_params=pltpu.CompilerParams(vmem_limit_bytes=VMEM_LIMIT),
        cost_estimate=pl.CostEstimate(flops=0, bytes_accessed=kinds * CAP * 2 * 65536, transcendentals=0),
        name="pack",
    )(plan, *pool)


def previous_rows(nbr_owner, nbr_slot, nbr_count):
    rows = jnp.concatenate([nbr_owner, nbr_slot, nbr_count[:, None]], axis=1)
    rows = jnp.concatenate([shifted(rows[-1:], "seq", 1), rows[:-1]], axis=0)
    return rows[:, :KMAX], rows[:, KMAX : 2 * KMAX], rows[:, 2 * KMAX]


def fetch_by_request(store, owners, slots):
    owners_axis = lax.axis_size("seq")
    stretches = owners.shape[0]
    depth = min(stretches, max(2, 2 * stretches * KMAX // owners_axis) + 1)
    owners, slots = owners.reshape(-1), slots.reshape(-1)
    order = jnp.arange(owners.shape[0], dtype=jnp.int32)
    before = (owners[:, None] == owners[None, :]) & (order[None, :] < order[:, None])
    target = owners * depth + jnp.sum(before.astype(jnp.int32), axis=1)
    hits = target[:, None] == jnp.arange(owners_axis * depth, dtype=jnp.int32)[None, :]
    table = jnp.sum(jnp.where(hits, slots[:, None], 0), axis=0).reshape(owners_axis, depth)
    asked = lax.all_to_all(table, "seq", split_axis=0, concat_axis=0, tiled=True)
    arrived = lax.all_to_all(store[asked], "seq", split_axis=0, concat_axis=0, tiled=True)
    fetched = arrived.reshape(owners_axis * depth, NLEN, store.shape[2])[target]
    return lax.all_gather(fetched, FEATURES, axis=2, tiled=True)


def four_pieces(value):
    across = swapped(value, "mp")
    return [value, swapped(value, "rep"), across, swapped(across, "rep")]


def fetch_all(store, owners, slots):
    seq = lax.axis_index("seq")
    everything = [store]
    for distance in range(1, lax.axis_size("seq")):
        for steps in (distance, -distance):
            everything.append(shifted(store, "seq", steps))
    ahead = owners - seq
    place = jnp.where(ahead == 0, 0, jnp.where(ahead < 0, -2 * ahead - 1, 2 * ahead))
    pool = jnp.concatenate(everything, axis=0)
    return pool[(place * store.shape[0] + slots).reshape(-1)]


def in_order_of_pieces(weight):
    block = 2 * lax.axis_index("mp") + lax.axis_index("rep")
    width = DE // 4
    return jnp.concatenate([lax.dynamic_slice_in_dim(weight, (block ^ i) * width, width, 0) for i in range(4)], axis=0)


def exchanged_table(codes):
    own_part = [codes]
    for offset in range(1, CHIPS):
        own_part.append(lax.ppermute(codes, "seq", [(chip, chip ^ offset) for chip in range(CHIPS)]))
    own_part = jnp.stack(own_part)
    return jnp.concatenate([own_part, swapped(own_part, "parts")], axis=0)


def streamed(queries, key_weight, value_weight, enc_gain, store, nbr_owner, nbr_slot, nbr_count):
    stretches = nbr_owner.shape[0]
    total = stretches * KMAX
    seq = lax.axis_index("seq")
    me = lax.axis_index("parts") * CHIPS + seq
    kept = jnp.arange(KMAX, dtype=jnp.int32)[None, :] < nbr_count[:, None]
    codes = jnp.where(kept, nbr_owner * ENTRIES_EACH + nbr_slot, -1).reshape(-1)
    table = exchanged_table(codes)
    early_up, early_down = shifted(store[:AHEAD], "seq", 1), shifted(store[:AHEAD], "seq", -1)
    plan = make_plan(me.reshape(1).astype(jnp.int32), table.reshape(-1)).reshape(-1)
    missing = plan[4 * LANES]

    offset = jnp.where(seq > 0, (seq ^ (seq - 1)) & 3, 0)
    behind = table[offset]
    asked = jnp.concatenate([jnp.where(seq > 0, behind[total - KMAX :], -1), codes[: total - KMAX]])
    asked = asked.reshape(stretches, KMAX)
    counts = jnp.sum((asked >= 0).astype(jnp.int32), axis=1)
    first = jnp.maximum(asked[:, 0], 0)
    asked = jnp.stack([first, jnp.where(asked[:, 1] >= 0, asked[:, 1], first)], axis=1).reshape(-1)

    def planned():
        slots = plan[3 * LANES : 4 * LANES][asked]
        pool = [store, early_up, early_down]
        held, pieces = (), []
        for number in range(ROUNDS + 1):
            *ways, mine = pack(plan, number, pool)
            arrived = [shifted(way, "seq", steps) for way, steps in zip(ways, (1, -1))]
            pieces.append([mine, swapped(mine, "rep"), swapped(mine, "mp")])
            if number == 0:
                mine, later_keys, later_values, later_gain = lax.optimization_barrier(
                    (mine, key_weight, value_weight, enc_gain)
                )
                ordered_gain = jnp.concatenate(four_pieces(later_gain[None]), axis=1)
                ordered = [in_order_of_pieces(weight) for weight in (later_keys, later_values)]
                after = (ordered_gain, *ordered)
            else:
                pieces[number - 1].append(swapped(pieces[number - 1][2], "rep"))
                held = project(ordered_gain, pieces[number - 1], *ordered, 3, total, (number - 1) * CAP, held)
                after = held
            if number < ROUNDS:
                arrived, pieces[number], after = lax.optimization_barrier((arrived, pieces[number], after))
                if number == 0:
                    ordered_gain, *ordered = after
                else:
                    held = after
                pool += arrived
        pieces[ROUNDS].append(swapped(pieces[ROUNDS][2], "rep"))
        held = project(ordered_gain, pieces[ROUNDS], *ordered, 3, total, ROUNDS * CAP, held)
        return (slots, *held)

    def whole():
        mine = fetch_all(store, asked >> 4, asked & (ENTRIES_EACH - 1))
        gain = jnp.concatenate(four_pieces(enc_gain[None]), axis=1)
        ordered = [in_order_of_pieces(weight) for weight in (key_weight, value_weight)]
        return (jnp.arange(total, dtype=jnp.int32), *project(gain, four_pieces(mine), *ordered, 4, total))

    slots, keys, values = lax.cond(missing == 0, planned, whole)
    return attend(slots, counts, queries, keys, values)


def requested(queries, key_weight, value_weight, enc_gain, store, nbr_owner, nbr_slot, nbr_count):
    gain = lax.all_gather(enc_gain, FEATURES, axis=0, tiled=True)[None]
    owners, slots, counts = previous_rows(nbr_owner, nbr_slot, nbr_count)
    total = owners.size
    pieces = [fetch_by_request(store, owners, slots)]
    keys, values = project(gain, pieces, key_weight, value_weight, 4, total)
    return attend(jnp.arange(total, dtype=jnp.int32), counts, queries, keys, values)


def solution(mesh):
    in_specs = (
        P(SEQ_SPEC, FEATURES),
        P(None, FEATURES),
        P(None, FEATURES),
        P(FEATURES),
        P(SEQ_SPEC, None, FEATURES),
        P(SEQ_SPEC, None),
        P(SEQ_SPEC, None),
        P(SEQ_SPEC),
    )
    out_specs = P(SEQ_SPEC, FEATURES)
    shape = dict(mesh.shape)
    small = shape == {"parts": 2, "seq": CHIPS, "mp": 2, "rep": 2}
    body = streamed if small else requested
    return jax.shard_map(body, mesh=mesh, in_specs=in_specs, out_specs=out_specs, check_vma=False)
```

```python
import math

import jax
import jax.numpy as jnp
from jax import lax
from jax.experimental import pallas as pl
from jax.experimental.pallas import tpu as pltpu
from jax.sharding import PartitionSpec as P

HEAD_DIM = 128
DE = 1024
NLEN = 128
STRETCH = 64
KMAX = 2
EPS = 1e-06

SEQ_SPEC = ("parts", "seq")
FEATURES = ("mp", "rep")
VMEM_LIMIT = 48 * 1024 * 1024

CHIPS = 4
ENTRIES_EACH = 16
AHEAD = 8
ROUNDS = 3
CAP = 6
GROUP = 3
FIRST_ROUND = ENTRIES_EACH + 2 * AHEAD
LANES = 128


def shifted(value, axis, steps):
    count = lax.axis_size(axis)
    first, last = max(0, -steps), min(count, count - steps)
    return lax.ppermute(value, axis, [(source, source + steps) for source in range(first, last)])


def swapped(value, axis):
    return lax.ppermute(value, axis, [(0, 1), (1, 0)])


def project(marks, gain, pieces, key_weight, value_weight, group, total, number=0, held=()):
    count, tokens, width = pieces[0].shape
    columns = key_weight.shape[1]
    steps = count // group
    base = number * (len(pieces) + steps)

    def kernel(marks_ref, gain_ref, *refs):
        *parts, key_ref, value_ref = refs[: len(pieces) + 2]
        keys_out, values_out, normed = refs[-3:]

        @pl.when(marks_ref[base + len(pieces) + pl.program_id(0)] > 0)
        def _():
            raw = [part[...].reshape(group * tokens, width).astype(jnp.float32) for part in parts]
            squares = sum(jnp.sum(part * part, axis=1, keepdims=True) for part in raw)
            scale = lax.rsqrt(squares / DE + EPS)
            for index, part in enumerate(raw):
                place = pl.ds(pl.multiple_of(marks_ref[base + index] * width, width), width)
                normed[:, place] = (part * scale * gain_ref[:, index * width : (index + 1) * width]).astype(jnp.bfloat16)
            states = normed[...]
            for weight, out in ((key_ref, keys_out), (value_ref, values_out)):
                product = jnp.dot(states, weight[...], preferred_element_type=jnp.float32)
                out[...] = product.astype(jnp.bfloat16).reshape(out.shape)

    out = jax.ShapeDtypeStruct((total, tokens, columns), jnp.bfloat16)
    piece_spec = pl.BlockSpec((group, tokens, width), lambda i, _: (i, 0, 0))
    weight_spec = pl.BlockSpec((DE, columns), lambda i, _: (0, 0))
    out_spec = pl.BlockSpec((group, tokens, columns), lambda i, _: (i + number * steps, 0, 0))
    operands = (marks, gain, *pieces, key_weight, value_weight, *held)
    return pl.pallas_call(
        kernel,
        out_shape=(out, out),
        grid_spec=pltpu.PrefetchScalarGridSpec(
            num_scalar_prefetch=1,
            grid=(steps,),
            in_specs=[pl.BlockSpec((1, DE), lambda i, _: (0, 0))]
            + [piece_spec] * len(pieces)
            + [weight_spec] * 2
            + [pl.BlockSpec(memory_space=pl.ANY)] * len(held),
            out_specs=(out_spec, out_spec),
            scratch_shapes=[pltpu.VMEM((group * tokens, DE), jnp.bfloat16)],
        ),
        input_output_aliases={len(operands) - len(held) + i: i for i in range(len(held))},
        compiler_params=pltpu.CompilerParams(vmem_limit_bytes=VMEM_LIMIT),
        cost_estimate=pl.CostEstimate(
            flops=4 * count * tokens * DE * columns,
            bytes_accessed=2 * (count * tokens * (DE + 2 * columns) + 2 * DE * columns),
            transcendentals=0,
        ),
        name="project",
    )(*operands)


SAME_COLUMNS = (((1,), (1,)), ((), ()))
SAME_ROWS = (((0,), (0,)), ((), ()))


def attend_kernel(slots, counts, query_ref, *refs):
    *entries, out_ref = refs
    keys, values = entries[: len(entries) // 2], entries[len(entries) // 2 :]
    together = len(keys) // KMAX
    wide = 2 * HEAD_DIM
    factor = math.log2(math.e) / math.sqrt(HEAD_DIM)
    count = [counts[pl.program_id(0) * together + g] for g in range(together)]
    work = [(g, start) for g in range(together) for start in range(0, query_ref.shape[1], wide)]

    def scored(g, start):
        query = query_ref[g * STRETCH : (g + 1) * STRETCH, start : start + wide]
        left, right = query[:, :HEAD_DIM], query[:, HEAD_DIM:]
        zero = jnp.zeros_like(left)
        both = jnp.concatenate([jnp.concatenate([left, zero], 1), jnp.concatenate([zero, right], 1)], 0)
        one, two = [
            lax.dot_general(
                keys[g * KMAX + k][0, :, start : start + wide], both, SAME_COLUMNS, preferred_element_type=jnp.float32
            )
            for k in range(KMAX)
        ]
        return one, jnp.where(count[g] == 2, two, -1e30)

    def weighed(one, two):
        top = jnp.maximum(one, two).max(0, keepdims=True)
        one, two = jnp.exp2((one - top) * factor), jnp.exp2((two - top) * factor)
        share = 1.0 / (one + two).sum(0, keepdims=True)
        return (one * share).astype(jnp.bfloat16), (two * share).astype(jnp.bfloat16)

    def mix(g, start, weights):
        mixed = sum(
            lax.dot_general(
                weights[k], values[g * KMAX + k][0, :, start : start + wide], SAME_ROWS, preferred_element_type=jnp.float32
            )
            for k in range(KMAX)
        )
        mixed = jnp.where(count[g] > 0, mixed, 0.0).astype(jnp.bfloat16)
        rows = slice(g * STRETCH, (g + 1) * STRETCH)
        out_ref[rows, start : start + HEAD_DIM] = mixed[:STRETCH, :HEAD_DIM]
        out_ref[rows, start + HEAD_DIM : start + wide] = mixed[STRETCH:, HEAD_DIM:]

    scores = [scored(*piece) for piece in work]
    weights = [weighed(*pair) for pair in scores]
    for piece, pair in zip(work, weights):
        mix(*piece, pair)


def attend(slots, counts, queries, keys, values, together=3):
    stretches = counts.shape[0]
    columns = queries.shape[1]

    def entry(i):
        return pl.BlockSpec((1, NLEN, columns), lambda step, slots, _: (slots[step * together * KMAX + i], 0, 0))

    query_spec = pl.BlockSpec((together * STRETCH, columns), lambda i, *_: (i, 0))
    entries = [entry(i) for i in range(together * KMAX)]
    return pl.pallas_call(
        attend_kernel,
        out_shape=jax.ShapeDtypeStruct(queries.shape, jnp.bfloat16),
        grid_spec=pltpu.PrefetchScalarGridSpec(
            num_scalar_prefetch=2,
            grid=(stretches // together,),
            in_specs=[query_spec] + entries * 2,
            out_specs=query_spec,
        ),
        compiler_params=pltpu.CompilerParams(vmem_limit_bytes=VMEM_LIMIT),
        cost_estimate=pl.CostEstimate(
            flops=8 * stretches * STRETCH * KMAX * NLEN * columns,
            bytes_accessed=4 * stretches * columns * (STRETCH + KMAX * NLEN),
            transcendentals=stretches * STRETCH * KMAX * NLEN * columns // HEAD_DIM,
        ),
        name="attend",
    )(slots, counts, queries, *[keys] * len(entries), *[values] * len(entries))


def plan_kernel(place, table, plan_ref, far_ref, loc_ref, lists_ref, need_ref, where_ref, picks_ref, slots_ref):
    f32 = jnp.float32
    rows, groups = 4 * CHIPS, 2 * CHIPS
    me = place[0]
    each = table.shape[0] // groups
    lane = lax.broadcasted_iota(jnp.int32, (1, LANES), 1)

    bases = []
    for group in range(groups):
        offset = jnp.bitwise_xor(me, group)
        bases.append(offset * each)
    need = []
    for group in range(groups):
        wanted = [bases[group] + j for j in range(each - KMAX)]
        if group % CHIPS > 0:
            wanted += [bases[group - 1] + each - KMAX + k for k in range(KMAX)]
        hit = jnp.zeros((1, LANES), f32)
        for index in wanted:
            hit = jnp.where(lane == table[index], 1.0, hit)
        need.append(hit)
        need_ref[group : group + 1, :] = hit
    for part in range(2):
        for down in range(2):
            for chip in range(CHIPS):
                reach = jnp.zeros((1, LANES), f32)
                for hops in range(1, CHIPS):
                    to = chip - hops if down else chip + hops
                    if 0 <= to < CHIPS:
                        reach = jnp.where(need[part * CHIPS + to] > 0, float(hops), reach)
                behind = lane >= chip * ENTRIES_EACH if down else lane < (chip + 1) * ENTRIES_EACH
                row = part * 2 * CHIPS + down * CHIPS + chip
                far_ref[row : row + 1, :] = jnp.where(behind, reach, 0.0)

    row = lax.broadcasted_iota(jnp.int32, (rows, LANES), 0)
    entry = lax.broadcasted_iota(jnp.int32, (rows, LANES), 1)
    chip, down = row & (CHIPS - 1), (row >> 2) & 1
    owner, slot = entry >> 4, entry & (ENTRIES_EACH - 1)
    source = jnp.where(down == 1, chip + 1, chip - 1)
    early = slot < AHEAD
    loc = jnp.where(
        owner == chip,
        slot,
        jnp.where((owner == source) & (owner < CHIPS) & early, ENTRIES_EACH + down * AHEAD + slot, -1),
    ).astype(f32)
    sent = jnp.where((owner == chip) & early, 1.0, 0.0)
    far = far_ref[...]
    needed = need_ref[...]
    swept = jnp.zeros((groups, LANES), f32)
    slot_of = jnp.zeros((groups, LANES), f32)
    lists = jnp.full((rows, LANES), -1.0, f32)
    picks = jnp.full((groups, LANES), -1.0, f32)
    one, two = lax.broadcasted_iota(jnp.int32, (LANES, LANES), 0), lax.broadcasted_iota(jnp.int32, (LANES, LANES), 1)
    earlier = jnp.where(one < two, 1.0, 0.0).astype(jnp.bfloat16)
    to, source = lax.broadcasted_iota(jnp.int32, (rows, rows), 0), lax.broadcasted_iota(jnp.int32, (rows, rows), 1)
    up_step = ((to >> 2) & 1 == 0) & (to & 3 > 0) & (source == to - 1)
    down_step = ((to >> 2) & 1 == 1) & (to & 3 < 3) & (source == to + 1)
    step = jnp.where(up_step | down_step, 1.0, 0.0).astype(jnp.bfloat16)
    entry_lane = entry[:groups]

    def ranked(mask):
        return jnp.dot(mask.astype(jnp.bfloat16), earlier, preferred_element_type=f32)

    for number in range(ROUNDS + 1):
        loc_ref[...] = loc
        for part in range(2):
            top = part * 2 * CHIPS
            where_ref[part * CHIPS : (part + 1) * CHIPS, :] = jnp.maximum(
                loc_ref[top : top + CHIPS, :], loc_ref[top + CHIPS : top + 2 * CHIPS, :]
            )
        held = where_ref[...]
        ready = jnp.where((needed > 0) & (held >= 0) & (swept == 0), 1.0, 0.0)
        rank = ranked(ready)
        taken = jnp.where((ready > 0) & (rank < CAP), 1.0, 0.0)
        swept = swept + taken
        slot_of = slot_of + taken * (rank + number * CAP)
        for b in range(CAP):
            pick = jnp.max(jnp.where((taken > 0) & (rank == b), held, -1.0), axis=1, keepdims=True)
            picks = jnp.where(entry_lane == number * CAP + b, pick, picks)
        if number == ROUNDS:
            break
        ready = jnp.where((far > 0) & (loc >= 0) & (sent == 0), 1.0, 0.0)
        rank = jnp.zeros((rows, LANES), f32)
        above = jnp.zeros((rows, 1), f32)
        for hops in range(CHIPS - 1, 0, -1):
            level = jnp.where(far == hops, ready, 0.0)
            rank = jnp.where(far == hops, ranked(level) + above, rank)
            above = above + jnp.sum(level, axis=1, keepdims=True)
        taken = jnp.where((ready > 0) & (rank < CAP), 1.0, 0.0)
        sent = sent + taken
        for b in range(CAP):
            pick = jnp.max(jnp.where((taken > 0) & (rank == b), loc, -1.0), axis=1, keepdims=True)
            lists = jnp.where(entry == number * CAP + b, pick, lists)
        came = jnp.dot(step, (taken * (rank + 1)).astype(jnp.bfloat16), preferred_element_type=f32)
        base = FIRST_ROUND + number * 2 * CAP + down * CAP - 1
        loc = jnp.where(came > 0, came + base.astype(f32), loc)
    lists_ref[...] = lists
    picks_ref[...] = picks
    slots_ref[...] = slot_of
    missing = jnp.sum(jnp.where((far > 0) & (sent == 0), 1.0, 0.0)) + jnp.sum(
        jnp.where((needed > 0) & (swept == 0), 1.0, 0.0)
    )
    mine = (me >> 2) * 2 * CHIPS + (me & 3)
    plan_ref[...] = jnp.zeros(plan_ref.shape, jnp.int32)
    plan_ref[0:1, :] = lists_ref[pl.ds(mine, 1), :].astype(jnp.int32)
    plan_ref[1:2, :] = lists_ref[pl.ds(mine + CHIPS, 1), :].astype(jnp.int32)
    plan_ref[2:3, :] = picks_ref[pl.ds(me, 1), :].astype(jnp.int32)
    plan_ref[3:4, :] = slots_ref[pl.ds(me, 1), :].astype(jnp.int32)
    plan_ref[4:5, :] = jnp.full((1, LANES), missing, f32).astype(jnp.int32)


def make_plan(place, table):
    rows, groups = 4 * CHIPS, 2 * CHIPS
    tall, short = pltpu.VMEM((rows, LANES), jnp.float32), pltpu.VMEM((groups, LANES), jnp.float32)
    return pl.pallas_call(
        plan_kernel,
        out_shape=jax.ShapeDtypeStruct((8, LANES), jnp.int32),
        in_specs=[pl.BlockSpec(memory_space=pltpu.SMEM)] * 2,
        out_specs=pl.BlockSpec(memory_space=pltpu.VMEM),
        scratch_shapes=[tall, tall, tall, short, short, short, short],
        name="plan",
    )(place, table)


def pack(plan, number, pool):
    kinds = 3 if number < ROUNDS else 1
    starts = [0]
    for array in pool:
        starts.append(starts[-1] + array.shape[0])

    def kernel(plan_ref, *refs):
        sources, outs = refs[: len(pool)], refs[len(pool) :]
        for kind, out in enumerate(outs):
            line = kind + 3 - kinds
            for b in range(CAP):
                at = plan_ref[line * LANES + number * CAP + b]
                for source, low, high in zip(sources, starts, starts[1:]):

                    @pl.when((at >= low) & (at < high))
                    def _(source=source, low=low, out=out, b=b, at=at):
                        out[b] = source[at - low]

    shape = jax.ShapeDtypeStruct((CAP,) + pool[0].shape[1:], pool[0].dtype)
    in_vmem = pl.BlockSpec(memory_space=pltpu.VMEM)
    return pl.pallas_call(
        kernel,
        out_shape=(shape,) * kinds,
        grid_spec=pltpu.PrefetchScalarGridSpec(
            num_scalar_prefetch=1, in_specs=[in_vmem] * len(pool), out_specs=(in_vmem,) * kinds
        ),
        compiler_params=pltpu.CompilerParams(vmem_limit_bytes=VMEM_LIMIT),
        cost_estimate=pl.CostEstimate(flops=0, bytes_accessed=kinds * CAP * 2 * 65536, transcendentals=0),
        name="pack",
    )(plan, *pool)


def previous_rows(nbr_owner, nbr_slot, nbr_count):
    rows = jnp.concatenate([nbr_owner, nbr_slot, nbr_count[:, None]], axis=1)
    rows = jnp.concatenate([shifted(rows[-1:], "seq", 1), rows[:-1]], axis=0)
    return rows[:, :KMAX], rows[:, KMAX : 2 * KMAX], rows[:, 2 * KMAX]


def fetch_by_request(store, owners, slots):
    owners_axis = lax.axis_size("seq")
    stretches = owners.shape[0]
    depth = min(stretches, max(2, 2 * stretches * KMAX // owners_axis) + 1)
    owners, slots = owners.reshape(-1), slots.reshape(-1)
    order = jnp.arange(owners.shape[0], dtype=jnp.int32)
    before = (owners[:, None] == owners[None, :]) & (order[None, :] < order[:, None])
    target = owners * depth + jnp.sum(before.astype(jnp.int32), axis=1)
    hits = target[:, None] == jnp.arange(owners_axis * depth, dtype=jnp.int32)[None, :]
    table = jnp.sum(jnp.where(hits, slots[:, None], 0), axis=0).reshape(owners_axis, depth)
    asked = lax.all_to_all(table, "seq", split_axis=0, concat_axis=0, tiled=True)
    arrived = lax.all_to_all(store[asked], "seq", split_axis=0, concat_axis=0, tiled=True)
    fetched = arrived.reshape(owners_axis * depth, NLEN, store.shape[2])[target]
    return lax.all_gather(fetched, FEATURES, axis=2, tiled=True)


def four_pieces(value):
    across = swapped(value, "mp")
    return [value, swapped(value, "rep"), across, swapped(across, "rep")]


def fetch_all(store, owners, slots):
    seq = lax.axis_index("seq")
    everything = [store]
    for distance in range(1, lax.axis_size("seq")):
        for steps in (distance, -distance):
            everything.append(shifted(store, "seq", steps))
    ahead = owners - seq
    place = jnp.where(ahead == 0, 0, jnp.where(ahead < 0, -2 * ahead - 1, 2 * ahead))
    pool = jnp.concatenate(everything, axis=0)
    return pool[(place * store.shape[0] + slots).reshape(-1)]


def places_of_pieces():
    block = 2 * lax.axis_index("mp") + lax.axis_index("rep")
    return jnp.stack([block ^ i for i in range(4)]).astype(jnp.int32)


def exchanged_table(codes):
    own_part = [codes]
    for offset in range(1, CHIPS):
        own_part.append(lax.ppermute(codes, "seq", [(chip, chip ^ offset) for chip in range(CHIPS)]))
    own_part = jnp.stack(own_part)
    return jnp.concatenate([own_part, swapped(own_part, "parts")], axis=0)


def streamed(queries, key_weight, value_weight, enc_gain, store, nbr_owner, nbr_slot, nbr_count):
    stretches = nbr_owner.shape[0]
    total = stretches * KMAX
    seq = lax.axis_index("seq")
    me = lax.axis_index("parts") * CHIPS + seq
    kept = jnp.arange(KMAX, dtype=jnp.int32)[None, :] < nbr_count[:, None]
    codes = jnp.where(kept, nbr_owner * ENTRIES_EACH + nbr_slot, -1).reshape(-1)
    table = exchanged_table(codes)
    early_up, early_down = shifted(store[:AHEAD], "seq", 1), shifted(store[:AHEAD], "seq", -1)
    plan = make_plan(me.reshape(1).astype(jnp.int32), table.reshape(-1)).reshape(-1)
    missing = plan[4 * LANES]

    offset = jnp.where(seq > 0, (seq ^ (seq - 1)) & 3, 0)
    behind = table[offset]
    asked = jnp.concatenate([jnp.where(seq > 0, behind[total - KMAX :], -1), codes[: total - KMAX]])
    asked = asked.reshape(stretches, KMAX)
    counts = jnp.sum((asked >= 0).astype(jnp.int32), axis=1)
    first = jnp.maximum(asked[:, 0], 0)
    asked = jnp.stack([first, jnp.where(asked[:, 1] >= 0, asked[:, 1], first)], axis=1).reshape(-1)

    plan, enc_gain = lax.optimization_barrier((plan, enc_gain))
    gain = jnp.concatenate(four_pieces(enc_gain[None]), axis=1)
    places = places_of_pieces()
    wanted = plan[2 * LANES : 2 * LANES + total].reshape(ROUNDS + 1, CAP)[:, ::GROUP] >= 0
    marks = jnp.concatenate([jnp.broadcast_to(places, (ROUNDS + 1, 4)), wanted.astype(jnp.int32)], axis=1).reshape(-1)
    planned_slots = plan[3 * LANES : 4 * LANES][asked]

    def planned():
        pool = [store, early_up, early_down]
        held, pieces = (), []

        def projected(number):
            return project(marks, gain, pieces[number], key_weight, value_weight, GROUP, total, number, held)

        for number in range(ROUNDS + 1):
            *ways, mine = pack(plan, number, pool)
            arrived = [shifted(way, "seq", steps) for way, steps in zip(ways, (1, -1))]
            pieces.append([mine, swapped(mine, "rep"), swapped(mine, "mp")])
            if number > 0:
                pieces[number - 1].append(swapped(pieces[number - 1][2], "rep"))
                held = projected(number - 1)
            arrived, pieces[number], held = lax.optimization_barrier((arrived, pieces[number], held))
            pool += arrived
        pieces[ROUNDS].append(swapped(pieces[ROUNDS][2], "rep"))
        return (planned_slots, *projected(ROUNDS))

    def whole():
        mine = fetch_all(store, asked >> 4, asked & (ENTRIES_EACH - 1))
        whole_marks = jnp.concatenate([places, jnp.ones((total // 4,), jnp.int32)])
        keys, values = project(whole_marks, gain, four_pieces(mine), key_weight, value_weight, 4, total)
        return jnp.arange(total, dtype=jnp.int32), keys, values

    slots, keys, values = lax.cond(missing == 0, planned, whole)
    return attend(slots, counts, queries, keys, values)


def requested(queries, key_weight, value_weight, enc_gain, store, nbr_owner, nbr_slot, nbr_count):
    gain = lax.all_gather(enc_gain, FEATURES, axis=0, tiled=True)[None]
    owners, slots, counts = previous_rows(nbr_owner, nbr_slot, nbr_count)
    total = owners.size
    pieces = [fetch_by_request(store, owners, slots)]
    marks = jnp.concatenate([jnp.zeros((1,), jnp.int32), jnp.ones((total // 4,), jnp.int32)])
    keys, values = project(marks, gain, pieces, key_weight, value_weight, 4, total)
    return attend(jnp.arange(total, dtype=jnp.int32), counts, queries, keys, values)


def solution(mesh):
    in_specs = (
        P(SEQ_SPEC, FEATURES),
        P(None, FEATURES),
        P(None, FEATURES),
        P(FEATURES),
        P(SEQ_SPEC, None, FEATURES),
        P(SEQ_SPEC, None),
        P(SEQ_SPEC, None),
        P(SEQ_SPEC),
    )
    out_specs = P(SEQ_SPEC, FEATURES)
    shape = dict(mesh.shape)
    small = shape == {"parts": 2, "seq": CHIPS, "mp": 2, "rep": 2}
    body = streamed if small else requested
    return jax.shard_map(body, mesh=mesh, in_specs=in_specs, out_specs=out_specs, check_vma=False)
```

```python
import math

import jax
import jax.numpy as jnp
from jax import lax
from jax.experimental import pallas as pl
from jax.experimental.pallas import tpu as pltpu
from jax.sharding import PartitionSpec as P

HEAD_DIM = 128
DE = 1024
NLEN = 128
STRETCH = 64
KMAX = 2
EPS = 1e-06

SEQ_SPEC = ("parts", "seq")
FEATURES = ("mp", "rep")
VMEM_LIMIT = 28 * 1024 * 1024

CHIPS = 4
ENTRIES_EACH = 16
AHEAD = 8
ROUNDS = 3
CAP = 6
GROUP = 3
FIRST_ROUND = ENTRIES_EACH + 2 * AHEAD
LANES = 128


def shifted(value, axis, steps):
    count = lax.axis_size(axis)
    first, last = max(0, -steps), min(count, count - steps)
    return lax.ppermute(value, axis, [(source, source + steps) for source in range(first, last)])


def swapped(value, axis):
    return lax.ppermute(value, axis, [(0, 1), (1, 0)])


def project(marks, gain, pieces, key_weight, value_weight, group, total, number=0, held=()):
    count, tokens, width = pieces[0].shape
    columns = key_weight.shape[1]
    steps = count // group
    base = number * (len(pieces) + steps)

    def kernel(marks_ref, gain_ref, *refs):
        parts, key_blocks, value_blocks = [refs[i * len(pieces) : (i + 1) * len(pieces)] for i in range(3)]
        keys_out, values_out = refs[-2:]

        @pl.when(marks_ref[base + len(pieces) + pl.program_id(0)] > 0)
        def _():
            raw = [part[...].reshape(group * tokens, width).astype(jnp.float32) for part in parts]
            squares = sum(jnp.sum(part * part, axis=1, keepdims=True) for part in raw)
            scale = lax.rsqrt(squares / DE + EPS)
            states = [
                (part * scale * gain_ref[:, index * width : (index + 1) * width]).astype(jnp.bfloat16)
                for index, part in enumerate(raw)
            ]
            for blocks, out in ((key_blocks, keys_out), (value_blocks, values_out)):
                product = sum(
                    jnp.dot(state, block[...], preferred_element_type=jnp.float32)
                    for state, block in zip(states, blocks)
                )
                out[...] = product.astype(jnp.bfloat16).reshape(out.shape)

    out = jax.ShapeDtypeStruct((total, tokens, columns), jnp.bfloat16)
    piece_spec = pl.BlockSpec((group, tokens, width), lambda i, _: (i, 0, 0))

    def weight_spec(piece):
        return pl.BlockSpec((width, columns), lambda i, marks: (marks[base + piece], 0))

    weight_specs = [weight_spec(piece) for piece in range(len(pieces))]
    out_spec = pl.BlockSpec((group, tokens, columns), lambda i, _: (i + number * steps, 0, 0))
    operands = (marks, gain, *pieces, *[key_weight] * len(pieces), *[value_weight] * len(pieces), *held)
    return pl.pallas_call(
        kernel,
        out_shape=(out, out),
        grid_spec=pltpu.PrefetchScalarGridSpec(
            num_scalar_prefetch=1,
            grid=(steps,),
            in_specs=[pl.BlockSpec((1, DE), lambda i, _: (0, 0))]
            + [piece_spec] * len(pieces)
            + weight_specs * 2
            + [pl.BlockSpec(memory_space=pl.ANY)] * len(held),
            out_specs=(out_spec, out_spec),
        ),
        input_output_aliases={len(operands) - len(held) + i: i for i in range(len(held))},
        compiler_params=pltpu.CompilerParams(vmem_limit_bytes=VMEM_LIMIT),
        cost_estimate=pl.CostEstimate(
            flops=4 * count * tokens * DE * columns,
            bytes_accessed=2 * (count * tokens * (DE + 2 * columns) + 2 * DE * columns),
            transcendentals=0,
        ),
        name="project",
    )(*operands)


SAME_COLUMNS = (((1,), (1,)), ((), ()))
SAME_ROWS = (((0,), (0,)), ((), ()))


def attend_kernel(slots, counts, query_ref, *refs):
    *entries, out_ref = refs
    keys, values = entries[: len(entries) // 2], entries[len(entries) // 2 :]
    together = len(keys) // KMAX
    wide = 2 * HEAD_DIM
    factor = math.log2(math.e) / math.sqrt(HEAD_DIM)
    count = [counts[pl.program_id(0) * together + g] for g in range(together)]
    work = [(g, start) for g in range(together) for start in range(0, query_ref.shape[1], wide)]

    def scored(g, start):
        query = query_ref[g * STRETCH : (g + 1) * STRETCH, start : start + wide]
        left, right = query[:, :HEAD_DIM], query[:, HEAD_DIM:]
        zero = jnp.zeros_like(left)
        both = jnp.concatenate([jnp.concatenate([left, zero], 1), jnp.concatenate([zero, right], 1)], 0)
        one, two = [
            lax.dot_general(
                keys[g * KMAX + k][0, :, start : start + wide], both, SAME_COLUMNS, preferred_element_type=jnp.float32
            )
            for k in range(KMAX)
        ]
        return one, jnp.where(count[g] == 2, two, -1e30)

    def weighed(one, two):
        top = jnp.maximum(one, two).max(0, keepdims=True)
        one, two = jnp.exp2((one - top) * factor), jnp.exp2((two - top) * factor)
        share = 1.0 / (one + two).sum(0, keepdims=True)
        return (one * share).astype(jnp.bfloat16), (two * share).astype(jnp.bfloat16)

    def mix(g, start, weights):
        mixed = sum(
            lax.dot_general(
                weights[k], values[g * KMAX + k][0, :, start : start + wide], SAME_ROWS, preferred_element_type=jnp.float32
            )
            for k in range(KMAX)
        )
        mixed = jnp.where(count[g] > 0, mixed, 0.0).astype(jnp.bfloat16)
        rows = slice(g * STRETCH, (g + 1) * STRETCH)
        out_ref[rows, start : start + HEAD_DIM] = mixed[:STRETCH, :HEAD_DIM]
        out_ref[rows, start + HEAD_DIM : start + wide] = mixed[STRETCH:, HEAD_DIM:]

    scores = [scored(*piece) for piece in work]
    weights = [weighed(*pair) for pair in scores]
    for piece, pair in zip(work, weights):
        mix(*piece, pair)


def attend(slots, counts, queries, keys, values, together=3):
    stretches = counts.shape[0]
    columns = queries.shape[1]

    def entry(i):
        return pl.BlockSpec((1, NLEN, columns), lambda step, slots, _: (slots[step * together * KMAX + i], 0, 0))

    query_spec = pl.BlockSpec((together * STRETCH, columns), lambda i, *_: (i, 0))
    entries = [entry(i) for i in range(together * KMAX)]
    return pl.pallas_call(
        attend_kernel,
        out_shape=jax.ShapeDtypeStruct(queries.shape, jnp.bfloat16),
        grid_spec=pltpu.PrefetchScalarGridSpec(
            num_scalar_prefetch=2,
            grid=(stretches // together,),
            in_specs=[query_spec] + entries * 2,
            out_specs=query_spec,
        ),
        compiler_params=pltpu.CompilerParams(vmem_limit_bytes=VMEM_LIMIT),
        cost_estimate=pl.CostEstimate(
            flops=8 * stretches * STRETCH * KMAX * NLEN * columns,
            bytes_accessed=4 * stretches * columns * (STRETCH + KMAX * NLEN),
            transcendentals=stretches * STRETCH * KMAX * NLEN * columns // HEAD_DIM,
        ),
        name="attend",
    )(slots, counts, queries, *[keys] * len(entries), *[values] * len(entries))


def plan_kernel(place, table, plan_ref, far_ref, loc_ref, lists_ref, need_ref, where_ref, picks_ref, slots_ref):
    f32 = jnp.float32
    rows, groups = 4 * CHIPS, 2 * CHIPS
    me = place[0]
    each = table.shape[0] // groups
    lane = lax.broadcasted_iota(jnp.int32, (1, LANES), 1)

    bases = []
    for group in range(groups):
        offset = jnp.bitwise_xor(me, group)
        bases.append(offset * each)
    need = []
    for group in range(groups):
        wanted = [bases[group] + j for j in range(each - KMAX)]
        if group % CHIPS > 0:
            wanted += [bases[group - 1] + each - KMAX + k for k in range(KMAX)]
        hit = jnp.zeros((1, LANES), f32)
        for index in wanted:
            hit = jnp.where(lane == table[index], 1.0, hit)
        need.append(hit)
        need_ref[group : group + 1, :] = hit
    for part in range(2):
        for down in range(2):
            for chip in range(CHIPS):
                reach = jnp.zeros((1, LANES), f32)
                for hops in range(1, CHIPS):
                    to = chip - hops if down else chip + hops
                    if 0 <= to < CHIPS:
                        reach = jnp.where(need[part * CHIPS + to] > 0, float(hops), reach)
                behind = lane >= chip * ENTRIES_EACH if down else lane < (chip + 1) * ENTRIES_EACH
                row = part * 2 * CHIPS + down * CHIPS + chip
                far_ref[row : row + 1, :] = jnp.where(behind, reach, 0.0)

    row = lax.broadcasted_iota(jnp.int32, (rows, LANES), 0)
    entry = lax.broadcasted_iota(jnp.int32, (rows, LANES), 1)
    chip, down = row & (CHIPS - 1), (row >> 2) & 1
    owner, slot = entry >> 4, entry & (ENTRIES_EACH - 1)
    source = jnp.where(down == 1, chip + 1, chip - 1)
    early = slot < AHEAD
    loc = jnp.where(
        owner == chip,
        slot,
        jnp.where((owner == source) & (owner < CHIPS) & early, ENTRIES_EACH + down * AHEAD + slot, -1),
    ).astype(f32)
    sent = jnp.where((owner == chip) & early, 1.0, 0.0)
    far = far_ref[...]
    needed = need_ref[...]
    swept = jnp.zeros((groups, LANES), f32)
    slot_of = jnp.zeros((groups, LANES), f32)
    lists = jnp.full((rows, LANES), -1.0, f32)
    picks = jnp.full((groups, LANES), -1.0, f32)
    one, two = lax.broadcasted_iota(jnp.int32, (LANES, LANES), 0), lax.broadcasted_iota(jnp.int32, (LANES, LANES), 1)
    earlier = jnp.where(one < two, 1.0, 0.0).astype(jnp.bfloat16)
    to, source = lax.broadcasted_iota(jnp.int32, (rows, rows), 0), lax.broadcasted_iota(jnp.int32, (rows, rows), 1)
    up_step = ((to >> 2) & 1 == 0) & (to & 3 > 0) & (source == to - 1)
    down_step = ((to >> 2) & 1 == 1) & (to & 3 < 3) & (source == to + 1)
    step = jnp.where(up_step | down_step, 1.0, 0.0).astype(jnp.bfloat16)
    entry_lane = entry[:groups]

    def ranked(mask):
        return jnp.dot(mask.astype(jnp.bfloat16), earlier, preferred_element_type=f32)

    for number in range(ROUNDS + 1):
        loc_ref[...] = loc
        for part in range(2):
            top = part * 2 * CHIPS
            where_ref[part * CHIPS : (part + 1) * CHIPS, :] = jnp.maximum(
                loc_ref[top : top + CHIPS, :], loc_ref[top + CHIPS : top + 2 * CHIPS, :]
            )
        held = where_ref[...]
        ready = jnp.where((needed > 0) & (held >= 0) & (swept == 0), 1.0, 0.0)
        rank = ranked(ready)
        taken = jnp.where((ready > 0) & (rank < CAP), 1.0, 0.0)
        swept = swept + taken
        slot_of = slot_of + taken * (rank + number * CAP)
        for b in range(CAP):
            pick = jnp.max(jnp.where((taken > 0) & (rank == b), held, -1.0), axis=1, keepdims=True)
            picks = jnp.where(entry_lane == number * CAP + b, pick, picks)
        if number == ROUNDS:
            break
        ready = jnp.where((far > 0) & (loc >= 0) & (sent == 0), 1.0, 0.0)
        rank = jnp.zeros((rows, LANES), f32)
        above = jnp.zeros((rows, 1), f32)
        for hops in range(CHIPS - 1, 0, -1):
            level = jnp.where(far == hops, ready, 0.0)
            rank = jnp.where(far == hops, ranked(level) + above, rank)
            above = above + jnp.sum(level, axis=1, keepdims=True)
        taken = jnp.where((ready > 0) & (rank < CAP), 1.0, 0.0)
        sent = sent + taken
        for b in range(CAP):
            pick = jnp.max(jnp.where((taken > 0) & (rank == b), loc, -1.0), axis=1, keepdims=True)
            lists = jnp.where(entry == number * CAP + b, pick, lists)
        came = jnp.dot(step, (taken * (rank + 1)).astype(jnp.bfloat16), preferred_element_type=f32)
        base = FIRST_ROUND + number * 2 * CAP + down * CAP - 1
        loc = jnp.where(came > 0, came + base.astype(f32), loc)
    lists_ref[...] = lists
    picks_ref[...] = picks
    slots_ref[...] = slot_of
    missing = jnp.sum(jnp.where((far > 0) & (sent == 0), 1.0, 0.0)) + jnp.sum(
        jnp.where((needed > 0) & (swept == 0), 1.0, 0.0)
    )
    mine = (me >> 2) * 2 * CHIPS + (me & 3)
    plan_ref[...] = jnp.zeros(plan_ref.shape, jnp.int32)
    plan_ref[0:1, :] = lists_ref[pl.ds(mine, 1), :].astype(jnp.int32)
    plan_ref[1:2, :] = lists_ref[pl.ds(mine + CHIPS, 1), :].astype(jnp.int32)
    plan_ref[2:3, :] = picks_ref[pl.ds(me, 1), :].astype(jnp.int32)
    plan_ref[3:4, :] = slots_ref[pl.ds(me, 1), :].astype(jnp.int32)
    plan_ref[4:5, :] = jnp.full((1, LANES), missing, f32).astype(jnp.int32)


def make_plan(place, table):
    rows, groups = 4 * CHIPS, 2 * CHIPS
    tall, short = pltpu.VMEM((rows, LANES), jnp.float32), pltpu.VMEM((groups, LANES), jnp.float32)
    return pl.pallas_call(
        plan_kernel,
        out_shape=jax.ShapeDtypeStruct((8, LANES), jnp.int32),
        in_specs=[pl.BlockSpec(memory_space=pltpu.SMEM)] * 2,
        out_specs=pl.BlockSpec(memory_space=pltpu.VMEM),
        scratch_shapes=[tall, tall, tall, short, short, short, short],
        name="plan",
    )(place, table)


def pack(plan, line, number, pool):
    lows, arrays = [low for low, _ in pool], [array for _, array in pool]

    def kernel(plan_ref, *refs):
        sources, out = refs[:-1], refs[-1]
        for b in range(CAP):
            at = plan_ref[line * LANES + number * CAP + b]
            for source, low in zip(sources, lows):

                @pl.when((at >= low) & (at < low + source.shape[0]))
                def _(source=source, low=low, b=b, at=at):
                    out[b] = source[at - low]

    in_vmem = pl.BlockSpec(memory_space=pltpu.VMEM)
    return pl.pallas_call(
        kernel,
        out_shape=jax.ShapeDtypeStruct((CAP,) + arrays[0].shape[1:], arrays[0].dtype),
        grid_spec=pltpu.PrefetchScalarGridSpec(num_scalar_prefetch=1, in_specs=[in_vmem] * len(pool), out_specs=in_vmem),
        compiler_params=pltpu.CompilerParams(vmem_limit_bytes=VMEM_LIMIT),
        cost_estimate=pl.CostEstimate(flops=0, bytes_accessed=CAP * 2 * 65536, transcendentals=0),
        name="pack",
    )(plan, *arrays)


def previous_rows(nbr_owner, nbr_slot, nbr_count):
    rows = jnp.concatenate([nbr_owner, nbr_slot, nbr_count[:, None]], axis=1)
    rows = jnp.concatenate([shifted(rows[-1:], "seq", 1), rows[:-1]], axis=0)
    return rows[:, :KMAX], rows[:, KMAX : 2 * KMAX], rows[:, 2 * KMAX]


def fetch_by_request(store, owners, slots):
    owners_axis = lax.axis_size("seq")
    stretches = owners.shape[0]
    depth = min(stretches, max(2, 2 * stretches * KMAX // owners_axis) + 1)
    owners, slots = owners.reshape(-1), slots.reshape(-1)
    order = jnp.arange(owners.shape[0], dtype=jnp.int32)
    before = (owners[:, None] == owners[None, :]) & (order[None, :] < order[:, None])
    target = owners * depth + jnp.sum(before.astype(jnp.int32), axis=1)
    hits = target[:, None] == jnp.arange(owners_axis * depth, dtype=jnp.int32)[None, :]
    table = jnp.sum(jnp.where(hits, slots[:, None], 0), axis=0).reshape(owners_axis, depth)
    asked = lax.all_to_all(table, "seq", split_axis=0, concat_axis=0, tiled=True)
    arrived = lax.all_to_all(store[asked], "seq", split_axis=0, concat_axis=0, tiled=True)
    fetched = arrived.reshape(owners_axis * depth, NLEN, store.shape[2])[target]
    return lax.all_gather(fetched, FEATURES, axis=2, tiled=True)


def four_pieces(value):
    across = swapped(value, "mp")
    return [value, swapped(value, "rep"), across, swapped(across, "rep")]


def fetch_all(store, owners, slots):
    seq = lax.axis_index("seq")
    everything = [store]
    for distance in range(1, lax.axis_size("seq")):
        for steps in (distance, -distance):
            everything.append(shifted(store, "seq", steps))
    ahead = owners - seq
    place = jnp.where(ahead == 0, 0, jnp.where(ahead < 0, -2 * ahead - 1, 2 * ahead))
    pool = jnp.concatenate(everything, axis=0)
    return pool[(place * store.shape[0] + slots).reshape(-1)]


def places_of_pieces():
    block = 2 * lax.axis_index("mp") + lax.axis_index("rep")
    return jnp.stack([block ^ i for i in range(4)]).astype(jnp.int32)


def exchanged_table(codes):
    own_part = [codes]
    for offset in range(1, CHIPS):
        own_part.append(lax.ppermute(codes, "seq", [(chip, chip ^ offset) for chip in range(CHIPS)]))
    own_part = jnp.stack(own_part)
    return jnp.concatenate([own_part, swapped(own_part, "parts")], axis=0)


def streamed(queries, key_weight, value_weight, enc_gain, store, nbr_owner, nbr_slot, nbr_count):
    stretches = nbr_owner.shape[0]
    total = stretches * KMAX
    seq = lax.axis_index("seq")
    me = lax.axis_index("parts") * CHIPS + seq
    kept = jnp.arange(KMAX, dtype=jnp.int32)[None, :] < nbr_count[:, None]
    codes = jnp.where(kept, nbr_owner * ENTRIES_EACH + nbr_slot, -1).reshape(-1)
    table = exchanged_table(codes)
    early_up, early_down = shifted(store[:AHEAD], "seq", 1), shifted(store[:AHEAD], "seq", -1)
    plan = make_plan(me.reshape(1).astype(jnp.int32), table.reshape(-1)).reshape(-1)
    missing = plan[4 * LANES]

    offset = jnp.where(seq > 0, (seq ^ (seq - 1)) & 3, 0)
    behind = table[offset]
    asked = jnp.concatenate([jnp.where(seq > 0, behind[total - KMAX :], -1), codes[: total - KMAX]])
    asked = asked.reshape(stretches, KMAX)
    counts = jnp.sum((asked >= 0).astype(jnp.int32), axis=1)
    first = jnp.maximum(asked[:, 0], 0)
    asked = jnp.stack([first, jnp.where(asked[:, 1] >= 0, asked[:, 1], first)], axis=1).reshape(-1)

    plan, enc_gain = lax.optimization_barrier((plan, enc_gain))
    gain = jnp.concatenate(four_pieces(enc_gain[None]), axis=1)
    places = places_of_pieces()
    wanted = plan[2 * LANES : 2 * LANES + total].reshape(ROUNDS + 1, CAP)[:, ::GROUP] >= 0
    marks = jnp.concatenate([jnp.broadcast_to(places, (ROUNDS + 1, 4)), wanted.astype(jnp.int32)], axis=1).reshape(-1)
    planned_slots = plan[3 * LANES : 4 * LANES][asked]

    def planned():
        up, down = [(0, store), (ENTRIES_EACH, early_up)], [(0, store), (ENTRIES_EACH + AHEAD, early_down)]
        held, pieces, slots = (), [], planned_slots

        def projected(number):
            return project(marks, gain, pieces[number], key_weight, value_weight, GROUP, total, number, held)

        for number in range(ROUNDS + 1):
            pool = up + down[1:]
            if number < ROUNDS:
                base = FIRST_ROUND + number * 2 * CAP
                up = up + [(base, shifted(pack(plan, 0, number, up), "seq", 1))]
                down = down + [(base + CAP, shifted(pack(plan, 1, number, down), "seq", -1))]
            mine = pack(plan, 2, number, pool)
            pieces.append([mine, swapped(mine, "rep"), swapped(mine, "mp")])
            if number > 0:
                pieces[number - 1].append(swapped(pieces[number - 1][2], "rep"))
                held = projected(number - 1)
            places_down, arrays = [low for low, _ in down], [array for _, array in down]
            arrays, pieces[number], held, slots = lax.optimization_barrier((arrays, pieces[number], held, slots))
            down = list(zip(places_down, arrays))
        pieces[ROUNDS].append(swapped(pieces[ROUNDS][2], "rep"))
        return (slots, *projected(ROUNDS))

    def whole():
        mine = fetch_all(store, asked >> 4, asked & (ENTRIES_EACH - 1))
        whole_marks = jnp.concatenate([places, jnp.ones((total // 4,), jnp.int32)])
        keys, values = project(whole_marks, gain, four_pieces(mine), key_weight, value_weight, 4, total)
        return jnp.arange(total, dtype=jnp.int32), keys, values

    slots, keys, values = lax.cond(missing == 0, planned, whole)
    return attend(slots, counts, queries, keys, values)


def requested(queries, key_weight, value_weight, enc_gain, store, nbr_owner, nbr_slot, nbr_count):
    gain = lax.all_gather(enc_gain, FEATURES, axis=0, tiled=True)[None]
    owners, slots, counts = previous_rows(nbr_owner, nbr_slot, nbr_count)
    total = owners.size
    pieces = [fetch_by_request(store, owners, slots)]
    marks = jnp.concatenate([jnp.zeros((1,), jnp.int32), jnp.ones((total // 4,), jnp.int32)])
    keys, values = project(marks, gain, pieces, key_weight, value_weight, 4, total)
    return attend(jnp.arange(total, dtype=jnp.int32), counts, queries, keys, values)


def solution(mesh):
    in_specs = (
        P(SEQ_SPEC, FEATURES),
        P(None, FEATURES),
        P(None, FEATURES),
        P(FEATURES),
        P(SEQ_SPEC, None, FEATURES),
        P(SEQ_SPEC, None),
        P(SEQ_SPEC, None),
        P(SEQ_SPEC),
    )
    out_specs = P(SEQ_SPEC, FEATURES)
    shape = dict(mesh.shape)
    small = shape == {"parts": 2, "seq": CHIPS, "mp": 2, "rep": 2}
    body = streamed if small else requested
    return jax.shard_map(body, mesh=mesh, in_specs=in_specs, out_specs=out_specs, check_vma=False)
```

```python
import math

import jax
import jax.numpy as jnp
from jax import lax
from jax.experimental import pallas as pl
from jax.experimental.pallas import tpu as pltpu
from jax.sharding import PartitionSpec as P

HEAD_DIM = 128
DE = 1024
NLEN = 128
STRETCH = 64
KMAX = 2
EPS = 1e-06

SEQ_SPEC = ("parts", "seq")
FEATURES = ("mp", "rep")
VMEM_LIMIT = 28 * 1024 * 1024

CHIPS = 4
ENTRIES_EACH = 16
AHEAD = 8
ROUNDS = 3
CAP = 6
GROUP = 3
FIRST_ROUND = ENTRIES_EACH + 2 * AHEAD
LANES = 128


def shifted(value, axis, steps):
    count = lax.axis_size(axis)
    first, last = max(0, -steps), min(count, count - steps)
    return lax.ppermute(value, axis, [(source, source + steps) for source in range(first, last)])


def swapped(value, axis):
    return lax.ppermute(value, axis, [(0, 1), (1, 0)])


def project(marks, gain, pieces, key_weight, value_weight, group, total, number=0, held=()):
    count, tokens, width = pieces[0].shape
    columns = key_weight.shape[1]
    steps = count // group
    base = number * (len(pieces) + steps)

    def kernel(marks_ref, gain_ref, *refs):
        parts, key_blocks, value_blocks = [refs[i * len(pieces) : (i + 1) * len(pieces)] for i in range(3)]
        keys_out, values_out = refs[-2:]

        @pl.when(marks_ref[base + len(pieces) + pl.program_id(0)] > 0)
        def _():
            raw = [part[...].reshape(group * tokens, width).astype(jnp.float32) for part in parts]
            squares = sum(jnp.sum(part * part, axis=1, keepdims=True) for part in raw)
            scale = lax.rsqrt(squares / DE + EPS)
            states = [
                (part * scale * gain_ref[:, index * width : (index + 1) * width]).astype(jnp.bfloat16)
                for index, part in enumerate(raw)
            ]
            for blocks, out in ((key_blocks, keys_out), (value_blocks, values_out)):
                product = sum(
                    jnp.dot(state, block[...], preferred_element_type=jnp.float32)
                    for state, block in zip(states, blocks)
                )
                out[...] = product.astype(jnp.bfloat16).reshape(out.shape)

    out = jax.ShapeDtypeStruct((total, tokens, columns), jnp.bfloat16)
    piece_spec = pl.BlockSpec((group, tokens, width), lambda i, _: (i, 0, 0))

    def weight_spec(piece):
        return pl.BlockSpec((width, columns), lambda i, marks: (marks[base + piece], 0))

    weight_specs = [weight_spec(piece) for piece in range(len(pieces))]
    out_spec = pl.BlockSpec((group, tokens, columns), lambda i, _: (i + number * steps, 0, 0))
    operands = (marks, gain, *pieces, *[key_weight] * len(pieces), *[value_weight] * len(pieces), *held)
    return pl.pallas_call(
        kernel,
        out_shape=(out, out),
        grid_spec=pltpu.PrefetchScalarGridSpec(
            num_scalar_prefetch=1,
            grid=(steps,),
            in_specs=[pl.BlockSpec((1, DE), lambda i, _: (0, 0))]
            + [piece_spec] * len(pieces)
            + weight_specs * 2
            + [pl.BlockSpec(memory_space=pl.ANY)] * len(held),
            out_specs=(out_spec, out_spec),
        ),
        input_output_aliases={len(operands) - len(held) + i: i for i in range(len(held))},
        compiler_params=pltpu.CompilerParams(vmem_limit_bytes=VMEM_LIMIT),
        cost_estimate=pl.CostEstimate(
            flops=4 * count * tokens * DE * columns,
            bytes_accessed=2 * (count * tokens * (DE + 2 * columns) + 2 * DE * columns),
            transcendentals=0,
        ),
        name="project",
    )(*operands)


SAME_COLUMNS = (((1,), (1,)), ((), ()))
SAME_ROWS = (((0,), (0,)), ((), ()))


def attend_kernel(slots, counts, query_ref, *refs):
    *entries, out_ref = refs
    keys, values = entries[: len(entries) // 2], entries[len(entries) // 2 :]
    together = len(keys) // KMAX
    wide = 2 * HEAD_DIM
    factor = math.log2(math.e) / math.sqrt(HEAD_DIM)
    count = [counts[pl.program_id(0) * together + g] for g in range(together)]
    work = [(g, start) for g in range(together) for start in range(0, query_ref.shape[1], wide)]

    def scored(g, start):
        query = query_ref[g * STRETCH : (g + 1) * STRETCH, start : start + wide]
        left, right = query[:, :HEAD_DIM], query[:, HEAD_DIM:]
        zero = jnp.zeros_like(left)
        both = jnp.concatenate([jnp.concatenate([left, zero], 1), jnp.concatenate([zero, right], 1)], 0)
        one, two = [
            lax.dot_general(
                keys[g * KMAX + k][0, :, start : start + wide], both, SAME_COLUMNS, preferred_element_type=jnp.float32
            )
            for k in range(KMAX)
        ]
        return one, jnp.where(count[g] == 2, two, -1e30)

    def weighed(one, two):
        top = jnp.maximum(one, two).max(0, keepdims=True)
        one, two = jnp.exp2((one - top) * factor), jnp.exp2((two - top) * factor)
        share = 1.0 / (one + two).sum(0, keepdims=True)
        return (one * share).astype(jnp.bfloat16), (two * share).astype(jnp.bfloat16)

    def mix(g, start, weights):
        mixed = sum(
            lax.dot_general(
                weights[k], values[g * KMAX + k][0, :, start : start + wide], SAME_ROWS, preferred_element_type=jnp.float32
            )
            for k in range(KMAX)
        )
        mixed = jnp.where(count[g] > 0, mixed, 0.0).astype(jnp.bfloat16)
        rows = slice(g * STRETCH, (g + 1) * STRETCH)
        out_ref[rows, start : start + HEAD_DIM] = mixed[:STRETCH, :HEAD_DIM]
        out_ref[rows, start + HEAD_DIM : start + wide] = mixed[STRETCH:, HEAD_DIM:]

    scores = [scored(*piece) for piece in work]
    weights = [weighed(*pair) for pair in scores]
    for piece, pair in zip(work, weights):
        mix(*piece, pair)


def attend(slots, counts, queries, keys, values, together=3):
    stretches = counts.shape[0]
    columns = queries.shape[1]

    def entry(i):
        return pl.BlockSpec((1, NLEN, columns), lambda step, slots, _: (slots[step * together * KMAX + i], 0, 0))

    query_spec = pl.BlockSpec((together * STRETCH, columns), lambda i, *_: (i, 0))
    entries = [entry(i) for i in range(together * KMAX)]
    return pl.pallas_call(
        attend_kernel,
        out_shape=jax.ShapeDtypeStruct(queries.shape, jnp.bfloat16),
        grid_spec=pltpu.PrefetchScalarGridSpec(
            num_scalar_prefetch=2,
            grid=(stretches // together,),
            in_specs=[query_spec] + entries * 2,
            out_specs=query_spec,
        ),
        compiler_params=pltpu.CompilerParams(vmem_limit_bytes=VMEM_LIMIT),
        cost_estimate=pl.CostEstimate(
            flops=8 * stretches * STRETCH * KMAX * NLEN * columns,
            bytes_accessed=4 * stretches * columns * (STRETCH + KMAX * NLEN),
            transcendentals=stretches * STRETCH * KMAX * NLEN * columns // HEAD_DIM,
        ),
        name="attend",
    )(slots, counts, queries, *[keys] * len(entries), *[values] * len(entries))


def plan_kernel(place, table, plan_ref, far_ref, loc_ref, lists_ref, need_ref, where_ref, picks_ref, slots_ref):
    f32 = jnp.float32
    rows, groups = 4 * CHIPS, 2 * CHIPS
    me = place[0]
    each = table.shape[0] // groups
    lane = lax.broadcasted_iota(jnp.int32, (1, LANES), 1)

    bases = []
    for group in range(groups):
        offset = jnp.bitwise_xor(me, group)
        bases.append(offset * each)
    need = []
    for group in range(groups):
        wanted = [bases[group] + j for j in range(each - KMAX)]
        if group % CHIPS > 0:
            wanted += [bases[group - 1] + each - KMAX + k for k in range(KMAX)]
        hit = jnp.zeros((1, LANES), f32)
        for index in wanted:
            hit = jnp.where(lane == table[index], 1.0, hit)
        need.append(hit)
        need_ref[group : group + 1, :] = hit
    for part in range(2):
        for down in range(2):
            for chip in range(CHIPS):
                reach = jnp.zeros((1, LANES), f32)
                for hops in range(1, CHIPS):
                    to = chip - hops if down else chip + hops
                    if 0 <= to < CHIPS:
                        reach = jnp.where(need[part * CHIPS + to] > 0, float(hops), reach)
                behind = lane >= chip * ENTRIES_EACH if down else lane < (chip + 1) * ENTRIES_EACH
                row = part * 2 * CHIPS + down * CHIPS + chip
                far_ref[row : row + 1, :] = jnp.where(behind, reach, 0.0)

    row = lax.broadcasted_iota(jnp.int32, (rows, LANES), 0)
    entry = lax.broadcasted_iota(jnp.int32, (rows, LANES), 1)
    chip, down = row & (CHIPS - 1), (row >> 2) & 1
    owner, slot = entry >> 4, entry & (ENTRIES_EACH - 1)
    source = jnp.where(down == 1, chip + 1, chip - 1)
    early = slot < AHEAD
    loc = jnp.where(
        owner == chip,
        slot,
        jnp.where((owner == source) & (owner < CHIPS) & early, ENTRIES_EACH + down * AHEAD + slot, -1),
    ).astype(f32)
    sent = jnp.where((owner == chip) & early, 1.0, 0.0)
    far = far_ref[...]
    needed = need_ref[...]
    swept = jnp.zeros((groups, LANES), f32)
    slot_of = jnp.zeros((groups, LANES), f32)
    lists = jnp.full((rows, LANES), -1.0, f32)
    picks = jnp.full((groups, LANES), -1.0, f32)
    one, two = lax.broadcasted_iota(jnp.int32, (LANES, LANES), 0), lax.broadcasted_iota(jnp.int32, (LANES, LANES), 1)
    earlier = jnp.where(one < two, 1.0, 0.0).astype(jnp.bfloat16)
    to, source = lax.broadcasted_iota(jnp.int32, (rows, rows), 0), lax.broadcasted_iota(jnp.int32, (rows, rows), 1)
    up_step = ((to >> 2) & 1 == 0) & (to & 3 > 0) & (source == to - 1)
    down_step = ((to >> 2) & 1 == 1) & (to & 3 < 3) & (source == to + 1)
    step = jnp.where(up_step | down_step, 1.0, 0.0).astype(jnp.bfloat16)
    entry_lane = entry[:groups]

    def ranked(mask):
        return jnp.dot(mask.astype(jnp.bfloat16), earlier, preferred_element_type=f32)

    for number in range(ROUNDS + 1):
        loc_ref[...] = loc
        for part in range(2):
            top = part * 2 * CHIPS
            where_ref[part * CHIPS : (part + 1) * CHIPS, :] = jnp.maximum(
                loc_ref[top : top + CHIPS, :], loc_ref[top + CHIPS : top + 2 * CHIPS, :]
            )
        held = where_ref[...]
        ready = jnp.where((needed > 0) & (held >= 0) & (swept == 0), 1.0, 0.0)
        rank = ranked(ready)
        taken = jnp.where((ready > 0) & (rank < CAP), 1.0, 0.0)
        swept = swept + taken
        slot_of = slot_of + taken * (rank + number * CAP)
        for b in range(CAP):
            pick = jnp.max(jnp.where((taken > 0) & (rank == b), held, -1.0), axis=1, keepdims=True)
            picks = jnp.where(entry_lane == number * CAP + b, pick, picks)
        if number == ROUNDS:
            break
        ready = jnp.where((far > 0) & (loc >= 0) & (sent == 0), 1.0, 0.0)
        rank = jnp.zeros((rows, LANES), f32)
        above = jnp.zeros((rows, 1), f32)
        for hops in range(CHIPS - 1, 0, -1):
            level = jnp.where(far == hops, ready, 0.0)
            rank = jnp.where(far == hops, ranked(level) + above, rank)
            above = above + jnp.sum(level, axis=1, keepdims=True)
        taken = jnp.where((ready > 0) & (rank < CAP), 1.0, 0.0)
        sent = sent + taken
        for b in range(CAP):
            pick = jnp.max(jnp.where((taken > 0) & (rank == b), loc, -1.0), axis=1, keepdims=True)
            lists = jnp.where(entry == number * CAP + b, pick, lists)
        came = jnp.dot(step, (taken * (rank + 1)).astype(jnp.bfloat16), preferred_element_type=f32)
        base = FIRST_ROUND + number * 2 * CAP + down * CAP - 1
        loc = jnp.where(came > 0, came + base.astype(f32), loc)
    lists_ref[...] = lists
    picks_ref[...] = picks
    slots_ref[...] = slot_of
    missing = jnp.sum(jnp.where((far > 0) & (sent == 0), 1.0, 0.0)) + jnp.sum(
        jnp.where((needed > 0) & (swept == 0), 1.0, 0.0)
    )
    mine = (me >> 2) * 2 * CHIPS + (me & 3)
    plan_ref[...] = jnp.zeros(plan_ref.shape, jnp.int32)
    plan_ref[0:1, :] = lists_ref[pl.ds(mine, 1), :].astype(jnp.int32)
    plan_ref[1:2, :] = lists_ref[pl.ds(mine + CHIPS, 1), :].astype(jnp.int32)
    plan_ref[2:3, :] = picks_ref[pl.ds(me, 1), :].astype(jnp.int32)
    plan_ref[3:4, :] = slots_ref[pl.ds(me, 1), :].astype(jnp.int32)
    plan_ref[4:5, :] = jnp.full((1, LANES), missing, f32).astype(jnp.int32)


def make_plan(place, table):
    rows, groups = 4 * CHIPS, 2 * CHIPS
    tall, short = pltpu.VMEM((rows, LANES), jnp.float32), pltpu.VMEM((groups, LANES), jnp.float32)
    return pl.pallas_call(
        plan_kernel,
        out_shape=jax.ShapeDtypeStruct((8, LANES), jnp.int32),
        in_specs=[pl.BlockSpec(memory_space=pltpu.SMEM)] * 2,
        out_specs=pl.BlockSpec(memory_space=pltpu.VMEM),
        scratch_shapes=[tall, tall, tall, short, short, short, short],
        name="plan",
    )(place, table)


def pack(plan, line, number, pool):
    lows, arrays = [low for low, _ in pool], [array for _, array in pool]

    def kernel(plan_ref, *refs):
        sources, out = refs[:-1], refs[-1]
        for b in range(CAP):
            at = plan_ref[line * LANES + number * CAP + b]
            for source, low in zip(sources, lows):

                @pl.when((at >= low) & (at < low + source.shape[0]))
                def _(source=source, low=low, b=b, at=at):
                    out[b] = source[at - low]

    in_vmem = pl.BlockSpec(memory_space=pltpu.VMEM)
    return pl.pallas_call(
        kernel,
        out_shape=jax.ShapeDtypeStruct((CAP,) + arrays[0].shape[1:], arrays[0].dtype),
        grid_spec=pltpu.PrefetchScalarGridSpec(num_scalar_prefetch=1, in_specs=[in_vmem] * len(pool), out_specs=in_vmem),
        compiler_params=pltpu.CompilerParams(vmem_limit_bytes=VMEM_LIMIT),
        cost_estimate=pl.CostEstimate(flops=0, bytes_accessed=CAP * 2 * 65536, transcendentals=0),
        name="pack",
    )(plan, *arrays)


def previous_rows(nbr_owner, nbr_slot, nbr_count):
    rows = jnp.concatenate([nbr_owner, nbr_slot, nbr_count[:, None]], axis=1)
    rows = jnp.concatenate([shifted(rows[-1:], "seq", 1), rows[:-1]], axis=0)
    return rows[:, :KMAX], rows[:, KMAX : 2 * KMAX], rows[:, 2 * KMAX]


def fetch_by_request(store, owners, slots):
    owners_axis = lax.axis_size("seq")
    stretches = owners.shape[0]
    depth = min(stretches, max(2, 2 * stretches * KMAX // owners_axis) + 1)
    owners, slots = owners.reshape(-1), slots.reshape(-1)
    order = jnp.arange(owners.shape[0], dtype=jnp.int32)
    before = (owners[:, None] == owners[None, :]) & (order[None, :] < order[:, None])
    target = owners * depth + jnp.sum(before.astype(jnp.int32), axis=1)
    hits = target[:, None] == jnp.arange(owners_axis * depth, dtype=jnp.int32)[None, :]
    table = jnp.sum(jnp.where(hits, slots[:, None], 0), axis=0).reshape(owners_axis, depth)
    asked = lax.all_to_all(table, "seq", split_axis=0, concat_axis=0, tiled=True)
    arrived = lax.all_to_all(store[asked], "seq", split_axis=0, concat_axis=0, tiled=True)
    fetched = arrived.reshape(owners_axis * depth, NLEN, store.shape[2])[target]
    return lax.all_gather(fetched, FEATURES, axis=2, tiled=True)


def four_pieces(value):
    across = swapped(value, "mp")
    return [value, swapped(value, "rep"), across, swapped(across, "rep")]


def fetch_all(store, owners, slots):
    seq = lax.axis_index("seq")
    everything = [store]
    for distance in range(1, lax.axis_size("seq")):
        for steps in (distance, -distance):
            everything.append(shifted(store, "seq", steps))
    ahead = owners - seq
    place = jnp.where(ahead == 0, 0, jnp.where(ahead < 0, -2 * ahead - 1, 2 * ahead))
    pool = jnp.concatenate(everything, axis=0)
    return pool[(place * store.shape[0] + slots).reshape(-1)]


def places_of_pieces():
    block = 2 * lax.axis_index("mp") + lax.axis_index("rep")
    return jnp.stack([block ^ i for i in range(4)]).astype(jnp.int32)


def after(pool, token):
    arrays, _ = lax.optimization_barrier(([array for _, array in pool], token))
    return [(low, array) for (low, _), array in zip(pool, arrays)]


def exchanged_table(codes):
    own_part = [codes]
    for offset in range(1, CHIPS):
        own_part.append(lax.ppermute(codes, "seq", [(chip, chip ^ offset) for chip in range(CHIPS)]))
    own_part = jnp.stack(own_part)
    return jnp.concatenate([own_part, swapped(own_part, "parts")], axis=0)


def streamed(queries, key_weight, value_weight, enc_gain, store, nbr_owner, nbr_slot, nbr_count):
    stretches = nbr_owner.shape[0]
    total = stretches * KMAX
    seq = lax.axis_index("seq")
    me = lax.axis_index("parts") * CHIPS + seq
    kept = jnp.arange(KMAX, dtype=jnp.int32)[None, :] < nbr_count[:, None]
    codes = jnp.where(kept, nbr_owner * ENTRIES_EACH + nbr_slot, -1).reshape(-1)
    table = exchanged_table(codes)
    early_up, early_down = shifted(store[:AHEAD], "seq", 1), shifted(store[:AHEAD], "seq", -1)
    plan = make_plan(me.reshape(1).astype(jnp.int32), table.reshape(-1)).reshape(-1)
    missing = plan[4 * LANES]

    offset = jnp.where(seq > 0, (seq ^ (seq - 1)) & 3, 0)
    behind = table[offset]
    asked = jnp.concatenate([jnp.where(seq > 0, behind[total - KMAX :], -1), codes[: total - KMAX]])
    asked = asked.reshape(stretches, KMAX)
    counts = jnp.sum((asked >= 0).astype(jnp.int32), axis=1)
    first = jnp.maximum(asked[:, 0], 0)
    asked = jnp.stack([first, jnp.where(asked[:, 1] >= 0, asked[:, 1], first)], axis=1).reshape(-1)

    plan, enc_gain = lax.optimization_barrier((plan, enc_gain))
    gain = jnp.concatenate(four_pieces(enc_gain[None]), axis=1)
    places = places_of_pieces()
    wanted = plan[2 * LANES : 2 * LANES + total].reshape(ROUNDS + 1, CAP)[:, ::GROUP] >= 0
    marks = jnp.concatenate([jnp.broadcast_to(places, (ROUNDS + 1, 4)), wanted.astype(jnp.int32)], axis=1).reshape(-1)
    planned_slots = plan[3 * LANES : 4 * LANES][asked]

    up, down = [(0, store), (ENTRIES_EACH, early_up)], [(0, store), (ENTRIES_EACH + AHEAD, early_down)]
    held, pieces = (), []

    def projected(number):
        return project(marks, gain, pieces[number], key_weight, value_weight, GROUP, total, number, held)

    for number in range(ROUNDS + 1):
        pool = up + down[1:]
        if number < ROUNDS:
            base = FIRST_ROUND + number * 2 * CAP
            going_up = pack(plan, 0, number, after(up, held))
            going_down = pack(plan, 1, number, after(down, going_up))
            up = up + [(base, shifted(going_up, "seq", 1))]
            down = down + [(base + CAP, shifted(going_down, "seq", -1))]
            pool = after(pool, going_down)
        mine = pack(plan, 2, number, pool)
        pieces.append([mine, swapped(mine, "rep"), swapped(mine, "mp")])
        if number > 0:
            pieces[number - 1].append(swapped(pieces[number - 1][2], "rep"))
            pieces[number - 1], _ = lax.optimization_barrier((pieces[number - 1], mine))
            held = projected(number - 1)
    pieces[ROUNDS], held = lax.optimization_barrier((pieces[ROUNDS], held))
    pieces[ROUNDS].append(swapped(pieces[ROUNDS][2], "rep"))
    keys, values = projected(ROUNDS)

    def whole(state):
        mine = fetch_all(store, asked >> 4, asked & (ENTRIES_EACH - 1))
        whole_marks = jnp.concatenate([places, jnp.ones((total // 4,), jnp.int32)])
        keys, values = project(whole_marks, gain, four_pieces(mine), key_weight, value_weight, 4, total)
        return jnp.zeros_like(state[0]), jnp.arange(total, dtype=jnp.int32), keys, values

    state = lax.while_loop(lambda state: state[0] > 0, whole, (missing, planned_slots, keys, values))
    return attend(state[1], counts, queries, *state[2:])


def requested(queries, key_weight, value_weight, enc_gain, store, nbr_owner, nbr_slot, nbr_count):
    gain = lax.all_gather(enc_gain, FEATURES, axis=0, tiled=True)[None]
    owners, slots, counts = previous_rows(nbr_owner, nbr_slot, nbr_count)
    total = owners.size
    pieces = [fetch_by_request(store, owners, slots)]
    marks = jnp.concatenate([jnp.zeros((1,), jnp.int32), jnp.ones((total // 4,), jnp.int32)])
    keys, values = project(marks, gain, pieces, key_weight, value_weight, 4, total)
    return attend(jnp.arange(total, dtype=jnp.int32), counts, queries, keys, values)


def solution(mesh):
    in_specs = (
        P(SEQ_SPEC, FEATURES),
        P(None, FEATURES),
        P(None, FEATURES),
        P(FEATURES),
        P(SEQ_SPEC, None, FEATURES),
        P(SEQ_SPEC, None),
        P(SEQ_SPEC, None),
        P(SEQ_SPEC),
    )
    out_specs = P(SEQ_SPEC, FEATURES)
    shape = dict(mesh.shape)
    small = shape == {"parts": 2, "seq": CHIPS, "mp": 2, "rep": 2}
    body = streamed if small else requested
    return jax.shard_map(body, mesh=mesh, in_specs=in_specs, out_specs=out_specs, check_vma=False)
```

```python
import math

import jax
import jax.numpy as jnp
from jax import lax
from jax.experimental import pallas as pl
from jax.experimental.pallas import tpu as pltpu
from jax.sharding import PartitionSpec as P

HEAD_DIM = 128
DE = 1024
NLEN = 128
STRETCH = 64
KMAX = 2
EPS = 1e-06

SEQ_SPEC = ("parts", "seq")
FEATURES = ("mp", "rep")
VMEM_LIMIT = 28 * 1024 * 1024

CHIPS = 4
ENTRIES_EACH = 16
AHEAD = 9
ROUNDS = 3
CAP = 6
GROUP = 3
FIRST_ROUND = ENTRIES_EACH + 2 * AHEAD
LANES = 128


def shifted(value, axis, steps):
    count = lax.axis_size(axis)
    first, last = max(0, -steps), min(count, count - steps)
    return lax.ppermute(value, axis, [(source, source + steps) for source in range(first, last)])


def swapped(value, axis):
    return lax.ppermute(value, axis, [(0, 1), (1, 0)])


def project(marks, gain, pieces, key_weight, value_weight, group, total, number=0, held=()):
    count, tokens, width = pieces[0].shape
    columns = key_weight.shape[1]
    steps = count // group
    base = number * (len(pieces) + steps)

    def kernel(marks_ref, gain_ref, *refs):
        parts, key_blocks, value_blocks = [refs[i * len(pieces) : (i + 1) * len(pieces)] for i in range(3)]
        keys_out, values_out = refs[-2:]

        @pl.when(marks_ref[base + len(pieces) + pl.program_id(0)] > 0)
        def _():
            raw = [part[...].reshape(group * tokens, width).astype(jnp.float32) for part in parts]
            squares = sum(jnp.sum(part * part, axis=1, keepdims=True) for part in raw)
            scale = lax.rsqrt(squares / DE + EPS)
            states = [
                (part * scale * gain_ref[:, index * width : (index + 1) * width]).astype(jnp.bfloat16)
                for index, part in enumerate(raw)
            ]
            for blocks, out in ((key_blocks, keys_out), (value_blocks, values_out)):
                product = sum(
                    jnp.dot(state, block[...], preferred_element_type=jnp.float32)
                    for state, block in zip(states, blocks)
                )
                out[...] = product.astype(jnp.bfloat16).reshape(out.shape)

    out = jax.ShapeDtypeStruct((total, tokens, columns), jnp.bfloat16)
    piece_spec = pl.BlockSpec((group, tokens, width), lambda i, _: (i, 0, 0))

    def weight_spec(piece):
        return pl.BlockSpec((width, columns), lambda i, marks: (marks[base + piece], 0))

    weight_specs = [weight_spec(piece) for piece in range(len(pieces))]
    out_spec = pl.BlockSpec((group, tokens, columns), lambda i, _: (i + number * steps, 0, 0))
    operands = (marks, gain, *pieces, *[key_weight] * len(pieces), *[value_weight] * len(pieces), *held)
    return pl.pallas_call(
        kernel,
        out_shape=(out, out),
        grid_spec=pltpu.PrefetchScalarGridSpec(
            num_scalar_prefetch=1,
            grid=(steps,),
            in_specs=[pl.BlockSpec((1, DE), lambda i, _: (0, 0))]
            + [piece_spec] * len(pieces)
            + weight_specs * 2
            + [pl.BlockSpec(memory_space=pl.ANY)] * len(held),
            out_specs=(out_spec, out_spec),
        ),
        input_output_aliases={len(operands) - len(held) + i: i for i in range(len(held))},
        compiler_params=pltpu.CompilerParams(vmem_limit_bytes=VMEM_LIMIT),
        cost_estimate=pl.CostEstimate(
            flops=4 * count * tokens * DE * columns,
            bytes_accessed=2 * (count * tokens * (DE + 2 * columns) + 2 * DE * columns),
            transcendentals=0,
        ),
        name="project",
    )(*operands)


SAME_COLUMNS = (((1,), (1,)), ((), ()))
SAME_ROWS = (((0,), (0,)), ((), ()))


def attend_kernel(slots, counts, query_ref, *refs):
    *entries, out_ref = refs
    keys, values = entries[: len(entries) // 2], entries[len(entries) // 2 :]
    together = len(keys) // KMAX
    wide = 2 * HEAD_DIM
    factor = math.log2(math.e) / math.sqrt(HEAD_DIM)
    count = [counts[pl.program_id(0) * together + g] for g in range(together)]
    work = [(g, start) for g in range(together) for start in range(0, query_ref.shape[1], wide)]

    def scored(g, start):
        query = query_ref[g * STRETCH : (g + 1) * STRETCH, start : start + wide]
        left, right = query[:, :HEAD_DIM], query[:, HEAD_DIM:]
        zero = jnp.zeros_like(left)
        both = jnp.concatenate([jnp.concatenate([left, zero], 1), jnp.concatenate([zero, right], 1)], 0)
        one, two = [
            lax.dot_general(
                keys[g * KMAX + k][0, :, start : start + wide], both, SAME_COLUMNS, preferred_element_type=jnp.float32
            )
            for k in range(KMAX)
        ]
        return one, jnp.where(count[g] == 2, two, -1e30)

    def weighed(one, two):
        top = jnp.maximum(one, two).max(0, keepdims=True)
        one, two = jnp.exp2((one - top) * factor), jnp.exp2((two - top) * factor)
        share = 1.0 / (one + two).sum(0, keepdims=True)
        return (one * share).astype(jnp.bfloat16), (two * share).astype(jnp.bfloat16)

    def mix(g, start, weights):
        mixed = sum(
            lax.dot_general(
                weights[k], values[g * KMAX + k][0, :, start : start + wide], SAME_ROWS, preferred_element_type=jnp.float32
            )
            for k in range(KMAX)
        )
        mixed = jnp.where(count[g] > 0, mixed, 0.0).astype(jnp.bfloat16)
        rows = slice(g * STRETCH, (g + 1) * STRETCH)
        out_ref[rows, start : start + HEAD_DIM] = mixed[:STRETCH, :HEAD_DIM]
        out_ref[rows, start + HEAD_DIM : start + wide] = mixed[STRETCH:, HEAD_DIM:]

    scores = [scored(*piece) for piece in work]
    weights = [weighed(*pair) for pair in scores]
    for piece, pair in zip(work, weights):
        mix(*piece, pair)


def attend(slots, counts, queries, keys, values, together=3):
    stretches = counts.shape[0]
    columns = queries.shape[1]

    def entry(i):
        return pl.BlockSpec((1, NLEN, columns), lambda step, slots, _: (slots[step * together * KMAX + i], 0, 0))

    query_spec = pl.BlockSpec((together * STRETCH, columns), lambda i, *_: (i, 0))
    entries = [entry(i) for i in range(together * KMAX)]
    return pl.pallas_call(
        attend_kernel,
        out_shape=jax.ShapeDtypeStruct(queries.shape, jnp.bfloat16),
        grid_spec=pltpu.PrefetchScalarGridSpec(
            num_scalar_prefetch=2,
            grid=(stretches // together,),
            in_specs=[query_spec] + entries * 2,
            out_specs=query_spec,
        ),
        compiler_params=pltpu.CompilerParams(vmem_limit_bytes=VMEM_LIMIT),
        cost_estimate=pl.CostEstimate(
            flops=8 * stretches * STRETCH * KMAX * NLEN * columns,
            bytes_accessed=4 * stretches * columns * (STRETCH + KMAX * NLEN),
            transcendentals=stretches * STRETCH * KMAX * NLEN * columns // HEAD_DIM,
        ),
        name="attend",
    )(slots, counts, queries, *[keys] * len(entries), *[values] * len(entries))


def plan_kernel(place, table, plan_ref, far_ref, loc_ref, lists_ref, need_ref, where_ref, picks_ref, slots_ref):
    f32 = jnp.float32
    rows, groups = 4 * CHIPS, 2 * CHIPS
    me = place[0]
    each = table.shape[0] // groups
    lane = lax.broadcasted_iota(jnp.int32, (1, LANES), 1)

    bases = []
    for group in range(groups):
        offset = jnp.bitwise_xor(me, group)
        bases.append(offset * each)
    need = []
    for group in range(groups):
        wanted = [bases[group] + j for j in range(each - KMAX)]
        if group % CHIPS > 0:
            wanted += [bases[group - 1] + each - KMAX + k for k in range(KMAX)]
        hit = jnp.zeros((1, LANES), f32)
        for index in wanted:
            hit = jnp.where(lane == table[index], 1.0, hit)
        need.append(hit)
        need_ref[group : group + 1, :] = hit
    for part in range(2):
        for down in range(2):
            for chip in range(CHIPS):
                reach = jnp.zeros((1, LANES), f32)
                for hops in range(1, CHIPS):
                    to = chip - hops if down else chip + hops
                    if 0 <= to < CHIPS:
                        reach = jnp.where(need[part * CHIPS + to] > 0, float(hops), reach)
                behind = lane >= chip * ENTRIES_EACH if down else lane < (chip + 1) * ENTRIES_EACH
                row = part * 2 * CHIPS + down * CHIPS + chip
                far_ref[row : row + 1, :] = jnp.where(behind, reach, 0.0)

    row = lax.broadcasted_iota(jnp.int32, (rows, LANES), 0)
    entry = lax.broadcasted_iota(jnp.int32, (rows, LANES), 1)
    chip, down = row & (CHIPS - 1), (row >> 2) & 1
    owner, slot = entry >> 4, entry & (ENTRIES_EACH - 1)
    source = jnp.where(down == 1, chip + 1, chip - 1)
    early = slot < AHEAD
    loc = jnp.where(
        owner == chip,
        slot,
        jnp.where((owner == source) & (owner < CHIPS) & early, ENTRIES_EACH + down * AHEAD + slot, -1),
    ).astype(f32)
    sent = jnp.where((owner == chip) & early, 1.0, 0.0)
    far = far_ref[...]
    needed = need_ref[...]
    swept = jnp.zeros((groups, LANES), f32)
    slot_of = jnp.zeros((groups, LANES), f32)
    lists = jnp.full((rows, LANES), -1.0, f32)
    picks = jnp.full((groups, LANES), -1.0, f32)
    one, two = lax.broadcasted_iota(jnp.int32, (LANES, LANES), 0), lax.broadcasted_iota(jnp.int32, (LANES, LANES), 1)
    earlier = jnp.where(one < two, 1.0, 0.0).astype(jnp.bfloat16)
    to, source = lax.broadcasted_iota(jnp.int32, (rows, rows), 0), lax.broadcasted_iota(jnp.int32, (rows, rows), 1)
    up_step = ((to >> 2) & 1 == 0) & (to & 3 > 0) & (source == to - 1)
    down_step = ((to >> 2) & 1 == 1) & (to & 3 < 3) & (source == to + 1)
    step = jnp.where(up_step | down_step, 1.0, 0.0).astype(jnp.bfloat16)
    entry_lane = entry[:groups]

    def ranked(mask):
        return jnp.dot(mask.astype(jnp.bfloat16), earlier, preferred_element_type=f32)

    for number in range(ROUNDS + 1):
        loc_ref[...] = loc
        for part in range(2):
            top = part * 2 * CHIPS
            where_ref[part * CHIPS : (part + 1) * CHIPS, :] = jnp.maximum(
                loc_ref[top : top + CHIPS, :], loc_ref[top + CHIPS : top + 2 * CHIPS, :]
            )
        held = where_ref[...]
        ready = jnp.where((needed > 0) & (held >= 0) & (swept == 0), 1.0, 0.0)
        rank = ranked(ready)
        taken = jnp.where((ready > 0) & (rank < CAP), 1.0, 0.0)
        swept = swept + taken
        slot_of = slot_of + taken * (rank + number * CAP)
        for b in range(CAP):
            pick = jnp.max(jnp.where((taken > 0) & (rank == b), held, -1.0), axis=1, keepdims=True)
            picks = jnp.where(entry_lane == number * CAP + b, pick, picks)
        if number == ROUNDS:
            break
        ready = jnp.where((far > 0) & (loc >= 0) & (sent == 0), 1.0, 0.0)
        rank = jnp.zeros((rows, LANES), f32)
        above = jnp.zeros((rows, 1), f32)
        for hops in range(CHIPS - 1, 0, -1):
            level = jnp.where(far == hops, ready, 0.0)
            rank = jnp.where(far == hops, ranked(level) + above, rank)
            above = above + jnp.sum(level, axis=1, keepdims=True)
        taken = jnp.where((ready > 0) & (rank < CAP), 1.0, 0.0)
        sent = sent + taken
        for b in range(CAP):
            pick = jnp.max(jnp.where((taken > 0) & (rank == b), loc, -1.0), axis=1, keepdims=True)
            lists = jnp.where(entry == number * CAP + b, pick, lists)
        came = jnp.dot(step, (taken * (rank + 1)).astype(jnp.bfloat16), preferred_element_type=f32)
        base = FIRST_ROUND + number * 2 * CAP + down * CAP - 1
        loc = jnp.where(came > 0, came + base.astype(f32), loc)
    lists_ref[...] = lists
    picks_ref[...] = picks
    slots_ref[...] = slot_of
    missing = jnp.sum(jnp.where((far > 0) & (sent == 0), 1.0, 0.0)) + jnp.sum(
        jnp.where((needed > 0) & (swept == 0), 1.0, 0.0)
    )
    mine = (me >> 2) * 2 * CHIPS + (me & 3)
    plan_ref[...] = jnp.zeros(plan_ref.shape, jnp.int32)
    plan_ref[0:1, :] = lists_ref[pl.ds(mine, 1), :].astype(jnp.int32)
    plan_ref[1:2, :] = lists_ref[pl.ds(mine + CHIPS, 1), :].astype(jnp.int32)
    plan_ref[2:3, :] = picks_ref[pl.ds(me, 1), :].astype(jnp.int32)
    plan_ref[3:4, :] = slots_ref[pl.ds(me, 1), :].astype(jnp.int32)
    plan_ref[4:5, :] = jnp.full((1, LANES), missing, f32).astype(jnp.int32)


def make_plan(place, table):
    rows, groups = 4 * CHIPS, 2 * CHIPS
    tall, short = pltpu.VMEM((rows, LANES), jnp.float32), pltpu.VMEM((groups, LANES), jnp.float32)
    return pl.pallas_call(
        plan_kernel,
        out_shape=jax.ShapeDtypeStruct((8, LANES), jnp.int32),
        in_specs=[pl.BlockSpec(memory_space=pltpu.SMEM)] * 2,
        out_specs=pl.BlockSpec(memory_space=pltpu.VMEM),
        scratch_shapes=[tall, tall, tall, short, short, short, short],
        name="plan",
    )(place, table)


def pack(plan, number, pool):
    lines = (0, 1, 2) if number < ROUNDS else (2,)
    starts = [0]
    for array in pool:
        starts.append(starts[-1] + array.shape[0])

    def kernel(plan_ref, *refs):
        sources, outs = refs[: len(pool)], refs[len(pool) :]
        for line, out in zip(lines, outs):
            for b in range(CAP):
                at = plan_ref[line * LANES + number * CAP + b]
                for source, low, high in zip(sources, starts, starts[1:]):

                    @pl.when((at >= low) & (at < high))
                    def _(source=source, low=low, out=out, b=b, at=at):
                        out[b] = source[at - low]

    in_vmem = pl.BlockSpec(memory_space=pltpu.VMEM)
    return pl.pallas_call(
        kernel,
        out_shape=(jax.ShapeDtypeStruct((CAP,) + pool[0].shape[1:], pool[0].dtype),) * len(lines),
        grid_spec=pltpu.PrefetchScalarGridSpec(
            num_scalar_prefetch=1, in_specs=[in_vmem] * len(pool), out_specs=(in_vmem,) * len(lines)
        ),
        compiler_params=pltpu.CompilerParams(vmem_limit_bytes=VMEM_LIMIT),
        cost_estimate=pl.CostEstimate(flops=0, bytes_accessed=len(lines) * CAP * 2 * 65536, transcendentals=0),
        name="pack",
    )(plan, *pool)


def previous_rows(nbr_owner, nbr_slot, nbr_count):
    rows = jnp.concatenate([nbr_owner, nbr_slot, nbr_count[:, None]], axis=1)
    rows = jnp.concatenate([shifted(rows[-1:], "seq", 1), rows[:-1]], axis=0)
    return rows[:, :KMAX], rows[:, KMAX : 2 * KMAX], rows[:, 2 * KMAX]


def fetch_by_request(store, owners, slots):
    owners_axis = lax.axis_size("seq")
    stretches = owners.shape[0]
    depth = min(stretches, max(2, 2 * stretches * KMAX // owners_axis) + 1)
    owners, slots = owners.reshape(-1), slots.reshape(-1)
    order = jnp.arange(owners.shape[0], dtype=jnp.int32)
    before = (owners[:, None] == owners[None, :]) & (order[None, :] < order[:, None])
    target = owners * depth + jnp.sum(before.astype(jnp.int32), axis=1)
    hits = target[:, None] == jnp.arange(owners_axis * depth, dtype=jnp.int32)[None, :]
    table = jnp.sum(jnp.where(hits, slots[:, None], 0), axis=0).reshape(owners_axis, depth)
    asked = lax.all_to_all(table, "seq", split_axis=0, concat_axis=0, tiled=True)
    arrived = lax.all_to_all(store[asked], "seq", split_axis=0, concat_axis=0, tiled=True)
    fetched = arrived.reshape(owners_axis * depth, NLEN, store.shape[2])[target]
    return lax.all_gather(fetched, FEATURES, axis=2, tiled=True)


def four_pieces(value):
    across = swapped(value, "mp")
    return [value, swapped(value, "rep"), across, swapped(across, "rep")]


def fetch_all(store, owners, slots):
    seq = lax.axis_index("seq")
    everything = [store]
    for distance in range(1, lax.axis_size("seq")):
        for steps in (distance, -distance):
            everything.append(shifted(store, "seq", steps))
    ahead = owners - seq
    place = jnp.where(ahead == 0, 0, jnp.where(ahead < 0, -2 * ahead - 1, 2 * ahead))
    pool = jnp.concatenate(everything, axis=0)
    return pool[(place * store.shape[0] + slots).reshape(-1)]


def places_of_pieces():
    block = 2 * lax.axis_index("mp") + lax.axis_index("rep")
    return jnp.stack([block ^ i for i in range(4)]).astype(jnp.int32)


def exchanged_table(codes):
    own_part = [codes]
    for offset in range(1, CHIPS):
        own_part.append(lax.ppermute(codes, "seq", [(chip, chip ^ offset) for chip in range(CHIPS)]))
    own_part = jnp.stack(own_part)
    return jnp.concatenate([own_part, swapped(own_part, "parts")], axis=0)


def streamed(queries, key_weight, value_weight, enc_gain, store, nbr_owner, nbr_slot, nbr_count):
    stretches = nbr_owner.shape[0]
    total = stretches * KMAX
    seq = lax.axis_index("seq")
    me = lax.axis_index("parts") * CHIPS + seq
    kept = jnp.arange(KMAX, dtype=jnp.int32)[None, :] < nbr_count[:, None]
    codes = jnp.where(kept, nbr_owner * ENTRIES_EACH + nbr_slot, -1).reshape(-1)
    early, codes = lax.optimization_barrier((store[:AHEAD], codes))
    table = exchanged_table(codes)
    early_up, early_down = shifted(early, "seq", 1), shifted(early, "seq", -1)
    plan = make_plan(me.reshape(1).astype(jnp.int32), table.reshape(-1)).reshape(-1)
    missing = plan[4 * LANES]

    offset = jnp.where(seq > 0, (seq ^ (seq - 1)) & 3, 0)
    behind = table[offset]
    asked = jnp.concatenate([jnp.where(seq > 0, behind[total - KMAX :], -1), codes[: total - KMAX]])
    asked = asked.reshape(stretches, KMAX)
    counts = jnp.sum((asked >= 0).astype(jnp.int32), axis=1)
    first = jnp.maximum(asked[:, 0], 0)
    asked = jnp.stack([first, jnp.where(asked[:, 1] >= 0, asked[:, 1], first)], axis=1).reshape(-1)

    places = places_of_pieces()
    wanted = plan[2 * LANES : 2 * LANES + (ROUNDS + 1) * CAP].reshape(ROUNDS + 1, CAP)[:, ::GROUP] >= 0
    marks = jnp.concatenate([jnp.broadcast_to(places, (ROUNDS + 1, 4)), wanted.astype(jnp.int32)], axis=1).reshape(-1)
    slots = plan[3 * LANES : 4 * LANES][asked]

    pool = [store, early_up, early_down]
    held, pieces, gain = (), [], None
    room = (ROUNDS + 1) * CAP

    def projected(number):
        return project(marks, gain, pieces[number], key_weight, value_weight, GROUP, room, number, held)

    for number in range(ROUNDS + 1):
        *ways, mine = pack(plan, number, pool)
        arrived = [shifted(way, "seq", steps) for way, steps in zip(ways, (1, -1))]
        pieces.append([mine, swapped(mine, "rep"), swapped(mine, "mp")])
        if number == 0:
            enc_gain, pieces[0][1] = lax.optimization_barrier((enc_gain, pieces[0][1]))
            gain = jnp.concatenate(four_pieces(enc_gain[None]), axis=1)
        else:
            pieces[number - 1].append(swapped(pieces[number - 1][2], "rep"))
            held = projected(number - 1)
        arrived, pieces[number], held, gain, slots, marks = lax.optimization_barrier(
            (arrived, pieces[number], held, gain, slots, marks)
        )
        pool += arrived
    pieces[ROUNDS].append(swapped(pieces[ROUNDS][2], "rep"))
    keys, values = projected(ROUNDS)

    def whole(state):
        mine = fetch_all(store, asked >> 4, asked & (ENTRIES_EACH - 1))
        whole_marks = jnp.concatenate([places, jnp.ones((total // 4,), jnp.int32)])
        keys, values = project(whole_marks, gain, four_pieces(mine), key_weight, value_weight, 4, room)
        return jnp.zeros_like(state[0]), jnp.arange(total, dtype=jnp.int32), keys, values

    state = lax.while_loop(lambda state: state[0] > 0, whole, (missing, slots, keys, values))
    return attend(state[1], counts, queries, *state[2:])


def requested(queries, key_weight, value_weight, enc_gain, store, nbr_owner, nbr_slot, nbr_count):
    gain = lax.all_gather(enc_gain, FEATURES, axis=0, tiled=True)[None]
    owners, slots, counts = previous_rows(nbr_owner, nbr_slot, nbr_count)
    total = owners.size
    pieces = [fetch_by_request(store, owners, slots)]
    marks = jnp.concatenate([jnp.zeros((1,), jnp.int32), jnp.ones((total // 4,), jnp.int32)])
    keys, values = project(marks, gain, pieces, key_weight, value_weight, 4, total)
    return attend(jnp.arange(total, dtype=jnp.int32), counts, queries, keys, values)


def solution(mesh):
    in_specs = (
        P(SEQ_SPEC, FEATURES),
        P(None, FEATURES),
        P(None, FEATURES),
        P(FEATURES),
        P(SEQ_SPEC, None, FEATURES),
        P(SEQ_SPEC, None),
        P(SEQ_SPEC, None),
        P(SEQ_SPEC),
    )
    out_specs = P(SEQ_SPEC, FEATURES)
    shape = dict(mesh.shape)
    small = shape == {"parts": 2, "seq": CHIPS, "mp": 2, "rep": 2}
    body = streamed if small else requested
    return jax.shard_map(body, mesh=mesh, in_specs=in_specs, out_specs=out_specs, check_vma=False)
```

```python
import math

import jax
import jax.numpy as jnp
from jax import lax
from jax.experimental import pallas as pl
from jax.experimental.pallas import tpu as pltpu
from jax.sharding import PartitionSpec as P

HEAD_DIM = 128
DE = 1024
NLEN = 128
STRETCH = 64
KMAX = 2
EPS = 1e-06

SEQ_SPEC = ("parts", "seq")
FEATURES = ("mp", "rep")
VMEM_LIMIT = 28 * 1024 * 1024

CHIPS = 4
ENTRIES_EACH = 16
HALF = 8
ROUNDS = 5
SWEEPS = ROUNDS + 2
CAP = 4
GROUP = 2
LANES = 128


def shifted(value, axis, steps):
    count = lax.axis_size(axis)
    first, last = max(0, -steps), min(count, count - steps)
    return lax.ppermute(value, axis, [(source, source + steps) for source in range(first, last)])


def swapped(value, axis):
    return lax.ppermute(value, axis, [(0, 1), (1, 0)])


def project(marks, gain, pieces, key_weight, value_weight, group, total, number=0, held=()):
    count, tokens, width = pieces[0].shape
    columns = key_weight.shape[1]
    steps = count // group
    base = number * (len(pieces) + steps)

    def kernel(marks_ref, gain_ref, *refs):
        parts, key_blocks, value_blocks = [refs[i * len(pieces) : (i + 1) * len(pieces)] for i in range(3)]
        keys_out, values_out = refs[-2:]

        @pl.when(marks_ref[base + len(pieces) + pl.program_id(0)] > 0)
        def _():
            raw = [part[...].reshape(group * tokens, width).astype(jnp.float32) for part in parts]
            squares = sum(jnp.sum(part * part, axis=1, keepdims=True) for part in raw)
            scale = lax.rsqrt(squares / DE + EPS)
            states = [
                (part * scale * gain_ref[:, index * width : (index + 1) * width]).astype(jnp.bfloat16)
                for index, part in enumerate(raw)
            ]
            for blocks, out in ((key_blocks, keys_out), (value_blocks, values_out)):
                product = sum(
                    jnp.dot(state, block[...], preferred_element_type=jnp.float32)
                    for state, block in zip(states, blocks)
                )
                out[...] = product.astype(jnp.bfloat16).reshape(out.shape)

    out = jax.ShapeDtypeStruct((total, tokens, columns), jnp.bfloat16)
    piece_spec = pl.BlockSpec((group, tokens, width), lambda i, _: (i, 0, 0))

    def weight_spec(piece):
        return pl.BlockSpec((width, columns), lambda i, marks: (marks[base + piece], 0))

    weight_specs = [weight_spec(piece) for piece in range(len(pieces))]
    out_spec = pl.BlockSpec((group, tokens, columns), lambda i, _: (i + number * steps, 0, 0))
    operands = (marks, gain, *pieces, *[key_weight] * len(pieces), *[value_weight] * len(pieces), *held)
    return pl.pallas_call(
        kernel,
        out_shape=(out, out),
        grid_spec=pltpu.PrefetchScalarGridSpec(
            num_scalar_prefetch=1,
            grid=(steps,),
            in_specs=[pl.BlockSpec((1, DE), lambda i, _: (0, 0))]
            + [piece_spec] * len(pieces)
            + weight_specs * 2
            + [pl.BlockSpec(memory_space=pl.ANY)] * len(held),
            out_specs=(out_spec, out_spec),
        ),
        input_output_aliases={len(operands) - len(held) + i: i for i in range(len(held))},
        compiler_params=pltpu.CompilerParams(vmem_limit_bytes=VMEM_LIMIT),
        cost_estimate=pl.CostEstimate(
            flops=4 * count * tokens * DE * columns,
            bytes_accessed=2 * (count * tokens * (DE + 2 * columns) + 2 * DE * columns),
            transcendentals=0,
        ),
        name="project",
    )(*operands)


SAME_COLUMNS = (((1,), (1,)), ((), ()))
SAME_ROWS = (((0,), (0,)), ((), ()))


def attend_kernel(slots, counts, query_ref, *refs):
    *entries, out_ref = refs
    keys, values = entries[: len(entries) // 2], entries[len(entries) // 2 :]
    together = len(keys) // KMAX
    wide = 2 * HEAD_DIM
    factor = math.log2(math.e) / math.sqrt(HEAD_DIM)
    count = [counts[pl.program_id(0) * together + g] for g in range(together)]
    work = [(g, start) for g in range(together) for start in range(0, query_ref.shape[1], wide)]

    def scored(g, start):
        query = query_ref[g * STRETCH : (g + 1) * STRETCH, start : start + wide]
        left, right = query[:, :HEAD_DIM], query[:, HEAD_DIM:]
        zero = jnp.zeros_like(left)
        both = jnp.concatenate([jnp.concatenate([left, zero], 1), jnp.concatenate([zero, right], 1)], 0)
        one, two = [
            lax.dot_general(
                keys[g * KMAX + k][0, :, start : start + wide], both, SAME_COLUMNS, preferred_element_type=jnp.float32
            )
            for k in range(KMAX)
        ]
        return one, jnp.where(count[g] == 2, two, -1e30)

    def weighed(one, two):
        top = jnp.maximum(one, two).max(0, keepdims=True)
        one, two = jnp.exp2((one - top) * factor), jnp.exp2((two - top) * factor)
        share = 1.0 / (one + two).sum(0, keepdims=True)
        return (one * share).astype(jnp.bfloat16), (two * share).astype(jnp.bfloat16)

    def mix(g, start, weights):
        mixed = sum(
            lax.dot_general(
                weights[k], values[g * KMAX + k][0, :, start : start + wide], SAME_ROWS, preferred_element_type=jnp.float32
            )
            for k in range(KMAX)
        )
        mixed = jnp.where(count[g] > 0, mixed, 0.0).astype(jnp.bfloat16)
        rows = slice(g * STRETCH, (g + 1) * STRETCH)
        out_ref[rows, start : start + HEAD_DIM] = mixed[:STRETCH, :HEAD_DIM]
        out_ref[rows, start + HEAD_DIM : start + wide] = mixed[STRETCH:, HEAD_DIM:]

    scores = [scored(*piece) for piece in work]
    weights = [weighed(*pair) for pair in scores]
    for piece, pair in zip(work, weights):
        mix(*piece, pair)


def attend(slots, counts, queries, keys, values, together=3):
    stretches = counts.shape[0]
    columns = queries.shape[1]

    def entry(i):
        return pl.BlockSpec((1, NLEN, columns), lambda step, slots, _: (slots[step * together * KMAX + i], 0, 0))

    query_spec = pl.BlockSpec((together * STRETCH, columns), lambda i, *_: (i, 0))
    entries = [entry(i) for i in range(together * KMAX)]
    return pl.pallas_call(
        attend_kernel,
        out_shape=jax.ShapeDtypeStruct(queries.shape, jnp.bfloat16),
        grid_spec=pltpu.PrefetchScalarGridSpec(
            num_scalar_prefetch=2,
            grid=(stretches // together,),
            in_specs=[query_spec] + entries * 2,
            out_specs=query_spec,
        ),
        compiler_params=pltpu.CompilerParams(vmem_limit_bytes=VMEM_LIMIT),
        cost_estimate=pl.CostEstimate(
            flops=8 * stretches * STRETCH * KMAX * NLEN * columns,
            bytes_accessed=4 * stretches * columns * (STRETCH + KMAX * NLEN),
            transcendentals=stretches * STRETCH * KMAX * NLEN * columns // HEAD_DIM,
        ),
        name="attend",
    )(slots, counts, queries, *[keys] * len(entries), *[values] * len(entries))


def plan_kernel(place, table, plan_ref, far_ref, need_ref, lists_ref, picks_ref, slots_ref):
    f32 = jnp.float32
    groups = 2 * CHIPS
    me = place[0]
    each = table.shape[0] // groups
    lane = lax.broadcasted_iota(jnp.int32, (1, LANES), 1)

    bases = [jnp.bitwise_xor(me, group) * each for group in range(groups)]
    need = []
    for group in range(groups):
        wanted = [bases[group] + j for j in range(each - KMAX)]
        if group % CHIPS > 0:
            wanted += [bases[group - 1] + each - KMAX + k for k in range(KMAX)]
        hit = jnp.zeros((1, LANES), f32)
        for index in wanted:
            hit = jnp.where(lane == table[index], 1.0, hit)
        need.append(hit)
        need_ref[group : group + 1, :] = hit
    for part in range(2):
        for chip in range(CHIPS):
            come = (chip - (lane >> 4)) & (CHIPS - 1)
            reach = jnp.zeros((1, LANES), f32)
            for hops in range(1, CHIPS):
                there = need[part * CHIPS + (chip + hops) % CHIPS] > 0
                reach = jnp.where(there & (come + hops < CHIPS), float(hops), reach)
            row = part * CHIPS + chip
            far_ref[row : row + 1, :] = reach

    row = lax.broadcasted_iota(jnp.int32, (groups, LANES), 0)
    entry = lax.broadcasted_iota(jnp.int32, (groups, LANES), 1)
    chip, owner, slot = row & (CHIPS - 1), entry >> 4, entry & (ENTRIES_EACH - 1)
    loc = jnp.where(owner == chip, slot, -1).astype(f32)
    sent = jnp.where(owner == chip, 1.0, 0.0)
    from_behind = owner == ((chip + CHIPS - 1) & (CHIPS - 1))
    halves = [from_behind & (slot < HALF), from_behind & (slot >= HALF)]
    flights = [jnp.where(half, slot + ENTRIES_EACH, -1).astype(f32) for half in halves]
    far, needed = far_ref[...], need_ref[...]
    swept = jnp.zeros((groups, LANES), f32)
    slot_of = jnp.zeros((groups, LANES), f32)
    lists = jnp.full((groups, LANES), -1.0, f32)
    picks = jnp.full((groups, LANES), -1.0, f32)
    one, two = lax.broadcasted_iota(jnp.int32, (LANES, LANES), 0), lax.broadcasted_iota(jnp.int32, (LANES, LANES), 1)
    earlier = jnp.where(one < two, 1.0, 0.0).astype(jnp.bfloat16)
    to, source = lax.broadcasted_iota(jnp.int32, (groups, groups), 0), lax.broadcasted_iota(jnp.int32, (groups, groups), 1)
    behind = jnp.where(to & (CHIPS - 1) == 0, to + CHIPS - 1, to - 1)
    step = jnp.where(source == behind, 1.0, 0.0).astype(jnp.bfloat16)

    def ranked(mask):
        return jnp.dot(mask.astype(jnp.bfloat16), earlier, preferred_element_type=f32)

    def listed(into, taken, rank, number):
        for b in range(CAP):
            pick = jnp.max(jnp.where((taken > 0) & (rank == b), loc, -1.0), axis=1, keepdims=True)
            into = jnp.where(entry == number * CAP + b, pick, into)
        return into

    for number in range(SWEEPS):
        loc = jnp.maximum(loc, flights[number])
        ready = jnp.where((needed > 0) & (loc >= 0) & (swept == 0), 1.0, 0.0)
        rank = ranked(ready)
        taken = jnp.where((ready > 0) & (rank < CAP), 1.0, 0.0)
        swept = swept + taken
        slot_of = slot_of + taken * (rank + number * CAP)
        picks = listed(picks, taken, rank, number)
        if number < ROUNDS:
            ready = jnp.where((far > 0) & (loc >= 0) & (sent == 0), 1.0, 0.0)
            rank = jnp.zeros((groups, LANES), f32)
            above = jnp.zeros((groups, 1), f32)
            for hops in range(CHIPS - 1, 0, -1):
                level = jnp.where(far == hops, ready, 0.0)
                rank = jnp.where(far == hops, ranked(level) + above, rank)
                above = above + jnp.sum(level, axis=1, keepdims=True)
            taken = jnp.where((ready > 0) & (rank < CAP), 1.0, 0.0)
            sent = sent + taken
            lists = listed(lists, taken, rank, number)
            came = jnp.dot(step, (taken * (rank + 1)).astype(jnp.bfloat16), preferred_element_type=f32)
            flights.append(jnp.where(came > 0, came + float(2 * ENTRIES_EACH + number * CAP - 1), -1.0))
    lists_ref[...] = lists
    picks_ref[...] = picks
    slots_ref[...] = slot_of
    missing = jnp.sum(jnp.where((far > 0) & (sent == 0), 1.0, 0.0)) + jnp.sum(
        jnp.where((needed > 0) & (swept == 0), 1.0, 0.0)
    )
    plan_ref[...] = jnp.zeros(plan_ref.shape, jnp.int32)
    for line, rows in enumerate((lists_ref, picks_ref, slots_ref)):
        plan_ref[line : line + 1, :] = rows[pl.ds(me, 1), :].astype(jnp.int32)
    plan_ref[3:4, :] = jnp.full((1, LANES), missing, f32).astype(jnp.int32)


def make_plan(place, table):
    return pl.pallas_call(
        plan_kernel,
        out_shape=jax.ShapeDtypeStruct((8, LANES), jnp.int32),
        in_specs=[pl.BlockSpec(memory_space=pltpu.SMEM)] * 2,
        out_specs=pl.BlockSpec(memory_space=pltpu.VMEM),
        scratch_shapes=[pltpu.VMEM((2 * CHIPS, LANES), jnp.float32)] * 5,
        name="plan",
    )(place, table)


def pack(plan, number, pool):
    lines = (0, 1) if number < ROUNDS else (1,)
    starts = [0]
    for array in pool:
        starts.append(starts[-1] + array.shape[0])

    def kernel(plan_ref, *refs):
        sources, outs = refs[: len(pool)], refs[len(pool) :]
        for line, out in zip(lines, outs):
            for b in range(CAP):
                at = plan_ref[line * LANES + number * CAP + b]
                for source, low, high in zip(sources, starts, starts[1:]):

                    @pl.when((at >= low) & (at < high))
                    def _(source=source, low=low, out=out, b=b, at=at):
                        out[b] = source[at - low]

    in_vmem = pl.BlockSpec(memory_space=pltpu.VMEM)
    return pl.pallas_call(
        kernel,
        out_shape=(jax.ShapeDtypeStruct((CAP,) + pool[0].shape[1:], pool[0].dtype),) * len(lines),
        grid_spec=pltpu.PrefetchScalarGridSpec(
            num_scalar_prefetch=1, in_specs=[in_vmem] * len(pool), out_specs=(in_vmem,) * len(lines)
        ),
        compiler_params=pltpu.CompilerParams(vmem_limit_bytes=VMEM_LIMIT),
        cost_estimate=pl.CostEstimate(flops=0, bytes_accessed=len(lines) * CAP * 2 * 65536, transcendentals=0),
        name="pack",
    )(plan, *pool)


def previous_rows(nbr_owner, nbr_slot, nbr_count):
    rows = jnp.concatenate([nbr_owner, nbr_slot, nbr_count[:, None]], axis=1)
    rows = jnp.concatenate([shifted(rows[-1:], "seq", 1), rows[:-1]], axis=0)
    return rows[:, :KMAX], rows[:, KMAX : 2 * KMAX], rows[:, 2 * KMAX]


def fetch_by_request(store, owners, slots):
    owners_axis = lax.axis_size("seq")
    stretches = owners.shape[0]
    depth = min(stretches, max(2, 2 * stretches * KMAX // owners_axis) + 1)
    owners, slots = owners.reshape(-1), slots.reshape(-1)
    order = jnp.arange(owners.shape[0], dtype=jnp.int32)
    before = (owners[:, None] == owners[None, :]) & (order[None, :] < order[:, None])
    target = owners * depth + jnp.sum(before.astype(jnp.int32), axis=1)
    hits = target[:, None] == jnp.arange(owners_axis * depth, dtype=jnp.int32)[None, :]
    table = jnp.sum(jnp.where(hits, slots[:, None], 0), axis=0).reshape(owners_axis, depth)
    asked = lax.all_to_all(table, "seq", split_axis=0, concat_axis=0, tiled=True)
    arrived = lax.all_to_all(store[asked], "seq", split_axis=0, concat_axis=0, tiled=True)
    fetched = arrived.reshape(owners_axis * depth, NLEN, store.shape[2])[target]
    return lax.all_gather(fetched, FEATURES, axis=2, tiled=True)


def onward(value):
    size = lax.axis_size("seq")
    return lax.ppermute(value, "seq", [(chip, (chip + 1) % size) for chip in range(size)])


def four_pieces(value):
    across = swapped(value, "mp")
    return [value, swapped(value, "rep"), across, swapped(across, "rep")]


def fetch_all(store, owners, slots):
    seq = lax.axis_index("seq")
    everything = [store]
    for distance in range(1, lax.axis_size("seq")):
        for steps in (distance, -distance):
            everything.append(shifted(store, "seq", steps))
    ahead = owners - seq
    place = jnp.where(ahead == 0, 0, jnp.where(ahead < 0, -2 * ahead - 1, 2 * ahead))
    pool = jnp.concatenate(everything, axis=0)
    return pool[(place * store.shape[0] + slots).reshape(-1)]


def places_of_pieces():
    block = 2 * lax.axis_index("mp") + lax.axis_index("rep")
    return jnp.stack([block ^ i for i in range(4)]).astype(jnp.int32)


def exchanged_table(codes):
    own_part = [codes]
    for offset in range(1, CHIPS):
        own_part.append(lax.ppermute(codes, "seq", [(chip, chip ^ offset) for chip in range(CHIPS)]))
    own_part = jnp.stack(own_part)
    return jnp.concatenate([own_part, swapped(own_part, "parts")], axis=0)


def streamed(queries, key_weight, value_weight, enc_gain, store, nbr_owner, nbr_slot, nbr_count):
    stretches = nbr_owner.shape[0]
    total = stretches * KMAX
    seq = lax.axis_index("seq")
    me = lax.axis_index("parts") * CHIPS + seq
    kept = jnp.arange(KMAX, dtype=jnp.int32)[None, :] < nbr_count[:, None]
    codes = jnp.where(kept, nbr_owner * ENTRIES_EACH + nbr_slot, -1).reshape(-1)
    first, second, codes = lax.optimization_barrier((store[:HALF], store[HALF:], codes))
    table = exchanged_table(codes)
    flights = [onward(first), onward(second)]
    plan = make_plan(me.reshape(1).astype(jnp.int32), table.reshape(-1)).reshape(-1)
    missing = plan[3 * LANES]

    offset = jnp.where(seq > 0, (seq ^ (seq - 1)) & 3, 0)
    behind = table[offset]
    asked = jnp.concatenate([jnp.where(seq > 0, behind[total - KMAX :], -1), codes[: total - KMAX]])
    asked = asked.reshape(stretches, KMAX)
    counts = jnp.sum((asked >= 0).astype(jnp.int32), axis=1)
    first = jnp.maximum(asked[:, 0], 0)
    asked = jnp.stack([first, jnp.where(asked[:, 1] >= 0, asked[:, 1], first)], axis=1).reshape(-1)

    places = places_of_pieces()
    wanted = plan[LANES : LANES + SWEEPS * CAP].reshape(SWEEPS, CAP)[:, ::GROUP] >= 0
    marks = jnp.concatenate([jnp.broadcast_to(places, (SWEEPS, 4)), wanted.astype(jnp.int32)], axis=1).reshape(-1)
    slots = plan[2 * LANES : 3 * LANES][asked]

    room = SWEEPS * CAP
    held, pieces, gain = (), [], None

    def projected(number):
        return project(marks, gain, pieces[number], key_weight, value_weight, GROUP, room, number, held)

    for number in range(SWEEPS):
        *ways, mine = pack(plan, number, [store] + flights[: number + 1])
        flights += [onward(way) for way in ways]
        pieces.append([mine, swapped(mine, "rep"), swapped(mine, "mp")])
        if number == 0:
            enc_gain, pieces[0][1] = lax.optimization_barrier((enc_gain, pieces[0][1]))
            gain = jnp.concatenate(four_pieces(enc_gain[None]), axis=1)
        if number > 1:
            held = projected(number - 2)
        if number > 0:
            pieces[number - 1].append(swapped(pieces[number - 1][2], "rep"))
        if number + 1 < SWEEPS:
            flights[number + 1], pieces[: number], held, gain, slots, marks = lax.optimization_barrier(
                (flights[number + 1], pieces[: number], held, gain, slots, marks)
            )
    held = projected(SWEEPS - 2)
    pieces[-1], held = lax.optimization_barrier((pieces[-1], held))
    pieces[-1].append(swapped(pieces[-1][2], "rep"))
    keys, values = projected(SWEEPS - 1)

    def whole(state):
        mine = fetch_all(store, asked >> 4, asked & (ENTRIES_EACH - 1))
        whole_marks = jnp.concatenate([places, jnp.ones((total // 4,), jnp.int32)])
        keys, values = project(whole_marks, gain, four_pieces(mine), key_weight, value_weight, 4, room)
        return jnp.zeros_like(state[0]), jnp.arange(total, dtype=jnp.int32), keys, values

    state = lax.while_loop(lambda state: state[0] > 0, whole, (missing, slots, keys, values))
    return attend(state[1], counts, queries, *state[2:])


def requested(queries, key_weight, value_weight, enc_gain, store, nbr_owner, nbr_slot, nbr_count):
    gain = lax.all_gather(enc_gain, FEATURES, axis=0, tiled=True)[None]
    owners, slots, counts = previous_rows(nbr_owner, nbr_slot, nbr_count)
    total = owners.size
    pieces = [fetch_by_request(store, owners, slots)]
    marks = jnp.concatenate([jnp.zeros((1,), jnp.int32), jnp.ones((total // 4,), jnp.int32)])
    keys, values = project(marks, gain, pieces, key_weight, value_weight, 4, total)
    return attend(jnp.arange(total, dtype=jnp.int32), counts, queries, keys, values)


def solution(mesh):
    in_specs = (
        P(SEQ_SPEC, FEATURES),
        P(None, FEATURES),
        P(None, FEATURES),
        P(FEATURES),
        P(SEQ_SPEC, None, FEATURES),
        P(SEQ_SPEC, None),
        P(SEQ_SPEC, None),
        P(SEQ_SPEC),
    )
    out_specs = P(SEQ_SPEC, FEATURES)
    shape = dict(mesh.shape)
    small = shape == {"parts": 2, "seq": CHIPS, "mp": 2, "rep": 2}
    body = streamed if small else requested
    return jax.shard_map(body, mesh=mesh, in_specs=in_specs, out_specs=out_specs, check_vma=False)
```

```python
import math

import jax
import jax.numpy as jnp
from jax import lax
from jax.experimental import pallas as pl
from jax.experimental.pallas import tpu as pltpu
from jax.sharding import PartitionSpec as P

HEAD_DIM = 128
DE = 1024
NLEN = 128
STRETCH = 64
KMAX = 2
EPS = 1e-06

SEQ_SPEC = ("parts", "seq")
FEATURES = ("mp", "rep")
VMEM_LIMIT = 28 * 1024 * 1024

CHIPS = 4
ENTRIES_EACH = 16
HALF = 8
ROUNDS = 5
SWEEPS = ROUNDS + 2
CAP = 4
GROUP = 2
LANES = 128

LITTLE = pl.CostEstimate(flops=1, bytes_accessed=1, transcendentals=0)


def shifted(value, axis, steps):
    count = lax.axis_size(axis)
    first, last = max(0, -steps), min(count, count - steps)
    return lax.ppermute(value, axis, [(source, source + steps) for source in range(first, last)])


def swapped(value, axis):
    return lax.ppermute(value, axis, [(0, 1), (1, 0)])


def project(marks, gain, pieces, key_weight, value_weight, group, total, number=0, held=()):
    count, tokens, width = pieces[0].shape
    columns = key_weight.shape[1]
    steps = count // group
    base = number * (len(pieces) + steps)

    def kernel(marks_ref, gain_ref, *refs):
        parts, key_blocks, value_blocks = [refs[i * len(pieces) : (i + 1) * len(pieces)] for i in range(3)]
        keys_out, values_out = refs[-2:]

        @pl.when(marks_ref[base + len(pieces) + pl.program_id(0)] > 0)
        def _():
            raw = [part[...].reshape(group * tokens, width).astype(jnp.float32) for part in parts]
            squares = sum(jnp.sum(part * part, axis=1, keepdims=True) for part in raw)
            scale = lax.rsqrt(squares / DE + EPS)
            states = [
                (part * scale * gain_ref[:, index * width : (index + 1) * width]).astype(jnp.bfloat16)
                for index, part in enumerate(raw)
            ]
            for blocks, out in ((key_blocks, keys_out), (value_blocks, values_out)):
                product = sum(
                    jnp.dot(state, block[...], preferred_element_type=jnp.float32)
                    for state, block in zip(states, blocks)
                )
                out[...] = product.astype(jnp.bfloat16).reshape(out.shape)

    out = jax.ShapeDtypeStruct((total, tokens, columns), jnp.bfloat16)
    piece_spec = pl.BlockSpec((group, tokens, width), lambda i, _: (i, 0, 0))

    def weight_spec(piece):
        return pl.BlockSpec((width, columns), lambda i, marks: (marks[base + piece], 0))

    weight_specs = [weight_spec(piece) for piece in range(len(pieces))]
    out_spec = pl.BlockSpec((group, tokens, columns), lambda i, _: (i + number * steps, 0, 0))
    operands = (marks, gain, *pieces, *[key_weight] * len(pieces), *[value_weight] * len(pieces), *held)
    return pl.pallas_call(
        kernel,
        out_shape=(out, out),
        grid_spec=pltpu.PrefetchScalarGridSpec(
            num_scalar_prefetch=1,
            grid=(steps,),
            in_specs=[pl.BlockSpec((1, DE), lambda i, _: (0, 0))]
            + [piece_spec] * len(pieces)
            + weight_specs * 2
            + [pl.BlockSpec(memory_space=pl.ANY)] * len(held),
            out_specs=(out_spec, out_spec),
        ),
        input_output_aliases={len(operands) - len(held) + i: i for i in range(len(held))},
        compiler_params=pltpu.CompilerParams(vmem_limit_bytes=VMEM_LIMIT),
        cost_estimate=LITTLE,
        name="project",
    )(*operands)


SAME_COLUMNS = (((1,), (1,)), ((), ()))
SAME_ROWS = (((0,), (0,)), ((), ()))


def attend_kernel(slots, counts, query_ref, *refs):
    *entries, out_ref = refs
    keys, values = entries[: len(entries) // 2], entries[len(entries) // 2 :]
    together = len(keys) // KMAX
    wide = 2 * HEAD_DIM
    factor = math.log2(math.e) / math.sqrt(HEAD_DIM)
    count = [counts[pl.program_id(0) * together + g] for g in range(together)]
    work = [(g, start) for g in range(together) for start in range(0, query_ref.shape[1], wide)]

    def scored(g, start):
        query = query_ref[g * STRETCH : (g + 1) * STRETCH, start : start + wide]
        left, right = query[:, :HEAD_DIM], query[:, HEAD_DIM:]
        zero = jnp.zeros_like(left)
        both = jnp.concatenate([jnp.concatenate([left, zero], 1), jnp.concatenate([zero, right], 1)], 0)
        one, two = [
            lax.dot_general(
                keys[g * KMAX + k][0, :, start : start + wide], both, SAME_COLUMNS, preferred_element_type=jnp.float32
            )
            for k in range(KMAX)
        ]
        return one, jnp.where(count[g] == 2, two, -1e30)

    def weighed(one, two):
        top = jnp.maximum(one, two).max(0, keepdims=True)
        one, two = jnp.exp2((one - top) * factor), jnp.exp2((two - top) * factor)
        share = 1.0 / (one + two).sum(0, keepdims=True)
        return (one * share).astype(jnp.bfloat16), (two * share).astype(jnp.bfloat16)

    def mix(g, start, weights):
        mixed = sum(
            lax.dot_general(
                weights[k], values[g * KMAX + k][0, :, start : start + wide], SAME_ROWS, preferred_element_type=jnp.float32
            )
            for k in range(KMAX)
        )
        mixed = jnp.where(count[g] > 0, mixed, 0.0).astype(jnp.bfloat16)
        rows = slice(g * STRETCH, (g + 1) * STRETCH)
        out_ref[rows, start : start + HEAD_DIM] = mixed[:STRETCH, :HEAD_DIM]
        out_ref[rows, start + HEAD_DIM : start + wide] = mixed[STRETCH:, HEAD_DIM:]

    scores = [scored(*piece) for piece in work]
    weights = [weighed(*pair) for pair in scores]
    for piece, pair in zip(work, weights):
        mix(*piece, pair)


def attend(slots, counts, queries, keys, values, together=3):
    stretches = counts.shape[0]
    columns = queries.shape[1]

    def entry(i):
        return pl.BlockSpec((1, NLEN, columns), lambda step, slots, _: (slots[step * together * KMAX + i], 0, 0))

    query_spec = pl.BlockSpec((together * STRETCH, columns), lambda i, *_: (i, 0))
    entries = [entry(i) for i in range(together * KMAX)]
    return pl.pallas_call(
        attend_kernel,
        out_shape=jax.ShapeDtypeStruct(queries.shape, jnp.bfloat16),
        grid_spec=pltpu.PrefetchScalarGridSpec(
            num_scalar_prefetch=2,
            grid=(stretches // together,),
            in_specs=[query_spec] + entries * 2,
            out_specs=query_spec,
        ),
        compiler_params=pltpu.CompilerParams(vmem_limit_bytes=VMEM_LIMIT),
        cost_estimate=LITTLE,
        name="attend",
    )(slots, counts, queries, *[keys] * len(entries), *[values] * len(entries))


def plan_kernel(place, table, plan_ref, far_ref, need_ref, lists_ref, picks_ref, slots_ref):
    f32 = jnp.float32
    groups = 2 * CHIPS
    me = place[0]
    each = table.shape[0] // groups
    lane = lax.broadcasted_iota(jnp.int32, (1, LANES), 1)

    bases = [jnp.bitwise_xor(me, group) * each for group in range(groups)]
    need = []
    for group in range(groups):
        wanted = [bases[group] + j for j in range(each - KMAX)]
        if group % CHIPS > 0:
            wanted += [bases[group - 1] + each - KMAX + k for k in range(KMAX)]
        hit = jnp.zeros((1, LANES), f32)
        for index in wanted:
            hit = jnp.where(lane == table[index], 1.0, hit)
        need.append(hit)
        need_ref[group : group + 1, :] = hit
    for part in range(2):
        for chip in range(CHIPS):
            come = (chip - (lane >> 4)) & (CHIPS - 1)
            reach = jnp.zeros((1, LANES), f32)
            for hops in range(1, CHIPS):
                there = need[part * CHIPS + (chip + hops) % CHIPS] > 0
                reach = jnp.where(there & (come + hops < CHIPS), float(hops), reach)
            row = part * CHIPS + chip
            far_ref[row : row + 1, :] = reach

    row = lax.broadcasted_iota(jnp.int32, (groups, LANES), 0)
    entry = lax.broadcasted_iota(jnp.int32, (groups, LANES), 1)
    chip, owner, slot = row & (CHIPS - 1), entry >> 4, entry & (ENTRIES_EACH - 1)
    loc = jnp.where(owner == chip, slot, -1).astype(f32)
    sent = jnp.where(owner == chip, 1.0, 0.0)
    from_behind = owner == ((chip + CHIPS - 1) & (CHIPS - 1))
    halves = [from_behind & (slot < HALF), from_behind & (slot >= HALF)]
    flights = [jnp.where(half, slot + ENTRIES_EACH, -1).astype(f32) for half in halves]
    far, needed = far_ref[...], need_ref[...]
    swept = jnp.zeros((groups, LANES), f32)
    slot_of = jnp.zeros((groups, LANES), f32)
    lists = jnp.full((groups, LANES), -1.0, f32)
    picks = jnp.full((groups, LANES), -1.0, f32)
    one, two = lax.broadcasted_iota(jnp.int32, (LANES, LANES), 0), lax.broadcasted_iota(jnp.int32, (LANES, LANES), 1)
    earlier = jnp.where(one < two, 1.0, 0.0).astype(jnp.bfloat16)
    to, source = lax.broadcasted_iota(jnp.int32, (groups, groups), 0), lax.broadcasted_iota(jnp.int32, (groups, groups), 1)
    behind = jnp.where(to & (CHIPS - 1) == 0, to + CHIPS - 1, to - 1)
    step = jnp.where(source == behind, 1.0, 0.0).astype(jnp.bfloat16)

    def ranked(mask):
        return jnp.dot(mask.astype(jnp.bfloat16), earlier, preferred_element_type=f32)

    def listed(into, taken, rank, number):
        for b in range(CAP):
            pick = jnp.max(jnp.where((taken > 0) & (rank == b), loc, -1.0), axis=1, keepdims=True)
            into = jnp.where(entry == number * CAP + b, pick, into)
        return into

    for number in range(SWEEPS):
        loc = jnp.maximum(loc, flights[number])
        ready = jnp.where((needed > 0) & (loc >= 0) & (swept == 0), 1.0, 0.0)
        rank = ranked(ready)
        taken = jnp.where((ready > 0) & (rank < CAP), 1.0, 0.0)
        swept = swept + taken
        slot_of = slot_of + taken * (rank + number * CAP)
        picks = listed(picks, taken, rank, number)
        if number < ROUNDS:
            ready = jnp.where((far > 0) & (loc >= 0) & (sent == 0), 1.0, 0.0)
            rank = jnp.zeros((groups, LANES), f32)
            above = jnp.zeros((groups, 1), f32)
            for hops in range(CHIPS - 1, 0, -1):
                level = jnp.where(far == hops, ready, 0.0)
                rank = jnp.where(far == hops, ranked(level) + above, rank)
                above = above + jnp.sum(level, axis=1, keepdims=True)
            taken = jnp.where((ready > 0) & (rank < CAP), 1.0, 0.0)
            sent = sent + taken
            lists = listed(lists, taken, rank, number)
            came = jnp.dot(step, (taken * (rank + 1)).astype(jnp.bfloat16), preferred_element_type=f32)
            flights.append(jnp.where(came > 0, came + float(2 * ENTRIES_EACH + number * CAP - 1), -1.0))
    lists_ref[...] = lists
    picks_ref[...] = picks
    slots_ref[...] = slot_of
    missing = jnp.sum(jnp.where((far > 0) & (sent == 0), 1.0, 0.0)) + jnp.sum(
        jnp.where((needed > 0) & (swept == 0), 1.0, 0.0)
    )
    plan_ref[...] = jnp.zeros(plan_ref.shape, jnp.int32)
    for line, rows in enumerate((lists_ref, picks_ref, slots_ref)):
        plan_ref[line : line + 1, :] = rows[pl.ds(me, 1), :].astype(jnp.int32)
    plan_ref[3:4, :] = jnp.full((1, LANES), missing, f32).astype(jnp.int32)


def make_plan(place, table):
    return pl.pallas_call(
        plan_kernel,
        out_shape=jax.ShapeDtypeStruct((8, LANES), jnp.int32),
        in_specs=[pl.BlockSpec(memory_space=pltpu.SMEM)] * 2,
        out_specs=pl.BlockSpec(memory_space=pltpu.VMEM),
        scratch_shapes=[pltpu.VMEM((2 * CHIPS, LANES), jnp.float32)] * 5,
        name="plan",
    )(place, table)


def pack(plan, number, pool):
    lines = (0, 1) if number < ROUNDS else (1,)
    starts = [0]
    for array in pool:
        starts.append(starts[-1] + array.shape[0])

    def kernel(plan_ref, *refs):
        sources, outs = refs[: len(pool)], refs[len(pool) :]
        for line, out in zip(lines, outs):
            for b in range(CAP):
                at = plan_ref[line * LANES + number * CAP + b]
                for source, low, high in zip(sources, starts, starts[1:]):

                    @pl.when((at >= low) & (at < high))
                    def _(source=source, low=low, out=out, b=b, at=at):
                        out[b] = source[at - low]

    in_vmem = pl.BlockSpec(memory_space=pltpu.VMEM)
    return pl.pallas_call(
        kernel,
        out_shape=(jax.ShapeDtypeStruct((CAP,) + pool[0].shape[1:], pool[0].dtype),) * len(lines),
        grid_spec=pltpu.PrefetchScalarGridSpec(
            num_scalar_prefetch=1, in_specs=[in_vmem] * len(pool), out_specs=(in_vmem,) * len(lines)
        ),
        compiler_params=pltpu.CompilerParams(vmem_limit_bytes=VMEM_LIMIT),
        cost_estimate=LITTLE,
        name="pack",
    )(plan, *pool)


def previous_rows(nbr_owner, nbr_slot, nbr_count):
    rows = jnp.concatenate([nbr_owner, nbr_slot, nbr_count[:, None]], axis=1)
    rows = jnp.concatenate([shifted(rows[-1:], "seq", 1), rows[:-1]], axis=0)
    return rows[:, :KMAX], rows[:, KMAX : 2 * KMAX], rows[:, 2 * KMAX]


def fetch_by_request(store, owners, slots):
    owners_axis = lax.axis_size("seq")
    stretches = owners.shape[0]
    depth = min(stretches, max(2, 2 * stretches * KMAX // owners_axis) + 1)
    owners, slots = owners.reshape(-1), slots.reshape(-1)
    order = jnp.arange(owners.shape[0], dtype=jnp.int32)
    before = (owners[:, None] == owners[None, :]) & (order[None, :] < order[:, None])
    target = owners * depth + jnp.sum(before.astype(jnp.int32), axis=1)
    hits = target[:, None] == jnp.arange(owners_axis * depth, dtype=jnp.int32)[None, :]
    table = jnp.sum(jnp.where(hits, slots[:, None], 0), axis=0).reshape(owners_axis, depth)
    asked = lax.all_to_all(table, "seq", split_axis=0, concat_axis=0, tiled=True)
    arrived = lax.all_to_all(store[asked], "seq", split_axis=0, concat_axis=0, tiled=True)
    fetched = arrived.reshape(owners_axis * depth, NLEN, store.shape[2])[target]
    return lax.all_gather(fetched, FEATURES, axis=2, tiled=True)


def onward(value):
    size = lax.axis_size("seq")
    return lax.ppermute(value, "seq", [(chip, (chip + 1) % size) for chip in range(size)])


def four_pieces(value):
    across = swapped(value, "mp")
    return [value, swapped(value, "rep"), across, swapped(across, "rep")]


def fetch_all(store, owners, slots):
    seq = lax.axis_index("seq")
    everything = [store]
    for distance in range(1, lax.axis_size("seq")):
        for steps in (distance, -distance):
            everything.append(shifted(store, "seq", steps))
    ahead = owners - seq
    place = jnp.where(ahead == 0, 0, jnp.where(ahead < 0, -2 * ahead - 1, 2 * ahead))
    pool = jnp.concatenate(everything, axis=0)
    return pool[(place * store.shape[0] + slots).reshape(-1)]


def places_of_pieces():
    block = 2 * lax.axis_index("mp") + lax.axis_index("rep")
    return jnp.stack([block ^ i for i in range(4)]).astype(jnp.int32)


def exchanged_table(codes):
    own_part = [codes]
    for offset in range(1, CHIPS):
        own_part.append(lax.ppermute(codes, "seq", [(chip, chip ^ offset) for chip in range(CHIPS)]))
    own_part = jnp.stack(own_part)
    return jnp.concatenate([own_part, swapped(own_part, "parts")], axis=0)


def streamed(queries, key_weight, value_weight, enc_gain, store, nbr_owner, nbr_slot, nbr_count):
    stretches = nbr_owner.shape[0]
    total = stretches * KMAX
    seq = lax.axis_index("seq")
    me = lax.axis_index("parts") * CHIPS + seq
    kept = jnp.arange(KMAX, dtype=jnp.int32)[None, :] < nbr_count[:, None]
    codes = jnp.where(kept, nbr_owner * ENTRIES_EACH + nbr_slot, -1).reshape(-1)
    first, second, codes = lax.optimization_barrier((store[:HALF], store[HALF:], codes))
    table = exchanged_table(codes)
    flights = [onward(first), onward(second)]
    plan = make_plan(me.reshape(1).astype(jnp.int32), table.reshape(-1)).reshape(-1)
    missing = plan[3 * LANES]

    offset = jnp.where(seq > 0, (seq ^ (seq - 1)) & 3, 0)
    behind = table[offset]
    asked = jnp.concatenate([jnp.where(seq > 0, behind[total - KMAX :], -1), codes[: total - KMAX]])
    asked = asked.reshape(stretches, KMAX)
    counts = jnp.sum((asked >= 0).astype(jnp.int32), axis=1)
    first = jnp.maximum(asked[:, 0], 0)
    asked = jnp.stack([first, jnp.where(asked[:, 1] >= 0, asked[:, 1], first)], axis=1).reshape(-1)

    places = places_of_pieces()
    wanted = plan[LANES : LANES + SWEEPS * CAP].reshape(SWEEPS, CAP)[:, ::GROUP] >= 0
    marks = jnp.concatenate([jnp.broadcast_to(places, (SWEEPS, 4)), wanted.astype(jnp.int32)], axis=1).reshape(-1)
    slots = plan[2 * LANES : 3 * LANES][asked]

    room = SWEEPS * CAP
    held, pieces, gain = (), [], None

    def projected(number):
        return project(marks, gain, pieces[number], key_weight, value_weight, GROUP, room, number, held)

    for number in range(SWEEPS):
        *ways, mine = pack(plan, number, [store] + flights[: number + 1])
        flights += [onward(way) for way in ways]
        pieces.append([mine, swapped(mine, "rep"), swapped(mine, "mp")])
        if number == 0:
            enc_gain, pieces[0][1] = lax.optimization_barrier((enc_gain, pieces[0][1]))
            gain = jnp.concatenate(four_pieces(enc_gain[None]), axis=1)
        if number > 1:
            if number + 1 < SWEEPS:
                pieces[number - 2], flights[number + 1] = lax.optimization_barrier((pieces[number - 2], flights[number + 1]))
            held = projected(number - 2)
        if number > 0:
            pieces[number - 1].append(swapped(pieces[number - 1][2], "rep"))
        if number + 1 < SWEEPS:
            flights[number + 1], pieces[: number], held, gain, slots, marks = lax.optimization_barrier(
                (flights[number + 1], pieces[: number], held, gain, slots, marks)
            )
    held = projected(SWEEPS - 2)
    pieces[-1], held = lax.optimization_barrier((pieces[-1], held))
    pieces[-1].append(swapped(pieces[-1][2], "rep"))
    keys, values = projected(SWEEPS - 1)

    def whole(state):
        mine = fetch_all(store, asked >> 4, asked & (ENTRIES_EACH - 1))
        whole_marks = jnp.concatenate([places, jnp.ones((total // 4,), jnp.int32)])
        keys, values = project(whole_marks, gain, four_pieces(mine), key_weight, value_weight, 4, room)
        return jnp.zeros_like(state[0]), jnp.arange(total, dtype=jnp.int32), keys, values

    state = lax.while_loop(lambda state: state[0] > 0, whole, (missing, slots, keys, values))
    return attend(state[1], counts, queries, *state[2:])


def requested(queries, key_weight, value_weight, enc_gain, store, nbr_owner, nbr_slot, nbr_count):
    gain = lax.all_gather(enc_gain, FEATURES, axis=0, tiled=True)[None]
    owners, slots, counts = previous_rows(nbr_owner, nbr_slot, nbr_count)
    total = owners.size
    pieces = [fetch_by_request(store, owners, slots)]
    marks = jnp.concatenate([jnp.zeros((1,), jnp.int32), jnp.ones((total // 4,), jnp.int32)])
    keys, values = project(marks, gain, pieces, key_weight, value_weight, 4, total)
    return attend(jnp.arange(total, dtype=jnp.int32), counts, queries, keys, values)


def solution(mesh):
    in_specs = (
        P(SEQ_SPEC, FEATURES),
        P(None, FEATURES),
        P(None, FEATURES),
        P(FEATURES),
        P(SEQ_SPEC, None, FEATURES),
        P(SEQ_SPEC, None),
        P(SEQ_SPEC, None),
        P(SEQ_SPEC),
    )
    out_specs = P(SEQ_SPEC, FEATURES)
    shape = dict(mesh.shape)
    small = shape == {"parts": 2, "seq": CHIPS, "mp": 2, "rep": 2}
    body = streamed if small else requested
    return jax.shard_map(body, mesh=mesh, in_specs=in_specs, out_specs=out_specs, check_vma=False)
```

```python
import math

import jax
import jax.numpy as jnp
from jax import lax
from jax.experimental import pallas as pl
from jax.experimental.pallas import tpu as pltpu
from jax.sharding import PartitionSpec as P

HEAD_DIM = 128
DE = 1024
NLEN = 128
STRETCH = 64
KMAX = 2
EPS = 1e-06

SEQ_SPEC = ("parts", "seq")
FEATURES = ("mp", "rep")
VMEM_LIMIT = 28 * 1024 * 1024

CHIPS = 4
ENTRIES_EACH = 16
HALF = 8
ROUNDS = 5
SWEEPS = ROUNDS + 2
CAP = 4
GROUP = 2
LANES = 128

LITTLE = pl.CostEstimate(flops=1, bytes_accessed=1, transcendentals=0)


def shifted(value, axis, steps):
    count = lax.axis_size(axis)
    first, last = max(0, -steps), min(count, count - steps)
    return lax.ppermute(value, axis, [(source, source + steps) for source in range(first, last)])


def swapped(value, axis):
    return lax.ppermute(value, axis, [(0, 1), (1, 0)])


def project(marks, gain, rounds, key_weight, value_weight, group, total, first=0, held=()):
    pieces = len(rounds[0])
    count, tokens, width = rounds[0][0].shape
    columns = key_weight.shape[1]
    each = count // group
    rows = group * tokens
    groups = total // group

    def kernel(marks_ref, gain_ref, *refs):
        arrays, blocks = refs[: len(rounds) * pieces], refs[len(rounds) * pieces : (len(rounds) + 2) * pieces]
        outs, normed = refs[-3:-1], refs[-1]
        step = pl.program_id(0)
        wanted = marks_ref[pieces + first + step] > 0
        for number in range(len(rounds)):
            parts = arrays[number * pieces : (number + 1) * pieces]

            @pl.when(wanted & (step >= number * each) & (step < (number + 1) * each))
            def _(number=number, parts=parts):
                at = pl.ds((step - number * each) * group, group)
                raw = [part[at].reshape(rows, width).astype(jnp.float32) for part in parts]
                squares = sum(jnp.sum(part * part, axis=1, keepdims=True) for part in raw)
                scale = lax.rsqrt(squares / DE + EPS)
                for index, part in enumerate(raw):
                    place = slice(index * width, (index + 1) * width)
                    normed[:, place] = (part * scale * gain_ref[:, place]).astype(jnp.bfloat16)

        @pl.when(wanted)
        def _():
            for out, weight in zip(outs, (blocks[:pieces], blocks[pieces:])):
                product = sum(
                    jnp.dot(
                        normed[:, index * width : (index + 1) * width], block[...], preferred_element_type=jnp.float32
                    )
                    for index, block in enumerate(weight)
                )
                out[...] = product.astype(jnp.bfloat16).reshape(out.shape)

    def weight_spec(piece):
        return pl.BlockSpec((width, columns), lambda i, marks: (marks[piece], 0))

    weight_specs = [weight_spec(piece) for piece in range(pieces)]
    out = jax.ShapeDtypeStruct((total, tokens, columns), jnp.bfloat16)
    out_spec = pl.BlockSpec((group, tokens, columns), lambda i, marks: (jnp.maximum(marks[pieces + groups + first + i], first), 0, 0))
    arrays = [piece for parts in rounds for piece in parts]
    operands = (marks, gain, *arrays, *[key_weight] * pieces, *[value_weight] * pieces, *held)
    return pl.pallas_call(
        kernel,
        out_shape=(out, out),
        grid_spec=pltpu.PrefetchScalarGridSpec(
            num_scalar_prefetch=1,
            grid=(len(rounds) * each,),
            in_specs=[pl.BlockSpec((1, DE), lambda i, _: (0, 0))]
            + [pl.BlockSpec(memory_space=pltpu.VMEM)] * len(arrays)
            + weight_specs * 2
            + [pl.BlockSpec(memory_space=pl.ANY)] * len(held),
            out_specs=(out_spec, out_spec),
            scratch_shapes=[pltpu.VMEM((rows, DE), jnp.bfloat16)],
        ),
        input_output_aliases={len(operands) - len(held) + i: i for i in range(len(held))},
        compiler_params=pltpu.CompilerParams(vmem_limit_bytes=40 * 1024 * 1024),
        cost_estimate=LITTLE,
        name="project",
    )(*operands)


SAME_COLUMNS = (((1,), (1,)), ((), ()))
SAME_ROWS = (((0,), (0,)), ((), ()))


def attend_kernel(slots, counts, query_ref, *refs):
    *entries, out_ref = refs
    keys, values = entries[: len(entries) // 2], entries[len(entries) // 2 :]
    together = len(keys) // KMAX
    wide = 2 * HEAD_DIM
    factor = math.log2(math.e) / math.sqrt(HEAD_DIM)
    count = [counts[pl.program_id(0) * together + g] for g in range(together)]
    work = [(g, start) for g in range(together) for start in range(0, query_ref.shape[1], wide)]

    def scored(g, start):
        query = query_ref[g * STRETCH : (g + 1) * STRETCH, start : start + wide]
        left, right = query[:, :HEAD_DIM], query[:, HEAD_DIM:]
        zero = jnp.zeros_like(left)
        both = jnp.concatenate([jnp.concatenate([left, zero], 1), jnp.concatenate([zero, right], 1)], 0)
        one, two = [
            lax.dot_general(
                keys[g * KMAX + k][0, :, start : start + wide], both, SAME_COLUMNS, preferred_element_type=jnp.float32
            )
            for k in range(KMAX)
        ]
        return one, jnp.where(count[g] == 2, two, -1e30)

    def weighed(one, two):
        top = jnp.maximum(one, two).max(0, keepdims=True)
        one, two = jnp.exp2((one - top) * factor), jnp.exp2((two - top) * factor)
        share = 1.0 / (one + two).sum(0, keepdims=True)
        return (one * share).astype(jnp.bfloat16), (two * share).astype(jnp.bfloat16)

    def mix(g, start, weights):
        mixed = sum(
            lax.dot_general(
                weights[k], values[g * KMAX + k][0, :, start : start + wide], SAME_ROWS, preferred_element_type=jnp.float32
            )
            for k in range(KMAX)
        )
        mixed = jnp.where(count[g] > 0, mixed, 0.0).astype(jnp.bfloat16)
        rows = slice(g * STRETCH, (g + 1) * STRETCH)
        out_ref[rows, start : start + HEAD_DIM] = mixed[:STRETCH, :HEAD_DIM]
        out_ref[rows, start + HEAD_DIM : start + wide] = mixed[STRETCH:, HEAD_DIM:]

    scores = [scored(*piece) for piece in work]
    weights = [weighed(*pair) for pair in scores]
    for piece, pair in zip(work, weights):
        mix(*piece, pair)


def attend(slots, counts, queries, keys, values, together=3):
    stretches = counts.shape[0]
    columns = queries.shape[1]

    def entry(i):
        return pl.BlockSpec((1, NLEN, columns), lambda step, slots, _: (slots[step * together * KMAX + i], 0, 0))

    query_spec = pl.BlockSpec((together * STRETCH, columns), lambda i, *_: (i, 0))
    entries = [entry(i) for i in range(together * KMAX)]
    return pl.pallas_call(
        attend_kernel,
        out_shape=jax.ShapeDtypeStruct(queries.shape, jnp.bfloat16),
        grid_spec=pltpu.PrefetchScalarGridSpec(
            num_scalar_prefetch=2,
            grid=(stretches // together,),
            in_specs=[query_spec] + entries * 2,
            out_specs=query_spec,
        ),
        compiler_params=pltpu.CompilerParams(vmem_limit_bytes=VMEM_LIMIT),
        cost_estimate=LITTLE,
        name="attend",
    )(slots, counts, queries, *[keys] * len(entries), *[values] * len(entries))


def plan_kernel(place, table, plan_ref, far_ref, need_ref, lists_ref, picks_ref, slots_ref):
    f32 = jnp.float32
    groups = 2 * CHIPS
    me = place[0]
    each = table.shape[0] // groups
    lane = lax.broadcasted_iota(jnp.int32, (1, LANES), 1)

    bases = [jnp.bitwise_xor(me, group) * each for group in range(groups)]
    need = []
    for group in range(groups):
        wanted = [bases[group] + j for j in range(each - KMAX)]
        if group % CHIPS > 0:
            wanted += [bases[group - 1] + each - KMAX + k for k in range(KMAX)]
        hit = jnp.zeros((1, LANES), f32)
        for index in wanted:
            hit = jnp.where(lane == table[index], 1.0, hit)
        need.append(hit)
        need_ref[group : group + 1, :] = hit
    for part in range(2):
        for chip in range(CHIPS):
            come = (chip - (lane >> 4)) & (CHIPS - 1)
            reach = jnp.zeros((1, LANES), f32)
            for hops in range(1, CHIPS):
                there = need[part * CHIPS + (chip + hops) % CHIPS] > 0
                reach = jnp.where(there & (come + hops < CHIPS), float(hops), reach)
            row = part * CHIPS + chip
            far_ref[row : row + 1, :] = reach

    row = lax.broadcasted_iota(jnp.int32, (groups, LANES), 0)
    entry = lax.broadcasted_iota(jnp.int32, (groups, LANES), 1)
    chip, owner, slot = row & (CHIPS - 1), entry >> 4, entry & (ENTRIES_EACH - 1)
    loc = jnp.where(owner == chip, slot, -1).astype(f32)
    sent = jnp.where(owner == chip, 1.0, 0.0)
    from_behind = owner == ((chip + CHIPS - 1) & (CHIPS - 1))
    halves = [from_behind & (slot < HALF), from_behind & (slot >= HALF)]
    flights = [jnp.where(half, slot + ENTRIES_EACH, -1).astype(f32) for half in halves]
    far, needed = far_ref[...], need_ref[...]
    swept = jnp.zeros((groups, LANES), f32)
    slot_of = jnp.zeros((groups, LANES), f32)
    lists = jnp.full((groups, LANES), -1.0, f32)
    picks = jnp.full((groups, LANES), -1.0, f32)
    one, two = lax.broadcasted_iota(jnp.int32, (LANES, LANES), 0), lax.broadcasted_iota(jnp.int32, (LANES, LANES), 1)
    earlier = jnp.where(one < two, 1.0, 0.0).astype(jnp.bfloat16)
    to, source = lax.broadcasted_iota(jnp.int32, (groups, groups), 0), lax.broadcasted_iota(jnp.int32, (groups, groups), 1)
    behind = jnp.where(to & (CHIPS - 1) == 0, to + CHIPS - 1, to - 1)
    step = jnp.where(source == behind, 1.0, 0.0).astype(jnp.bfloat16)

    def ranked(mask):
        return jnp.dot(mask.astype(jnp.bfloat16), earlier, preferred_element_type=f32)

    def listed(into, taken, rank, number):
        for b in range(CAP):
            pick = jnp.max(jnp.where((taken > 0) & (rank == b), loc, -1.0), axis=1, keepdims=True)
            into = jnp.where(entry == number * CAP + b, pick, into)
        return into

    for number in range(SWEEPS):
        loc = jnp.maximum(loc, flights[number])
        ready = jnp.where((needed > 0) & (loc >= 0) & (swept == 0), 1.0, 0.0)
        rank = ranked(ready)
        taken = jnp.where((ready > 0) & (rank < CAP), 1.0, 0.0)
        swept = swept + taken
        slot_of = slot_of + taken * (rank + number * CAP)
        picks = listed(picks, taken, rank, number)
        if number < ROUNDS:
            ready = jnp.where((far > 0) & (loc >= 0) & (sent == 0), 1.0, 0.0)
            rank = jnp.zeros((groups, LANES), f32)
            above = jnp.zeros((groups, 1), f32)
            for hops in range(CHIPS - 1, 0, -1):
                level = jnp.where(far == hops, ready, 0.0)
                rank = jnp.where(far == hops, ranked(level) + above, rank)
                above = above + jnp.sum(level, axis=1, keepdims=True)
            taken = jnp.where((ready > 0) & (rank < CAP), 1.0, 0.0)
            sent = sent + taken
            lists = listed(lists, taken, rank, number)
            came = jnp.dot(step, (taken * (rank + 1)).astype(jnp.bfloat16), preferred_element_type=f32)
            flights.append(jnp.where(came > 0, came + float(2 * ENTRIES_EACH + number * CAP - 1), -1.0))
    lists_ref[...] = lists
    picks_ref[...] = picks
    slots_ref[...] = slot_of
    missing = jnp.sum(jnp.where((far > 0) & (sent == 0), 1.0, 0.0)) + jnp.sum(
        jnp.where((needed > 0) & (swept == 0), 1.0, 0.0)
    )
    plan_ref[...] = jnp.zeros(plan_ref.shape, jnp.int32)
    for line, rows in enumerate((lists_ref, picks_ref, slots_ref)):
        plan_ref[line : line + 1, :] = rows[pl.ds(me, 1), :].astype(jnp.int32)
    plan_ref[3:4, :] = jnp.full((1, LANES), missing, f32).astype(jnp.int32)


def make_plan(place, table):
    return pl.pallas_call(
        plan_kernel,
        out_shape=jax.ShapeDtypeStruct((8, LANES), jnp.int32),
        in_specs=[pl.BlockSpec(memory_space=pltpu.SMEM)] * 2,
        out_specs=pl.BlockSpec(memory_space=pltpu.VMEM),
        scratch_shapes=[pltpu.VMEM((2 * CHIPS, LANES), jnp.float32)] * 5,
        name="plan",
    )(place, table)


def pack(plan, number, pool):
    lines = (0, 1) if number < ROUNDS else (1,)
    starts = [0]
    for array in pool:
        starts.append(starts[-1] + array.shape[0])

    def kernel(plan_ref, *refs):
        sources, outs = refs[: len(pool)], refs[len(pool) :]
        for line, out in zip(lines, outs):
            for b in range(CAP):
                at = plan_ref[line * LANES + number * CAP + b]
                for source, low, high in zip(sources, starts, starts[1:]):

                    @pl.when((at >= low) & (at < high))
                    def _(source=source, low=low, out=out, b=b, at=at):
                        out[b] = source[at - low]

    in_vmem = pl.BlockSpec(memory_space=pltpu.VMEM)
    return pl.pallas_call(
        kernel,
        out_shape=(jax.ShapeDtypeStruct((CAP,) + pool[0].shape[1:], pool[0].dtype),) * len(lines),
        grid_spec=pltpu.PrefetchScalarGridSpec(
            num_scalar_prefetch=1, in_specs=[in_vmem] * len(pool), out_specs=(in_vmem,) * len(lines)
        ),
        compiler_params=pltpu.CompilerParams(vmem_limit_bytes=VMEM_LIMIT),
        cost_estimate=LITTLE,
        name="pack",
    )(plan, *pool)


def previous_rows(nbr_owner, nbr_slot, nbr_count):
    rows = jnp.concatenate([nbr_owner, nbr_slot, nbr_count[:, None]], axis=1)
    rows = jnp.concatenate([shifted(rows[-1:], "seq", 1), rows[:-1]], axis=0)
    return rows[:, :KMAX], rows[:, KMAX : 2 * KMAX], rows[:, 2 * KMAX]


def fetch_by_request(store, owners, slots):
    owners_axis = lax.axis_size("seq")
    stretches = owners.shape[0]
    depth = min(stretches, max(2, 2 * stretches * KMAX // owners_axis) + 1)
    owners, slots = owners.reshape(-1), slots.reshape(-1)
    order = jnp.arange(owners.shape[0], dtype=jnp.int32)
    before = (owners[:, None] == owners[None, :]) & (order[None, :] < order[:, None])
    target = owners * depth + jnp.sum(before.astype(jnp.int32), axis=1)
    hits = target[:, None] == jnp.arange(owners_axis * depth, dtype=jnp.int32)[None, :]
    table = jnp.sum(jnp.where(hits, slots[:, None], 0), axis=0).reshape(owners_axis, depth)
    asked = lax.all_to_all(table, "seq", split_axis=0, concat_axis=0, tiled=True)
    arrived = lax.all_to_all(store[asked], "seq", split_axis=0, concat_axis=0, tiled=True)
    fetched = arrived.reshape(owners_axis * depth, NLEN, store.shape[2])[target]
    return lax.all_gather(fetched, FEATURES, axis=2, tiled=True)


def onward(value):
    size = lax.axis_size("seq")
    return lax.ppermute(value, "seq", [(chip, (chip + 1) % size) for chip in range(size)])


def four_pieces(value):
    across = swapped(value, "mp")
    return [value, swapped(value, "rep"), across, swapped(across, "rep")]


def fetch_all(store, owners, slots):
    seq = lax.axis_index("seq")
    everything = [store]
    for distance in range(1, lax.axis_size("seq")):
        for steps in (distance, -distance):
            everything.append(shifted(store, "seq", steps))
    ahead = owners - seq
    place = jnp.where(ahead == 0, 0, jnp.where(ahead < 0, -2 * ahead - 1, 2 * ahead))
    pool = jnp.concatenate(everything, axis=0)
    return pool[(place * store.shape[0] + slots).reshape(-1)]


def places_of_pieces():
    block = 2 * lax.axis_index("mp") + lax.axis_index("rep")
    return jnp.stack([block ^ i for i in range(4)]).astype(jnp.int32)


def every_group(places, groups):
    return jnp.concatenate([places, jnp.ones((groups,), jnp.int32), jnp.arange(groups, dtype=jnp.int32)])


def exchanged_table(codes):
    own_part = [codes]
    for offset in range(1, CHIPS):
        own_part.append(lax.ppermute(codes, "seq", [(chip, chip ^ offset) for chip in range(CHIPS)]))
    own_part = jnp.stack(own_part)
    return jnp.concatenate([own_part, swapped(own_part, "parts")], axis=0)


def streamed(queries, key_weight, value_weight, enc_gain, store, nbr_owner, nbr_slot, nbr_count):
    stretches = nbr_owner.shape[0]
    total = stretches * KMAX
    seq = lax.axis_index("seq")
    me = lax.axis_index("parts") * CHIPS + seq
    kept = jnp.arange(KMAX, dtype=jnp.int32)[None, :] < nbr_count[:, None]
    codes = jnp.where(kept, nbr_owner * ENTRIES_EACH + nbr_slot, -1).reshape(-1)
    first, second, codes, enc_gain = lax.optimization_barrier((store[:HALF], store[HALF:], codes, enc_gain))
    table = exchanged_table(codes)
    flights = [onward(first), onward(second)]
    gain = jnp.concatenate(four_pieces(enc_gain[None]), axis=1)
    plan = make_plan(me.reshape(1).astype(jnp.int32), table.reshape(-1)).reshape(-1)
    missing = plan[3 * LANES]

    offset = jnp.where(seq > 0, (seq ^ (seq - 1)) & 3, 0)
    behind = table[offset]
    asked = jnp.concatenate([jnp.where(seq > 0, behind[total - KMAX :], -1), codes[: total - KMAX]])
    asked = asked.reshape(stretches, KMAX)
    counts = jnp.sum((asked >= 0).astype(jnp.int32), axis=1)
    first = jnp.maximum(asked[:, 0], 0)
    asked = jnp.stack([first, jnp.where(asked[:, 1] >= 0, asked[:, 1], first)], axis=1).reshape(-1)

    places = places_of_pieces()
    room = SWEEPS * CAP
    wanted = plan[LANES : LANES + room].reshape(room // GROUP, GROUP)[:, 0] >= 0
    group = jnp.arange(room // GROUP, dtype=jnp.int32)
    latest = jnp.max(jnp.where((group[None, :] <= group[:, None]) & wanted[None, :], group[None, :], 0), axis=1)
    marks = jnp.concatenate([places, wanted.astype(jnp.int32), latest])
    slots = plan[2 * LANES : 3 * LANES][asked]

    pieces = []
    for number in range(SWEEPS):
        *ways, mine = pack(plan, number, [store] + flights[: number + 1])
        flights += [onward(way) for way in ways]
        pieces.append([mine, swapped(mine, "rep"), swapped(mine, "mp")])
        if number > 0:
            pieces[number - 1].append(swapped(pieces[number - 1][2], "rep"))
        if number + 1 < SWEEPS:
            across = [parts[2] for parts in pieces[:number]]
            flights[number + 1], across, pieces[number][1], gain, slots, marks = lax.optimization_barrier(
                (flights[number + 1], across, pieces[number][1], gain, slots, marks)
            )
            for parts, arrived in zip(pieces, across):
                parts[2] = arrived
    pieces[:-1], _ = lax.optimization_barrier((pieces[:-1], mine))
    held = project(marks, gain, pieces[:-1], key_weight, value_weight, GROUP, room)
    pieces[-1], held = lax.optimization_barrier((pieces[-1], held))
    pieces[-1].append(swapped(pieces[-1][2], "rep"))
    done = (SWEEPS - 1) * CAP // GROUP
    keys, values = project(marks, gain, pieces[-1:], key_weight, value_weight, GROUP, room, done, held)

    def whole(state):
        mine = fetch_all(store, asked >> 4, asked & (ENTRIES_EACH - 1))
        marks = every_group(places, room // 4)
        keys, values = project(marks, gain, [four_pieces(mine)], key_weight, value_weight, 4, room)
        return jnp.zeros_like(state[0]), jnp.arange(total, dtype=jnp.int32), keys, values

    state = lax.while_loop(lambda state: state[0] > 0, whole, (missing, slots, keys, values))
    return attend(state[1], counts, queries, *state[2:])


def requested(queries, key_weight, value_weight, enc_gain, store, nbr_owner, nbr_slot, nbr_count):
    gain = lax.all_gather(enc_gain, FEATURES, axis=0, tiled=True)[None]
    owners, slots, counts = previous_rows(nbr_owner, nbr_slot, nbr_count)
    total = owners.size
    pieces = [fetch_by_request(store, owners, slots)]
    marks = every_group(jnp.zeros((1,), jnp.int32), total // 4)
    keys, values = project(marks, gain, [pieces], key_weight, value_weight, 4, total)
    return attend(jnp.arange(total, dtype=jnp.int32), counts, queries, keys, values)


def solution(mesh):
    in_specs = (
        P(SEQ_SPEC, FEATURES),
        P(None, FEATURES),
        P(None, FEATURES),
        P(FEATURES),
        P(SEQ_SPEC, None, FEATURES),
        P(SEQ_SPEC, None),
        P(SEQ_SPEC, None),
        P(SEQ_SPEC),
    )
    out_specs = P(SEQ_SPEC, FEATURES)
    shape = dict(mesh.shape)
    small = shape == {"parts": 2, "seq": CHIPS, "mp": 2, "rep": 2}
    body = streamed if small else requested
    return jax.shard_map(body, mesh=mesh, in_specs=in_specs, out_specs=out_specs, check_vma=False)
```

```python
import math

import jax
import jax.numpy as jnp
from jax import lax
from jax.experimental import pallas as pl
from jax.experimental.pallas import tpu as pltpu
from jax.sharding import PartitionSpec as P

HEAD_DIM = 128
DE = 1024
NLEN = 128
STRETCH = 64
KMAX = 2
EPS = 1e-06

SEQ_SPEC = ("parts", "seq")
FEATURES = ("mp", "rep")
VMEM_LIMIT = 28 * 1024 * 1024

CHIPS = 4
ENTRIES_EACH = 16
HALF = 8
ROUNDS = 5
SWEEPS = ROUNDS + 2
CAP = 4
GROUP = 2
LANES = 128

LITTLE = pl.CostEstimate(flops=1, bytes_accessed=1, transcendentals=0)


def shifted(value, axis, steps):
    count = lax.axis_size(axis)
    first, last = max(0, -steps), min(count, count - steps)
    return lax.ppermute(value, axis, [(source, source + steps) for source in range(first, last)])


def swapped(value, axis):
    return lax.ppermute(value, axis, [(0, 1), (1, 0)])


def project(marks, gain, rounds, key_weight, value_weight, group, total, first=0, held=()):
    pieces = len(rounds[0])
    count, tokens, width = rounds[0][0].shape
    columns = key_weight.shape[1]
    each = count // group
    rows = group * tokens
    groups = total // group

    def kernel(marks_ref, gain_ref, *refs):
        arrays, weights = refs[: len(rounds) * pieces], refs[len(rounds) * pieces : len(rounds) * pieces + 2]
        *outs, normed, key_rows, value_rows, sems = refs[-6:]
        step = pl.program_id(0)
        ordered = (key_rows, value_rows)
        copies = [
            pltpu.make_async_copy(
                weight.at[pl.ds(pl.multiple_of(marks_ref[piece] * width, width), width)],
                rows_ref.at[pl.ds(piece * width, width)],
                sems.at[which * pieces + piece],
            )
            for which, (weight, rows_ref) in enumerate(zip(weights, ordered))
            for piece in range(pieces)
        ]

        @pl.when(step == 0)
        def _():
            for copy in copies:
                copy.start()

        wanted = marks_ref[pieces + first + step] > 0
        for number in range(len(rounds)):
            parts = arrays[number * pieces : (number + 1) * pieces]

            @pl.when(wanted & (step >= number * each) & (step < (number + 1) * each))
            def _(number=number, parts=parts):
                at = pl.ds((step - number * each) * group, group)
                raw = [part[at].reshape(rows, width).astype(jnp.float32) for part in parts]
                squares = sum(jnp.sum(part * part, axis=1, keepdims=True) for part in raw)
                scale = lax.rsqrt(squares / DE + EPS)
                for index, part in enumerate(raw):
                    place = slice(index * width, (index + 1) * width)
                    normed[:, place] = (part * scale * gain_ref[:, place]).astype(jnp.bfloat16)

        @pl.when(step == 0)
        def _():
            for copy in copies:
                copy.wait()

        @pl.when(wanted)
        def _():
            states = normed[...]
            for out, weight in zip(outs, ordered):
                product = jnp.dot(states, weight[...], preferred_element_type=jnp.float32)
                out[...] = product.astype(jnp.bfloat16).reshape(out.shape)

    out = jax.ShapeDtypeStruct((total, tokens, columns), jnp.bfloat16)
    out_spec = pl.BlockSpec((group, tokens, columns), lambda i, marks: (jnp.maximum(marks[pieces + groups + first + i], first), 0, 0))
    arrays = [piece for parts in rounds for piece in parts]
    operands = (marks, gain, *arrays, key_weight, value_weight, *held)
    return pl.pallas_call(
        kernel,
        out_shape=(out, out),
        grid_spec=pltpu.PrefetchScalarGridSpec(
            num_scalar_prefetch=1,
            grid=(len(rounds) * each,),
            in_specs=[pl.BlockSpec((1, DE), lambda i, _: (0, 0))]
            + [pl.BlockSpec(memory_space=pltpu.VMEM)] * len(arrays)
            + [pl.BlockSpec(memory_space=pl.ANY)] * (2 + len(held)),
            out_specs=(out_spec, out_spec),
            scratch_shapes=[pltpu.VMEM((rows, DE), jnp.bfloat16)]
            + [pltpu.VMEM((DE, columns), jnp.bfloat16)] * 2
            + [pltpu.SemaphoreType.DMA((2 * pieces,))],
        ),
        input_output_aliases={len(operands) - len(held) + i: i for i in range(len(held))},
        compiler_params=pltpu.CompilerParams(vmem_limit_bytes=VMEM_LIMIT),
        cost_estimate=LITTLE,
        name="project",
    )(*operands)


SAME_COLUMNS = (((1,), (1,)), ((), ()))
SAME_ROWS = (((0,), (0,)), ((), ()))


def attend_kernel(slots, counts, query_ref, *refs):
    *entries, out_ref = refs
    keys, values = entries[: len(entries) // 2], entries[len(entries) // 2 :]
    together = len(keys) // KMAX
    wide = 2 * HEAD_DIM
    factor = math.log2(math.e) / math.sqrt(HEAD_DIM)
    count = [counts[pl.program_id(0) * together + g] for g in range(together)]
    work = [(g, start) for g in range(together) for start in range(0, query_ref.shape[1], wide)]

    def scored(g, start):
        query = query_ref[g * STRETCH : (g + 1) * STRETCH, start : start + wide]
        left, right = query[:, :HEAD_DIM], query[:, HEAD_DIM:]
        zero = jnp.zeros_like(left)
        both = jnp.concatenate([jnp.concatenate([left, zero], 1), jnp.concatenate([zero, right], 1)], 0)
        one, two = [
            lax.dot_general(
                keys[g * KMAX + k][0, :, start : start + wide], both, SAME_COLUMNS, preferred_element_type=jnp.float32
            )
            for k in range(KMAX)
        ]
        return one, jnp.where(count[g] == 2, two, -1e30)

    def weighed(one, two):
        top = jnp.maximum(one, two).max(0, keepdims=True)
        one, two = jnp.exp2((one - top) * factor), jnp.exp2((two - top) * factor)
        share = 1.0 / (one + two).sum(0, keepdims=True)
        return (one * share).astype(jnp.bfloat16), (two * share).astype(jnp.bfloat16)

    def mix(g, start, weights):
        mixed = sum(
            lax.dot_general(
                weights[k], values[g * KMAX + k][0, :, start : start + wide], SAME_ROWS, preferred_element_type=jnp.float32
            )
            for k in range(KMAX)
        )
        mixed = jnp.where(count[g] > 0, mixed, 0.0).astype(jnp.bfloat16)
        rows = slice(g * STRETCH, (g + 1) * STRETCH)
        out_ref[rows, start : start + HEAD_DIM] = mixed[:STRETCH, :HEAD_DIM]
        out_ref[rows, start + HEAD_DIM : start + wide] = mixed[STRETCH:, HEAD_DIM:]

    scores = [scored(*piece) for piece in work]
    weights = [weighed(*pair) for pair in scores]
    for piece, pair in zip(work, weights):
        mix(*piece, pair)


def attend(slots, counts, queries, keys, values, together=3):
    stretches = counts.shape[0]
    columns = queries.shape[1]

    def entry(i):
        return pl.BlockSpec((1, NLEN, columns), lambda step, slots, _: (slots[step * together * KMAX + i], 0, 0))

    query_spec = pl.BlockSpec((together * STRETCH, columns), lambda i, *_: (i, 0))
    entries = [entry(i) for i in range(together * KMAX)]
    return pl.pallas_call(
        attend_kernel,
        out_shape=jax.ShapeDtypeStruct(queries.shape, jnp.bfloat16),
        grid_spec=pltpu.PrefetchScalarGridSpec(
            num_scalar_prefetch=2,
            grid=(stretches // together,),
            in_specs=[query_spec] + entries * 2,
            out_specs=query_spec,
        ),
        compiler_params=pltpu.CompilerParams(vmem_limit_bytes=VMEM_LIMIT),
        cost_estimate=LITTLE,
        name="attend",
    )(slots, counts, queries, *[keys] * len(entries), *[values] * len(entries))


def plan_kernel(place, table, plan_ref, far_ref, need_ref, lists_ref, picks_ref, slots_ref):
    f32 = jnp.float32
    groups = 2 * CHIPS
    me = place[0]
    each = table.shape[0] // groups
    lane = lax.broadcasted_iota(jnp.int32, (1, LANES), 1)

    bases = [jnp.bitwise_xor(me, group) * each for group in range(groups)]
    need = []
    for group in range(groups):
        wanted = [bases[group] + j for j in range(each - KMAX)]
        if group % CHIPS > 0:
            wanted += [bases[group - 1] + each - KMAX + k for k in range(KMAX)]
        hit = jnp.zeros((1, LANES), f32)
        for index in wanted:
            hit = jnp.where(lane == table[index], 1.0, hit)
        need.append(hit)
        need_ref[group : group + 1, :] = hit
    for part in range(2):
        for chip in range(CHIPS):
            come = (chip - (lane >> 4)) & (CHIPS - 1)
            reach = jnp.zeros((1, LANES), f32)
            for hops in range(1, CHIPS):
                there = need[part * CHIPS + (chip + hops) % CHIPS] > 0
                reach = jnp.where(there & (come + hops < CHIPS), float(hops), reach)
            row = part * CHIPS + chip
            far_ref[row : row + 1, :] = reach

    row = lax.broadcasted_iota(jnp.int32, (groups, LANES), 0)
    entry = lax.broadcasted_iota(jnp.int32, (groups, LANES), 1)
    chip, owner, slot = row & (CHIPS - 1), entry >> 4, entry & (ENTRIES_EACH - 1)
    loc = jnp.where(owner == chip, slot, -1).astype(f32)
    sent = jnp.where(owner == chip, 1.0, 0.0)
    from_behind = owner == ((chip + CHIPS - 1) & (CHIPS - 1))
    halves = [from_behind & (slot < HALF), from_behind & (slot >= HALF)]
    flights = [jnp.where(half, slot + ENTRIES_EACH, -1).astype(f32) for half in halves]
    far, needed = far_ref[...], need_ref[...]
    swept = jnp.zeros((groups, LANES), f32)
    slot_of = jnp.zeros((groups, LANES), f32)
    lists = jnp.full((groups, LANES), -1.0, f32)
    picks = jnp.full((groups, LANES), -1.0, f32)
    one, two = lax.broadcasted_iota(jnp.int32, (LANES, LANES), 0), lax.broadcasted_iota(jnp.int32, (LANES, LANES), 1)
    earlier = jnp.where(one < two, 1.0, 0.0).astype(jnp.bfloat16)
    to, source = lax.broadcasted_iota(jnp.int32, (groups, groups), 0), lax.broadcasted_iota(jnp.int32, (groups, groups), 1)
    behind = jnp.where(to & (CHIPS - 1) == 0, to + CHIPS - 1, to - 1)
    step = jnp.where(source == behind, 1.0, 0.0).astype(jnp.bfloat16)

    def ranked(mask):
        return jnp.dot(mask.astype(jnp.bfloat16), earlier, preferred_element_type=f32)

    def listed(into, taken, rank, number):
        for b in range(CAP):
            pick = jnp.max(jnp.where((taken > 0) & (rank == b), loc, -1.0), axis=1, keepdims=True)
            into = jnp.where(entry == number * CAP + b, pick, into)
        return into

    for number in range(SWEEPS):
        loc = jnp.maximum(loc, flights[number])
        ready = jnp.where((needed > 0) & (loc >= 0) & (swept == 0), 1.0, 0.0)
        rank = ranked(ready)
        taken = jnp.where((ready > 0) & (rank < CAP), 1.0, 0.0)
        swept = swept + taken
        slot_of = slot_of + taken * (rank + number * CAP)
        picks = listed(picks, taken, rank, number)
        if number < ROUNDS:
            ready = jnp.where((far > 0) & (loc >= 0) & (sent == 0), 1.0, 0.0)
            rank = jnp.zeros((groups, LANES), f32)
            above = jnp.zeros((groups, 1), f32)
            for hops in range(CHIPS - 1, 0, -1):
                level = jnp.where(far == hops, ready, 0.0)
                rank = jnp.where(far == hops, ranked(level) + above, rank)
                above = above + jnp.sum(level, axis=1, keepdims=True)
            taken = jnp.where((ready > 0) & (rank < CAP), 1.0, 0.0)
            sent = sent + taken
            lists = listed(lists, taken, rank, number)
            came = jnp.dot(step, (taken * (rank + 1)).astype(jnp.bfloat16), preferred_element_type=f32)
            flights.append(jnp.where(came > 0, came + float(2 * ENTRIES_EACH + number * CAP - 1), -1.0))
    lists_ref[...] = lists
    picks_ref[...] = picks
    slots_ref[...] = slot_of
    missing = jnp.sum(jnp.where((far > 0) & (sent == 0), 1.0, 0.0)) + jnp.sum(
        jnp.where((needed > 0) & (swept == 0), 1.0, 0.0)
    )
    plan_ref[...] = jnp.zeros(plan_ref.shape, jnp.int32)
    for line, rows in enumerate((lists_ref, picks_ref, slots_ref)):
        plan_ref[line : line + 1, :] = rows[pl.ds(me, 1), :].astype(jnp.int32)
    plan_ref[3:4, :] = jnp.full((1, LANES), missing, f32).astype(jnp.int32)


def make_plan(place, table):
    return pl.pallas_call(
        plan_kernel,
        out_shape=jax.ShapeDtypeStruct((8, LANES), jnp.int32),
        in_specs=[pl.BlockSpec(memory_space=pltpu.SMEM)] * 2,
        out_specs=pl.BlockSpec(memory_space=pltpu.VMEM),
        scratch_shapes=[pltpu.VMEM((2 * CHIPS, LANES), jnp.float32)] * 5,
        name="plan",
    )(place, table)


def pack(plan, number, pool):
    lines = (0, 1) if number < ROUNDS else (1,)
    starts = [0]
    for array in pool:
        starts.append(starts[-1] + array.shape[0])

    def kernel(plan_ref, *refs):
        sources, outs = refs[: len(pool)], refs[len(pool) :]
        for line, out in zip(lines, outs):
            for b in range(CAP):
                at = plan_ref[line * LANES + number * CAP + b]
                for source, low, high in zip(sources, starts, starts[1:]):

                    @pl.when((at >= low) & (at < high))
                    def _(source=source, low=low, out=out, b=b, at=at):
                        out[b] = source[at - low]

    in_vmem = pl.BlockSpec(memory_space=pltpu.VMEM)
    return pl.pallas_call(
        kernel,
        out_shape=(jax.ShapeDtypeStruct((CAP,) + pool[0].shape[1:], pool[0].dtype),) * len(lines),
        grid_spec=pltpu.PrefetchScalarGridSpec(
            num_scalar_prefetch=1, in_specs=[in_vmem] * len(pool), out_specs=(in_vmem,) * len(lines)
        ),
        compiler_params=pltpu.CompilerParams(vmem_limit_bytes=VMEM_LIMIT),
        cost_estimate=LITTLE,
        name="pack",
    )(plan, *pool)


def previous_rows(nbr_owner, nbr_slot, nbr_count):
    rows = jnp.concatenate([nbr_owner, nbr_slot, nbr_count[:, None]], axis=1)
    rows = jnp.concatenate([shifted(rows[-1:], "seq", 1), rows[:-1]], axis=0)
    return rows[:, :KMAX], rows[:, KMAX : 2 * KMAX], rows[:, 2 * KMAX]


def fetch_by_request(store, owners, slots):
    owners_axis = lax.axis_size("seq")
    stretches = owners.shape[0]
    depth = min(stretches, max(2, 2 * stretches * KMAX // owners_axis) + 1)
    owners, slots = owners.reshape(-1), slots.reshape(-1)
    order = jnp.arange(owners.shape[0], dtype=jnp.int32)
    before = (owners[:, None] == owners[None, :]) & (order[None, :] < order[:, None])
    target = owners * depth + jnp.sum(before.astype(jnp.int32), axis=1)
    hits = target[:, None] == jnp.arange(owners_axis * depth, dtype=jnp.int32)[None, :]
    table = jnp.sum(jnp.where(hits, slots[:, None], 0), axis=0).reshape(owners_axis, depth)
    asked = lax.all_to_all(table, "seq", split_axis=0, concat_axis=0, tiled=True)
    arrived = lax.all_to_all(store[asked], "seq", split_axis=0, concat_axis=0, tiled=True)
    fetched = arrived.reshape(owners_axis * depth, NLEN, store.shape[2])[target]
    return lax.all_gather(fetched, FEATURES, axis=2, tiled=True)


def onward(value):
    size = lax.axis_size("seq")
    return lax.ppermute(value, "seq", [(chip, (chip + 1) % size) for chip in range(size)])


def four_pieces(value):
    across = swapped(value, "mp")
    return [value, swapped(value, "rep"), across, swapped(across, "rep")]


def fetch_all(store, owners, slots):
    seq = lax.axis_index("seq")
    everything = [store]
    for distance in range(1, lax.axis_size("seq")):
        for steps in (distance, -distance):
            everything.append(shifted(store, "seq", steps))
    ahead = owners - seq
    place = jnp.where(ahead == 0, 0, jnp.where(ahead < 0, -2 * ahead - 1, 2 * ahead))
    pool = jnp.concatenate(everything, axis=0)
    return pool[(place * store.shape[0] + slots).reshape(-1)]


def places_of_pieces():
    block = 2 * lax.axis_index("mp") + lax.axis_index("rep")
    return jnp.stack([block ^ i for i in range(4)]).astype(jnp.int32)


def every_group(places, groups):
    return jnp.concatenate([places, jnp.ones((groups,), jnp.int32), jnp.arange(groups, dtype=jnp.int32)])


def exchanged_table(codes):
    own_part = [codes]
    for offset in range(1, CHIPS):
        own_part.append(lax.ppermute(codes, "seq", [(chip, chip ^ offset) for chip in range(CHIPS)]))
    own_part = jnp.stack(own_part)
    return jnp.concatenate([own_part, swapped(own_part, "parts")], axis=0)


def streamed(queries, key_weight, value_weight, enc_gain, store, nbr_owner, nbr_slot, nbr_count):
    stretches = nbr_owner.shape[0]
    total = stretches * KMAX
    seq = lax.axis_index("seq")
    me = lax.axis_index("parts") * CHIPS + seq
    kept = jnp.arange(KMAX, dtype=jnp.int32)[None, :] < nbr_count[:, None]
    codes = jnp.where(kept, nbr_owner * ENTRIES_EACH + nbr_slot, -1).reshape(-1)
    first, second, codes, enc_gain = lax.optimization_barrier((store[:HALF], store[HALF:], codes, enc_gain))
    table = exchanged_table(codes)
    flights = [onward(first), onward(second)]
    gain = jnp.concatenate(four_pieces(enc_gain[None]), axis=1)
    plan = make_plan(me.reshape(1).astype(jnp.int32), table.reshape(-1)).reshape(-1)
    missing = plan[3 * LANES]

    offset = jnp.where(seq > 0, (seq ^ (seq - 1)) & 3, 0)
    behind = table[offset]
    asked = jnp.concatenate([jnp.where(seq > 0, behind[total - KMAX :], -1), codes[: total - KMAX]])
    asked = asked.reshape(stretches, KMAX)
    counts = jnp.sum((asked >= 0).astype(jnp.int32), axis=1)
    first = jnp.maximum(asked[:, 0], 0)
    asked = jnp.stack([first, jnp.where(asked[:, 1] >= 0, asked[:, 1], first)], axis=1).reshape(-1)

    places = places_of_pieces()
    room = SWEEPS * CAP
    wanted = plan[LANES : LANES + room].reshape(room // GROUP, GROUP)[:, 0] >= 0
    group = jnp.arange(room // GROUP, dtype=jnp.int32)
    latest = jnp.max(jnp.where((group[None, :] <= group[:, None]) & wanted[None, :], group[None, :], 0), axis=1)
    marks = jnp.concatenate([places, wanted.astype(jnp.int32), latest])
    slots = plan[2 * LANES : 3 * LANES][asked]

    pieces, held = [], ()
    for number in range(SWEEPS):
        *ways, mine = pack(plan, number, [store] + flights[: number + 1])
        flights += [onward(way) for way in ways]
        pieces.append([mine, swapped(mine, "rep"), swapped(mine, "mp")])
        if number > 0:
            pieces[number - 1].append(swapped(pieces[number - 1][2], "rep"))
        if number == SWEEPS - 3:
            ripe, pieces[number - 1][2] = lax.optimization_barrier((pieces[:2], pieces[number - 1][2]))
            held = project(marks, gain, ripe, key_weight, value_weight, GROUP, room)
        if number + 1 < SWEEPS:
            across = [parts[2] for parts in pieces[:number]] if number + 2 < SWEEPS else []
            came = slice(number + 1, number + 2 if number + 3 < SWEEPS else None)
            flights[came], across, pieces[number][1], gain, slots, marks, held = lax.optimization_barrier(
                (flights[came], across, pieces[number][1], gain, slots, marks, held)
            )
            for parts, arrived in zip(pieces, across):
                parts[2] = arrived
    ripe, _ = lax.optimization_barrier((pieces[2:-2], mine))
    held = project(marks, gain, ripe, key_weight, value_weight, GROUP, room, 2 * CAP // GROUP, held)
    late, held = lax.optimization_barrier(([parts[:3] for parts in pieces[-2:]], held))
    late = [[*parts, swapped(parts[2], "rep")] for parts in late]
    done = (SWEEPS - 2) * CAP // GROUP
    keys, values = project(marks, gain, late, key_weight, value_weight, GROUP, room, done, held)

    def whole(state):
        mine = fetch_all(store, asked >> 4, asked & (ENTRIES_EACH - 1))
        marks = every_group(places, room // 4)
        keys, values = project(marks, gain, [four_pieces(mine)], key_weight, value_weight, 4, room)
        return jnp.zeros_like(state[0]), jnp.arange(total, dtype=jnp.int32), keys, values

    state = lax.while_loop(lambda state: state[0] > 0, whole, (missing, slots, keys, values))
    return attend(state[1], counts, queries, *state[2:])


def requested(queries, key_weight, value_weight, enc_gain, store, nbr_owner, nbr_slot, nbr_count):
    gain = lax.all_gather(enc_gain, FEATURES, axis=0, tiled=True)[None]
    owners, slots, counts = previous_rows(nbr_owner, nbr_slot, nbr_count)
    total = owners.size
    pieces = [fetch_by_request(store, owners, slots)]
    marks = every_group(jnp.zeros((1,), jnp.int32), total // 4)
    keys, values = project(marks, gain, [pieces], key_weight, value_weight, 4, total)
    return attend(jnp.arange(total, dtype=jnp.int32), counts, queries, keys, values)


def solution(mesh):
    in_specs = (
        P(SEQ_SPEC, FEATURES),
        P(None, FEATURES),
        P(None, FEATURES),
        P(FEATURES),
        P(SEQ_SPEC, None, FEATURES),
        P(SEQ_SPEC, None),
        P(SEQ_SPEC, None),
        P(SEQ_SPEC),
    )
    out_specs = P(SEQ_SPEC, FEATURES)
    shape = dict(mesh.shape)
    small = shape == {"parts": 2, "seq": CHIPS, "mp": 2, "rep": 2}
    body = streamed if small else requested
    return jax.shard_map(body, mesh=mesh, in_specs=in_specs, out_specs=out_specs, check_vma=False)
```

```python
import math

import jax
import jax.numpy as jnp
from jax import lax
from jax.experimental import pallas as pl
from jax.experimental.pallas import tpu as pltpu
from jax.sharding import PartitionSpec as P

HEAD_DIM = 128
DE = 1024
NLEN = 128
STRETCH = 64
KMAX = 2
EPS = 1e-06

SEQ_SPEC = ("parts", "seq")
FEATURES = ("mp", "rep")
VMEM_LIMIT = 28 * 1024 * 1024

CHIPS = 4
ENTRIES_EACH = 16
HALF = 8
ROUNDS = 5
CAP = 4
GROUP = 2
SWEEPS = ROUNDS + 1
SWEPT = (CAP,) * ROUNDS + (2 * CAP,)
LANES = 128

LITTLE = pl.CostEstimate(flops=1, bytes_accessed=1, transcendentals=0)


def shifted(value, axis, steps):
    count = lax.axis_size(axis)
    first, last = max(0, -steps), min(count, count - steps)
    return lax.ppermute(value, axis, [(source, source + steps) for source in range(first, last)])


def swapped(value, axis):
    return lax.ppermute(value, axis, [(0, 1), (1, 0)])


def project(marks, gain, rounds, key_weight, value_weight, group, total, first=0, held=()):
    pieces = len(rounds[0])
    count, tokens, width = rounds[0][0].shape
    columns = key_weight.shape[1]
    each = count // group
    rows = group * tokens
    groups = total // group

    def kernel(marks_ref, gain_ref, *refs):
        arrays, weights = refs[: len(rounds) * pieces], refs[len(rounds) * pieces : len(rounds) * pieces + 2]
        *outs, normed, key_rows, value_rows, sems = refs[-6:]
        step = pl.program_id(0)
        ordered = (key_rows, value_rows)
        copies = [
            pltpu.make_async_copy(
                weight.at[pl.ds(pl.multiple_of(marks_ref[piece] * width, width), width)],
                rows_ref.at[pl.ds(piece * width, width)],
                sems.at[which * pieces + piece],
            )
            for which, (weight, rows_ref) in enumerate(zip(weights, ordered))
            for piece in range(pieces)
        ]

        @pl.when(step == 0)
        def _():
            for copy in copies:
                copy.start()

        wanted = marks_ref[pieces + first + step] > 0
        for number in range(len(rounds)):
            parts = arrays[number * pieces : (number + 1) * pieces]

            @pl.when(wanted & (step >= number * each) & (step < (number + 1) * each))
            def _(number=number, parts=parts):
                at = pl.ds((step - number * each) * group, group)
                raw = [part[at].reshape(rows, width).astype(jnp.float32) for part in parts]
                squares = sum(jnp.sum(part * part, axis=1, keepdims=True) for part in raw)
                scale = lax.rsqrt(squares / DE + EPS)
                for index, part in enumerate(raw):
                    place = slice(index * width, (index + 1) * width)
                    normed[:, place] = (part * scale * gain_ref[:, place]).astype(jnp.bfloat16)

        @pl.when(step == 0)
        def _():
            for copy in copies:
                copy.wait()

        @pl.when(wanted)
        def _():
            states = normed[...]
            for out, weight in zip(outs, ordered):
                product = jnp.dot(states, weight[...], preferred_element_type=jnp.float32)
                out[...] = product.astype(jnp.bfloat16).reshape(out.shape)

    out = jax.ShapeDtypeStruct((total, tokens, columns), jnp.bfloat16)
    out_spec = pl.BlockSpec((group, tokens, columns), lambda i, marks: (jnp.maximum(marks[pieces + groups + first + i], first), 0, 0))
    arrays = [piece for parts in rounds for piece in parts]
    operands = (marks, gain, *arrays, key_weight, value_weight, *held)
    return pl.pallas_call(
        kernel,
        out_shape=(out, out),
        grid_spec=pltpu.PrefetchScalarGridSpec(
            num_scalar_prefetch=1,
            grid=(len(rounds) * each,),
            in_specs=[pl.BlockSpec((1, DE), lambda i, _: (0, 0))]
            + [pl.BlockSpec(memory_space=pltpu.VMEM)] * len(arrays)
            + [pl.BlockSpec(memory_space=pl.ANY)] * (2 + len(held)),
            out_specs=(out_spec, out_spec),
            scratch_shapes=[pltpu.VMEM((rows, DE), jnp.bfloat16)]
            + [pltpu.VMEM((DE, columns), jnp.bfloat16)] * 2
            + [pltpu.SemaphoreType.DMA((2 * pieces,))],
        ),
        input_output_aliases={len(operands) - len(held) + i: i for i in range(len(held))},
        compiler_params=pltpu.CompilerParams(vmem_limit_bytes=VMEM_LIMIT),
        cost_estimate=LITTLE,
        name="project",
    )(*operands)


SAME_COLUMNS = (((1,), (1,)), ((), ()))
SAME_ROWS = (((0,), (0,)), ((), ()))


def attend_kernel(slots, counts, query_ref, *refs):
    *entries, out_ref = refs
    keys, values = entries[: len(entries) // 2], entries[len(entries) // 2 :]
    together = len(keys) // KMAX
    wide = 2 * HEAD_DIM
    factor = math.log2(math.e) / math.sqrt(HEAD_DIM)
    count = [counts[pl.program_id(0) * together + g] for g in range(together)]
    work = [(g, start) for g in range(together) for start in range(0, query_ref.shape[1], wide)]

    def scored(g, start):
        query = query_ref[g * STRETCH : (g + 1) * STRETCH, start : start + wide]
        left, right = query[:, :HEAD_DIM], query[:, HEAD_DIM:]
        zero = jnp.zeros_like(left)
        both = jnp.concatenate([jnp.concatenate([left, zero], 1), jnp.concatenate([zero, right], 1)], 0)
        one, two = [
            lax.dot_general(
                keys[g * KMAX + k][0, :, start : start + wide], both, SAME_COLUMNS, preferred_element_type=jnp.float32
            )
            for k in range(KMAX)
        ]
        return one, jnp.where(count[g] == 2, two, -1e30)

    def weighed(one, two):
        top = jnp.maximum(one, two).max(0, keepdims=True)
        one, two = jnp.exp2((one - top) * factor), jnp.exp2((two - top) * factor)
        share = 1.0 / (one + two).sum(0, keepdims=True)
        return (one * share).astype(jnp.bfloat16), (two * share).astype(jnp.bfloat16)

    def mix(g, start, weights):
        rows = jnp.concatenate([values[g * KMAX + k][0, :, start : start + wide] for k in range(KMAX)], 0)
        mixed = lax.dot_general(jnp.concatenate(weights, 0), rows, SAME_ROWS, preferred_element_type=jnp.float32)
        mixed = jnp.where(count[g] > 0, mixed, 0.0).astype(jnp.bfloat16)
        rows = slice(g * STRETCH, (g + 1) * STRETCH)
        out_ref[rows, start : start + HEAD_DIM] = mixed[:STRETCH, :HEAD_DIM]
        out_ref[rows, start + HEAD_DIM : start + wide] = mixed[STRETCH:, HEAD_DIM:]

    scores = [scored(*piece) for piece in work]
    weights = [weighed(*pair) for pair in scores]
    for piece, pair in zip(work, weights):
        mix(*piece, pair)


def attend(slots, counts, queries, keys, values, together=3):
    stretches = counts.shape[0]
    columns = queries.shape[1]

    def entry(i):
        return pl.BlockSpec((1, NLEN, columns), lambda step, slots, _: (slots[step * together * KMAX + i], 0, 0))

    query_spec = pl.BlockSpec((together * STRETCH, columns), lambda i, *_: (i, 0))
    entries = [entry(i) for i in range(together * KMAX)]
    return pl.pallas_call(
        attend_kernel,
        out_shape=jax.ShapeDtypeStruct(queries.shape, jnp.bfloat16),
        grid_spec=pltpu.PrefetchScalarGridSpec(
            num_scalar_prefetch=2,
            grid=(stretches // together,),
            in_specs=[query_spec] + entries * 2,
            out_specs=query_spec,
        ),
        compiler_params=pltpu.CompilerParams(vmem_limit_bytes=60 * 1024 * 1024),
        cost_estimate=LITTLE,
        name="attend",
    )(slots, counts, queries, *[keys] * len(entries), *[values] * len(entries))


def plan_kernel(place, table, plan_ref, far_ref, need_ref, lists_ref, picks_ref, slots_ref):
    f32 = jnp.float32
    groups = 2 * CHIPS
    me = place[0]
    each = table.shape[0] // groups
    lane = lax.broadcasted_iota(jnp.int32, (1, LANES), 1)

    bases = [jnp.bitwise_xor(me, group) * each for group in range(groups)]
    need = []
    for group in range(groups):
        wanted = [bases[group] + j for j in range(each - KMAX)]
        if group % CHIPS > 0:
            wanted += [bases[group - 1] + each - KMAX + k for k in range(KMAX)]
        hit = jnp.zeros((1, LANES), f32)
        for index in wanted:
            hit = jnp.where(lane == table[index], 1.0, hit)
        need.append(hit)
        need_ref[group : group + 1, :] = hit
    for part in range(2):
        for chip in range(CHIPS):
            come = (chip - (lane >> 4)) & (CHIPS - 1)
            reach = jnp.zeros((1, LANES), f32)
            for hops in range(1, CHIPS):
                there = need[part * CHIPS + (chip + hops) % CHIPS] > 0
                reach = jnp.where(there & (come + hops < CHIPS), float(hops), reach)
            row = part * CHIPS + chip
            far_ref[row : row + 1, :] = reach

    row = lax.broadcasted_iota(jnp.int32, (groups, LANES), 0)
    entry = lax.broadcasted_iota(jnp.int32, (groups, LANES), 1)
    chip, owner, slot = row & (CHIPS - 1), entry >> 4, entry & (ENTRIES_EACH - 1)
    loc = jnp.where(owner == chip, slot, -1).astype(f32)
    sent = jnp.where(owner == chip, 1.0, 0.0)
    from_behind = owner == ((chip + CHIPS - 1) & (CHIPS - 1))
    halves = [from_behind & (slot < HALF), from_behind & (slot >= HALF)]
    flights = [jnp.where(half, slot + ENTRIES_EACH, -1).astype(f32) for half in halves]
    far, needed = far_ref[...], need_ref[...]
    swept = jnp.zeros((groups, LANES), f32)
    slot_of = jnp.zeros((groups, LANES), f32)
    lists = jnp.full((groups, LANES), -1.0, f32)
    picks = jnp.full((groups, LANES), -1.0, f32)
    one, two = lax.broadcasted_iota(jnp.int32, (LANES, LANES), 0), lax.broadcasted_iota(jnp.int32, (LANES, LANES), 1)
    earlier = jnp.where(one < two, 1.0, 0.0).astype(jnp.bfloat16)
    to, source = lax.broadcasted_iota(jnp.int32, (groups, groups), 0), lax.broadcasted_iota(jnp.int32, (groups, groups), 1)
    behind = jnp.where(to & (CHIPS - 1) == 0, to + CHIPS - 1, to - 1)
    step = jnp.where(source == behind, 1.0, 0.0).astype(jnp.bfloat16)

    def ranked(mask):
        return jnp.dot(mask.astype(jnp.bfloat16), earlier, preferred_element_type=f32)

    def listed(into, taken, rank, number, cap):
        for b in range(cap):
            pick = jnp.max(jnp.where((taken > 0) & (rank == b), loc, -1.0), axis=1, keepdims=True)
            into = jnp.where(entry == number * CAP + b, pick, into)
        return into

    for number in range(SWEEPS):
        loc = jnp.maximum(loc, flights[number])
        if number == ROUNDS:
            loc = jnp.maximum(loc, flights[number + 1])
        ready = jnp.where((needed > 0) & (loc >= 0) & (swept == 0), 1.0, 0.0)
        rank = ranked(ready)
        taken = jnp.where((ready > 0) & (rank < SWEPT[number]), 1.0, 0.0)
        swept = swept + taken
        slot_of = slot_of + taken * (rank + number * CAP)
        picks = listed(picks, taken, rank, number, SWEPT[number])
        if number < ROUNDS:
            ready = jnp.where((far > 0) & (loc >= 0) & (sent == 0), 1.0, 0.0)
            rank = jnp.zeros((groups, LANES), f32)
            above = jnp.zeros((groups, 1), f32)
            for hops in range(CHIPS - 1, 0, -1):
                level = jnp.where(far == hops, ready, 0.0)
                rank = jnp.where(far == hops, ranked(level) + above, rank)
                above = above + jnp.sum(level, axis=1, keepdims=True)
            taken = jnp.where((ready > 0) & (rank < CAP), 1.0, 0.0)
            sent = sent + taken
            lists = listed(lists, taken, rank, number, CAP)
            came = jnp.dot(step, (taken * (rank + 1)).astype(jnp.bfloat16), preferred_element_type=f32)
            flights.append(jnp.where(came > 0, came + float(2 * ENTRIES_EACH + number * CAP - 1), -1.0))
    lists_ref[...] = lists
    picks_ref[...] = picks
    slots_ref[...] = slot_of
    missing = jnp.sum(jnp.where((far > 0) & (sent == 0), 1.0, 0.0)) + jnp.sum(
        jnp.where((needed > 0) & (swept == 0), 1.0, 0.0)
    )
    plan_ref[...] = jnp.zeros(plan_ref.shape, jnp.int32)
    for line, rows in enumerate((lists_ref, picks_ref, slots_ref)):
        plan_ref[line : line + 1, :] = rows[pl.ds(me, 1), :].astype(jnp.int32)
    plan_ref[3:4, :] = jnp.full((1, LANES), missing, f32).astype(jnp.int32)


def make_plan(place, table):
    return pl.pallas_call(
        plan_kernel,
        out_shape=jax.ShapeDtypeStruct((8, LANES), jnp.int32),
        in_specs=[pl.BlockSpec(memory_space=pltpu.SMEM)] * 2,
        out_specs=pl.BlockSpec(memory_space=pltpu.VMEM),
        scratch_shapes=[pltpu.VMEM((2 * CHIPS, LANES), jnp.float32)] * 5,
        name="plan",
    )(place, table)


def pack(plan, number, pool):
    lines, caps = ((0, 1), (CAP, CAP)) if number < ROUNDS else ((1,), SWEPT[-1:])
    starts = [0]
    for array in pool:
        starts.append(starts[-1] + array.shape[0])

    def kernel(plan_ref, *refs):
        sources, outs = refs[: len(pool)], refs[len(pool) :]
        for line, out in zip(lines, outs):
            for b in range(out.shape[0]):
                at = plan_ref[line * LANES + number * CAP + b]
                for source, low, high in zip(sources, starts, starts[1:]):

                    @pl.when((at >= low) & (at < high))
                    def _(source=source, low=low, out=out, b=b, at=at):
                        out[b] = source[at - low]

    in_vmem = pl.BlockSpec(memory_space=pltpu.VMEM)
    return pl.pallas_call(
        kernel,
        out_shape=tuple(jax.ShapeDtypeStruct((cap,) + pool[0].shape[1:], pool[0].dtype) for cap in caps),
        grid_spec=pltpu.PrefetchScalarGridSpec(
            num_scalar_prefetch=1, in_specs=[in_vmem] * len(pool), out_specs=(in_vmem,) * len(lines)
        ),
        compiler_params=pltpu.CompilerParams(vmem_limit_bytes=VMEM_LIMIT),
        cost_estimate=LITTLE,
        name="pack",
    )(plan, *pool)


def previous_rows(nbr_owner, nbr_slot, nbr_count):
    rows = jnp.concatenate([nbr_owner, nbr_slot, nbr_count[:, None]], axis=1)
    rows = jnp.concatenate([shifted(rows[-1:], "seq", 1), rows[:-1]], axis=0)
    return rows[:, :KMAX], rows[:, KMAX : 2 * KMAX], rows[:, 2 * KMAX]


def fetch_by_request(store, owners, slots):
    owners_axis = lax.axis_size("seq")
    stretches = owners.shape[0]
    depth = min(stretches, max(2, 2 * stretches * KMAX // owners_axis) + 1)
    owners, slots = owners.reshape(-1), slots.reshape(-1)
    order = jnp.arange(owners.shape[0], dtype=jnp.int32)
    before = (owners[:, None] == owners[None, :]) & (order[None, :] < order[:, None])
    target = owners * depth + jnp.sum(before.astype(jnp.int32), axis=1)
    hits = target[:, None] == jnp.arange(owners_axis * depth, dtype=jnp.int32)[None, :]
    table = jnp.sum(jnp.where(hits, slots[:, None], 0), axis=0).reshape(owners_axis, depth)
    asked = lax.all_to_all(table, "seq", split_axis=0, concat_axis=0, tiled=True)
    arrived = lax.all_to_all(store[asked], "seq", split_axis=0, concat_axis=0, tiled=True)
    fetched = arrived.reshape(owners_axis * depth, NLEN, store.shape[2])[target]
    return lax.all_gather(fetched, FEATURES, axis=2, tiled=True)


def onward(value):
    size = lax.axis_size("seq")
    return lax.ppermute(value, "seq", [(chip, (chip + 1) % size) for chip in range(size)])


def four_pieces(value):
    across = swapped(value, "mp")
    return [value, swapped(value, "rep"), across, swapped(across, "rep")]


def fetch_all(store, owners, slots):
    seq = lax.axis_index("seq")
    everything = [store]
    for distance in range(1, lax.axis_size("seq")):
        for steps in (distance, -distance):
            everything.append(shifted(store, "seq", steps))
    ahead = owners - seq
    place = jnp.where(ahead == 0, 0, jnp.where(ahead < 0, -2 * ahead - 1, 2 * ahead))
    pool = jnp.concatenate(everything, axis=0)
    return pool[(place * store.shape[0] + slots).reshape(-1)]


def places_of_pieces():
    block = 2 * lax.axis_index("mp") + lax.axis_index("rep")
    return jnp.stack([block ^ i for i in range(4)]).astype(jnp.int32)


def every_group(places, groups):
    return jnp.concatenate([places, jnp.ones((groups,), jnp.int32), jnp.arange(groups, dtype=jnp.int32)])


def exchanged_table(codes):
    own_part = [codes]
    for offset in range(1, CHIPS):
        own_part.append(lax.ppermute(codes, "seq", [(chip, chip ^ offset) for chip in range(CHIPS)]))
    own_part = jnp.stack(own_part)
    return jnp.concatenate([own_part, swapped(own_part, "parts")], axis=0)


def streamed(queries, key_weight, value_weight, enc_gain, store, nbr_owner, nbr_slot, nbr_count):
    stretches = nbr_owner.shape[0]
    total = stretches * KMAX
    seq = lax.axis_index("seq")
    me = lax.axis_index("parts") * CHIPS + seq
    kept = jnp.arange(KMAX, dtype=jnp.int32)[None, :] < nbr_count[:, None]
    codes = jnp.where(kept, nbr_owner * ENTRIES_EACH + nbr_slot, -1).reshape(-1)
    first, second, codes, enc_gain = lax.optimization_barrier((store[:HALF], store[HALF:], codes, enc_gain))
    table = exchanged_table(codes)
    flights = [onward(first), onward(second)]
    gain = jnp.concatenate(four_pieces(enc_gain[None]), axis=1)
    plan = make_plan(me.reshape(1).astype(jnp.int32), table.reshape(-1)).reshape(-1)
    missing = plan[3 * LANES]

    offset = jnp.where(seq > 0, (seq ^ (seq - 1)) & 3, 0)
    behind = table[offset]
    asked = jnp.concatenate([jnp.where(seq > 0, behind[total - KMAX :], -1), codes[: total - KMAX]])
    asked = asked.reshape(stretches, KMAX)
    counts = jnp.sum((asked >= 0).astype(jnp.int32), axis=1)
    first = jnp.maximum(asked[:, 0], 0)
    asked = jnp.stack([first, jnp.where(asked[:, 1] >= 0, asked[:, 1], first)], axis=1).reshape(-1)

    places = places_of_pieces()
    room = sum(SWEPT)
    wanted = plan[LANES : LANES + room].reshape(room // GROUP, GROUP)[:, 0] >= 0
    group = jnp.arange(room // GROUP, dtype=jnp.int32)
    latest = jnp.max(jnp.where((group[None, :] <= group[:, None]) & wanted[None, :], group[None, :], 0), axis=1)
    marks = jnp.concatenate([places, wanted.astype(jnp.int32), latest])
    slots = plan[2 * LANES : 3 * LANES][asked]

    pieces, held = [], ()
    for number in range(SWEEPS):
        *ways, mine = pack(plan, number, [store] + flights[: number + 1 if number < ROUNDS else None])
        flights += [onward(way) for way in ways]
        pieces.append([mine, swapped(mine, "rep"), swapped(mine, "mp")])
        if number > 0:
            pieces[number - 1].append(swapped(pieces[number - 1][2], "rep"))
        if number == SWEEPS - 2:
            ripe, pieces[number - 1][2] = lax.optimization_barrier((pieces[:2], pieces[number - 1][2]))
            held = project(marks, gain, ripe, key_weight, value_weight, GROUP, room)
        if number + 1 < SWEEPS:
            across = [parts[2] for parts in pieces[:number]] if number + 2 < SWEEPS else []
            came = slice(number + 1, number + 2 if number + 2 < SWEEPS else None)
            flights[came], across, pieces[number][1], gain, slots, marks, held = lax.optimization_barrier(
                (flights[came], across, pieces[number][1], gain, slots, marks, held)
            )
            for parts, arrived in zip(pieces, across):
                parts[2] = arrived
    ripe, _ = lax.optimization_barrier((pieces[2:-1], mine))
    held = project(marks, gain, ripe, key_weight, value_weight, GROUP, room, 2 * CAP // GROUP, held)
    late, held = lax.optimization_barrier((pieces[-1], held))
    late = [*late, swapped(late[2], "rep")]
    done = (SWEEPS - 1) * CAP // GROUP
    keys, values = project(marks, gain, [late], key_weight, value_weight, GROUP, room, done, held)

    def whole(state):
        mine = fetch_all(store, asked >> 4, asked & (ENTRIES_EACH - 1))
        marks = every_group(places, room // 4)
        keys, values = project(marks, gain, [four_pieces(mine)], key_weight, value_weight, 4, room)
        return jnp.zeros_like(state[0]), jnp.arange(total, dtype=jnp.int32), keys, values

    state = lax.while_loop(lambda state: state[0] > 0, whole, (missing, slots, keys, values))
    return attend(state[1], counts, queries, *state[2:])


def requested(queries, key_weight, value_weight, enc_gain, store, nbr_owner, nbr_slot, nbr_count):
    gain = lax.all_gather(enc_gain, FEATURES, axis=0, tiled=True)[None]
    owners, slots, counts = previous_rows(nbr_owner, nbr_slot, nbr_count)
    total = owners.size
    pieces = [fetch_by_request(store, owners, slots)]
    marks = every_group(jnp.zeros((1,), jnp.int32), total // 4)
    keys, values = project(marks, gain, [pieces], key_weight, value_weight, 4, total)
    return attend(jnp.arange(total, dtype=jnp.int32), counts, queries, keys, values)


def solution(mesh):
    in_specs = (
        P(SEQ_SPEC, FEATURES),
        P(None, FEATURES),
        P(None, FEATURES),
        P(FEATURES),
        P(SEQ_SPEC, None, FEATURES),
        P(SEQ_SPEC, None),
        P(SEQ_SPEC, None),
        P(SEQ_SPEC),
    )
    out_specs = P(SEQ_SPEC, FEATURES)
    shape = dict(mesh.shape)
    small = shape == {"parts": 2, "seq": CHIPS, "mp": 2, "rep": 2}
    body = streamed if small else requested
    return jax.shard_map(body, mesh=mesh, in_specs=in_specs, out_specs=out_specs, check_vma=False)
```

```python
import math

import jax
import jax.numpy as jnp
from jax import lax
from jax.experimental import pallas as pl
from jax.experimental.pallas import tpu as pltpu
from jax.sharding import PartitionSpec as P

HEAD_DIM = 128
DE = 1024
NLEN = 128
STRETCH = 64
KMAX = 2
EPS = 1e-06

SEQ_SPEC = ("parts", "seq")
FEATURES = ("mp", "rep")
VMEM_LIMIT = 28 * 1024 * 1024

CHIPS = 4
ENTRIES_EACH = 16
HALF = 8
ROUNDS = 5
CAP = 4
GROUP = 2
SWEEPS = ROUNDS + 1
SWEPT = (CAP,) * ROUNDS + (2 * CAP,)
LANES = 128

LITTLE = pl.CostEstimate(flops=1, bytes_accessed=1, transcendentals=0)


def shifted(value, axis, steps):
    count = lax.axis_size(axis)
    first, last = max(0, -steps), min(count, count - steps)
    return lax.ppermute(value, axis, [(source, source + steps) for source in range(first, last)])


def swapped(value, axis):
    return lax.ppermute(value, axis, [(0, 1), (1, 0)])


def project(marks, gain, rounds, key_weight, value_weight, group, total, first=0, held=()):
    pieces = len(rounds[0])
    count, tokens, width = rounds[0][0].shape
    columns = key_weight.shape[1]
    each = count // group
    rows = group * tokens
    groups = total // group

    def kernel(marks_ref, gain_ref, *refs):
        arrays, weights = refs[: len(rounds) * pieces], refs[len(rounds) * pieces : len(rounds) * pieces + 2]
        *outs, normed, key_rows, value_rows, sems = refs[-6:]
        step = pl.program_id(0)
        ordered = (key_rows, value_rows)
        copies = [
            pltpu.make_async_copy(
                weight.at[pl.ds(pl.multiple_of(marks_ref[piece] * width, width), width)],
                rows_ref.at[pl.ds(piece * width, width)],
                sems.at[which * pieces + piece],
            )
            for which, (weight, rows_ref) in enumerate(zip(weights, ordered))
            for piece in range(pieces)
        ]

        @pl.when(step == 0)
        def _():
            for copy in copies:
                copy.start()

        wanted = marks_ref[pieces + first + step] > 0
        for number in range(len(rounds)):
            parts = arrays[number * pieces : (number + 1) * pieces]

            @pl.when(wanted & (step >= number * each) & (step < (number + 1) * each))
            def _(number=number, parts=parts):
                at = pl.ds((step - number * each) * group, group)
                raw = [part[at].reshape(rows, width).astype(jnp.float32) for part in parts]
                squares = sum(jnp.sum(part * part, axis=1, keepdims=True) for part in raw)
                scale = lax.rsqrt(squares / DE + EPS)
                for index, part in enumerate(raw):
                    place = slice(index * width, (index + 1) * width)
                    normed[:, place] = (part * scale * gain_ref[:, place]).astype(jnp.bfloat16)

        @pl.when(step == 0)
        def _():
            for copy in copies:
                copy.wait()

        @pl.when(wanted)
        def _():
            states = normed[...]
            for out, weight in zip(outs, ordered):
                product = jnp.dot(states, weight[...], preferred_element_type=jnp.float32)
                out[...] = product.astype(jnp.bfloat16).reshape(out.shape)

    out = jax.ShapeDtypeStruct((total, tokens, columns), jnp.bfloat16)
    out_spec = pl.BlockSpec((group, tokens, columns), lambda i, marks: (jnp.maximum(marks[pieces + groups + first + i], first), 0, 0))
    arrays = [piece for parts in rounds for piece in parts]
    operands = (marks, gain, *arrays, key_weight, value_weight, *held)
    return pl.pallas_call(
        kernel,
        out_shape=(out, out),
        grid_spec=pltpu.PrefetchScalarGridSpec(
            num_scalar_prefetch=1,
            grid=(len(rounds) * each,),
            in_specs=[pl.BlockSpec((1, DE), lambda i, _: (0, 0))]
            + [pl.BlockSpec(memory_space=pltpu.VMEM)] * len(arrays)
            + [pl.BlockSpec(memory_space=pl.ANY)] * (2 + len(held)),
            out_specs=(out_spec, out_spec),
            scratch_shapes=[pltpu.VMEM((rows, DE), jnp.bfloat16)]
            + [pltpu.VMEM((DE, columns), jnp.bfloat16)] * 2
            + [pltpu.SemaphoreType.DMA((2 * pieces,))],
        ),
        input_output_aliases={len(operands) - len(held) + i: i for i in range(len(held))},
        compiler_params=pltpu.CompilerParams(vmem_limit_bytes=52 * 1024 * 1024),
        cost_estimate=LITTLE,
        name="project",
    )(*operands)


SAME_COLUMNS = (((1,), (1,)), ((), ()))
SAME_ROWS = (((0,), (0,)), ((), ()))


def attend_kernel(slots, counts, query_ref, *refs):
    *entries, out_ref = refs
    keys, values = entries[: len(entries) // 2], entries[len(entries) // 2 :]
    together = len(keys) // KMAX
    wide = 2 * HEAD_DIM
    factor = math.log2(math.e) / math.sqrt(HEAD_DIM)
    count = [counts[pl.program_id(0) * together + g] for g in range(together)]
    work = [(g, start) for g in range(together) for start in range(0, query_ref.shape[1], wide)]

    def scored(g, start):
        query = query_ref[g * STRETCH : (g + 1) * STRETCH, start : start + wide]
        left, right = query[:, :HEAD_DIM], query[:, HEAD_DIM:]
        zero = jnp.zeros_like(left)
        both = jnp.concatenate([jnp.concatenate([left, zero], 1), jnp.concatenate([zero, right], 1)], 0)
        one, two = [
            lax.dot_general(
                keys[g * KMAX + k][0, :, start : start + wide], both, SAME_COLUMNS, preferred_element_type=jnp.float32
            )
            for k in range(KMAX)
        ]
        return one, jnp.where(count[g] == 2, two, -1e30)

    def weighed(one, two):
        top = jnp.maximum(one, two).max(0, keepdims=True)
        one, two = jnp.exp2((one - top) * factor), jnp.exp2((two - top) * factor)
        share = 1.0 / (one + two).sum(0, keepdims=True)
        return (one * share).astype(jnp.bfloat16), (two * share).astype(jnp.bfloat16)

    def mix(g, start, weights):
        rows = jnp.concatenate([values[g * KMAX + k][0, :, start : start + wide] for k in range(KMAX)], 0)
        mixed = lax.dot_general(jnp.concatenate(weights, 0), rows, SAME_ROWS, preferred_element_type=jnp.float32)
        mixed = jnp.where(count[g] > 0, mixed, 0.0).astype(jnp.bfloat16)
        rows = slice(g * STRETCH, (g + 1) * STRETCH)
        out_ref[rows, start : start + HEAD_DIM] = mixed[:STRETCH, :HEAD_DIM]
        out_ref[rows, start + HEAD_DIM : start + wide] = mixed[STRETCH:, HEAD_DIM:]

    scores = [scored(*piece) for piece in work]
    weights = [weighed(*pair) for pair in scores]
    for piece, pair in zip(work, weights):
        mix(*piece, pair)


def attend(slots, counts, queries, keys, values, together=3):
    stretches = counts.shape[0]
    columns = queries.shape[1]

    def entry(i):
        return pl.BlockSpec((1, NLEN, columns), lambda step, slots, _: (slots[step * together * KMAX + i], 0, 0))

    query_spec = pl.BlockSpec((together * STRETCH, columns), lambda i, *_: (i, 0))
    entries = [entry(i) for i in range(together * KMAX)]
    return pl.pallas_call(
        attend_kernel,
        out_shape=jax.ShapeDtypeStruct(queries.shape, jnp.bfloat16),
        grid_spec=pltpu.PrefetchScalarGridSpec(
            num_scalar_prefetch=2,
            grid=(stretches // together,),
            in_specs=[query_spec] + entries * 2,
            out_specs=query_spec,
        ),
        compiler_params=pltpu.CompilerParams(vmem_limit_bytes=60 * 1024 * 1024),
        cost_estimate=LITTLE,
        name="attend",
    )(slots, counts, queries, *[keys] * len(entries), *[values] * len(entries))


def plan_kernel(place, table, plan_ref, far_ref, need_ref, lists_ref, picks_ref, slots_ref):
    f32 = jnp.float32
    groups = 2 * CHIPS
    me = place[0]
    each = table.shape[0] // groups
    lane = lax.broadcasted_iota(jnp.int32, (1, LANES), 1)

    bases = [jnp.bitwise_xor(me, group) * each for group in range(groups)]
    need = []
    for group in range(groups):
        wanted = [bases[group] + j for j in range(each - KMAX)]
        if group % CHIPS > 0:
            wanted += [bases[group - 1] + each - KMAX + k for k in range(KMAX)]
        hit = jnp.zeros((1, LANES), f32)
        for index in wanted:
            hit = jnp.where(lane == table[index], 1.0, hit)
        need.append(hit)
        need_ref[group : group + 1, :] = hit
    for part in range(2):
        for chip in range(CHIPS):
            come = (chip - (lane >> 4)) & (CHIPS - 1)
            reach = jnp.zeros((1, LANES), f32)
            for hops in range(1, CHIPS):
                there = need[part * CHIPS + (chip + hops) % CHIPS] > 0
                reach = jnp.where(there & (come + hops < CHIPS), float(hops), reach)
            row = part * CHIPS + chip
            far_ref[row : row + 1, :] = reach

    row = lax.broadcasted_iota(jnp.int32, (groups, LANES), 0)
    entry = lax.broadcasted_iota(jnp.int32, (groups, LANES), 1)
    chip, owner, slot = row & (CHIPS - 1), entry >> 4, entry & (ENTRIES_EACH - 1)
    loc = jnp.where(owner == chip, slot, -1).astype(f32)
    sent = jnp.where(owner == chip, 1.0, 0.0)
    from_behind = owner == ((chip + CHIPS - 1) & (CHIPS - 1))
    halves = [from_behind & (slot < HALF), from_behind & (slot >= HALF)]
    flights = [jnp.where(half, slot + ENTRIES_EACH, -1).astype(f32) for half in halves]
    far, needed = far_ref[...], need_ref[...]
    swept = jnp.zeros((groups, LANES), f32)
    slot_of = jnp.zeros((groups, LANES), f32)
    lists = jnp.full((groups, LANES), -1.0, f32)
    picks = jnp.full((groups, LANES), -1.0, f32)
    one, two = lax.broadcasted_iota(jnp.int32, (LANES, LANES), 0), lax.broadcasted_iota(jnp.int32, (LANES, LANES), 1)
    earlier = jnp.where(one < two, 1.0, 0.0).astype(jnp.bfloat16)
    to, source = lax.broadcasted_iota(jnp.int32, (groups, groups), 0), lax.broadcasted_iota(jnp.int32, (groups, groups), 1)
    behind = jnp.where(to & (CHIPS - 1) == 0, to + CHIPS - 1, to - 1)
    step = jnp.where(source == behind, 1.0, 0.0).astype(jnp.bfloat16)

    def ranked(mask):
        return jnp.dot(mask.astype(jnp.bfloat16), earlier, preferred_element_type=f32)

    def listed(into, taken, rank, number, cap):
        for b in range(cap):
            pick = jnp.max(jnp.where((taken > 0) & (rank == b), loc, -1.0), axis=1, keepdims=True)
            into = jnp.where(entry == number * CAP + b, pick, into)
        return into

    for number in range(SWEEPS):
        loc = jnp.maximum(loc, flights[number])
        if number == ROUNDS:
            loc = jnp.maximum(loc, flights[number + 1])
        ready = jnp.where((needed > 0) & (loc >= 0) & (swept == 0), 1.0, 0.0)
        rank = ranked(ready)
        taken = jnp.where((ready > 0) & (rank < SWEPT[number]), 1.0, 0.0)
        swept = swept + taken
        slot_of = slot_of + taken * (rank + number * CAP)
        picks = listed(picks, taken, rank, number, SWEPT[number])
        if number < ROUNDS:
            ready = jnp.where((far > 0) & (loc >= 0) & (sent == 0), 1.0, 0.0)
            rank = jnp.zeros((groups, LANES), f32)
            above = jnp.zeros((groups, 1), f32)
            for hops in range(CHIPS - 1, 0, -1):
                level = jnp.where(far == hops, ready, 0.0)
                rank = jnp.where(far == hops, ranked(level) + above, rank)
                above = above + jnp.sum(level, axis=1, keepdims=True)
            taken = jnp.where((ready > 0) & (rank < CAP), 1.0, 0.0)
            sent = sent + taken
            lists = listed(lists, taken, rank, number, CAP)
            came = jnp.dot(step, (taken * (rank + 1)).astype(jnp.bfloat16), preferred_element_type=f32)
            flights.append(jnp.where(came > 0, came + float(2 * ENTRIES_EACH + number * CAP - 1), -1.0))
    lists_ref[...] = lists
    picks_ref[...] = picks
    slots_ref[...] = slot_of
    missing = jnp.sum(jnp.where((far > 0) & (sent == 0), 1.0, 0.0)) + jnp.sum(
        jnp.where((needed > 0) & (swept == 0), 1.0, 0.0)
    )
    plan_ref[...] = jnp.zeros(plan_ref.shape, jnp.int32)
    for line, rows in enumerate((lists_ref, picks_ref, slots_ref)):
        plan_ref[line : line + 1, :] = rows[pl.ds(me, 1), :].astype(jnp.int32)
    plan_ref[3:4, :] = jnp.full((1, LANES), missing, f32).astype(jnp.int32)


def make_plan(place, table):
    return pl.pallas_call(
        plan_kernel,
        out_shape=jax.ShapeDtypeStruct((8, LANES), jnp.int32),
        in_specs=[pl.BlockSpec(memory_space=pltpu.SMEM)] * 2,
        out_specs=pl.BlockSpec(memory_space=pltpu.VMEM),
        scratch_shapes=[pltpu.VMEM((2 * CHIPS, LANES), jnp.float32)] * 5,
        name="plan",
    )(place, table)


def pack(plan, number, pool):
    lines, caps = ((0, 1), (CAP, CAP)) if number < ROUNDS else ((1,), SWEPT[-1:])
    starts = [0]
    for array in pool:
        starts.append(starts[-1] + array.shape[0])

    def kernel(plan_ref, *refs):
        sources, outs = refs[: len(pool)], refs[len(pool) :]
        for line, out in zip(lines, outs):
            for b in range(out.shape[0]):
                at = plan_ref[line * LANES + number * CAP + b]
                for source, low, high in zip(sources, starts, starts[1:]):

                    @pl.when((at >= low) & (at < high))
                    def _(source=source, low=low, out=out, b=b, at=at):
                        out[b] = source[at - low]

    in_vmem = pl.BlockSpec(memory_space=pltpu.VMEM)
    return pl.pallas_call(
        kernel,
        out_shape=tuple(jax.ShapeDtypeStruct((cap,) + pool[0].shape[1:], pool[0].dtype) for cap in caps),
        grid_spec=pltpu.PrefetchScalarGridSpec(
            num_scalar_prefetch=1, in_specs=[in_vmem] * len(pool), out_specs=(in_vmem,) * len(lines)
        ),
        compiler_params=pltpu.CompilerParams(vmem_limit_bytes=VMEM_LIMIT),
        cost_estimate=LITTLE,
        name="pack",
    )(plan, *pool)


def previous_rows(nbr_owner, nbr_slot, nbr_count):
    rows = jnp.concatenate([nbr_owner, nbr_slot, nbr_count[:, None]], axis=1)
    rows = jnp.concatenate([shifted(rows[-1:], "seq", 1), rows[:-1]], axis=0)
    return rows[:, :KMAX], rows[:, KMAX : 2 * KMAX], rows[:, 2 * KMAX]


def fetch_by_request(store, owners, slots):
    owners_axis = lax.axis_size("seq")
    stretches = owners.shape[0]
    depth = min(stretches, max(2, 2 * stretches * KMAX // owners_axis) + 1)
    owners, slots = owners.reshape(-1), slots.reshape(-1)
    order = jnp.arange(owners.shape[0], dtype=jnp.int32)
    before = (owners[:, None] == owners[None, :]) & (order[None, :] < order[:, None])
    target = owners * depth + jnp.sum(before.astype(jnp.int32), axis=1)
    hits = target[:, None] == jnp.arange(owners_axis * depth, dtype=jnp.int32)[None, :]
    table = jnp.sum(jnp.where(hits, slots[:, None], 0), axis=0).reshape(owners_axis, depth)
    asked = lax.all_to_all(table, "seq", split_axis=0, concat_axis=0, tiled=True)
    arrived = lax.all_to_all(store[asked], "seq", split_axis=0, concat_axis=0, tiled=True)
    fetched = arrived.reshape(owners_axis * depth, NLEN, store.shape[2])[target]
    return lax.all_gather(fetched, FEATURES, axis=2, tiled=True)


def onward(value):
    size = lax.axis_size("seq")
    return lax.ppermute(value, "seq", [(chip, (chip + 1) % size) for chip in range(size)])


def four_pieces(value):
    across = swapped(value, "mp")
    return [value, swapped(value, "rep"), across, swapped(across, "rep")]


def fetch_all(store, owners, slots):
    seq = lax.axis_index("seq")
    everything = [store]
    for distance in range(1, lax.axis_size("seq")):
        for steps in (distance, -distance):
            everything.append(shifted(store, "seq", steps))
    ahead = owners - seq
    place = jnp.where(ahead == 0, 0, jnp.where(ahead < 0, -2 * ahead - 1, 2 * ahead))
    pool = jnp.concatenate(everything, axis=0)
    return pool[(place * store.shape[0] + slots).reshape(-1)]


def places_of_pieces():
    block = 2 * lax.axis_index("mp") + lax.axis_index("rep")
    return jnp.stack([block ^ i for i in range(4)]).astype(jnp.int32)


def every_group(places, groups):
    return jnp.concatenate([places, jnp.ones((groups,), jnp.int32), jnp.arange(groups, dtype=jnp.int32)])


def exchanged_table(codes):
    own_part = [codes]
    for offset in range(1, CHIPS):
        own_part.append(lax.ppermute(codes, "seq", [(chip, chip ^ offset) for chip in range(CHIPS)]))
    own_part = jnp.stack(own_part)
    return jnp.concatenate([own_part, swapped(own_part, "parts")], axis=0)


def streamed(queries, key_weight, value_weight, enc_gain, store, nbr_owner, nbr_slot, nbr_count):
    stretches = nbr_owner.shape[0]
    total = stretches * KMAX
    seq = lax.axis_index("seq")
    me = lax.axis_index("parts") * CHIPS + seq
    kept = jnp.arange(KMAX, dtype=jnp.int32)[None, :] < nbr_count[:, None]
    codes = jnp.where(kept, nbr_owner * ENTRIES_EACH + nbr_slot, -1).reshape(-1)
    first, second, codes, enc_gain = lax.optimization_barrier((store[:HALF], store[HALF:], codes, enc_gain))
    table = exchanged_table(codes)
    flights = [onward(first), onward(second)]
    gain = jnp.concatenate(four_pieces(enc_gain[None]), axis=1)
    plan = make_plan(me.reshape(1).astype(jnp.int32), table.reshape(-1)).reshape(-1)
    missing = plan[3 * LANES]

    offset = jnp.where(seq > 0, (seq ^ (seq - 1)) & 3, 0)
    behind = table[offset]
    asked = jnp.concatenate([jnp.where(seq > 0, behind[total - KMAX :], -1), codes[: total - KMAX]])
    asked = asked.reshape(stretches, KMAX)
    counts = jnp.sum((asked >= 0).astype(jnp.int32), axis=1)
    first = jnp.maximum(asked[:, 0], 0)
    asked = jnp.stack([first, jnp.where(asked[:, 1] >= 0, asked[:, 1], first)], axis=1).reshape(-1)

    places = places_of_pieces()
    room = sum(SWEPT)
    wanted = plan[LANES : LANES + room].reshape(room // GROUP, GROUP)[:, 0] >= 0
    group = jnp.arange(room // GROUP, dtype=jnp.int32)
    latest = jnp.max(jnp.where((group[None, :] <= group[:, None]) & wanted[None, :], group[None, :], 0), axis=1)
    marks = jnp.concatenate([places, wanted.astype(jnp.int32), latest])
    slots = plan[2 * LANES : 3 * LANES][asked]

    pieces, held = [], ()
    for number in range(SWEEPS):
        *ways, mine = pack(plan, number, [store] + flights[: number + 1 if number < ROUNDS else None])
        flights += [onward(way) for way in ways]
        pieces.append([mine, swapped(mine, "rep"), swapped(mine, "mp")])
        if number > 0:
            pieces[number - 1].append(swapped(pieces[number - 1][2], "rep"))
        if number == SWEEPS - 2:
            ripe, pieces[number - 1][2] = lax.optimization_barrier((pieces[:2], pieces[number - 1][2]))
            held = project(marks, gain, ripe, key_weight, value_weight, GROUP, room)
        if number + 1 < SWEEPS:
            across = [parts[2] for parts in pieces[:number]] if number + 2 < SWEEPS else []
            came = slice(number + 1, number + 2 if number + 2 < SWEEPS else None)
            flights[came], across, pieces[number][1], gain, slots, marks, held = lax.optimization_barrier(
                (flights[came], across, pieces[number][1], gain, slots, marks, held)
            )
            for parts, arrived in zip(pieces, across):
                parts[2] = arrived
    ripe, _ = lax.optimization_barrier((pieces[2:-1], mine))
    held = project(marks, gain, ripe, key_weight, value_weight, GROUP, room, 2 * CAP // GROUP, held)
    late, held = lax.optimization_barrier((pieces[-1], held))
    late = [*late, swapped(late[2], "rep")]
    done = (SWEEPS - 1) * CAP // GROUP
    keys, values = project(marks, gain, [late], key_weight, value_weight, GROUP, room, done, held)

    def whole(state):
        mine = fetch_all(store, asked >> 4, asked & (ENTRIES_EACH - 1))
        marks = every_group(places, room // 4)
        keys, values = project(marks, gain, [four_pieces(mine)], key_weight, value_weight, 4, room)
        return jnp.zeros_like(state[0]), jnp.arange(total, dtype=jnp.int32), keys, values

    state = lax.while_loop(lambda state: state[0] > 0, whole, (missing, slots, keys, values))
    return attend(state[1], counts, queries, *state[2:])


def requested(queries, key_weight, value_weight, enc_gain, store, nbr_owner, nbr_slot, nbr_count):
    gain = lax.all_gather(enc_gain, FEATURES, axis=0, tiled=True)[None]
    owners, slots, counts = previous_rows(nbr_owner, nbr_slot, nbr_count)
    total = owners.size
    pieces = [fetch_by_request(store, owners, slots)]
    marks = every_group(jnp.zeros((1,), jnp.int32), total // 4)
    keys, values = project(marks, gain, [pieces], key_weight, value_weight, 4, total)
    return attend(jnp.arange(total, dtype=jnp.int32), counts, queries, keys, values)


def solution(mesh):
    in_specs = (
        P(SEQ_SPEC, FEATURES),
        P(None, FEATURES),
        P(None, FEATURES),
        P(FEATURES),
        P(SEQ_SPEC, None, FEATURES),
        P(SEQ_SPEC, None),
        P(SEQ_SPEC, None),
        P(SEQ_SPEC),
    )
    out_specs = P(SEQ_SPEC, FEATURES)
    shape = dict(mesh.shape)
    small = shape == {"parts": 2, "seq": CHIPS, "mp": 2, "rep": 2}
    body = streamed if small else requested
    return jax.shard_map(body, mesh=mesh, in_specs=in_specs, out_specs=out_specs, check_vma=False)
```

```python
import math

import jax
import jax.numpy as jnp
from jax import lax
from jax.experimental import pallas as pl
from jax.experimental.pallas import tpu as pltpu
from jax.sharding import PartitionSpec as P

HEAD_DIM = 128
DE = 1024
NLEN = 128
STRETCH = 64
KMAX = 2
EPS = 1e-06

SEQ_SPEC = ("parts", "seq")
FEATURES = ("mp", "rep")
VMEM_LIMIT = 28 * 1024 * 1024

CHIPS = 4
ENTRIES_EACH = 16
HALF = 8
ROUNDS = 5
CAP = 4
GROUP = 2
SWEEPS = ROUNDS + 1
SWEPT = (CAP,) * ROUNDS + (2 * CAP,)
LANES = 128

LITTLE = pl.CostEstimate(flops=1, bytes_accessed=1, transcendentals=0)


def shifted(value, axis, steps):
    count = lax.axis_size(axis)
    first, last = max(0, -steps), min(count, count - steps)
    return lax.ppermute(value, axis, [(source, source + steps) for source in range(first, last)])


def swapped(value, axis):
    return lax.ppermute(value, axis, [(0, 1), (1, 0)])


def project(marks, gain, rounds, key_weight, value_weight, group, total, first=0, held=()):
    pieces = len(rounds[0])
    count, tokens, width = rounds[0][0].shape
    columns = key_weight.shape[1]
    each = count // group
    rows = group * tokens
    groups = total // group

    def kernel(marks_ref, gain_ref, *refs):
        arrays, weights = refs[: len(rounds) * pieces], refs[len(rounds) * pieces : len(rounds) * pieces + 2]
        *outs, normed, key_rows, value_rows, sems = refs[-6:]
        step = pl.program_id(0)
        ordered = (key_rows, value_rows)
        copies = [
            pltpu.make_async_copy(
                weight.at[pl.ds(pl.multiple_of(marks_ref[piece] * width, width), width)],
                rows_ref.at[pl.ds(piece * width, width)],
                sems.at[which * pieces + piece],
            )
            for which, (weight, rows_ref) in enumerate(zip(weights, ordered))
            for piece in range(pieces)
        ]

        @pl.when(step == 0)
        def _():
            for copy in copies:
                copy.start()

        wanted = marks_ref[pieces + first + step] > 0
        for number in range(len(rounds)):
            parts = arrays[number * pieces : (number + 1) * pieces]

            @pl.when(wanted & (step >= number * each) & (step < (number + 1) * each))
            def _(number=number, parts=parts):
                at = pl.ds((step - number * each) * group, group)
                raw = [part[at].reshape(rows, width).astype(jnp.float32) for part in parts]
                squares = sum(jnp.sum(part * part, axis=1, keepdims=True) for part in raw)
                scale = lax.rsqrt(squares / DE + EPS)
                for index, part in enumerate(raw):
                    place = slice(index * width, (index + 1) * width)
                    normed[:, place] = (part * scale * gain_ref[:, place]).astype(jnp.bfloat16)

        @pl.when(step == 0)
        def _():
            for copy in copies:
                copy.wait()

        @pl.when(wanted)
        def _():
            states = normed[...]
            for out, weight in zip(outs, ordered):
                product = jnp.dot(states, weight[...], preferred_element_type=jnp.float32)
                out[...] = product.astype(jnp.bfloat16).reshape(out.shape)

    out = jax.ShapeDtypeStruct((total, tokens, columns), jnp.bfloat16)
    out_spec = pl.BlockSpec((group, tokens, columns), lambda i, marks: (jnp.maximum(marks[pieces + groups + first + i], first), 0, 0))
    arrays = [piece for parts in rounds for piece in parts]
    operands = (marks, gain, *arrays, key_weight, value_weight, *held)
    return pl.pallas_call(
        kernel,
        out_shape=(out, out),
        grid_spec=pltpu.PrefetchScalarGridSpec(
            num_scalar_prefetch=1,
            grid=(len(rounds) * each,),
            in_specs=[pl.BlockSpec((1, DE), lambda i, _: (0, 0))]
            + [pl.BlockSpec(memory_space=pltpu.VMEM)] * len(arrays)
            + [pl.BlockSpec(memory_space=pl.ANY)] * (2 + len(held)),
            out_specs=(out_spec, out_spec),
            scratch_shapes=[pltpu.VMEM((rows, DE), jnp.bfloat16)]
            + [pltpu.VMEM((DE, columns), jnp.bfloat16)] * 2
            + [pltpu.SemaphoreType.DMA((2 * pieces,))],
        ),
        input_output_aliases={len(operands) - len(held) + i: i for i in range(len(held))},
        compiler_params=pltpu.CompilerParams(vmem_limit_bytes=VMEM_LIMIT),
        cost_estimate=LITTLE,
        name="project",
    )(*operands)


SAME_COLUMNS = (((1,), (1,)), ((), ()))
SAME_ROWS = (((0,), (0,)), ((), ()))


def attend_kernel(slots, counts, query_ref, *refs):
    *entries, out_ref = refs
    keys, values = entries[: len(entries) // 2], entries[len(entries) // 2 :]
    together = len(keys) // KMAX
    wide = 2 * HEAD_DIM
    factor = math.log2(math.e) / math.sqrt(HEAD_DIM)
    count = [counts[pl.program_id(0) * together + g] for g in range(together)]
    work = [(g, start) for g in range(together) for start in range(0, query_ref.shape[1], wide)]

    def scored(g, start):
        query = query_ref[g * STRETCH : (g + 1) * STRETCH, start : start + wide]
        left, right = query[:, :HEAD_DIM], query[:, HEAD_DIM:]
        zero = jnp.zeros_like(left)
        both = jnp.concatenate([jnp.concatenate([left, zero], 1), jnp.concatenate([zero, right], 1)], 0)
        one, two = [
            lax.dot_general(
                keys[g * KMAX + k][0, :, start : start + wide], both, SAME_COLUMNS, preferred_element_type=jnp.float32
            )
            for k in range(KMAX)
        ]
        return one, jnp.where(count[g] == 2, two, -1e30)

    def weighed(one, two):
        top = jnp.maximum(one, two).max(0, keepdims=True)
        one, two = jnp.exp2((one - top) * factor), jnp.exp2((two - top) * factor)
        share = 1.0 / (one + two).sum(0, keepdims=True)
        return (one * share).astype(jnp.bfloat16), (two * share).astype(jnp.bfloat16)

    def mix(g, start, weights):
        rows = jnp.concatenate([values[g * KMAX + k][0, :, start : start + wide] for k in range(KMAX)], 0)
        mixed = lax.dot_general(jnp.concatenate(weights, 0), rows, SAME_ROWS, preferred_element_type=jnp.float32)
        mixed = jnp.where(count[g] > 0, mixed, 0.0).astype(jnp.bfloat16)
        rows = slice(g * STRETCH, (g + 1) * STRETCH)
        out_ref[rows, start : start + HEAD_DIM] = mixed[:STRETCH, :HEAD_DIM]
        out_ref[rows, start + HEAD_DIM : start + wide] = mixed[STRETCH:, HEAD_DIM:]

    scores = [scored(*piece) for piece in work]
    weights = [weighed(*pair) for pair in scores]
    for piece, pair in zip(work, weights):
        mix(*piece, pair)


def attend(slots, counts, queries, keys, values, together=3):
    stretches = counts.shape[0]
    columns = queries.shape[1]

    def entry(i):
        return pl.BlockSpec((1, NLEN, columns), lambda step, slots, _: (slots[step * together * KMAX + i], 0, 0))

    query_spec = pl.BlockSpec((together * STRETCH, columns), lambda i, *_: (i, 0))
    entries = [entry(i) for i in range(together * KMAX)]
    return pl.pallas_call(
        attend_kernel,
        out_shape=jax.ShapeDtypeStruct(queries.shape, jnp.bfloat16),
        grid_spec=pltpu.PrefetchScalarGridSpec(
            num_scalar_prefetch=2,
            grid=(stretches // together,),
            in_specs=[query_spec] + entries * 2,
            out_specs=query_spec,
        ),
        compiler_params=pltpu.CompilerParams(vmem_limit_bytes=VMEM_LIMIT),
        cost_estimate=LITTLE,
        name="attend",
    )(slots, counts, queries, *[keys] * len(entries), *[values] * len(entries))


def plan_kernel(place, table, plan_ref, far_ref, need_ref, lists_ref, picks_ref, slots_ref):
    f32 = jnp.float32
    groups = 2 * CHIPS
    me = place[0]
    each = table.shape[0] // groups
    lane = lax.broadcasted_iota(jnp.int32, (1, LANES), 1)

    bases = [jnp.bitwise_xor(me, group) * each for group in range(groups)]
    need = []
    for group in range(groups):
        wanted = [bases[group] + j for j in range(each - KMAX)]
        if group % CHIPS > 0:
            wanted += [bases[group - 1] + each - KMAX + k for k in range(KMAX)]
        hit = jnp.zeros((1, LANES), f32)
        for index in wanted:
            hit = jnp.where(lane == table[index], 1.0, hit)
        need.append(hit)
        need_ref[group : group + 1, :] = hit
    for part in range(2):
        for chip in range(CHIPS):
            come = (chip - (lane >> 4)) & (CHIPS - 1)
            reach = jnp.zeros((1, LANES), f32)
            for hops in range(1, CHIPS):
                there = need[part * CHIPS + (chip + hops) % CHIPS] > 0
                reach = jnp.where(there & (come + hops < CHIPS), float(hops), reach)
            row = part * CHIPS + chip
            far_ref[row : row + 1, :] = reach

    row = lax.broadcasted_iota(jnp.int32, (groups, LANES), 0)
    entry = lax.broadcasted_iota(jnp.int32, (groups, LANES), 1)
    chip, owner, slot = row & (CHIPS - 1), entry >> 4, entry & (ENTRIES_EACH - 1)
    loc = jnp.where(owner == chip, slot, -1).astype(f32)
    sent = jnp.where(owner == chip, 1.0, 0.0)
    from_behind = owner == ((chip + CHIPS - 1) & (CHIPS - 1))
    halves = [from_behind & (slot < HALF), from_behind & (slot >= HALF)]
    flights = [jnp.where(half, slot + ENTRIES_EACH, -1).astype(f32) for half in halves]
    far, needed = far_ref[...], need_ref[...]
    swept = jnp.zeros((groups, LANES), f32)
    slot_of = jnp.zeros((groups, LANES), f32)
    lists = jnp.full((groups, LANES), -1.0, f32)
    picks = jnp.full((groups, LANES), -1.0, f32)
    one, two = lax.broadcasted_iota(jnp.int32, (LANES, LANES), 0), lax.broadcasted_iota(jnp.int32, (LANES, LANES), 1)
    earlier = jnp.where(one < two, 1.0, 0.0).astype(jnp.bfloat16)
    to, source = lax.broadcasted_iota(jnp.int32, (groups, groups), 0), lax.broadcasted_iota(jnp.int32, (groups, groups), 1)
    behind = jnp.where(to & (CHIPS - 1) == 0, to + CHIPS - 1, to - 1)
    step = jnp.where(source == behind, 1.0, 0.0).astype(jnp.bfloat16)

    def ranked(mask):
        return jnp.dot(mask.astype(jnp.bfloat16), earlier, preferred_element_type=f32)

    def listed(into, taken, rank, number, cap):
        for b in range(cap):
            pick = jnp.max(jnp.where((taken > 0) & (rank == b), loc, -1.0), axis=1, keepdims=True)
            into = jnp.where(entry == number * CAP + b, pick, into)
        return into

    for number in range(SWEEPS):
        loc = jnp.maximum(loc, flights[number])
        if number == ROUNDS:
            loc = jnp.maximum(loc, flights[number + 1])
        ready = jnp.where((needed > 0) & (loc >= 0) & (swept == 0), 1.0, 0.0)
        rank = ranked(ready)
        taken = jnp.where((ready > 0) & (rank < SWEPT[number]), 1.0, 0.0)
        swept = swept + taken
        slot_of = slot_of + taken * (rank + number * CAP)
        picks = listed(picks, taken, rank, number, SWEPT[number])
        if number < ROUNDS:
            ready = jnp.where((far > 0) & (loc >= 0) & (sent == 0), 1.0, 0.0)
            rank = jnp.zeros((groups, LANES), f32)
            above = jnp.zeros((groups, 1), f32)
            for hops in range(CHIPS - 1, 0, -1):
                level = jnp.where(far == hops, ready, 0.0)
                rank = jnp.where(far == hops, ranked(level) + above, rank)
                above = above + jnp.sum(level, axis=1, keepdims=True)
            taken = jnp.where((ready > 0) & (rank < CAP), 1.0, 0.0)
            sent = sent + taken
            lists = listed(lists, taken, rank, number, CAP)
            came = jnp.dot(step, (taken * (rank + 1)).astype(jnp.bfloat16), preferred_element_type=f32)
            flights.append(jnp.where(came > 0, came + float(2 * ENTRIES_EACH + number * CAP - 1), -1.0))
    lists_ref[...] = lists
    picks_ref[...] = picks
    slots_ref[...] = slot_of
    missing = jnp.sum(jnp.where((far > 0) & (sent == 0), 1.0, 0.0)) + jnp.sum(
        jnp.where((needed > 0) & (swept == 0), 1.0, 0.0)
    )
    plan_ref[...] = jnp.zeros(plan_ref.shape, jnp.int32)
    for line, rows in enumerate((lists_ref, picks_ref, slots_ref)):
        plan_ref[line : line + 1, :] = rows[pl.ds(me, 1), :].astype(jnp.int32)
    plan_ref[3:4, :] = jnp.full((1, LANES), missing, f32).astype(jnp.int32)


def make_plan(place, table):
    return pl.pallas_call(
        plan_kernel,
        out_shape=jax.ShapeDtypeStruct((8, LANES), jnp.int32),
        in_specs=[pl.BlockSpec(memory_space=pltpu.SMEM)] * 2,
        out_specs=pl.BlockSpec(memory_space=pltpu.VMEM),
        scratch_shapes=[pltpu.VMEM((2 * CHIPS, LANES), jnp.float32)] * 5,
        name="plan",
    )(place, table)


def pack(plan, number, pool):
    lines, caps = ((0, 1), (CAP, CAP)) if number < ROUNDS else ((1,), SWEPT[-1:])
    starts = [0]
    for array in pool:
        starts.append(starts[-1] + array.shape[0])

    def kernel(plan_ref, *refs):
        sources, outs = refs[: len(pool)], refs[len(pool) :]
        for line, out in zip(lines, outs):
            for b in range(out.shape[0]):
                at = plan_ref[line * LANES + number * CAP + b]
                for source, low, high in zip(sources, starts, starts[1:]):

                    @pl.when((at >= low) & (at < high))
                    def _(source=source, low=low, out=out, b=b, at=at):
                        out[b] = source[at - low]

    in_vmem = pl.BlockSpec(memory_space=pltpu.VMEM)
    return pl.pallas_call(
        kernel,
        out_shape=tuple(jax.ShapeDtypeStruct((cap,) + pool[0].shape[1:], pool[0].dtype) for cap in caps),
        grid_spec=pltpu.PrefetchScalarGridSpec(
            num_scalar_prefetch=1, in_specs=[in_vmem] * len(pool), out_specs=(in_vmem,) * len(lines)
        ),
        compiler_params=pltpu.CompilerParams(vmem_limit_bytes=VMEM_LIMIT),
        cost_estimate=LITTLE,
        name="pack",
    )(plan, *pool)


def previous_rows(nbr_owner, nbr_slot, nbr_count):
    rows = jnp.concatenate([nbr_owner, nbr_slot, nbr_count[:, None]], axis=1)
    rows = jnp.concatenate([shifted(rows[-1:], "seq", 1), rows[:-1]], axis=0)
    return rows[:, :KMAX], rows[:, KMAX : 2 * KMAX], rows[:, 2 * KMAX]


def fetch_by_request(store, owners, slots):
    owners_axis = lax.axis_size("seq")
    stretches = owners.shape[0]
    depth = min(stretches, max(2, 2 * stretches * KMAX // owners_axis) + 1)
    owners, slots = owners.reshape(-1), slots.reshape(-1)
    order = jnp.arange(owners.shape[0], dtype=jnp.int32)
    before = (owners[:, None] == owners[None, :]) & (order[None, :] < order[:, None])
    target = owners * depth + jnp.sum(before.astype(jnp.int32), axis=1)
    hits = target[:, None] == jnp.arange(owners_axis * depth, dtype=jnp.int32)[None, :]
    table = jnp.sum(jnp.where(hits, slots[:, None], 0), axis=0).reshape(owners_axis, depth)
    asked = lax.all_to_all(table, "seq", split_axis=0, concat_axis=0, tiled=True)
    arrived = lax.all_to_all(store[asked], "seq", split_axis=0, concat_axis=0, tiled=True)
    fetched = arrived.reshape(owners_axis * depth, NLEN, store.shape[2])[target]
    return lax.all_gather(fetched, FEATURES, axis=2, tiled=True)


def onward(value):
    size = lax.axis_size("seq")
    return lax.ppermute(value, "seq", [(chip, (chip + 1) % size) for chip in range(size)])


def four_pieces(value):
    across = swapped(value, "mp")
    return [value, swapped(value, "rep"), across, swapped(across, "rep")]


def fetch_all(store, owners, slots):
    seq = lax.axis_index("seq")
    everything = [store]
    for distance in range(1, lax.axis_size("seq")):
        for steps in (distance, -distance):
            everything.append(shifted(store, "seq", steps))
    ahead = owners - seq
    place = jnp.where(ahead == 0, 0, jnp.where(ahead < 0, -2 * ahead - 1, 2 * ahead))
    pool = jnp.concatenate(everything, axis=0)
    return pool[(place * store.shape[0] + slots).reshape(-1)]


def places_of_pieces():
    block = 2 * lax.axis_index("mp") + lax.axis_index("rep")
    return jnp.stack([block ^ i for i in range(4)]).astype(jnp.int32)


def every_group(places, groups):
    return jnp.concatenate([places, jnp.ones((groups,), jnp.int32), jnp.arange(groups, dtype=jnp.int32)])


def exchanged_table(codes):
    own_part = [codes]
    for offset in range(1, CHIPS):
        own_part.append(lax.ppermute(codes, "seq", [(chip, chip ^ offset) for chip in range(CHIPS)]))
    own_part = jnp.stack(own_part)
    return jnp.concatenate([own_part, swapped(own_part, "parts")], axis=0)


def streamed(queries, key_weight, value_weight, enc_gain, store, nbr_owner, nbr_slot, nbr_count):
    stretches = nbr_owner.shape[0]
    total = stretches * KMAX
    seq = lax.axis_index("seq")
    me = lax.axis_index("parts") * CHIPS + seq
    kept = jnp.arange(KMAX, dtype=jnp.int32)[None, :] < nbr_count[:, None]
    codes = jnp.where(kept, nbr_owner * ENTRIES_EACH + nbr_slot, -1).reshape(-1)
    first, second, codes, enc_gain = lax.optimization_barrier((store[:HALF], store[HALF:], codes, enc_gain))
    table = exchanged_table(codes)
    flights = [onward(first), onward(second)]
    gain = jnp.concatenate(four_pieces(enc_gain[None]), axis=1)
    plan = make_plan(me.reshape(1).astype(jnp.int32), table.reshape(-1)).reshape(-1)
    missing = plan[3 * LANES]

    offset = jnp.where(seq > 0, (seq ^ (seq - 1)) & 3, 0)
    behind = table[offset]
    asked = jnp.concatenate([jnp.where(seq > 0, behind[total - KMAX :], -1), codes[: total - KMAX]])
    asked = asked.reshape(stretches, KMAX)
    counts = jnp.sum((asked >= 0).astype(jnp.int32), axis=1)
    first = jnp.maximum(asked[:, 0], 0)
    asked = jnp.stack([first, jnp.where(asked[:, 1] >= 0, asked[:, 1], first)], axis=1).reshape(-1)

    places = places_of_pieces()
    room = sum(SWEPT)
    wanted = plan[LANES : LANES + room].reshape(room // GROUP, GROUP)[:, 0] >= 0
    group = jnp.arange(room // GROUP, dtype=jnp.int32)
    latest = jnp.max(jnp.where((group[None, :] <= group[:, None]) & wanted[None, :], group[None, :], 0), axis=1)
    marks = jnp.concatenate([places, wanted.astype(jnp.int32), latest])
    slots = plan[2 * LANES : 3 * LANES][asked]

    pieces, held = [], ()
    for number in range(SWEEPS):
        *ways, mine = pack(plan, number, [store] + flights[: number + 1 if number < ROUNDS else None])
        flights += [onward(way) for way in ways]
        pieces.append([mine, swapped(mine, "rep"), swapped(mine, "mp")])
        if number > 0:
            pieces[number - 1].append(swapped(pieces[number - 1][2], "rep"))
        if number == SWEEPS - 2:
            ripe, pieces[number - 1][2] = lax.optimization_barrier((pieces[:2], pieces[number - 1][2]))
            held = project(marks, gain, ripe, key_weight, value_weight, GROUP, room)
        if number + 1 < SWEEPS:
            across = [parts[2] for parts in pieces[:number]] if number + 2 < SWEEPS else []
            came = slice(number + 1, number + 2 if number + 2 < SWEEPS else None)
            flights[came], across, pieces[number][1], gain, slots, marks, held = lax.optimization_barrier(
                (flights[came], across, pieces[number][1], gain, slots, marks, held)
            )
            for parts, arrived in zip(pieces, across):
                parts[2] = arrived
    ripe, _ = lax.optimization_barrier((pieces[2:-1], mine))
    held = project(marks, gain, ripe, key_weight, value_weight, GROUP, room, 2 * CAP // GROUP, held)
    late, held = lax.optimization_barrier((pieces[-1], held))
    late = [*late, swapped(late[2], "rep")]
    done = (SWEEPS - 1) * CAP // GROUP
    keys, values = project(marks, gain, [late], key_weight, value_weight, GROUP, room, done, held)

    result = attend(slots, counts, queries, keys, values)

    def whole(state):
        mine = fetch_all(store, asked >> 4, asked & (ENTRIES_EACH - 1))
        marks = every_group(places, total // 4)
        keys, values = project(marks, gain, [four_pieces(mine)], key_weight, value_weight, 4, total)
        order = jnp.arange(total, dtype=jnp.int32)
        return jnp.zeros_like(state[0]), attend(order, counts, queries, keys, values)

    return lax.while_loop(lambda state: state[0] > 0, whole, (missing, result))[1]


def requested(queries, key_weight, value_weight, enc_gain, store, nbr_owner, nbr_slot, nbr_count):
    gain = lax.all_gather(enc_gain, FEATURES, axis=0, tiled=True)[None]
    owners, slots, counts = previous_rows(nbr_owner, nbr_slot, nbr_count)
    total = owners.size
    pieces = [fetch_by_request(store, owners, slots)]
    marks = every_group(jnp.zeros((1,), jnp.int32), total // 4)
    keys, values = project(marks, gain, [pieces], key_weight, value_weight, 4, total)
    return attend(jnp.arange(total, dtype=jnp.int32), counts, queries, keys, values)


def solution(mesh):
    in_specs = (
        P(SEQ_SPEC, FEATURES),
        P(None, FEATURES),
        P(None, FEATURES),
        P(FEATURES),
        P(SEQ_SPEC, None, FEATURES),
        P(SEQ_SPEC, None),
        P(SEQ_SPEC, None),
        P(SEQ_SPEC),
    )
    out_specs = P(SEQ_SPEC, FEATURES)
    shape = dict(mesh.shape)
    small = shape == {"parts": 2, "seq": CHIPS, "mp": 2, "rep": 2}
    body = streamed if small else requested
    return jax.shard_map(body, mesh=mesh, in_specs=in_specs, out_specs=out_specs, check_vma=False)
```

```python
import math

import jax
import jax.numpy as jnp
from jax import lax
from jax.experimental import pallas as pl
from jax.experimental.pallas import tpu as pltpu
from jax.sharding import PartitionSpec as P

HEAD_DIM = 128
DE = 1024
NLEN = 128
STRETCH = 64
KMAX = 2
EPS = 1e-06

SEQ_SPEC = ("parts", "seq")
FEATURES = ("mp", "rep")
MIB = 1024 * 1024

CHIPS = 4
ENTRIES_EACH = 16
HALF = 8
ROUNDS = 5
CAP = 4
GROUP = 2
SWEEPS = ROUNDS + 1
SWEPT = (CAP,) * ROUNDS + (2 * CAP,)
LANES = 128

LITTLE = pl.CostEstimate(flops=1, bytes_accessed=1, transcendentals=0)


def shifted(value, axis, steps):
    count = lax.axis_size(axis)
    first, last = max(0, -steps), min(count, count - steps)
    return lax.ppermute(value, axis, [(source, source + steps) for source in range(first, last)])


def swapped(value, axis):
    return lax.ppermute(value, axis, [(0, 1), (1, 0)])


def project(marks, gain, rounds, key_weight, value_weight, group, total, first=0, held=()):
    pieces = len(rounds[0])
    count, tokens, width = rounds[0][0].shape
    columns = key_weight.shape[1]
    each = count // group
    rows = group * tokens
    groups = total // group

    def kernel(marks_ref, gain_ref, *refs):
        arrays, weights = refs[: len(rounds) * pieces], refs[len(rounds) * pieces : len(rounds) * pieces + 2]
        *outs, normed, key_rows, value_rows, sems = refs[-6:]
        step = pl.program_id(0)
        ordered = (key_rows, value_rows)
        copies = [
            pltpu.make_async_copy(
                weight.at[pl.ds(pl.multiple_of(marks_ref[piece] * width, width), width)],
                rows_ref.at[pl.ds(piece * width, width)],
                sems.at[which * pieces + piece],
            )
            for which, (weight, rows_ref) in enumerate(zip(weights, ordered))
            for piece in range(pieces)
        ]

        @pl.when(step == 0)
        def _():
            for copy in copies:
                copy.start()

        wanted = marks_ref[pieces + first + step] > 0
        for number in range(len(rounds)):
            parts = arrays[number * pieces : (number + 1) * pieces]

            @pl.when(wanted & (step >= number * each) & (step < (number + 1) * each))
            def _(number=number, parts=parts):
                at = pl.ds((step - number * each) * group, group)
                raw = [part[at].reshape(rows, width).astype(jnp.float32) for part in parts]
                squares = sum(jnp.sum(part * part, axis=1, keepdims=True) for part in raw)
                scale = lax.rsqrt(squares / DE + EPS)
                for index, part in enumerate(raw):
                    place = slice(index * width, (index + 1) * width)
                    normed[:, place] = (part * scale * gain_ref[:, place]).astype(jnp.bfloat16)

        @pl.when(step == 0)
        def _():
            for copy in copies:
                copy.wait()

        @pl.when(wanted)
        def _():
            states = normed[...]
            for out, weight in zip(outs, ordered):
                product = jnp.dot(states, weight[...], preferred_element_type=jnp.float32)
                out[...] = product.astype(jnp.bfloat16).reshape(out.shape)

    out = jax.ShapeDtypeStruct((total, tokens, columns), jnp.bfloat16)
    out_spec = pl.BlockSpec((group, tokens, columns), lambda i, marks: (jnp.maximum(marks[pieces + groups + first + i], first), 0, 0))
    arrays = [piece for parts in rounds for piece in parts]
    operands = (marks, gain, *arrays, key_weight, value_weight, *held)
    return pl.pallas_call(
        kernel,
        out_shape=(out, out),
        grid_spec=pltpu.PrefetchScalarGridSpec(
            num_scalar_prefetch=1,
            grid=(len(rounds) * each,),
            in_specs=[pl.BlockSpec((1, DE), lambda i, _: (0, 0))]
            + [pl.BlockSpec(memory_space=pltpu.VMEM)] * len(arrays)
            + [pl.BlockSpec(memory_space=pl.ANY)] * (2 + len(held)),
            out_specs=(out_spec, out_spec),
            scratch_shapes=[pltpu.VMEM((rows, DE), jnp.bfloat16)]
            + [pltpu.VMEM((DE, columns), jnp.bfloat16)] * 2
            + [pltpu.SemaphoreType.DMA((2 * pieces,))],
        ),
        input_output_aliases={len(operands) - len(held) + i: i for i in range(len(held))},
        compiler_params=pltpu.CompilerParams(vmem_limit_bytes=20 * MIB),
        cost_estimate=LITTLE,
        name="project",
    )(*operands)


SAME_COLUMNS = (((1,), (1,)), ((), ()))
SAME_ROWS = (((0,), (0,)), ((), ()))


def attend_kernel(slots, counts, query_ref, *refs):
    *entries, out_ref = refs
    keys, values = entries[: len(entries) // 2], entries[len(entries) // 2 :]
    together = len(keys) // KMAX
    wide = 2 * HEAD_DIM
    factor = math.log2(math.e) / math.sqrt(HEAD_DIM)
    count = [counts[pl.program_id(0) * together + g] for g in range(together)]
    work = [(g, start) for g in range(together) for start in range(0, query_ref.shape[1], wide)]

    def scored(g, start):
        query = query_ref[g * STRETCH : (g + 1) * STRETCH, start : start + wide]
        left, right = query[:, :HEAD_DIM], query[:, HEAD_DIM:]
        zero = jnp.zeros_like(left)
        both = jnp.concatenate([jnp.concatenate([left, zero], 1), jnp.concatenate([zero, right], 1)], 0)
        one, two = [
            lax.dot_general(
                keys[g * KMAX + k][0, :, start : start + wide], both, SAME_COLUMNS, preferred_element_type=jnp.float32
            )
            for k in range(KMAX)
        ]
        return one, jnp.where(count[g] == 2, two, -1e30)

    def weighed(one, two):
        top = jnp.maximum(one, two).max(0, keepdims=True)
        one, two = jnp.exp2((one - top) * factor), jnp.exp2((two - top) * factor)
        share = 1.0 / (one + two).sum(0, keepdims=True)
        return (one * share).astype(jnp.bfloat16), (two * share).astype(jnp.bfloat16)

    def mix(g, start, weights):
        rows = jnp.concatenate([values[g * KMAX + k][0, :, start : start + wide] for k in range(KMAX)], 0)
        mixed = lax.dot_general(jnp.concatenate(weights, 0), rows, SAME_ROWS, preferred_element_type=jnp.float32)
        mixed = jnp.where(count[g] > 0, mixed, 0.0).astype(jnp.bfloat16)
        rows = slice(g * STRETCH, (g + 1) * STRETCH)
        out_ref[rows, start : start + HEAD_DIM] = mixed[:STRETCH, :HEAD_DIM]
        out_ref[rows, start + HEAD_DIM : start + wide] = mixed[STRETCH:, HEAD_DIM:]

    scores = [scored(*piece) for piece in work]
    weights = [weighed(*pair) for pair in scores]
    for piece, pair in zip(work, weights):
        mix(*piece, pair)


def attend(slots, counts, queries, keys, values, together=3):
    stretches = counts.shape[0]
    columns = queries.shape[1]

    def entry(i):
        return pl.BlockSpec((1, NLEN, columns), lambda step, slots, _: (slots[step * together * KMAX + i], 0, 0))

    query_spec = pl.BlockSpec((together * STRETCH, columns), lambda i, *_: (i, 0))
    entries = [entry(i) for i in range(together * KMAX)]
    return pl.pallas_call(
        attend_kernel,
        out_shape=jax.ShapeDtypeStruct(queries.shape, jnp.bfloat16),
        grid_spec=pltpu.PrefetchScalarGridSpec(
            num_scalar_prefetch=2,
            grid=(stretches // together,),
            in_specs=[query_spec] + entries * 2,
            out_specs=query_spec,
        ),
        compiler_params=pltpu.CompilerParams(vmem_limit_bytes=16 * MIB),
        cost_estimate=LITTLE,
        name="attend",
    )(slots, counts, queries, *[keys] * len(entries), *[values] * len(entries))


def plan_kernel(place, table, plan_ref, far_ref, need_ref, lists_ref, picks_ref, slots_ref):
    f32 = jnp.float32
    groups = 2 * CHIPS
    me = place[0]
    each = table.shape[0] // groups
    lane = lax.broadcasted_iota(jnp.int32, (1, LANES), 1)

    bases = [jnp.bitwise_xor(me, group) * each for group in range(groups)]
    need = []
    for group in range(groups):
        wanted = [bases[group] + j for j in range(each - KMAX)]
        if group % CHIPS > 0:
            wanted += [bases[group - 1] + each - KMAX + k for k in range(KMAX)]
        hit = jnp.zeros((1, LANES), f32)
        for index in wanted:
            hit = jnp.where(lane == table[index], 1.0, hit)
        need.append(hit)
        need_ref[group : group + 1, :] = hit
    for part in range(2):
        for chip in range(CHIPS):
            come = (chip - (lane >> 4)) & (CHIPS - 1)
            reach = jnp.zeros((1, LANES), f32)
            for hops in range(1, CHIPS):
                there = need[part * CHIPS + (chip + hops) % CHIPS] > 0
                reach = jnp.where(there & (come + hops < CHIPS), float(hops), reach)
            row = part * CHIPS + chip
            far_ref[row : row + 1, :] = reach

    row = lax.broadcasted_iota(jnp.int32, (groups, LANES), 0)
    entry = lax.broadcasted_iota(jnp.int32, (groups, LANES), 1)
    chip, owner, slot = row & (CHIPS - 1), entry >> 4, entry & (ENTRIES_EACH - 1)
    loc = jnp.where(owner == chip, slot, -1).astype(f32)
    sent = jnp.where(owner == chip, 1.0, 0.0)
    from_behind = owner == ((chip + CHIPS - 1) & (CHIPS - 1))
    halves = [from_behind & (slot < HALF), from_behind & (slot >= HALF)]
    flights = [jnp.where(half, slot + ENTRIES_EACH, -1).astype(f32) for half in halves]
    far, needed = far_ref[...], need_ref[...]
    swept = jnp.zeros((groups, LANES), f32)
    slot_of = jnp.zeros((groups, LANES), f32)
    lists = jnp.full((groups, LANES), -1.0, f32)
    picks = jnp.full((groups, LANES), -1.0, f32)
    one, two = lax.broadcasted_iota(jnp.int32, (LANES, LANES), 0), lax.broadcasted_iota(jnp.int32, (LANES, LANES), 1)
    earlier = jnp.where(one < two, 1.0, 0.0).astype(jnp.bfloat16)
    to, source = lax.broadcasted_iota(jnp.int32, (groups, groups), 0), lax.broadcasted_iota(jnp.int32, (groups, groups), 1)
    behind = jnp.where(to & (CHIPS - 1) == 0, to + CHIPS - 1, to - 1)
    step = jnp.where(source == behind, 1.0, 0.0).astype(jnp.bfloat16)

    def ranked(mask):
        return jnp.dot(mask.astype(jnp.bfloat16), earlier, preferred_element_type=f32)

    def listed(into, taken, rank, number, cap):
        for b in range(cap):
            pick = jnp.max(jnp.where((taken > 0) & (rank == b), loc, -1.0), axis=1, keepdims=True)
            into = jnp.where(entry == number * CAP + b, pick, into)
        return into

    for number in range(SWEEPS):
        loc = jnp.maximum(loc, flights[number])
        if number == ROUNDS:
            loc = jnp.maximum(loc, flights[number + 1])
        ready = jnp.where((needed > 0) & (loc >= 0) & (swept == 0), 1.0, 0.0)
        rank = ranked(ready)
        taken = jnp.where((ready > 0) & (rank < SWEPT[number]), 1.0, 0.0)
        swept = swept + taken
        slot_of = slot_of + taken * (rank + number * CAP)
        picks = listed(picks, taken, rank, number, SWEPT[number])
        if number < ROUNDS:
            ready = jnp.where((far > 0) & (loc >= 0) & (sent == 0), 1.0, 0.0)
            rank = jnp.zeros((groups, LANES), f32)
            above = jnp.zeros((groups, 1), f32)
            for hops in range(CHIPS - 1, 0, -1):
                level = jnp.where(far == hops, ready, 0.0)
                rank = jnp.where(far == hops, ranked(level) + above, rank)
                above = above + jnp.sum(level, axis=1, keepdims=True)
            taken = jnp.where((ready > 0) & (rank < CAP), 1.0, 0.0)
            sent = sent + taken
            lists = listed(lists, taken, rank, number, CAP)
            came = jnp.dot(step, (taken * (rank + 1)).astype(jnp.bfloat16), preferred_element_type=f32)
            flights.append(jnp.where(came > 0, came + float(2 * ENTRIES_EACH + number * CAP - 1), -1.0))
    lists_ref[...] = lists
    picks_ref[...] = picks
    slots_ref[...] = slot_of
    missing = jnp.sum(jnp.where((far > 0) & (sent == 0), 1.0, 0.0)) + jnp.sum(
        jnp.where((needed > 0) & (swept == 0), 1.0, 0.0)
    )
    plan_ref[...] = jnp.zeros(plan_ref.shape, jnp.int32)
    for line, rows in enumerate((lists_ref, picks_ref, slots_ref)):
        plan_ref[line : line + 1, :] = rows[pl.ds(me, 1), :].astype(jnp.int32)
    plan_ref[3:4, :] = jnp.full((1, LANES), missing, f32).astype(jnp.int32)


def make_plan(place, table):
    return pl.pallas_call(
        plan_kernel,
        out_shape=jax.ShapeDtypeStruct((8, LANES), jnp.int32),
        in_specs=[pl.BlockSpec(memory_space=pltpu.SMEM)] * 2,
        out_specs=pl.BlockSpec(memory_space=pltpu.VMEM),
        scratch_shapes=[pltpu.VMEM((2 * CHIPS, LANES), jnp.float32)] * 5,
        name="plan",
    )(place, table)


def pack(plan, number, pool):
    lines, caps = ((0, 1), (CAP, CAP)) if number < ROUNDS else ((1,), SWEPT[-1:])
    starts = [0]
    for array in pool:
        starts.append(starts[-1] + array.shape[0])

    def kernel(plan_ref, *refs):
        sources, outs = refs[: len(pool)], refs[len(pool) :]
        for line, out in zip(lines, outs):
            for b in range(out.shape[0]):
                at = plan_ref[line * LANES + number * CAP + b]
                for source, low, high in zip(sources, starts, starts[1:]):

                    @pl.when((at >= low) & (at < high))
                    def _(source=source, low=low, out=out, b=b, at=at):
                        out[b] = source[at - low]

    in_vmem = pl.BlockSpec(memory_space=pltpu.VMEM)
    return pl.pallas_call(
        kernel,
        out_shape=tuple(jax.ShapeDtypeStruct((cap,) + pool[0].shape[1:], pool[0].dtype) for cap in caps),
        grid_spec=pltpu.PrefetchScalarGridSpec(
            num_scalar_prefetch=1, in_specs=[in_vmem] * len(pool), out_specs=(in_vmem,) * len(lines)
        ),
        compiler_params=pltpu.CompilerParams(vmem_limit_bytes=12 * MIB),
        cost_estimate=LITTLE,
        name="pack",
    )(plan, *pool)


def previous_rows(nbr_owner, nbr_slot, nbr_count):
    rows = jnp.concatenate([nbr_owner, nbr_slot, nbr_count[:, None]], axis=1)
    rows = jnp.concatenate([shifted(rows[-1:], "seq", 1), rows[:-1]], axis=0)
    return rows[:, :KMAX], rows[:, KMAX : 2 * KMAX], rows[:, 2 * KMAX]


def fetch_by_request(store, owners, slots):
    owners_axis = lax.axis_size("seq")
    stretches = owners.shape[0]
    depth = min(stretches, max(2, 2 * stretches * KMAX // owners_axis) + 1)
    owners, slots = owners.reshape(-1), slots.reshape(-1)
    order = jnp.arange(owners.shape[0], dtype=jnp.int32)
    before = (owners[:, None] == owners[None, :]) & (order[None, :] < order[:, None])
    target = owners * depth + jnp.sum(before.astype(jnp.int32), axis=1)
    hits = target[:, None] == jnp.arange(owners_axis * depth, dtype=jnp.int32)[None, :]
    table = jnp.sum(jnp.where(hits, slots[:, None], 0), axis=0).reshape(owners_axis, depth)
    asked = lax.all_to_all(table, "seq", split_axis=0, concat_axis=0, tiled=True)
    arrived = lax.all_to_all(store[asked], "seq", split_axis=0, concat_axis=0, tiled=True)
    fetched = arrived.reshape(owners_axis * depth, NLEN, store.shape[2])[target]
    return lax.all_gather(fetched, FEATURES, axis=2, tiled=True)


def onward(value):
    size = lax.axis_size("seq")
    return lax.ppermute(value, "seq", [(chip, (chip + 1) % size) for chip in range(size)])


def four_pieces(value):
    across = swapped(value, "mp")
    return [value, swapped(value, "rep"), across, swapped(across, "rep")]


def fetch_all(store, owners, slots):
    seq = lax.axis_index("seq")
    everything = [store]
    for distance in range(1, lax.axis_size("seq")):
        for steps in (distance, -distance):
            everything.append(shifted(store, "seq", steps))
    ahead = owners - seq
    place = jnp.where(ahead == 0, 0, jnp.where(ahead < 0, -2 * ahead - 1, 2 * ahead))
    pool = jnp.concatenate(everything, axis=0)
    return pool[(place * store.shape[0] + slots).reshape(-1)]


def places_of_pieces():
    block = 2 * lax.axis_index("mp") + lax.axis_index("rep")
    return jnp.stack([block ^ i for i in range(4)]).astype(jnp.int32)


def every_group(places, groups):
    return jnp.concatenate([places, jnp.ones((groups,), jnp.int32), jnp.arange(groups, dtype=jnp.int32)])


def exchanged_table(codes):
    own_part = [codes]
    for offset in range(1, CHIPS):
        own_part.append(lax.ppermute(codes, "seq", [(chip, chip ^ offset) for chip in range(CHIPS)]))
    own_part = jnp.stack(own_part)
    return jnp.concatenate([own_part, swapped(own_part, "parts")], axis=0)


def streamed(queries, key_weight, value_weight, enc_gain, store, nbr_owner, nbr_slot, nbr_count):
    stretches = nbr_owner.shape[0]
    total = stretches * KMAX
    seq = lax.axis_index("seq")
    me = lax.axis_index("parts") * CHIPS + seq
    kept = jnp.arange(KMAX, dtype=jnp.int32)[None, :] < nbr_count[:, None]
    codes = jnp.where(kept, nbr_owner * ENTRIES_EACH + nbr_slot, -1).reshape(-1)
    first, second, codes, enc_gain = lax.optimization_barrier((store[:HALF], store[HALF:], codes, enc_gain))
    table = exchanged_table(codes)
    flights = [onward(first), onward(second)]
    gain = jnp.concatenate(four_pieces(enc_gain[None]), axis=1)
    plan = make_plan(me.reshape(1).astype(jnp.int32), table.reshape(-1)).reshape(-1)
    missing = plan[3 * LANES]

    offset = jnp.where(seq > 0, (seq ^ (seq - 1)) & 3, 0)
    behind = table[offset]
    asked = jnp.concatenate([jnp.where(seq > 0, behind[total - KMAX :], -1), codes[: total - KMAX]])
    asked = asked.reshape(stretches, KMAX)
    counts = jnp.sum((asked >= 0).astype(jnp.int32), axis=1)
    first = jnp.maximum(asked[:, 0], 0)
    asked = jnp.stack([first, jnp.where(asked[:, 1] >= 0, asked[:, 1], first)], axis=1).reshape(-1)

    places = places_of_pieces()
    room = sum(SWEPT)
    wanted = plan[LANES : LANES + room].reshape(room // GROUP, GROUP)[:, 0] >= 0
    group = jnp.arange(room // GROUP, dtype=jnp.int32)
    latest = jnp.max(jnp.where((group[None, :] <= group[:, None]) & wanted[None, :], group[None, :], 0), axis=1)
    marks = jnp.concatenate([places, wanted.astype(jnp.int32), latest])
    slots = plan[2 * LANES : 3 * LANES][asked]

    pieces, held = [], ()
    for number in range(SWEEPS):
        *ways, mine = pack(plan, number, [store] + flights[: number + 1 if number < ROUNDS else None])
        flights += [onward(way) for way in ways]
        pieces.append([mine, swapped(mine, "rep"), swapped(mine, "mp")])
        if number > 0:
            pieces[number - 1].append(swapped(pieces[number - 1][2], "rep"))
        if number == SWEEPS - 2:
            ripe, pieces[number - 1][2] = lax.optimization_barrier((pieces[:2], pieces[number - 1][2]))
            held = project(marks, gain, ripe, key_weight, value_weight, GROUP, room)
        if number + 1 < SWEEPS:
            across = [parts[2] for parts in pieces[:number]] if number + 2 < SWEEPS else []
            came = slice(number + 1, number + 2 if number + 2 < SWEEPS else None)
            flights[came], across, pieces[number][1], gain, slots, marks, held = lax.optimization_barrier(
                (flights[came], across, pieces[number][1], gain, slots, marks, held)
            )
            for parts, arrived in zip(pieces, across):
                parts[2] = arrived
    ripe, _ = lax.optimization_barrier((pieces[2:-1], mine))
    held = project(marks, gain, ripe, key_weight, value_weight, GROUP, room, 2 * CAP // GROUP, held)
    late, held = lax.optimization_barrier((pieces[-1], held))
    late = [*late, swapped(late[2], "rep")]
    done = (SWEEPS - 1) * CAP // GROUP
    keys, values = project(marks, gain, [late], key_weight, value_weight, GROUP, room, done, held)

    result = attend(slots, counts, queries, keys, values)

    def whole(state):
        mine = fetch_all(store, asked >> 4, asked & (ENTRIES_EACH - 1))
        marks = every_group(places, total // 4)
        keys, values = project(marks, gain, [four_pieces(mine)], key_weight, value_weight, 4, total)
        order = jnp.arange(total, dtype=jnp.int32)
        return jnp.zeros_like(state[0]), attend(order, counts, queries, keys, values)

    return lax.while_loop(lambda state: state[0] > 0, whole, (missing, result))[1]


def requested(queries, key_weight, value_weight, enc_gain, store, nbr_owner, nbr_slot, nbr_count):
    gain = lax.all_gather(enc_gain, FEATURES, axis=0, tiled=True)[None]
    owners, slots, counts = previous_rows(nbr_owner, nbr_slot, nbr_count)
    total = owners.size
    pieces = [fetch_by_request(store, owners, slots)]
    marks = every_group(jnp.zeros((1,), jnp.int32), total // 4)
    keys, values = project(marks, gain, [pieces], key_weight, value_weight, 4, total)
    return attend(jnp.arange(total, dtype=jnp.int32), counts, queries, keys, values)


def solution(mesh):
    in_specs = (
        P(SEQ_SPEC, FEATURES),
        P(None, FEATURES),
        P(None, FEATURES),
        P(FEATURES),
        P(SEQ_SPEC, None, FEATURES),
        P(SEQ_SPEC, None),
        P(SEQ_SPEC, None),
        P(SEQ_SPEC),
    )
    out_specs = P(SEQ_SPEC, FEATURES)
    shape = dict(mesh.shape)
    small = shape == {"parts": 2, "seq": CHIPS, "mp": 2, "rep": 2}
    body = streamed if small else requested
    return jax.shard_map(body, mesh=mesh, in_specs=in_specs, out_specs=out_specs, check_vma=False)
```

```python
import math

import jax
import jax.numpy as jnp
from jax import lax
from jax.experimental import pallas as pl
from jax.experimental.pallas import tpu as pltpu
from jax.sharding import PartitionSpec as P

HEAD_DIM = 128
DE = 1024
NLEN = 128
STRETCH = 64
KMAX = 2
EPS = 1e-06

SEQ_SPEC = ("parts", "seq")
FEATURES = ("mp", "rep")
VMEM_LIMIT = 28 * 1024 * 1024

CHIPS = 4
ENTRIES_EACH = 16
HALF = 8
ROUNDS = 5
CAP = 4
GROUP = 2
SWEEPS = ROUNDS + 1
SWEPT = (CAP,) * ROUNDS + (2 * CAP,)
LANES = 128

LITTLE = pl.CostEstimate(flops=1, bytes_accessed=1, transcendentals=0)


def shifted(value, axis, steps):
    count = lax.axis_size(axis)
    first, last = max(0, -steps), min(count, count - steps)
    return lax.ppermute(value, axis, [(source, source + steps) for source in range(first, last)])


def swapped(value, axis):
    return lax.ppermute(value, axis, [(0, 1), (1, 0)])


def project(marks, gain, rounds, key_weight, value_weight, group, total, first=0, held=()):
    pieces = len(rounds[0])
    count, tokens, width = rounds[0][0].shape
    columns = key_weight.shape[1]
    each = count // group
    rows = group * tokens
    groups = total // group

    def kernel(marks_ref, gain_ref, *refs):
        arrays, weights = refs[: len(rounds) * pieces], refs[len(rounds) * pieces : len(rounds) * pieces + 2]
        *outs, normed, key_rows, value_rows, sems = refs[-6:]
        step = pl.program_id(0)
        ordered = (key_rows, value_rows)
        copies = [
            pltpu.make_async_copy(
                weight.at[pl.ds(pl.multiple_of(marks_ref[piece] * width, width), width)],
                rows_ref.at[pl.ds(piece * width, width)],
                sems.at[which * pieces + piece],
            )
            for which, (weight, rows_ref) in enumerate(zip(weights, ordered))
            for piece in range(pieces)
        ]

        @pl.when(step == 0)
        def _():
            for copy in copies:
                copy.start()

        wanted = marks_ref[pieces + first + step] > 0
        for number in range(len(rounds)):
            parts = arrays[number * pieces : (number + 1) * pieces]

            @pl.when(wanted & (step >= number * each) & (step < (number + 1) * each))
            def _(number=number, parts=parts):
                at = pl.ds((step - number * each) * group, group)
                raw = [part[at].reshape(rows, width).astype(jnp.float32) for part in parts]
                squares = sum(jnp.sum(part * part, axis=1, keepdims=True) for part in raw)
                scale = lax.rsqrt(squares / DE + EPS)
                for index, part in enumerate(raw):
                    place = slice(index * width, (index + 1) * width)
                    normed[:, place] = (part * scale * gain_ref[:, place]).astype(jnp.bfloat16)

        @pl.when(step == 0)
        def _():
            for copy in copies:
                copy.wait()

        @pl.when(wanted)
        def _():
            states = normed[...]
            for out, weight in zip(outs, ordered):
                product = jnp.dot(states, weight[...], preferred_element_type=jnp.float32)
                out[...] = product.astype(jnp.bfloat16).reshape(out.shape)

    out = jax.ShapeDtypeStruct((total, tokens, columns), jnp.bfloat16)
    out_spec = pl.BlockSpec((group, tokens, columns), lambda i, marks: (jnp.maximum(marks[pieces + groups + first + i], first), 0, 0))
    arrays = [piece for parts in rounds for piece in parts]
    operands = (marks, gain, *arrays, key_weight, value_weight, *held)
    return pl.pallas_call(
        kernel,
        out_shape=(out, out),
        grid_spec=pltpu.PrefetchScalarGridSpec(
            num_scalar_prefetch=1,
            grid=(len(rounds) * each,),
            in_specs=[pl.BlockSpec((1, DE), lambda i, _: (0, 0))]
            + [pl.BlockSpec(memory_space=pltpu.VMEM)] * len(arrays)
            + [pl.BlockSpec(memory_space=pl.ANY)] * (2 + len(held)),
            out_specs=(out_spec, out_spec),
            scratch_shapes=[pltpu.VMEM((rows, DE), jnp.bfloat16)]
            + [pltpu.VMEM((DE, columns), jnp.bfloat16)] * 2
            + [pltpu.SemaphoreType.DMA((2 * pieces,))],
        ),
        input_output_aliases={len(operands) - len(held) + i: i for i in range(len(held))},
        compiler_params=pltpu.CompilerParams(vmem_limit_bytes=47 * 1024 * 1024),
        cost_estimate=LITTLE,
        name="project",
    )(*operands)


SAME_COLUMNS = (((1,), (1,)), ((), ()))
SAME_ROWS = (((0,), (0,)), ((), ()))


def attend_kernel(slots, counts, query_ref, *refs):
    *entries, out_ref = refs
    keys, values = entries[: len(entries) // 2], entries[len(entries) // 2 :]
    together = len(keys) // KMAX
    wide = 2 * HEAD_DIM
    factor = math.log2(math.e) / math.sqrt(HEAD_DIM)
    count = [counts[pl.program_id(0) * together + g] for g in range(together)]
    work = [(g, start) for g in range(together) for start in range(0, query_ref.shape[1], wide)]

    def scored(g, start):
        query = query_ref[g * STRETCH : (g + 1) * STRETCH, start : start + wide]
        left, right = query[:, :HEAD_DIM], query[:, HEAD_DIM:]
        zero = jnp.zeros_like(left)
        both = jnp.concatenate([jnp.concatenate([left, zero], 1), jnp.concatenate([zero, right], 1)], 0)
        one, two = [
            lax.dot_general(
                keys[g * KMAX + k][0, :, start : start + wide], both, SAME_COLUMNS, preferred_element_type=jnp.float32
            )
            for k in range(KMAX)
        ]
        return one, jnp.where(count[g] == 2, two, -1e30)

    def weighed(one, two):
        top = jnp.maximum(one, two).max(0, keepdims=True)
        one, two = jnp.exp2((one - top) * factor), jnp.exp2((two - top) * factor)
        share = 1.0 / (one + two).sum(0, keepdims=True)
        return (one * share).astype(jnp.bfloat16), (two * share).astype(jnp.bfloat16)

    def mix(g, start, weights):
        rows = jnp.concatenate([values[g * KMAX + k][0, :, start : start + wide] for k in range(KMAX)], 0)
        mixed = lax.dot_general(jnp.concatenate(weights, 0), rows, SAME_ROWS, preferred_element_type=jnp.float32)
        mixed = jnp.where(count[g] > 0, mixed, 0.0).astype(jnp.bfloat16)
        rows = slice(g * STRETCH, (g + 1) * STRETCH)
        out_ref[rows, start : start + HEAD_DIM] = mixed[:STRETCH, :HEAD_DIM]
        out_ref[rows, start + HEAD_DIM : start + wide] = mixed[STRETCH:, HEAD_DIM:]

    scores = [scored(*piece) for piece in work]
    weights = [weighed(*pair) for pair in scores]
    for piece, pair in zip(work, weights):
        mix(*piece, pair)


def attend(slots, counts, queries, keys, values, together=3):
    stretches = counts.shape[0]
    columns = queries.shape[1]

    def entry(i):
        return pl.BlockSpec((1, NLEN, columns), lambda step, slots, _: (slots[step * together * KMAX + i], 0, 0))

    query_spec = pl.BlockSpec((together * STRETCH, columns), lambda i, *_: (i, 0))
    entries = [entry(i) for i in range(together * KMAX)]
    return pl.pallas_call(
        attend_kernel,
        out_shape=jax.ShapeDtypeStruct(queries.shape, jnp.bfloat16),
        grid_spec=pltpu.PrefetchScalarGridSpec(
            num_scalar_prefetch=2,
            grid=(stretches // together,),
            in_specs=[query_spec] + entries * 2,
            out_specs=query_spec,
        ),
        compiler_params=pltpu.CompilerParams(vmem_limit_bytes=60 * 1024 * 1024),
        cost_estimate=LITTLE,
        name="attend",
    )(slots, counts, queries, *[keys] * len(entries), *[values] * len(entries))


def plan_kernel(place, table, plan_ref, far_ref, need_ref, lists_ref, picks_ref, slots_ref):
    f32 = jnp.float32
    groups = 2 * CHIPS
    me = place[0]
    each = table.shape[0] // groups
    lane = lax.broadcasted_iota(jnp.int32, (1, LANES), 1)

    bases = [jnp.bitwise_xor(me, group) * each for group in range(groups)]
    need = []
    for group in range(groups):
        wanted = [bases[group] + j for j in range(each - KMAX)]
        if group % CHIPS > 0:
            wanted += [bases[group - 1] + each - KMAX + k for k in range(KMAX)]
        hit = jnp.zeros((1, LANES), f32)
        for index in wanted:
            hit = jnp.where(lane == table[index], 1.0, hit)
        need.append(hit)
        need_ref[group : group + 1, :] = hit
    for part in range(2):
        for chip in range(CHIPS):
            come = (chip - (lane >> 4)) & (CHIPS - 1)
            reach = jnp.zeros((1, LANES), f32)
            for hops in range(1, CHIPS):
                there = need[part * CHIPS + (chip + hops) % CHIPS] > 0
                reach = jnp.where(there & (come + hops < CHIPS), float(hops), reach)
            row = part * CHIPS + chip
            far_ref[row : row + 1, :] = reach

    row = lax.broadcasted_iota(jnp.int32, (groups, LANES), 0)
    entry = lax.broadcasted_iota(jnp.int32, (groups, LANES), 1)
    chip, owner, slot = row & (CHIPS - 1), entry >> 4, entry & (ENTRIES_EACH - 1)
    loc = jnp.where(owner == chip, slot, -1).astype(f32)
    sent = jnp.where(owner == chip, 1.0, 0.0)
    from_behind = owner == ((chip + CHIPS - 1) & (CHIPS - 1))
    halves = [from_behind & (slot < HALF), from_behind & (slot >= HALF)]
    flights = [jnp.where(half, slot + ENTRIES_EACH, -1).astype(f32) for half in halves]
    far, needed = far_ref[...], need_ref[...]
    swept = jnp.zeros((groups, LANES), f32)
    slot_of = jnp.zeros((groups, LANES), f32)
    lists = jnp.full((groups, LANES), -1.0, f32)
    picks = jnp.full((groups, LANES), -1.0, f32)
    one, two = lax.broadcasted_iota(jnp.int32, (LANES, LANES), 0), lax.broadcasted_iota(jnp.int32, (LANES, LANES), 1)
    earlier = jnp.where(one < two, 1.0, 0.0).astype(jnp.bfloat16)
    to, source = lax.broadcasted_iota(jnp.int32, (groups, groups), 0), lax.broadcasted_iota(jnp.int32, (groups, groups), 1)
    behind = jnp.where(to & (CHIPS - 1) == 0, to + CHIPS - 1, to - 1)
    step = jnp.where(source == behind, 1.0, 0.0).astype(jnp.bfloat16)

    def ranked(mask):
        return jnp.dot(mask.astype(jnp.bfloat16), earlier, preferred_element_type=f32)

    def listed(into, taken, rank, number, cap):
        for b in range(cap):
            pick = jnp.max(jnp.where((taken > 0) & (rank == b), loc, -1.0), axis=1, keepdims=True)
            into = jnp.where(entry == number * CAP + b, pick, into)
        return into

    for number in range(SWEEPS):
        loc = jnp.maximum(loc, flights[number])
        if number == ROUNDS:
            loc = jnp.maximum(loc, flights[number + 1])
        ready = jnp.where((needed > 0) & (loc >= 0) & (swept == 0), 1.0, 0.0)
        rank = ranked(ready)
        taken = jnp.where((ready > 0) & (rank < SWEPT[number]), 1.0, 0.0)
        swept = swept + taken
        slot_of = slot_of + taken * (rank + number * CAP)
        picks = listed(picks, taken, rank, number, SWEPT[number])
        if number < ROUNDS:
            ready = jnp.where((far > 0) & (loc >= 0) & (sent == 0), 1.0, 0.0)
            rank = jnp.zeros((groups, LANES), f32)
            above = jnp.zeros((groups, 1), f32)
            for hops in range(CHIPS - 1, 0, -1):
                level = jnp.where(far == hops, ready, 0.0)
                rank = jnp.where(far == hops, ranked(level) + above, rank)
                above = above + jnp.sum(level, axis=1, keepdims=True)
            taken = jnp.where((ready > 0) & (rank < CAP), 1.0, 0.0)
            sent = sent + taken
            lists = listed(lists, taken, rank, number, CAP)
            came = jnp.dot(step, (taken * (rank + 1)).astype(jnp.bfloat16), preferred_element_type=f32)
            flights.append(jnp.where(came > 0, came + float(2 * ENTRIES_EACH + number * CAP - 1), -1.0))
    lists_ref[...] = lists
    picks_ref[...] = picks
    slots_ref[...] = slot_of
    missing = jnp.sum(jnp.where((far > 0) & (sent == 0), 1.0, 0.0)) + jnp.sum(
        jnp.where((needed > 0) & (swept == 0), 1.0, 0.0)
    )
    plan_ref[...] = jnp.zeros(plan_ref.shape, jnp.int32)
    for line, rows in enumerate((lists_ref, picks_ref, slots_ref)):
        plan_ref[line : line + 1, :] = rows[pl.ds(me, 1), :].astype(jnp.int32)
    plan_ref[3:4, :] = jnp.full((1, LANES), missing, f32).astype(jnp.int32)


def make_plan(place, table):
    return pl.pallas_call(
        plan_kernel,
        out_shape=jax.ShapeDtypeStruct((8, LANES), jnp.int32),
        in_specs=[pl.BlockSpec(memory_space=pltpu.SMEM)] * 2,
        out_specs=pl.BlockSpec(memory_space=pltpu.VMEM),
        scratch_shapes=[pltpu.VMEM((2 * CHIPS, LANES), jnp.float32)] * 5,
        name="plan",
    )(place, table)


def pack(plan, number, pool):
    lines, caps = ((0, 1), (CAP, CAP)) if number < ROUNDS else ((1,), SWEPT[-1:])
    starts = [0]
    for array in pool:
        starts.append(starts[-1] + array.shape[0])

    def kernel(plan_ref, *refs):
        sources, outs = refs[: len(pool)], refs[len(pool) :]
        for line, out in zip(lines, outs):
            for b in range(out.shape[0]):
                at = plan_ref[line * LANES + number * CAP + b]
                for source, low, high in zip(sources, starts, starts[1:]):

                    @pl.when((at >= low) & (at < high))
                    def _(source=source, low=low, out=out, b=b, at=at):
                        out[b] = source[at - low]

    in_vmem = pl.BlockSpec(memory_space=pltpu.VMEM)
    return pl.pallas_call(
        kernel,
        out_shape=tuple(jax.ShapeDtypeStruct((cap,) + pool[0].shape[1:], pool[0].dtype) for cap in caps),
        grid_spec=pltpu.PrefetchScalarGridSpec(
            num_scalar_prefetch=1, in_specs=[in_vmem] * len(pool), out_specs=(in_vmem,) * len(lines)
        ),
        compiler_params=pltpu.CompilerParams(vmem_limit_bytes=VMEM_LIMIT),
        cost_estimate=LITTLE,
        name="pack",
    )(plan, *pool)


def previous_rows(nbr_owner, nbr_slot, nbr_count):
    rows = jnp.concatenate([nbr_owner, nbr_slot, nbr_count[:, None]], axis=1)
    rows = jnp.concatenate([shifted(rows[-1:], "seq", 1), rows[:-1]], axis=0)
    return rows[:, :KMAX], rows[:, KMAX : 2 * KMAX], rows[:, 2 * KMAX]


def fetch_by_request(store, owners, slots):
    owners_axis = lax.axis_size("seq")
    stretches = owners.shape[0]
    depth = min(stretches, max(2, 2 * stretches * KMAX // owners_axis) + 1)
    owners, slots = owners.reshape(-1), slots.reshape(-1)
    order = jnp.arange(owners.shape[0], dtype=jnp.int32)
    before = (owners[:, None] == owners[None, :]) & (order[None, :] < order[:, None])
    target = owners * depth + jnp.sum(before.astype(jnp.int32), axis=1)
    hits = target[:, None] == jnp.arange(owners_axis * depth, dtype=jnp.int32)[None, :]
    table = jnp.sum(jnp.where(hits, slots[:, None], 0), axis=0).reshape(owners_axis, depth)
    asked = lax.all_to_all(table, "seq", split_axis=0, concat_axis=0, tiled=True)
    arrived = lax.all_to_all(store[asked], "seq", split_axis=0, concat_axis=0, tiled=True)
    fetched = arrived.reshape(owners_axis * depth, NLEN, store.shape[2])[target]
    return lax.all_gather(fetched, FEATURES, axis=2, tiled=True)


def onward(value):
    size = lax.axis_size("seq")
    return lax.ppermute(value, "seq", [(chip, (chip + 1) % size) for chip in range(size)])


def four_pieces(value):
    across = swapped(value, "mp")
    return [value, swapped(value, "rep"), across, swapped(across, "rep")]


def fetch_all(store, owners, slots):
    seq = lax.axis_index("seq")
    everything = [store]
    for distance in range(1, lax.axis_size("seq")):
        for steps in (distance, -distance):
            everything.append(shifted(store, "seq", steps))
    ahead = owners - seq
    place = jnp.where(ahead == 0, 0, jnp.where(ahead < 0, -2 * ahead - 1, 2 * ahead))
    pool = jnp.concatenate(everything, axis=0)
    return pool[(place * store.shape[0] + slots).reshape(-1)]


def places_of_pieces():
    block = 2 * lax.axis_index("mp") + lax.axis_index("rep")
    return jnp.stack([block ^ i for i in range(4)]).astype(jnp.int32)


def every_group(places, groups):
    return jnp.concatenate([places, jnp.ones((groups,), jnp.int32), jnp.arange(groups, dtype=jnp.int32)])


def exchanged_table(codes):
    own_part = [codes]
    for offset in range(1, CHIPS):
        own_part.append(lax.ppermute(codes, "seq", [(chip, chip ^ offset) for chip in range(CHIPS)]))
    own_part = jnp.stack(own_part)
    return jnp.concatenate([own_part, swapped(own_part, "parts")], axis=0)


def streamed(queries, key_weight, value_weight, enc_gain, store, nbr_owner, nbr_slot, nbr_count):
    stretches = nbr_owner.shape[0]
    total = stretches * KMAX
    seq = lax.axis_index("seq")
    me = lax.axis_index("parts") * CHIPS + seq
    kept = jnp.arange(KMAX, dtype=jnp.int32)[None, :] < nbr_count[:, None]
    codes = jnp.where(kept, nbr_owner * ENTRIES_EACH + nbr_slot, -1).reshape(-1)
    first, second, codes, enc_gain = lax.optimization_barrier((store[:HALF], store[HALF:], codes, enc_gain))
    table = exchanged_table(codes)
    flights = [onward(first), onward(second)]
    gain = jnp.concatenate(four_pieces(enc_gain[None]), axis=1)
    plan = make_plan(me.reshape(1).astype(jnp.int32), table.reshape(-1)).reshape(-1)
    missing = plan[3 * LANES]

    offset = jnp.where(seq > 0, (seq ^ (seq - 1)) & 3, 0)
    behind = table[offset]
    asked = jnp.concatenate([jnp.where(seq > 0, behind[total - KMAX :], -1), codes[: total - KMAX]])
    asked = asked.reshape(stretches, KMAX)
    counts = jnp.sum((asked >= 0).astype(jnp.int32), axis=1)
    first = jnp.maximum(asked[:, 0], 0)
    asked = jnp.stack([first, jnp.where(asked[:, 1] >= 0, asked[:, 1], first)], axis=1).reshape(-1)

    places = places_of_pieces()
    room = sum(SWEPT)
    wanted = plan[LANES : LANES + room].reshape(room // GROUP, GROUP)[:, 0] >= 0
    group = jnp.arange(room // GROUP, dtype=jnp.int32)
    latest = jnp.max(jnp.where((group[None, :] <= group[:, None]) & wanted[None, :], group[None, :], 0), axis=1)
    marks = jnp.concatenate([places, wanted.astype(jnp.int32), latest])
    slots = plan[2 * LANES : 3 * LANES][asked]

    pieces, held = [], ()
    for number in range(SWEEPS):
        *ways, mine = pack(plan, number, [store] + flights[: number + 1 if number < ROUNDS else None])
        flights += [onward(way) for way in ways]
        pieces.append([mine, swapped(mine, "rep"), swapped(mine, "mp")])
        if number > 0:
            pieces[number - 1].append(swapped(pieces[number - 1][2], "rep"))
        if number == SWEEPS - 2:
            ripe, pieces[number - 1][2] = lax.optimization_barrier((pieces[:2], pieces[number - 1][2]))
            held = project(marks, gain, ripe, key_weight, value_weight, GROUP, room)
        if number + 1 < SWEEPS:
            across = [parts[2] for parts in pieces[:number]] if number + 2 < SWEEPS else []
            came = slice(number + 1, number + 2 if number + 2 < SWEEPS else None)
            flights[came], across, pieces[number][1], gain, slots, marks, held = lax.optimization_barrier(
                (flights[came], across, pieces[number][1], gain, slots, marks, held)
            )
            for parts, arrived in zip(pieces, across):
                parts[2] = arrived
    ripe, _ = lax.optimization_barrier((pieces[2:-1], mine))
    held = project(marks, gain, ripe, key_weight, value_weight, GROUP, room, 2 * CAP // GROUP, held)
    late, held = lax.optimization_barrier((pieces[-1], held))
    late = [*late, swapped(late[2], "rep")]
    done = (SWEEPS - 1) * CAP // GROUP
    keys, values = project(marks, gain, [late], key_weight, value_weight, GROUP, room, done, held)

    def whole(state):
        mine = fetch_all(store, asked >> 4, asked & (ENTRIES_EACH - 1))
        marks = every_group(places, room // 4)
        keys, values = project(marks, gain, [four_pieces(mine)], key_weight, value_weight, 4, room)
        return jnp.zeros_like(state[0]), jnp.arange(total, dtype=jnp.int32), keys, values

    state = lax.while_loop(lambda state: state[0] > 0, whole, (missing, slots, keys, values))
    return attend(state[1], counts, queries, *state[2:])


def requested(queries, key_weight, value_weight, enc_gain, store, nbr_owner, nbr_slot, nbr_count):
    gain = lax.all_gather(enc_gain, FEATURES, axis=0, tiled=True)[None]
    owners, slots, counts = previous_rows(nbr_owner, nbr_slot, nbr_count)
    total = owners.size
    pieces = [fetch_by_request(store, owners, slots)]
    marks = every_group(jnp.zeros((1,), jnp.int32), total // 4)
    keys, values = project(marks, gain, [pieces], key_weight, value_weight, 4, total)
    return attend(jnp.arange(total, dtype=jnp.int32), counts, queries, keys, values)


def solution(mesh):
    in_specs = (
        P(SEQ_SPEC, FEATURES),
        P(None, FEATURES),
        P(None, FEATURES),
        P(FEATURES),
        P(SEQ_SPEC, None, FEATURES),
        P(SEQ_SPEC, None),
        P(SEQ_SPEC, None),
        P(SEQ_SPEC),
    )
    out_specs = P(SEQ_SPEC, FEATURES)
    shape = dict(mesh.shape)
    small = shape == {"parts": 2, "seq": CHIPS, "mp": 2, "rep": 2}
    body = streamed if small else requested
    return jax.shard_map(body, mesh=mesh, in_specs=in_specs, out_specs=out_specs, check_vma=False)
```

```python
import math

import jax
import jax.numpy as jnp
from jax import lax
from jax.experimental import pallas as pl
from jax.experimental.pallas import tpu as pltpu
from jax.sharding import PartitionSpec as P

HEAD_DIM = 128
DE = 1024
NLEN = 128
STRETCH = 64
KMAX = 2
EPS = 1e-06

SEQ_SPEC = ("parts", "seq")
FEATURES = ("mp", "rep")
MIB = 1024 * 1024

CHIPS = 4
ENTRIES_EACH = 16
HALF = 8
ROUNDS = 5
CAP = 4
GROUP = 2
SWEEPS = ROUNDS + 1
SWEPT = (CAP,) * ROUNDS + (2 * CAP,)
LANES = 128

LITTLE = pl.CostEstimate(flops=1, bytes_accessed=1, transcendentals=0)


def shifted(value, axis, steps):
    count = lax.axis_size(axis)
    first, last = max(0, -steps), min(count, count - steps)
    return lax.ppermute(value, axis, [(source, source + steps) for source in range(first, last)])


def swapped(value, axis):
    return lax.ppermute(value, axis, [(0, 1), (1, 0)])


def project(marks, gain, rounds, key_weight, value_weight, group, total, first=0, held=()):
    pieces = len(rounds[0])
    count, tokens, width = rounds[0][0].shape
    columns = key_weight.shape[1]
    each = count // group
    rows = group * tokens
    groups = total // group

    def kernel(marks_ref, gain_ref, *refs):
        arrays, weights = refs[: len(rounds) * pieces], refs[len(rounds) * pieces : len(rounds) * pieces + 2]
        *outs, normed, key_rows, value_rows, sems = refs[-6:]
        step = pl.program_id(0)
        ordered = (key_rows, value_rows)
        copies = [
            pltpu.make_async_copy(
                weight.at[pl.ds(pl.multiple_of(marks_ref[piece] * width, width), width)],
                rows_ref.at[pl.ds(piece * width, width)],
                sems.at[which * pieces + piece],
            )
            for which, (weight, rows_ref) in enumerate(zip(weights, ordered))
            for piece in range(pieces)
        ]

        @pl.when(step == 0)
        def _():
            for copy in copies:
                copy.start()

        wanted = marks_ref[pieces + first + step] > 0
        for number in range(len(rounds)):
            parts = arrays[number * pieces : (number + 1) * pieces]

            @pl.when(wanted & (step >= number * each) & (step < (number + 1) * each))
            def _(number=number, parts=parts):
                at = pl.ds((step - number * each) * group, group)
                raw = [part[at].reshape(rows, width).astype(jnp.float32) for part in parts]
                squares = sum(jnp.sum(part * part, axis=1, keepdims=True) for part in raw)
                scale = lax.rsqrt(squares / DE + EPS)
                for index, part in enumerate(raw):
                    place = slice(index * width, (index + 1) * width)
                    normed[:, place] = (part * scale * gain_ref[:, place]).astype(jnp.bfloat16)

        @pl.when(step == 0)
        def _():
            for copy in copies:
                copy.wait()

        @pl.when(wanted)
        def _():
            states = normed[...]
            for out, weight in zip(outs, ordered):
                product = jnp.dot(states, weight[...], preferred_element_type=jnp.float32)
                out[...] = product.astype(jnp.bfloat16).reshape(out.shape)

    out = jax.ShapeDtypeStruct((total, tokens, columns), jnp.bfloat16)
    out_spec = pl.BlockSpec((group, tokens, columns), lambda i, marks: (jnp.maximum(marks[pieces + groups + first + i], first), 0, 0))
    arrays = [piece for parts in rounds for piece in parts]
    operands = (marks, gain, *arrays, key_weight, value_weight, *held)
    return pl.pallas_call(
        kernel,
        out_shape=(out, out),
        grid_spec=pltpu.PrefetchScalarGridSpec(
            num_scalar_prefetch=1,
            grid=(len(rounds) * each,),
            in_specs=[pl.BlockSpec((1, DE), lambda i, _: (0, 0))]
            + [pl.BlockSpec(memory_space=pltpu.VMEM)] * len(arrays)
            + [pl.BlockSpec(memory_space=pl.ANY)] * (2 + len(held)),
            out_specs=(out_spec, out_spec),
            scratch_shapes=[pltpu.VMEM((rows, DE), jnp.bfloat16)]
            + [pltpu.VMEM((DE, columns), jnp.bfloat16)] * 2
            + [pltpu.SemaphoreType.DMA((2 * pieces,))],
        ),
        input_output_aliases={len(operands) - len(held) + i: i for i in range(len(held))},
        compiler_params=pltpu.CompilerParams(vmem_limit_bytes=20 * MIB),
        cost_estimate=LITTLE,
        name="project",
    )(*operands)


SAME_COLUMNS = (((1,), (1,)), ((), ()))
SAME_ROWS = (((0,), (0,)), ((), ()))


def attend_kernel(slots, counts, query_ref, *refs):
    *entries, out_ref = refs
    keys, values = entries[: len(entries) // 2], entries[len(entries) // 2 :]
    together = len(keys) // KMAX
    wide = 2 * HEAD_DIM
    factor = math.log2(math.e) / math.sqrt(HEAD_DIM)
    count = [counts[pl.program_id(0) * together + g] for g in range(together)]
    work = [(g, start) for g in range(together) for start in range(0, query_ref.shape[1], wide)]

    def scored(g, start):
        query = query_ref[g * STRETCH : (g + 1) * STRETCH, start : start + wide]
        left, right = query[:, :HEAD_DIM], query[:, HEAD_DIM:]
        zero = jnp.zeros_like(left)
        both = jnp.concatenate([jnp.concatenate([left, zero], 1), jnp.concatenate([zero, right], 1)], 0)
        one, two = [
            lax.dot_general(
                keys[g * KMAX + k][0, :, start : start + wide], both, SAME_COLUMNS, preferred_element_type=jnp.float32
            )
            for k in range(KMAX)
        ]
        return one, jnp.where(count[g] == 2, two, -1e30)

    def weighed(one, two):
        top = jnp.maximum(one, two).max(0, keepdims=True)
        one, two = jnp.exp2((one - top) * factor), jnp.exp2((two - top) * factor)
        share = 1.0 / (one + two).sum(0, keepdims=True)
        return (one * share).astype(jnp.bfloat16), (two * share).astype(jnp.bfloat16)

    def mix(g, start, weights):
        rows = jnp.concatenate([values[g * KMAX + k][0, :, start : start + wide] for k in range(KMAX)], 0)
        mixed = lax.dot_general(jnp.concatenate(weights, 0), rows, SAME_ROWS, preferred_element_type=jnp.float32)
        mixed = jnp.where(count[g] > 0, mixed, 0.0).astype(jnp.bfloat16)
        rows = slice(g * STRETCH, (g + 1) * STRETCH)
        out_ref[rows, start : start + HEAD_DIM] = mixed[:STRETCH, :HEAD_DIM]
        out_ref[rows, start + HEAD_DIM : start + wide] = mixed[STRETCH:, HEAD_DIM:]

    scores = [scored(*piece) for piece in work]
    weights = [weighed(*pair) for pair in scores]
    for piece, pair in zip(work, weights):
        mix(*piece, pair)


def attend(slots, counts, queries, keys, values, together=3):
    stretches = counts.shape[0]
    columns = queries.shape[1]

    def entry(i):
        return pl.BlockSpec((1, NLEN, columns), lambda step, slots, _: (slots[step * together * KMAX + i], 0, 0))

    query_spec = pl.BlockSpec((together * STRETCH, columns), lambda i, *_: (i, 0))
    entries = [entry(i) for i in range(together * KMAX)]
    return pl.pallas_call(
        attend_kernel,
        out_shape=jax.ShapeDtypeStruct(queries.shape, jnp.bfloat16),
        grid_spec=pltpu.PrefetchScalarGridSpec(
            num_scalar_prefetch=2,
            grid=(stretches // together,),
            in_specs=[query_spec] + entries * 2,
            out_specs=query_spec,
        ),
        compiler_params=pltpu.CompilerParams(vmem_limit_bytes=60 * MIB),
        cost_estimate=LITTLE,
        name="attend",
    )(slots, counts, queries, *[keys] * len(entries), *[values] * len(entries))


def plan_kernel(place, table, plan_ref, far_ref, need_ref, lists_ref, picks_ref, slots_ref):
    f32 = jnp.float32
    groups = 2 * CHIPS
    me = place[0]
    each = table.shape[0] // groups
    lane = lax.broadcasted_iota(jnp.int32, (1, LANES), 1)

    bases = [jnp.bitwise_xor(me, group) * each for group in range(groups)]
    need = []
    for group in range(groups):
        wanted = [bases[group] + j for j in range(each - KMAX)]
        if group % CHIPS > 0:
            wanted += [bases[group - 1] + each - KMAX + k for k in range(KMAX)]
        hit = jnp.zeros((1, LANES), f32)
        for index in wanted:
            hit = jnp.where(lane == table[index], 1.0, hit)
        need.append(hit)
        need_ref[group : group + 1, :] = hit
    for part in range(2):
        for chip in range(CHIPS):
            come = (chip - (lane >> 4)) & (CHIPS - 1)
            reach = jnp.zeros((1, LANES), f32)
            for hops in range(1, CHIPS):
                there = need[part * CHIPS + (chip + hops) % CHIPS] > 0
                reach = jnp.where(there & (come + hops < CHIPS), float(hops), reach)
            row = part * CHIPS + chip
            far_ref[row : row + 1, :] = reach

    row = lax.broadcasted_iota(jnp.int32, (groups, LANES), 0)
    entry = lax.broadcasted_iota(jnp.int32, (groups, LANES), 1)
    chip, owner, slot = row & (CHIPS - 1), entry >> 4, entry & (ENTRIES_EACH - 1)
    loc = jnp.where(owner == chip, slot, -1).astype(f32)
    sent = jnp.where(owner == chip, 1.0, 0.0)
    from_behind = owner == ((chip + CHIPS - 1) & (CHIPS - 1))
    halves = [from_behind & (slot < HALF), from_behind & (slot >= HALF)]
    flights = [jnp.where(half, slot + ENTRIES_EACH, -1).astype(f32) for half in halves]
    far, needed = far_ref[...], need_ref[...]
    swept = jnp.zeros((groups, LANES), f32)
    slot_of = jnp.zeros((groups, LANES), f32)
    lists = jnp.full((groups, LANES), -1.0, f32)
    picks = jnp.full((groups, LANES), -1.0, f32)
    one, two = lax.broadcasted_iota(jnp.int32, (LANES, LANES), 0), lax.broadcasted_iota(jnp.int32, (LANES, LANES), 1)
    earlier = jnp.where(one < two, 1.0, 0.0).astype(jnp.bfloat16)
    to, source = lax.broadcasted_iota(jnp.int32, (groups, groups), 0), lax.broadcasted_iota(jnp.int32, (groups, groups), 1)
    behind = jnp.where(to & (CHIPS - 1) == 0, to + CHIPS - 1, to - 1)
    step = jnp.where(source == behind, 1.0, 0.0).astype(jnp.bfloat16)

    def ranked(mask):
        return jnp.dot(mask.astype(jnp.bfloat16), earlier, preferred_element_type=f32)

    def listed(into, taken, rank, number, cap):
        for b in range(cap):
            pick = jnp.max(jnp.where((taken > 0) & (rank == b), loc, -1.0), axis=1, keepdims=True)
            into = jnp.where(entry == number * CAP + b, pick, into)
        return into

    for number in range(SWEEPS):
        loc = jnp.maximum(loc, flights[number])
        if number == ROUNDS:
            loc = jnp.maximum(loc, flights[number + 1])
        ready = jnp.where((needed > 0) & (loc >= 0) & (swept == 0), 1.0, 0.0)
        rank = ranked(ready)
        taken = jnp.where((ready > 0) & (rank < SWEPT[number]), 1.0, 0.0)
        swept = swept + taken
        slot_of = slot_of + taken * (rank + number * CAP)
        picks = listed(picks, taken, rank, number, SWEPT[number])
        if number < ROUNDS:
            ready = jnp.where((far > 0) & (loc >= 0) & (sent == 0), 1.0, 0.0)
            rank = jnp.zeros((groups, LANES), f32)
            above = jnp.zeros((groups, 1), f32)
            for hops in range(CHIPS - 1, 0, -1):
                level = jnp.where(far == hops, ready, 0.0)
                rank = jnp.where(far == hops, ranked(level) + above, rank)
                above = above + jnp.sum(level, axis=1, keepdims=True)
            taken = jnp.where((ready > 0) & (rank < CAP), 1.0, 0.0)
            sent = sent + taken
            lists = listed(lists, taken, rank, number, CAP)
            came = jnp.dot(step, (taken * (rank + 1)).astype(jnp.bfloat16), preferred_element_type=f32)
            flights.append(jnp.where(came > 0, came + float(2 * ENTRIES_EACH + number * CAP - 1), -1.0))
    lists_ref[...] = lists
    picks_ref[...] = picks
    slots_ref[...] = slot_of
    missing = jnp.sum(jnp.where((far > 0) & (sent == 0), 1.0, 0.0)) + jnp.sum(
        jnp.where((needed > 0) & (swept == 0), 1.0, 0.0)
    )
    plan_ref[...] = jnp.zeros(plan_ref.shape, jnp.int32)
    for line, rows in enumerate((lists_ref, picks_ref, slots_ref)):
        plan_ref[line : line + 1, :] = rows[pl.ds(me, 1), :].astype(jnp.int32)
    plan_ref[3:4, :] = jnp.full((1, LANES), missing, f32).astype(jnp.int32)


def make_plan(place, table):
    return pl.pallas_call(
        plan_kernel,
        out_shape=jax.ShapeDtypeStruct((8, LANES), jnp.int32),
        in_specs=[pl.BlockSpec(memory_space=pltpu.SMEM)] * 2,
        out_specs=pl.BlockSpec(memory_space=pltpu.VMEM),
        scratch_shapes=[pltpu.VMEM((2 * CHIPS, LANES), jnp.float32)] * 5,
        name="plan",
    )(place, table)


def pack(plan, number, pool):
    lines, caps = ((0, 1), (CAP, CAP)) if number < ROUNDS else ((1,), SWEPT[-1:])
    starts = [0]
    for array in pool:
        starts.append(starts[-1] + array.shape[0])

    def kernel(plan_ref, *refs):
        sources, outs = refs[: len(pool)], refs[len(pool) :]
        for line, out in zip(lines, outs):
            for b in range(out.shape[0]):
                at = plan_ref[line * LANES + number * CAP + b]
                for source, low, high in zip(sources, starts, starts[1:]):

                    @pl.when((at >= low) & (at < high))
                    def _(source=source, low=low, out=out, b=b, at=at):
                        out[b] = source[at - low]

    in_vmem = pl.BlockSpec(memory_space=pltpu.VMEM)
    return pl.pallas_call(
        kernel,
        out_shape=tuple(jax.ShapeDtypeStruct((cap,) + pool[0].shape[1:], pool[0].dtype) for cap in caps),
        grid_spec=pltpu.PrefetchScalarGridSpec(
            num_scalar_prefetch=1, in_specs=[in_vmem] * len(pool), out_specs=(in_vmem,) * len(lines)
        ),
        compiler_params=pltpu.CompilerParams(vmem_limit_bytes=12 * MIB),
        cost_estimate=LITTLE,
        name="pack",
    )(plan, *pool)


def previous_rows(nbr_owner, nbr_slot, nbr_count):
    rows = jnp.concatenate([nbr_owner, nbr_slot, nbr_count[:, None]], axis=1)
    rows = jnp.concatenate([shifted(rows[-1:], "seq", 1), rows[:-1]], axis=0)
    return rows[:, :KMAX], rows[:, KMAX : 2 * KMAX], rows[:, 2 * KMAX]


def fetch_by_request(store, owners, slots):
    owners_axis = lax.axis_size("seq")
    stretches = owners.shape[0]
    depth = min(stretches, max(2, 2 * stretches * KMAX // owners_axis) + 1)
    owners, slots = owners.reshape(-1), slots.reshape(-1)
    order = jnp.arange(owners.shape[0], dtype=jnp.int32)
    before = (owners[:, None] == owners[None, :]) & (order[None, :] < order[:, None])
    target = owners * depth + jnp.sum(before.astype(jnp.int32), axis=1)
    hits = target[:, None] == jnp.arange(owners_axis * depth, dtype=jnp.int32)[None, :]
    table = jnp.sum(jnp.where(hits, slots[:, None], 0), axis=0).reshape(owners_axis, depth)
    asked = lax.all_to_all(table, "seq", split_axis=0, concat_axis=0, tiled=True)
    arrived = lax.all_to_all(store[asked], "seq", split_axis=0, concat_axis=0, tiled=True)
    fetched = arrived.reshape(owners_axis * depth, NLEN, store.shape[2])[target]
    return lax.all_gather(fetched, FEATURES, axis=2, tiled=True)


def onward(value):
    size = lax.axis_size("seq")
    return lax.ppermute(value, "seq", [(chip, (chip + 1) % size) for chip in range(size)])


def four_pieces(value):
    across = swapped(value, "mp")
    return [value, swapped(value, "rep"), across, swapped(across, "rep")]


def fetch_all(store, owners, slots):
    seq = lax.axis_index("seq")
    everything = [store]
    for distance in range(1, lax.axis_size("seq")):
        for steps in (distance, -distance):
            everything.append(shifted(store, "seq", steps))
    ahead = owners - seq
    place = jnp.where(ahead == 0, 0, jnp.where(ahead < 0, -2 * ahead - 1, 2 * ahead))
    pool = jnp.concatenate(everything, axis=0)
    return pool[(place * store.shape[0] + slots).reshape(-1)]


def places_of_pieces():
    block = 2 * lax.axis_index("mp") + lax.axis_index("rep")
    return jnp.stack([block ^ i for i in range(4)]).astype(jnp.int32)


def every_group(places, groups):
    return jnp.concatenate([places, jnp.ones((groups,), jnp.int32), jnp.arange(groups, dtype=jnp.int32)])


def exchanged_table(codes):
    own_part = [codes]
    for offset in range(1, CHIPS):
        own_part.append(lax.ppermute(codes, "seq", [(chip, chip ^ offset) for chip in range(CHIPS)]))
    own_part = jnp.stack(own_part)
    return jnp.concatenate([own_part, swapped(own_part, "parts")], axis=0)


def streamed(queries, key_weight, value_weight, enc_gain, store, nbr_owner, nbr_slot, nbr_count):
    stretches = nbr_owner.shape[0]
    total = stretches * KMAX
    seq = lax.axis_index("seq")
    me = lax.axis_index("parts") * CHIPS + seq
    kept = jnp.arange(KMAX, dtype=jnp.int32)[None, :] < nbr_count[:, None]
    codes = jnp.where(kept, nbr_owner * ENTRIES_EACH + nbr_slot, -1).reshape(-1)
    first, second, codes, enc_gain = lax.optimization_barrier((store[:HALF], store[HALF:], codes, enc_gain))
    table = exchanged_table(codes)
    flights = [onward(first), onward(second)]
    gain = jnp.concatenate(four_pieces(enc_gain[None]), axis=1)
    plan = make_plan(me.reshape(1).astype(jnp.int32), table.reshape(-1)).reshape(-1)
    missing = plan[3 * LANES]

    offset = jnp.where(seq > 0, (seq ^ (seq - 1)) & 3, 0)
    behind = table[offset]
    asked = jnp.concatenate([jnp.where(seq > 0, behind[total - KMAX :], -1), codes[: total - KMAX]])
    asked = asked.reshape(stretches, KMAX)
    counts = jnp.sum((asked >= 0).astype(jnp.int32), axis=1)
    first = jnp.maximum(asked[:, 0], 0)
    asked = jnp.stack([first, jnp.where(asked[:, 1] >= 0, asked[:, 1], first)], axis=1).reshape(-1)

    places = places_of_pieces()
    room = sum(SWEPT)
    wanted = plan[LANES : LANES + room].reshape(room // GROUP, GROUP)[:, 0] >= 0
    group = jnp.arange(room // GROUP, dtype=jnp.int32)
    latest = jnp.max(jnp.where((group[None, :] <= group[:, None]) & wanted[None, :], group[None, :], 0), axis=1)
    marks = jnp.concatenate([places, wanted.astype(jnp.int32), latest])
    slots = plan[2 * LANES : 3 * LANES][asked]

    pieces, held = [], ()
    for number in range(SWEEPS):
        *ways, mine = pack(plan, number, [store] + flights[: number + 1 if number < ROUNDS else None])
        flights += [onward(way) for way in ways]
        pieces.append([mine, swapped(mine, "rep"), swapped(mine, "mp")])
        if number > 0:
            pieces[number - 1].append(swapped(pieces[number - 1][2], "rep"))
        if number == SWEEPS - 2:
            ripe, pieces[number - 1][2] = lax.optimization_barrier((pieces[:2], pieces[number - 1][2]))
            held = project(marks, gain, ripe, key_weight, value_weight, GROUP, room)
        if number + 1 < SWEEPS:
            across = [parts[2] for parts in pieces[:number]] if number + 2 < SWEEPS else []
            came = slice(number + 1, number + 2 if number + 2 < SWEEPS else None)
            flights[came], across, pieces[number][1], gain, slots, marks, held = lax.optimization_barrier(
                (flights[came], across, pieces[number][1], gain, slots, marks, held)
            )
            for parts, arrived in zip(pieces, across):
                parts[2] = arrived
    ripe, _ = lax.optimization_barrier((pieces[2:-1], mine))
    held = project(marks, gain, ripe, key_weight, value_weight, GROUP, room, 2 * CAP // GROUP, held)
    late, held = lax.optimization_barrier((pieces[-1], held))
    late = [*late, swapped(late[2], "rep")]
    done = (SWEEPS - 1) * CAP // GROUP
    keys, values = project(marks, gain, [late], key_weight, value_weight, GROUP, room, done, held)

    def whole(state):
        mine = fetch_all(store, asked >> 4, asked & (ENTRIES_EACH - 1))
        marks = every_group(places, room // 4)
        keys, values = project(marks, gain, [four_pieces(mine)], key_weight, value_weight, 4, room)
        return jnp.zeros_like(state[0]), jnp.arange(total, dtype=jnp.int32), keys, values

    state = lax.while_loop(lambda state: state[0] > 0, whole, (missing, slots, keys, values))
    return attend(state[1], counts, queries, *state[2:])


def requested(queries, key_weight, value_weight, enc_gain, store, nbr_owner, nbr_slot, nbr_count):
    gain = lax.all_gather(enc_gain, FEATURES, axis=0, tiled=True)[None]
    owners, slots, counts = previous_rows(nbr_owner, nbr_slot, nbr_count)
    total = owners.size
    pieces = [fetch_by_request(store, owners, slots)]
    marks = every_group(jnp.zeros((1,), jnp.int32), total // 4)
    keys, values = project(marks, gain, [pieces], key_weight, value_weight, 4, total)
    return attend(jnp.arange(total, dtype=jnp.int32), counts, queries, keys, values)


def solution(mesh):
    in_specs = (
        P(SEQ_SPEC, FEATURES),
        P(None, FEATURES),
        P(None, FEATURES),
        P(FEATURES),
        P(SEQ_SPEC, None, FEATURES),
        P(SEQ_SPEC, None),
        P(SEQ_SPEC, None),
        P(SEQ_SPEC),
    )
    out_specs = P(SEQ_SPEC, FEATURES)
    shape = dict(mesh.shape)
    small = shape == {"parts": 2, "seq": CHIPS, "mp": 2, "rep": 2}
    body = streamed if small else requested
    return jax.shard_map(body, mesh=mesh, in_specs=in_specs, out_specs=out_specs, check_vma=False)
```

```python
import math

import jax
import jax.numpy as jnp
from jax import lax
from jax.experimental import pallas as pl
from jax.experimental.pallas import tpu as pltpu
from jax.sharding import PartitionSpec as P

HEAD_DIM = 128
DE = 1024
NLEN = 128
STRETCH = 64
KMAX = 2
EPS = 1e-06

SEQ_SPEC = ("parts", "seq")
FEATURES = ("mp", "rep")
MIB = 1024 * 1024

CHIPS = 4
ENTRIES_EACH = 16
HALF = 8
ROUNDS = 5
CAP = 4
GROUP = 2
SWEEPS = ROUNDS + 1
LARGE = 176
SWEPT = (CAP,) * ROUNDS + (2 * CAP,)
LANES = 128

LITTLE = pl.CostEstimate(flops=1, bytes_accessed=1, transcendentals=0)


def shifted(value, axis, steps):
    count = lax.axis_size(axis)
    first, last = max(0, -steps), min(count, count - steps)
    return lax.ppermute(value, axis, [(source, source + steps) for source in range(first, last)])


def swapped(value, axis):
    return lax.ppermute(value, axis, [(0, 1), (1, 0)])


def project(marks, gain, rounds, key_weight, value_weight, group, total, first=0, held=()):
    pieces = len(rounds[0])
    count, tokens, width = rounds[0][0].shape
    columns = key_weight.shape[1]
    each = count // group
    rows = group * tokens
    groups = (marks.shape[0] - pieces) // 2

    def kernel(marks_ref, gain_ref, *refs):
        arrays, weights = refs[: len(rounds) * pieces], refs[len(rounds) * pieces : len(rounds) * pieces + 2]
        *outs, normed, key_rows, value_rows, sems = refs[-6:]
        step = pl.program_id(0)
        ordered = (key_rows, value_rows)
        copies = [
            pltpu.make_async_copy(
                weight.at[pl.ds(pl.multiple_of(marks_ref[piece] * width, width), width)],
                rows_ref.at[pl.ds(piece * width, width)],
                sems.at[which * pieces + piece],
            )
            for which, (weight, rows_ref) in enumerate(zip(weights, ordered))
            for piece in range(pieces)
        ]

        @pl.when(step == 0)
        def _():
            for copy in copies:
                copy.start()

        wanted = marks_ref[pieces + first + step] > 0
        for number in range(len(rounds)):
            parts = arrays[number * pieces : (number + 1) * pieces]

            @pl.when(wanted & (step >= number * each) & (step < (number + 1) * each))
            def _(number=number, parts=parts):
                at = pl.ds((step - number * each) * group, group)
                raw = [part[at].reshape(rows, width).astype(jnp.float32) for part in parts]
                squares = sum(jnp.sum(part * part, axis=1, keepdims=True) for part in raw)
                scale = lax.rsqrt(squares / DE + EPS)
                for index, part in enumerate(raw):
                    place = slice(index * width, (index + 1) * width)
                    normed[:, place] = (part * scale * gain_ref[:, place]).astype(jnp.bfloat16)

        @pl.when(step == 0)
        def _():
            for copy in copies:
                copy.wait()

        @pl.when(wanted)
        def _():
            states = normed[...]
            for out, weight in zip(outs, ordered):
                product = jnp.dot(states, weight[...], preferred_element_type=jnp.float32)
                out[...] = product.astype(jnp.bfloat16).reshape(out.shape)

    out = jax.ShapeDtypeStruct((total, tokens, columns), jnp.bfloat16)
    out_spec = pl.BlockSpec((group, tokens, columns), lambda i, marks: (jnp.maximum(marks[pieces + groups + first + i], first), 0, 0))
    arrays = [piece for parts in rounds for piece in parts]
    operands = (marks, gain, *arrays, key_weight, value_weight, *held)
    return pl.pallas_call(
        kernel,
        out_shape=(out, out),
        grid_spec=pltpu.PrefetchScalarGridSpec(
            num_scalar_prefetch=1,
            grid=(len(rounds) * each,),
            in_specs=[pl.BlockSpec((1, DE), lambda i, _: (0, 0))]
            + [pl.BlockSpec(memory_space=pltpu.VMEM)] * len(arrays)
            + [pl.BlockSpec(memory_space=pl.ANY)] * (2 + len(held)),
            out_specs=(out_spec, out_spec),
            scratch_shapes=[pltpu.VMEM((rows, DE), jnp.bfloat16)]
            + [pltpu.VMEM((DE, columns), jnp.bfloat16)] * 2
            + [pltpu.SemaphoreType.DMA((2 * pieces,))],
        ),
        input_output_aliases={len(operands) - len(held) + i: i for i in range(len(held))},
        compiler_params=pltpu.CompilerParams(vmem_limit_bytes=20 * MIB),
        cost_estimate=LITTLE,
        name="project",
    )(*operands)


SAME_COLUMNS = (((1,), (1,)), ((), ()))
SAME_ROWS = (((0,), (0,)), ((), ()))


def attend_kernel(slots, counts, query_ref, *refs):
    *entries, out_ref = refs
    keys, values = entries[: len(entries) // 2], entries[len(entries) // 2 :]
    together = len(keys) // KMAX
    wide = 2 * HEAD_DIM
    factor = math.log2(math.e) / math.sqrt(HEAD_DIM)
    count = [counts[pl.program_id(0) * together + g] for g in range(together)]
    work = [(g, start) for g in range(together) for start in range(0, query_ref.shape[1], wide)]

    def scored(g, start):
        query = query_ref[g * STRETCH : (g + 1) * STRETCH, start : start + wide]
        left, right = query[:, :HEAD_DIM], query[:, HEAD_DIM:]
        zero = jnp.zeros_like(left)
        both = jnp.concatenate([jnp.concatenate([left, zero], 1), jnp.concatenate([zero, right], 1)], 0)
        one, two = [
            lax.dot_general(
                keys[g * KMAX + k][0, :, start : start + wide], both, SAME_COLUMNS, preferred_element_type=jnp.float32
            )
            for k in range(KMAX)
        ]
        return one, jnp.where(count[g] == 2, two, -1e30)

    def weighed(one, two):
        top = jnp.maximum(one, two).max(0, keepdims=True)
        one, two = jnp.exp2((one - top) * factor), jnp.exp2((two - top) * factor)
        share = 1.0 / (one + two).sum(0, keepdims=True)
        return (one * share).astype(jnp.bfloat16), (two * share).astype(jnp.bfloat16)

    def mix(g, start, weights):
        rows = jnp.concatenate([values[g * KMAX + k][0, :, start : start + wide] for k in range(KMAX)], 0)
        mixed = lax.dot_general(jnp.concatenate(weights, 0), rows, SAME_ROWS, preferred_element_type=jnp.float32)
        mixed = jnp.where(count[g] > 0, mixed, 0.0).astype(jnp.bfloat16)
        rows = slice(g * STRETCH, (g + 1) * STRETCH)
        out_ref[rows, start : start + HEAD_DIM] = mixed[:STRETCH, :HEAD_DIM]
        out_ref[rows, start + HEAD_DIM : start + wide] = mixed[STRETCH:, HEAD_DIM:]

    scores = [scored(*piece) for piece in work]
    weights = [weighed(*pair) for pair in scores]
    for piece, pair in zip(work, weights):
        mix(*piece, pair)


def attend(slots, counts, queries, keys, values, together=3):
    stretches = counts.shape[0]
    columns = queries.shape[1]

    def entry(i):
        return pl.BlockSpec((1, NLEN, columns), lambda step, slots, _: (slots[step * together * KMAX + i], 0, 0))

    query_spec = pl.BlockSpec((together * STRETCH, columns), lambda i, *_: (i, 0))
    entries = [entry(i) for i in range(together * KMAX)]
    return pl.pallas_call(
        attend_kernel,
        out_shape=jax.ShapeDtypeStruct(queries.shape, jnp.bfloat16),
        grid_spec=pltpu.PrefetchScalarGridSpec(
            num_scalar_prefetch=2,
            grid=(stretches // together,),
            in_specs=[query_spec] + entries * 2,
            out_specs=query_spec,
        ),
        compiler_params=pltpu.CompilerParams(vmem_limit_bytes=60 * MIB),
        cost_estimate=LITTLE,
        name="attend",
    )(slots, counts, queries, *[keys] * len(entries), *[values] * len(entries))


def plan_kernel(place, table, plan_ref, far_ref, need_ref, lists_ref, picks_ref, slots_ref):
    f32 = jnp.float32
    groups = 2 * CHIPS
    me = place[0]
    each = table.shape[0] // groups
    lane = lax.broadcasted_iota(jnp.int32, (1, LANES), 1)

    bases = [jnp.bitwise_xor(me, group) * each for group in range(groups)]
    need = []
    for group in range(groups):
        wanted = [bases[group] + j for j in range(each - KMAX)]
        if group % CHIPS > 0:
            wanted += [bases[group - 1] + each - KMAX + k for k in range(KMAX)]
        hit = jnp.zeros((1, LANES), f32)
        for index in wanted:
            hit = jnp.where(lane == table[index], 1.0, hit)
        need.append(hit)
        need_ref[group : group + 1, :] = hit
    for part in range(2):
        for chip in range(CHIPS):
            come = (chip - (lane >> 4)) & (CHIPS - 1)
            reach = jnp.zeros((1, LANES), f32)
            for hops in range(1, CHIPS):
                there = need[part * CHIPS + (chip + hops) % CHIPS] > 0
                reach = jnp.where(there & (come + hops < CHIPS), float(hops), reach)
            row = part * CHIPS + chip
            far_ref[row : row + 1, :] = reach

    row = lax.broadcasted_iota(jnp.int32, (groups, LANES), 0)
    entry = lax.broadcasted_iota(jnp.int32, (groups, LANES), 1)
    chip, owner, slot = row & (CHIPS - 1), entry >> 4, entry & (ENTRIES_EACH - 1)
    loc = jnp.where(owner == chip, slot, -1).astype(f32)
    sent = jnp.where(owner == chip, 1.0, 0.0)
    from_behind = owner == ((chip + CHIPS - 1) & (CHIPS - 1))
    halves = [from_behind & (slot < HALF), from_behind & (slot >= HALF)]
    flights = [jnp.where(half, slot + ENTRIES_EACH, -1).astype(f32) for half in halves]
    far, needed = far_ref[...], need_ref[...]
    swept = jnp.zeros((groups, LANES), f32)
    slot_of = jnp.zeros((groups, LANES), f32)
    lists = jnp.full((groups, LANES), -1.0, f32)
    picks = jnp.full((groups, LANES), -1.0, f32)
    one, two = lax.broadcasted_iota(jnp.int32, (LANES, LANES), 0), lax.broadcasted_iota(jnp.int32, (LANES, LANES), 1)
    earlier = jnp.where(one < two, 1.0, 0.0).astype(jnp.bfloat16)
    to, source = lax.broadcasted_iota(jnp.int32, (groups, groups), 0), lax.broadcasted_iota(jnp.int32, (groups, groups), 1)
    behind = jnp.where(to & (CHIPS - 1) == 0, to + CHIPS - 1, to - 1)
    step = jnp.where(source == behind, 1.0, 0.0).astype(jnp.bfloat16)

    def ranked(mask):
        return jnp.dot(mask.astype(jnp.bfloat16), earlier, preferred_element_type=f32)

    def listed(into, taken, rank, number, cap):
        for b in range(cap):
            pick = jnp.max(jnp.where((taken > 0) & (rank == b), loc, -1.0), axis=1, keepdims=True)
            into = jnp.where(entry == number * CAP + b, pick, into)
        return into

    for number in range(SWEEPS):
        loc = jnp.maximum(loc, flights[number])
        if number == ROUNDS:
            loc = jnp.maximum(loc, flights[number + 1])
        ready = jnp.where((needed > 0) & (loc >= 0) & (swept == 0), 1.0, 0.0)
        rank = ranked(ready)
        taken = jnp.where((ready > 0) & (rank < SWEPT[number]), 1.0, 0.0)
        swept = swept + taken
        slot_of = slot_of + taken * (rank + number * CAP)
        picks = listed(picks, taken, rank, number, SWEPT[number])
        if number < ROUNDS:
            ready = jnp.where((far > 0) & (loc >= 0) & (sent == 0), 1.0, 0.0)
            rank = jnp.zeros((groups, LANES), f32)
            above = jnp.zeros((groups, 1), f32)
            for hops in range(CHIPS - 1, 0, -1):
                level = jnp.where(far == hops, ready, 0.0)
                rank = jnp.where(far == hops, ranked(level) + above, rank)
                above = above + jnp.sum(level, axis=1, keepdims=True)
            taken = jnp.where((ready > 0) & (rank < CAP), 1.0, 0.0)
            sent = sent + taken
            lists = listed(lists, taken, rank, number, CAP)
            came = jnp.dot(step, (taken * (rank + 1)).astype(jnp.bfloat16), preferred_element_type=f32)
            flights.append(jnp.where(came > 0, came + float(2 * ENTRIES_EACH + number * CAP - 1), -1.0))
    lists_ref[...] = lists
    picks_ref[...] = picks
    slots_ref[...] = slot_of
    missing = jnp.sum(jnp.where((far > 0) & (sent == 0), 1.0, 0.0)) + jnp.sum(
        jnp.where((needed > 0) & (swept == 0), 1.0, 0.0)
    )
    plan_ref[...] = jnp.zeros(plan_ref.shape, jnp.int32)
    for line, rows in enumerate((lists_ref, picks_ref, slots_ref)):
        plan_ref[line : line + 1, :] = rows[pl.ds(me, 1), :].astype(jnp.int32)
    plan_ref[3:4, :] = jnp.full((1, LANES), missing, f32).astype(jnp.int32)


def make_plan(place, table):
    return pl.pallas_call(
        plan_kernel,
        out_shape=jax.ShapeDtypeStruct((8, LANES), jnp.int32),
        in_specs=[pl.BlockSpec(memory_space=pltpu.SMEM)] * 2,
        out_specs=pl.BlockSpec(memory_space=pltpu.VMEM),
        scratch_shapes=[pltpu.VMEM((2 * CHIPS, LANES), jnp.float32)] * 5,
        name="plan",
    )(place, table)


def pack(plan, number, pool):
    lines, caps = ((0, 1), (CAP, CAP)) if number < ROUNDS else ((1,), SWEPT[-1:])
    starts = [0]
    for array in pool:
        starts.append(starts[-1] + array.shape[0])

    def kernel(plan_ref, *refs):
        sources, outs = refs[: len(pool)], refs[len(pool) :]
        for line, out in zip(lines, outs):
            for b in range(out.shape[0]):
                at = plan_ref[line * LANES + number * CAP + b]
                for source, low, high in zip(sources, starts, starts[1:]):

                    @pl.when((at >= low) & (at < high))
                    def _(source=source, low=low, out=out, b=b, at=at):
                        out[b] = source[at - low]

    in_vmem = pl.BlockSpec(memory_space=pltpu.VMEM)
    return pl.pallas_call(
        kernel,
        out_shape=tuple(jax.ShapeDtypeStruct((cap,) + pool[0].shape[1:], pool[0].dtype) for cap in caps),
        grid_spec=pltpu.PrefetchScalarGridSpec(
            num_scalar_prefetch=1, in_specs=[in_vmem] * len(pool), out_specs=(in_vmem,) * len(lines)
        ),
        compiler_params=pltpu.CompilerParams(vmem_limit_bytes=12 * MIB),
        cost_estimate=LITTLE,
        name="pack",
    )(plan, *pool)


def previous_rows(nbr_owner, nbr_slot, nbr_count):
    rows = jnp.concatenate([nbr_owner, nbr_slot, nbr_count[:, None]], axis=1)
    rows = jnp.concatenate([shifted(rows[-1:], "seq", 1), rows[:-1]], axis=0)
    return rows[:, :KMAX], rows[:, KMAX : 2 * KMAX], rows[:, 2 * KMAX]


def fetch_by_request(store, owners, slots):
    owners_axis = lax.axis_size("seq")
    stretches = owners.shape[0]
    depth = min(stretches, max(2, 2 * stretches * KMAX // owners_axis) + 1)
    owners, slots = owners.reshape(-1), slots.reshape(-1)
    order = jnp.arange(owners.shape[0], dtype=jnp.int32)
    before = (owners[:, None] == owners[None, :]) & (order[None, :] < order[:, None])
    target = owners * depth + jnp.sum(before.astype(jnp.int32), axis=1)
    hits = target[:, None] == jnp.arange(owners_axis * depth, dtype=jnp.int32)[None, :]
    table = jnp.sum(jnp.where(hits, slots[:, None], 0), axis=0).reshape(owners_axis, depth)
    asked = lax.all_to_all(table, "seq", split_axis=0, concat_axis=0, tiled=True)
    arrived = lax.all_to_all(store[asked], "seq", split_axis=0, concat_axis=0, tiled=True)
    fetched = arrived.reshape(owners_axis * depth, NLEN, store.shape[2])[target]
    return lax.all_gather(fetched, FEATURES, axis=2, tiled=True)


def onward(value):
    size = lax.axis_size("seq")
    return lax.ppermute(value, "seq", [(chip, (chip + 1) % size) for chip in range(size)])


def four_pieces(value):
    across = swapped(value, "mp")
    return [value, swapped(value, "rep"), across, swapped(across, "rep")]


def fetch_all(store, owners, slots):
    seq = lax.axis_index("seq")
    everything = [store]
    for distance in range(1, lax.axis_size("seq")):
        for steps in (distance, -distance):
            everything.append(shifted(store, "seq", steps))
    ahead = owners - seq
    place = jnp.where(ahead == 0, 0, jnp.where(ahead < 0, -2 * ahead - 1, 2 * ahead))
    pool = jnp.concatenate(everything, axis=0)
    return pool[(place * store.shape[0] + slots).reshape(-1)]


def places_of_pieces():
    block = 2 * lax.axis_index("mp") + lax.axis_index("rep")
    return jnp.stack([block ^ i for i in range(4)]).astype(jnp.int32)


def every_group(places, groups):
    return jnp.concatenate([places, jnp.ones((groups,), jnp.int32), jnp.arange(groups, dtype=jnp.int32)])


def exchanged_table(codes):
    own_part = [codes]
    for offset in range(1, CHIPS):
        own_part.append(lax.ppermute(codes, "seq", [(chip, chip ^ offset) for chip in range(CHIPS)]))
    own_part = jnp.stack(own_part)
    return jnp.concatenate([own_part, swapped(own_part, "parts")], axis=0)


def streamed(queries, key_weight, value_weight, enc_gain, store, nbr_owner, nbr_slot, nbr_count):
    stretches = nbr_owner.shape[0]
    total = stretches * KMAX
    seq = lax.axis_index("seq")
    me = lax.axis_index("parts") * CHIPS + seq
    kept = jnp.arange(KMAX, dtype=jnp.int32)[None, :] < nbr_count[:, None]
    codes = jnp.where(kept, nbr_owner * ENTRIES_EACH + nbr_slot, -1).reshape(-1)
    first, second, codes, enc_gain = lax.optimization_barrier((store[:HALF], store[HALF:], codes, enc_gain))
    table = exchanged_table(codes)
    flights = [onward(first), onward(second)]
    gain = jnp.concatenate(four_pieces(enc_gain[None]), axis=1)
    plan = make_plan(me.reshape(1).astype(jnp.int32), table.reshape(-1)).reshape(-1)
    missing = plan[3 * LANES]

    offset = jnp.where(seq > 0, (seq ^ (seq - 1)) & 3, 0)
    behind = table[offset]
    asked = jnp.concatenate([jnp.where(seq > 0, behind[total - KMAX :], -1), codes[: total - KMAX]])
    asked = asked.reshape(stretches, KMAX)
    counts = jnp.sum((asked >= 0).astype(jnp.int32), axis=1)
    first = jnp.maximum(asked[:, 0], 0)
    asked = jnp.stack([first, jnp.where(asked[:, 1] >= 0, asked[:, 1], first)], axis=1).reshape(-1)

    places = places_of_pieces()
    room = sum(SWEPT)
    wanted = plan[LANES : LANES + room].reshape(room // GROUP, GROUP)[:, 0] >= 0
    group = jnp.arange(room // GROUP, dtype=jnp.int32)
    latest = jnp.max(jnp.where((group[None, :] <= group[:, None]) & wanted[None, :], group[None, :], 0), axis=1)
    marks = jnp.concatenate([places, wanted.astype(jnp.int32), latest])
    slots = plan[2 * LANES : 3 * LANES][asked]

    pieces, held = [], ()
    for number in range(SWEEPS):
        *ways, mine = pack(plan, number, [store] + flights[: number + 1 if number < ROUNDS else None])
        flights += [onward(way) for way in ways]
        pieces.append([mine, swapped(mine, "rep"), swapped(mine, "mp")])
        if number > 0:
            pieces[number - 1].append(swapped(pieces[number - 1][2], "rep"))
        if number == SWEEPS - 2:
            ripe, pieces[number - 1][2] = lax.optimization_barrier((pieces[:2], pieces[number - 1][2]))
            held = project(marks, gain, ripe, key_weight, value_weight, GROUP, LARGE)
        if number + 1 < SWEEPS:
            across = [parts[2] for parts in pieces[:number]] if number + 2 < SWEEPS else []
            came = slice(number + 1, number + 2 if number + 2 < SWEEPS else None)
            flights[came], across, pieces[number][1], gain, slots, marks, held = lax.optimization_barrier(
                (flights[came], across, pieces[number][1], gain, slots, marks, held)
            )
            for parts, arrived in zip(pieces, across):
                parts[2] = arrived
    ripe, _ = lax.optimization_barrier((pieces[2:-1], mine))
    held = project(marks, gain, ripe, key_weight, value_weight, GROUP, LARGE, 2 * CAP // GROUP, held)
    late, held = lax.optimization_barrier((pieces[-1], held))
    late = [*late, swapped(late[2], "rep")]
    done = (SWEEPS - 1) * CAP // GROUP
    keys, values = project(marks, gain, [late], key_weight, value_weight, GROUP, LARGE, done, held)

    def whole(state):
        mine = fetch_all(store, asked >> 4, asked & (ENTRIES_EACH - 1))
        marks = every_group(places, room // 4)
        keys, values = project(marks, gain, [four_pieces(mine)], key_weight, value_weight, 4, LARGE)
        return jnp.zeros_like(state[0]), jnp.arange(total, dtype=jnp.int32), keys, values

    state = lax.while_loop(lambda state: state[0] > 0, whole, (missing, slots, keys, values))
    return attend(state[1], counts, queries, *state[2:])


def requested(queries, key_weight, value_weight, enc_gain, store, nbr_owner, nbr_slot, nbr_count):
    gain = lax.all_gather(enc_gain, FEATURES, axis=0, tiled=True)[None]
    owners, slots, counts = previous_rows(nbr_owner, nbr_slot, nbr_count)
    total = owners.size
    pieces = [fetch_by_request(store, owners, slots)]
    marks = every_group(jnp.zeros((1,), jnp.int32), total // 4)
    keys, values = project(marks, gain, [pieces], key_weight, value_weight, 4, total)
    return attend(jnp.arange(total, dtype=jnp.int32), counts, queries, keys, values)


def solution(mesh):
    in_specs = (
        P(SEQ_SPEC, FEATURES),
        P(None, FEATURES),
        P(None, FEATURES),
        P(FEATURES),
        P(SEQ_SPEC, None, FEATURES),
        P(SEQ_SPEC, None),
        P(SEQ_SPEC, None),
        P(SEQ_SPEC),
    )
    out_specs = P(SEQ_SPEC, FEATURES)
    shape = dict(mesh.shape)
    small = shape == {"parts": 2, "seq": CHIPS, "mp": 2, "rep": 2}
    body = streamed if small else requested
    return jax.shard_map(body, mesh=mesh, in_specs=in_specs, out_specs=out_specs, check_vma=False)
```

```python
import math

import jax
import jax.numpy as jnp
from jax import lax
from jax.experimental import pallas as pl
from jax.experimental.pallas import tpu as pltpu
from jax.sharding import PartitionSpec as P

HEAD_DIM = 128
DE = 1024
NLEN = 128
STRETCH = 64
KMAX = 2
EPS = 1e-06

SEQ_SPEC = ("parts", "seq")
FEATURES = ("mp", "rep")
MIB = 1024 * 1024

CHIPS = 4
ENTRIES_EACH = 16
HALF = 8
ROUNDS = 5
CAP = 4
GROUP = 2
SWEEPS = ROUNDS + 1
LARGE = 176
SWEPT = (CAP,) * ROUNDS + (2 * CAP,)
LANES = 128

LITTLE = pl.CostEstimate(flops=1, bytes_accessed=1, transcendentals=0)


def shifted(value, axis, steps):
    count = lax.axis_size(axis)
    first, last = max(0, -steps), min(count, count - steps)
    return lax.ppermute(value, axis, [(source, source + steps) for source in range(first, last)])


def swapped(value, axis):
    return lax.ppermute(value, axis, [(0, 1), (1, 0)])


def project(marks, gain, rounds, key_weight, value_weight, group, total, first=0, held=()):
    pieces = len(rounds[0])
    count, tokens, width = rounds[0][0].shape
    columns = key_weight.shape[1]
    each = count // group
    rows = group * tokens
    groups = (marks.shape[0] - pieces) // 2

    def kernel(marks_ref, gain_ref, *refs):
        arrays, weights = refs[: len(rounds) * pieces], refs[len(rounds) * pieces : len(rounds) * pieces + 2]
        *outs, normed, key_rows, value_rows, sems = refs[-6:]
        step = pl.program_id(0)
        ordered = (key_rows, value_rows)
        copies = [
            pltpu.make_async_copy(
                weight.at[pl.ds(pl.multiple_of(marks_ref[piece] * width, width), width)],
                rows_ref.at[pl.ds(piece * width, width)],
                sems.at[which * pieces + piece],
            )
            for which, (weight, rows_ref) in enumerate(zip(weights, ordered))
            for piece in range(pieces)
        ]

        @pl.when(step == 0)
        def _():
            for copy in copies:
                copy.start()

        wanted = marks_ref[pieces + first + step] > 0
        for number in range(len(rounds)):
            parts = arrays[number * pieces : (number + 1) * pieces]

            @pl.when(wanted & (step >= number * each) & (step < (number + 1) * each))
            def _(number=number, parts=parts):
                at = pl.ds((step - number * each) * group, group)
                raw = [part[at].reshape(rows, width).astype(jnp.float32) for part in parts]
                squares = sum(jnp.sum(part * part, axis=1, keepdims=True) for part in raw)
                scale = lax.rsqrt(squares / DE + EPS)
                for index, part in enumerate(raw):
                    place = slice(index * width, (index + 1) * width)
                    normed[:, place] = (part * scale * gain_ref[:, place]).astype(jnp.bfloat16)

        @pl.when(step == 0)
        def _():
            for copy in copies:
                copy.wait()

        @pl.when(wanted)
        def _():
            states = normed[...]
            for out, weight in zip(outs, ordered):
                product = jnp.dot(states, weight[...], preferred_element_type=jnp.float32)
                out[...] = product.astype(jnp.bfloat16).reshape(out.shape)

    out = jax.ShapeDtypeStruct((total, tokens, columns), jnp.bfloat16)
    out_spec = pl.BlockSpec((group, tokens, columns), lambda i, marks: (jnp.maximum(marks[pieces + groups + first + i], first), 0, 0))
    arrays = [piece for parts in rounds for piece in parts]
    operands = (marks, gain, *arrays, key_weight, value_weight, *held)
    return pl.pallas_call(
        kernel,
        out_shape=(out, out),
        grid_spec=pltpu.PrefetchScalarGridSpec(
            num_scalar_prefetch=1,
            grid=(len(rounds) * each,),
            in_specs=[pl.BlockSpec((1, DE), lambda i, _: (0, 0))]
            + [pl.BlockSpec(memory_space=pltpu.VMEM)] * len(arrays)
            + [pl.BlockSpec(memory_space=pl.ANY)] * (2 + len(held)),
            out_specs=(out_spec, out_spec),
            scratch_shapes=[pltpu.VMEM((rows, DE), jnp.bfloat16)]
            + [pltpu.VMEM((DE, columns), jnp.bfloat16)] * 2
            + [pltpu.SemaphoreType.DMA((2 * pieces,))],
        ),
        input_output_aliases={len(operands) - len(held) + i: i for i in range(len(held))},
        compiler_params=pltpu.CompilerParams(vmem_limit_bytes=20 * MIB),
        cost_estimate=LITTLE,
        name="project",
    )(*operands)


SAME_COLUMNS = (((1,), (1,)), ((), ()))
SAME_ROWS = (((0,), (0,)), ((), ()))


def attend_kernel(slots, counts, query_ref, *refs):
    *entries, out_ref = refs
    keys, values = entries[: len(entries) // 2], entries[len(entries) // 2 :]
    together = len(keys) // KMAX
    wide = 2 * HEAD_DIM
    factor = math.log2(math.e) / math.sqrt(HEAD_DIM)
    count = [counts[pl.program_id(0) * together + g] for g in range(together)]
    work = [(g, start) for g in range(together) for start in range(0, query_ref.shape[1], wide)]

    def scored(g, start):
        query = query_ref[g * STRETCH : (g + 1) * STRETCH, start : start + wide]
        left, right = query[:, :HEAD_DIM], query[:, HEAD_DIM:]
        zero = jnp.zeros_like(left)
        both = jnp.concatenate([jnp.concatenate([left, zero], 1), jnp.concatenate([zero, right], 1)], 0)
        one, two = [
            lax.dot_general(
                keys[g * KMAX + k][0, :, start : start + wide], both, SAME_COLUMNS, preferred_element_type=jnp.float32
            )
            for k in range(KMAX)
        ]
        return one, jnp.where(count[g] == 2, two, -1e30)

    def weighed(one, two):
        top = jnp.maximum(one, two).max(0, keepdims=True)
        one, two = jnp.exp2((one - top) * factor), jnp.exp2((two - top) * factor)
        share = 1.0 / (one + two).sum(0, keepdims=True)
        return (one * share).astype(jnp.bfloat16), (two * share).astype(jnp.bfloat16)

    def mix(g, start, weights):
        rows = jnp.concatenate([values[g * KMAX + k][0, :, start : start + wide] for k in range(KMAX)], 0)
        mixed = lax.dot_general(jnp.concatenate(weights, 0), rows, SAME_ROWS, preferred_element_type=jnp.float32)
        mixed = jnp.where(count[g] > 0, mixed, 0.0).astype(jnp.bfloat16)
        rows = slice(g * STRETCH, (g + 1) * STRETCH)
        out_ref[rows, start : start + HEAD_DIM] = mixed[:STRETCH, :HEAD_DIM]
        out_ref[rows, start + HEAD_DIM : start + wide] = mixed[STRETCH:, HEAD_DIM:]

    scores = [scored(*piece) for piece in work]
    weights = [weighed(*pair) for pair in scores]
    for piece, pair in zip(work, weights):
        mix(*piece, pair)


def attend(slots, counts, queries, keys, values, together=3):
    stretches = counts.shape[0]
    columns = queries.shape[1]

    def entry(i):
        return pl.BlockSpec((1, NLEN, columns), lambda step, slots, _: (slots[step * together * KMAX + i], 0, 0))

    query_spec = pl.BlockSpec((together * STRETCH, columns), lambda i, *_: (i, 0))
    entries = [entry(i) for i in range(together * KMAX)]
    return pl.pallas_call(
        attend_kernel,
        out_shape=jax.ShapeDtypeStruct(queries.shape, jnp.bfloat16),
        grid_spec=pltpu.PrefetchScalarGridSpec(
            num_scalar_prefetch=2,
            grid=(stretches // together,),
            in_specs=[query_spec] + entries * 2,
            out_specs=query_spec,
        ),
        compiler_params=pltpu.CompilerParams(vmem_limit_bytes=60 * MIB),
        cost_estimate=LITTLE,
        name="attend",
    )(slots, counts, queries, *[keys] * len(entries), *[values] * len(entries))


def plan_kernel(place, table, plan_ref, far_ref, need_ref, lists_ref, picks_ref, slots_ref):
    f32 = jnp.float32
    groups = 2 * CHIPS
    me = place[0]
    each = table.shape[0] // groups
    lane = lax.broadcasted_iota(jnp.int32, (1, LANES), 1)

    bases = [jnp.bitwise_xor(me, group) * each for group in range(groups)]
    need = []
    for group in range(groups):
        wanted = [bases[group] + j for j in range(each - KMAX)]
        if group % CHIPS > 0:
            wanted += [bases[group - 1] + each - KMAX + k for k in range(KMAX)]
        hit = jnp.zeros((1, LANES), f32)
        for index in wanted:
            hit = jnp.where(lane == table[index], 1.0, hit)
        need.append(hit)
        need_ref[group : group + 1, :] = hit
    for part in range(2):
        for chip in range(CHIPS):
            come = (chip - (lane >> 4)) & (CHIPS - 1)
            reach = jnp.zeros((1, LANES), f32)
            for hops in range(1, CHIPS):
                there = need[part * CHIPS + (chip + hops) % CHIPS] > 0
                reach = jnp.where(there & (come + hops < CHIPS), float(hops), reach)
            row = part * CHIPS + chip
            far_ref[row : row + 1, :] = reach

    row = lax.broadcasted_iota(jnp.int32, (groups, LANES), 0)
    entry = lax.broadcasted_iota(jnp.int32, (groups, LANES), 1)
    chip, owner, slot = row & (CHIPS - 1), entry >> 4, entry & (ENTRIES_EACH - 1)
    loc = jnp.where(owner == chip, slot, -1).astype(f32)
    sent = jnp.where(owner == chip, 1.0, 0.0)
    from_behind = owner == ((chip + CHIPS - 1) & (CHIPS - 1))
    halves = [from_behind & (slot < HALF), from_behind & (slot >= HALF)]
    flights = [jnp.where(half, slot + ENTRIES_EACH, -1).astype(f32) for half in halves]
    far, needed = far_ref[...], need_ref[...]
    swept = jnp.zeros((groups, LANES), f32)
    slot_of = jnp.zeros((groups, LANES), f32)
    lists = jnp.full((groups, LANES), -1.0, f32)
    picks = jnp.full((groups, LANES), -1.0, f32)
    one, two = lax.broadcasted_iota(jnp.int32, (LANES, LANES), 0), lax.broadcasted_iota(jnp.int32, (LANES, LANES), 1)
    earlier = jnp.where(one < two, 1.0, 0.0).astype(jnp.bfloat16)
    to, source = lax.broadcasted_iota(jnp.int32, (groups, groups), 0), lax.broadcasted_iota(jnp.int32, (groups, groups), 1)
    behind = jnp.where(to & (CHIPS - 1) == 0, to + CHIPS - 1, to - 1)
    step = jnp.where(source == behind, 1.0, 0.0).astype(jnp.bfloat16)

    def ranked(mask):
        return jnp.dot(mask.astype(jnp.bfloat16), earlier, preferred_element_type=f32)

    def listed(into, taken, rank, number, cap):
        for b in range(cap):
            pick = jnp.max(jnp.where((taken > 0) & (rank == b), loc, -1.0), axis=1, keepdims=True)
            into = jnp.where(entry == number * CAP + b, pick, into)
        return into

    for number in range(SWEEPS):
        loc = jnp.maximum(loc, flights[number])
        if number == ROUNDS:
            loc = jnp.maximum(loc, flights[number + 1])
        ready = jnp.where((needed > 0) & (loc >= 0) & (swept == 0), 1.0, 0.0)
        rank = ranked(ready)
        taken = jnp.where((ready > 0) & (rank < SWEPT[number]), 1.0, 0.0)
        swept = swept + taken
        slot_of = slot_of + taken * (rank + number * CAP)
        picks = listed(picks, taken, rank, number, SWEPT[number])
        if number < ROUNDS:
            ready = jnp.where((far > 0) & (loc >= 0) & (sent == 0), 1.0, 0.0)
            rank = jnp.zeros((groups, LANES), f32)
            above = jnp.zeros((groups, 1), f32)
            for hops in range(CHIPS - 1, 0, -1):
                level = jnp.where(far == hops, ready, 0.0)
                rank = jnp.where(far == hops, ranked(level) + above, rank)
                above = above + jnp.sum(level, axis=1, keepdims=True)
            taken = jnp.where((ready > 0) & (rank < CAP), 1.0, 0.0)
            sent = sent + taken
            lists = listed(lists, taken, rank, number, CAP)
            came = jnp.dot(step, (taken * (rank + 1)).astype(jnp.bfloat16), preferred_element_type=f32)
            flights.append(jnp.where(came > 0, came + float(2 * ENTRIES_EACH + number * CAP - 1), -1.0))
    lists_ref[...] = lists
    picks_ref[...] = picks
    slots_ref[...] = slot_of
    missing = jnp.sum(jnp.where((far > 0) & (sent == 0), 1.0, 0.0)) + jnp.sum(
        jnp.where((needed > 0) & (swept == 0), 1.0, 0.0)
    )
    plan_ref[...] = jnp.zeros(plan_ref.shape, jnp.int32)
    for line, rows in enumerate((lists_ref, picks_ref, slots_ref)):
        plan_ref[line : line + 1, :] = rows[pl.ds(me, 1), :].astype(jnp.int32)
    plan_ref[3:4, :] = jnp.full((1, LANES), missing, f32).astype(jnp.int32)


def make_plan(place, table):
    return pl.pallas_call(
        plan_kernel,
        out_shape=jax.ShapeDtypeStruct((8, LANES), jnp.int32),
        in_specs=[pl.BlockSpec(memory_space=pltpu.SMEM)] * 2,
        out_specs=pl.BlockSpec(memory_space=pltpu.VMEM),
        scratch_shapes=[pltpu.VMEM((2 * CHIPS, LANES), jnp.float32)] * 5,
        name="plan",
    )(place, table)


def pack(plan, number, pool):
    lines, caps = ((0, 1), (CAP, CAP)) if number < ROUNDS else ((1,), SWEPT[-1:])
    starts = [0]
    for array in pool:
        starts.append(starts[-1] + array.shape[0])

    def kernel(plan_ref, *refs):
        sources, outs = refs[: len(pool)], refs[len(pool) :]
        for line, out in zip(lines, outs):
            for b in range(out.shape[0]):
                at = plan_ref[line * LANES + number * CAP + b]
                for source, low, high in zip(sources, starts, starts[1:]):

                    @pl.when((at >= low) & (at < high))
                    def _(source=source, low=low, out=out, b=b, at=at):
                        out[b] = source[at - low]

    in_vmem = pl.BlockSpec(memory_space=pltpu.VMEM)
    return pl.pallas_call(
        kernel,
        out_shape=tuple(jax.ShapeDtypeStruct((cap,) + pool[0].shape[1:], pool[0].dtype) for cap in caps),
        grid_spec=pltpu.PrefetchScalarGridSpec(
            num_scalar_prefetch=1, in_specs=[in_vmem] * len(pool), out_specs=(in_vmem,) * len(lines)
        ),
        compiler_params=pltpu.CompilerParams(vmem_limit_bytes=12 * MIB),
        cost_estimate=LITTLE,
        name="pack",
    )(plan, *pool)


def previous_rows(nbr_owner, nbr_slot, nbr_count):
    rows = jnp.concatenate([nbr_owner, nbr_slot, nbr_count[:, None]], axis=1)
    rows = jnp.concatenate([shifted(rows[-1:], "seq", 1), rows[:-1]], axis=0)
    return rows[:, :KMAX], rows[:, KMAX : 2 * KMAX], rows[:, 2 * KMAX]


def fetch_by_request(store, owners, slots):
    owners_axis = lax.axis_size("seq")
    stretches = owners.shape[0]
    depth = min(stretches, max(2, 2 * stretches * KMAX // owners_axis) + 1)
    owners, slots = owners.reshape(-1), slots.reshape(-1)
    order = jnp.arange(owners.shape[0], dtype=jnp.int32)
    before = (owners[:, None] == owners[None, :]) & (order[None, :] < order[:, None])
    target = owners * depth + jnp.sum(before.astype(jnp.int32), axis=1)
    hits = target[:, None] == jnp.arange(owners_axis * depth, dtype=jnp.int32)[None, :]
    table = jnp.sum(jnp.where(hits, slots[:, None], 0), axis=0).reshape(owners_axis, depth)
    asked = lax.all_to_all(table, "seq", split_axis=0, concat_axis=0, tiled=True)
    arrived = lax.all_to_all(store[asked], "seq", split_axis=0, concat_axis=0, tiled=True)
    fetched = arrived.reshape(owners_axis * depth, NLEN, store.shape[2])[target]
    return lax.all_gather(fetched, FEATURES, axis=2, tiled=True)


def onward(value):
    size = lax.axis_size("seq")
    return lax.ppermute(value, "seq", [(chip, (chip + 1) % size) for chip in range(size)])


def four_pieces(value):
    across = swapped(value, "mp")
    return [value, swapped(value, "rep"), across, swapped(across, "rep")]


def fetch_all(store, owners, slots):
    seq = lax.axis_index("seq")
    everything = [store]
    for distance in range(1, lax.axis_size("seq")):
        for steps in (distance, -distance):
            everything.append(shifted(store, "seq", steps))
    ahead = owners - seq
    place = jnp.where(ahead == 0, 0, jnp.where(ahead < 0, -2 * ahead - 1, 2 * ahead))
    pool = jnp.concatenate(everything, axis=0)
    return pool[(place * store.shape[0] + slots).reshape(-1)]


def places_of_pieces():
    block = 2 * lax.axis_index("mp") + lax.axis_index("rep")
    return jnp.stack([block ^ i for i in range(4)]).astype(jnp.int32)


def every_group(places, groups):
    return jnp.concatenate([places, jnp.ones((groups,), jnp.int32), jnp.arange(groups, dtype=jnp.int32)])


def exchanged_table(codes):
    own_part = [codes]
    for offset in range(1, CHIPS):
        own_part.append(lax.ppermute(codes, "seq", [(chip, chip ^ offset) for chip in range(CHIPS)]))
    own_part = jnp.stack(own_part)
    return jnp.concatenate([own_part, swapped(own_part, "parts")], axis=0)


def streamed(queries, key_weight, value_weight, enc_gain, store, nbr_owner, nbr_slot, nbr_count):
    stretches = nbr_owner.shape[0]
    total = stretches * KMAX
    seq = lax.axis_index("seq")
    me = lax.axis_index("parts") * CHIPS + seq
    kept = jnp.arange(KMAX, dtype=jnp.int32)[None, :] < nbr_count[:, None]
    codes = jnp.where(kept, nbr_owner * ENTRIES_EACH + nbr_slot, -1).reshape(-1)
    first, second, codes, enc_gain = lax.optimization_barrier((store[:HALF], store[HALF:], codes, enc_gain))
    table = exchanged_table(codes)
    flights = [onward(first), onward(second)]
    gain = jnp.concatenate(four_pieces(enc_gain[None]), axis=1)
    plan = make_plan(me.reshape(1).astype(jnp.int32), table.reshape(-1)).reshape(-1)
    missing = plan[3 * LANES]

    offset = jnp.where(seq > 0, (seq ^ (seq - 1)) & 3, 0)
    behind = table[offset]
    asked = jnp.concatenate([jnp.where(seq > 0, behind[total - KMAX :], -1), codes[: total - KMAX]])
    asked = asked.reshape(stretches, KMAX)
    counts = jnp.sum((asked >= 0).astype(jnp.int32), axis=1)
    first = jnp.maximum(asked[:, 0], 0)
    asked = jnp.stack([first, jnp.where(asked[:, 1] >= 0, asked[:, 1], first)], axis=1).reshape(-1)

    places = places_of_pieces()
    room = sum(SWEPT)
    wanted = plan[LANES : LANES + room].reshape(room // GROUP, GROUP)[:, 0] >= 0
    group = jnp.arange(room // GROUP, dtype=jnp.int32)
    latest = jnp.max(jnp.where((group[None, :] <= group[:, None]) & wanted[None, :], group[None, :], 0), axis=1)
    marks = jnp.concatenate([places, wanted.astype(jnp.int32), latest])
    slots = plan[2 * LANES : 3 * LANES][asked]

    pieces, held = [], ()
    for number in range(SWEEPS):
        *ways, mine = pack(plan, number, [store] + flights[: number + 1 if number < ROUNDS else None])
        flights += [onward(way) for way in ways]
        pieces.append([mine, swapped(mine, "rep"), swapped(mine, "mp")])
        if number > 0:
            pieces[number - 1].append(swapped(pieces[number - 1][2], "rep"))
        if number == SWEEPS - 2:
            ripe, pieces[number - 1][2] = lax.optimization_barrier((pieces[:2], pieces[number - 1][2]))
            held = project(marks, gain, ripe, key_weight, value_weight, GROUP, LARGE)
        if number + 1 < SWEEPS:
            across = [parts[2] for parts in pieces[:number]] if number + 2 < SWEEPS else []
            came = slice(number + 1, number + 2 if number + 2 < SWEEPS else None)
            flights[came], across, pieces[number][1], gain, slots, marks, counts, held = lax.optimization_barrier(
                (flights[came], across, pieces[number][1], gain, slots, marks, counts, held)
            )
            for parts, arrived in zip(pieces, across):
                parts[2] = arrived
    ripe, _ = lax.optimization_barrier((pieces[2:-1], mine))
    held = project(marks, gain, ripe, key_weight, value_weight, GROUP, LARGE, 2 * CAP // GROUP, held)
    late, held = lax.optimization_barrier((pieces[-1], held))
    late = [*late, swapped(late[2], "rep")]
    done = (SWEEPS - 1) * CAP // GROUP
    keys, values = project(marks, gain, [late], key_weight, value_weight, GROUP, LARGE, done, held)

    def whole(state):
        mine = fetch_all(store, asked >> 4, asked & (ENTRIES_EACH - 1))
        marks = every_group(places, room // 4)
        keys, values = project(marks, gain, [four_pieces(mine)], key_weight, value_weight, 4, LARGE)
        return jnp.zeros_like(state[0]), jnp.arange(total, dtype=jnp.int32), keys, values

    state = lax.while_loop(lambda state: state[0] > 0, whole, (missing, slots, keys, values))
    return attend(state[1], counts, queries, *state[2:])


def requested(queries, key_weight, value_weight, enc_gain, store, nbr_owner, nbr_slot, nbr_count):
    gain = lax.all_gather(enc_gain, FEATURES, axis=0, tiled=True)[None]
    owners, slots, counts = previous_rows(nbr_owner, nbr_slot, nbr_count)
    total = owners.size
    pieces = [fetch_by_request(store, owners, slots)]
    marks = every_group(jnp.zeros((1,), jnp.int32), total // 4)
    keys, values = project(marks, gain, [pieces], key_weight, value_weight, 4, total)
    return attend(jnp.arange(total, dtype=jnp.int32), counts, queries, keys, values)


def solution(mesh):
    in_specs = (
        P(SEQ_SPEC, FEATURES),
        P(None, FEATURES),
        P(None, FEATURES),
        P(FEATURES),
        P(SEQ_SPEC, None, FEATURES),
        P(SEQ_SPEC, None),
        P(SEQ_SPEC, None),
        P(SEQ_SPEC),
    )
    out_specs = P(SEQ_SPEC, FEATURES)
    shape = dict(mesh.shape)
    small = shape == {"parts": 2, "seq": CHIPS, "mp": 2, "rep": 2}
    body = streamed if small else requested
    return jax.shard_map(body, mesh=mesh, in_specs=in_specs, out_specs=out_specs, check_vma=False)
```
